32 devices in a mesh: lat: 4 (over y, x), lon: 8 (over z, core).
Axes of the slice: x: 2, y: 2, z: 4, core: 2. Of those that a mesh axis runs over, the one named last changes fastest.
Arguments:
- fields: bfloat16 [2, 24, 192, 512], P(None, 'lat', 'lon'), may hold values from -6 to 6
- cotangent: bfloat16 [2, 24, 192, 512], P(None, 'lat', 'lon'), may hold values from -6 to 6
- qkv_weight: bfloat16 [512, 1536], replicated, may hold values from -1 to 1, as said below
- proj_weight: bfloat16 [512, 512], replicated, may hold values from -0.25 to 0.25
Outputs:
- field_out: bfloat16 [2, 24, 192, 512], P(None, 'lat', 'lon')
- d_fields: bfloat16 [2, 24, 192, 512], P(None, 'lat', 'lon')
- qkv_grad: float32 [512, 1536], P('lon')
- proj_grad: float32 [512, 512], P(None, 'lon')
The draws below stay inside these ranges and needn't reach their ends.
Inputs may be any that keep to these rules, and one draw needn't show every extreme that they name: `qkv_weight`: projection weights for inputs of 512 features; columns in the order queries, keys, values, head by head.
All inputs are finite; a program needn't handle non-finite values.
Results may differ from the reference program's by a relative error of at most 0.015.
Values may be sent and summed in bfloat16 or wider, within the bound.
No kernel may reach another device: no remote copies, remote signals or barrier semaphores. Data moves between devices by JAX's collectives and lax.ppermute only.
A program may use at most 64 MiB of HBM per device.

```python
import jax
import jax.numpy as jnp
from jax import lax

D = 512
HEADS = 8
LEVELS = 2
WIN_LAT = 6
WIN_LON = 12
NLAT = 24
NLON = 192


def draw_qkv_weight(key, part):
    key = jax.random.fold_in(key, 7)
    key_first = jax.random.fold_in(key, 0)
    fan_scale = D ** (-0.5)
    return (jnp.clip(jax.random.normal(key_first, (D, 3 * D), jnp.float32), -6.0, 6.0) * fan_scale).astype(jnp.bfloat16)


def spiked(drawn, stream_key, source, target, blocks, factor):
    def block_of(axis_at):
        return (jnp.arange(drawn.shape[axis_at]) // (drawn.shape[axis_at] // blocks)).reshape((-1,) + (1,) * (drawn.ndim - 1 - axis_at))

    one_side = jax.random.permutation(stream_key, blocks)[block_of(target)]
    far = (block_of(target) + blocks // 2) % blocks
    return jnp.where((block_of(source) == one_side) | (block_of(source) == far), factor * drawn, drawn)


def shard_levels(key, extent, shards, smallest, high):
    gain, own = 1.0, jax.random.fold_in(key, 6)
    for dim, blocks in shards:
        steps = jnp.exp(jax.random.uniform(jax.random.fold_in(own, dim), (blocks,), jnp.float32, smallest / len(shards), high / len(shards)))
        gain = gain * jnp.repeat(steps, extent[dim] // blocks).reshape([-1 if axis == dim else 1 for axis in range(len(extent))])
    return gain


def normal_values(key, shape, scale, bound, cuts=(), held_as=jnp.bfloat16):
    values = jax.random.normal(key, shape, jnp.float32) * scale
    if len(cuts) > 0:
        values = shard_levels(key, shape, cuts, -0.22, 0.18) * values
    return jnp.clip(values, min=-bound, max=bound).astype(held_as)


def bell_draw_with(stream_key, extent, spread, bound, cuts, heavy, kind=jnp.bfloat16):
    drawn = spread * jax.random.normal(stream_key, extent, jnp.float32)
    if cuts:
        drawn = drawn * shard_levels(stream_key, extent, cuts, -0.22, 0.18)
    return jnp.clip(spiked(drawn, jax.random.fold_in(stream_key, 3), *heavy), -bound, bound).astype(kind)


def setup_inputs(seed: int = 0) -> dict:
    splits = jax.random.split(jax.random.key(seed), 5)
    fields = bell_draw_with(splits[0], (LEVELS, NLAT, NLON, D), 1.0, 6.0, ((1, 4), (2, 8)), (2, 3, 8, 2.0))
    cotangent = bell_draw_with(splits[1], (LEVELS, NLAT, NLON, D), 1.0, 6.0, ((1, 4), (2, 8)), (2, 3, 8, 2.0))
    qkv_weight = draw_qkv_weight(jax.random.fold_in(splits[4], 71), 0)
    proj_weight = normal_values(splits[3], (D, D), D ** -0.5, 0.25)
    return dict(fields=fields, cotangent=cotangent, qkv_weight=qkv_weight, proj_weight=proj_weight)


epsilon = 1e-05

def to_windows(tokens, win_lat, win_lon):
    levels, row_count, col_count, feature = tokens.shape
    shaped = tokens.reshape(levels, row_count // win_lat, win_lat, col_count // win_lon, win_lon, feature)
    shaped = shaped.transpose(1, 3, 0, 2, 4, 5)
    return shaped.reshape(-1, levels * win_lat * win_lon, feature)

def from_windows(windows, levels, row_count, col_count, win_lat, win_lon):
    feature = windows.shape[-1]
    shaped = windows.reshape(row_count // win_lat, col_count // win_lon, levels, win_lat, win_lon, feature)
    shaped = shaped.transpose(2, 0, 3, 1, 4, 5)
    return shaped.reshape(levels, row_count, col_count, feature)

def block_band(piece_in, piece_grad, region, qkv_weight, proj_weight):
    levels, row_count, col_count, feature = piece_in.shape
    head_count = HEADS
    head_size = feature // head_count
    factor = head_size ** (-0.5)
    win_size = levels * WIN_LAT * WIN_LON
    inputs_f = piece_in.astype(jnp.float32)
    token_mean = lax.optimization_barrier(jnp.mean(inputs_f, -1, keepdims=True))
    centred = inputs_f - token_mean
    variance = lax.optimization_barrier(jnp.mean(centred * centred, -1, keepdims=True))
    inv_std = lax.rsqrt(variance + epsilon)
    normed = centred * inv_std
    normed_b = normed.astype(jnp.bfloat16)
    windows = to_windows(normed_b, WIN_LAT, WIN_LON)
    win_count = windows.shape[0]
    projected = jnp.einsum('wtd,de->wte', windows.astype(jnp.float32), qkv_weight.astype(jnp.float32)).astype(jnp.bfloat16)
    split_proj = projected.reshape(win_count, win_size, 3, head_count, head_size)
    queries = split_proj[:, :, 0]
    keys_all = split_proj[:, :, 1]
    values = split_proj[:, :, 2]
    scores = jnp.einsum('wqhd,wkhd->whqk', queries.astype(jnp.float32), keys_all.astype(jnp.float32)) * factor
    region_w = to_windows(region[..., None], WIN_LAT, WIN_LON)[..., 0]
    allowed = region_w[:, None, :, None] == region_w[:, None, None, :]
    scores = jnp.where(allowed, scores, -1e+30)
    row_peak = lax.optimization_barrier(jnp.max(scores, -1, keepdims=True))
    exponent = jnp.exp(scores - row_peak)
    attn_probs = exponent / lax.optimization_barrier(jnp.sum(exponent, -1, keepdims=True))
    probs_b = attn_probs.astype(jnp.bfloat16)
    mixed = jnp.einsum('whqk,wkhd->wqhd', probs_b.astype(jnp.float32), values.astype(jnp.float32))
    mixed = mixed.astype(jnp.bfloat16).reshape(win_count, win_size, feature)
    attended = jnp.einsum('wtc,cd->wtd', mixed.astype(jnp.float32), proj_weight.astype(jnp.float32))
    attended = from_windows(attended, levels, row_count, col_count, WIN_LAT, WIN_LON)
    output = (inputs_f + attended).astype(jnp.bfloat16)
    grads_w = to_windows(piece_grad, WIN_LAT, WIN_LON).astype(jnp.float32)
    d_mixed = jnp.einsum('wtd,cd->wtc', grads_w, proj_weight.astype(jnp.float32)).astype(jnp.bfloat16)
    proj_part = jnp.einsum('wtc,wtd->cd', mixed.astype(jnp.float32), grads_w)
    d_heads = d_mixed.reshape(win_count, win_size, head_count, head_size).astype(jnp.float32)
    d_probs = jnp.einsum('wqhd,wkhd->whqk', d_heads, values.astype(jnp.float32))
    d_values = jnp.einsum('whqk,wqhd->wkhd', probs_b.astype(jnp.float32), d_heads).astype(jnp.bfloat16)
    d_scores = (attn_probs * (d_probs - lax.optimization_barrier(jnp.sum(d_probs * attn_probs, -1, keepdims=True))) * factor).astype(jnp.bfloat16)
    d_queries = jnp.einsum('whqk,wkhd->wqhd', d_scores.astype(jnp.float32), keys_all.astype(jnp.float32)).astype(jnp.bfloat16)
    d_keys = jnp.einsum('whqk,wqhd->wkhd', d_scores.astype(jnp.float32), queries.astype(jnp.float32)).astype(jnp.bfloat16)
    d_projected = jnp.concatenate([d_queries.reshape(win_count, win_size, feature), d_keys.reshape(win_count, win_size, feature), d_values.reshape(win_count, win_size, feature)], -1)
    qkv_part = jnp.einsum('wtd,wte->de', windows.astype(jnp.float32), d_projected.astype(jnp.float32))
    d_normed = jnp.einsum('wte,de->wtd', d_projected.astype(jnp.float32), qkv_weight.astype(jnp.float32))
    d_normed = from_windows(d_normed, levels, row_count, col_count, WIN_LAT, WIN_LON)
    d_inputs = piece_grad.astype(jnp.float32) + inv_std * (d_normed - lax.optimization_barrier(jnp.mean(d_normed, -1, keepdims=True)) - normed * lax.optimization_barrier(jnp.mean(d_normed * normed, -1, keepdims=True)))
    return (output, d_inputs.astype(jnp.bfloat16), qkv_part, proj_part)

def reference(fields, cotangent, qkv_weight, proj_weight):
    levels, row_count, col_count, feature = fields.shape
    half_lat = WIN_LAT // 2
    half_lon = WIN_LON // 2
    rolled = jnp.roll(fields, (-half_lat, -half_lon), axis=(1, 2))
    rolled_grad = jnp.roll(cotangent, (-half_lat, -half_lon), axis=(1, 2))
    band_count = row_count // WIN_LAT
    band_in = rolled.reshape(levels, band_count, WIN_LAT, col_count, feature).transpose(1, 0, 2, 3, 4)
    band_grad = rolled_grad.reshape(levels, band_count, WIN_LAT, col_count, feature).transpose(1, 0, 2, 3, 4)
    row_ids = jnp.arange(row_count, dtype=jnp.int32).reshape(band_count, WIN_LAT)

    def one_band(packed):
        piece_in, piece_grad, band_rows = packed
        region = (band_rows >= row_count - half_lat).astype(jnp.int32)
        region = jnp.broadcast_to(region[None, :, None], (levels, WIN_LAT, col_count))
        return block_band(piece_in, piece_grad, region, qkv_weight, proj_weight)
    outputs, d_inputs, qkv_parts, proj_parts = lax.map(one_band, (band_in, band_grad, row_ids))
    qkv_grad = lax.optimization_barrier(jnp.sum(qkv_parts, 0))
    proj_grad = lax.optimization_barrier(jnp.sum(proj_parts, 0))
    outputs = outputs.transpose(1, 0, 2, 3, 4).reshape(levels, row_count, col_count, feature)
    d_inputs = d_inputs.transpose(1, 0, 2, 3, 4).reshape(levels, row_count, col_count, feature)
    field_out = jnp.roll(outputs, (half_lat, half_lon), axis=(1, 2))
    d_fields = jnp.roll(d_inputs, (half_lat, half_lon), axis=(1, 2))
    return (field_out, d_fields, qkv_grad, proj_grad)
```

```python
import functools

import jax
import jax.numpy as jnp
from jax import lax
from jax.experimental import pallas as pl
from jax.experimental.pallas import tpu as pltpu
from jax.sharding import PartitionSpec as P

HEADS = 8
WIN_LAT = 6
WIN_LON = 12
LEVELS = 2
COLS = 24
HALF_LAT = WIN_LAT // 2
HALF_LON = WIN_LON // 2
INNER = COLS - HALF_LON
HALF = LEVELS * HALF_LAT * WIN_LON
WIN = 2 * HALF
TOKENS = 2 * WIN
LAT_ROWS = LEVELS * HALF_LAT * INNER
LON_ROWS = LEVELS * HALF_LAT * HALF_LON
LANES = 128

epsilon = 1e-05
BF = jnp.bfloat16
F32 = jnp.float32


def dot(a, b, dims):
    return lax.dot_general(a, b, (dims, ((), ())), preferred_element_type=F32)


NN = ((1,), (0,))
NT = ((1,), (1,))
TN = ((0,), (0,))


def div(x, by):
    return (x * ((65536 + by - 1) // by)) >> 16


def own_token(level, row, col):
    return level * (WIN_LAT * COLS) + row * COLS + col


def lat_piece_token(s, first):
    level = div(s, HALF_LAT * INNER)
    rest = s - level * (HALF_LAT * INNER)
    row = div(rest, INNER)
    return own_token(level, first + row, HALF_LON + rest - row * INNER)


def lon_piece_token(s, first):
    level = div(s, HALF_LAT * HALF_LON)
    rest = s - level * (HALF_LAT * HALF_LON)
    row = div(rest, HALF_LON)
    return own_token(level, first + row, rest - row * HALF_LON)


def window_sources(v):
    level = div(v, HALF_LAT * WIN_LON)
    rest = v - level * (HALF_LAT * WIN_LON)
    row = div(rest, WIN_LON)
    return level, row, rest - row * WIN_LON


def inner_window_own(v, kept):
    level, row, col = window_sources(v)
    return own_token(level, kept + row, HALF_LON + col)


def inner_window_lat(v):
    level, row, col = window_sources(v)
    return level * (HALF_LAT * INNER) + row * INNER + col


def outer_window_own(v, kept):
    level, row, col = window_sources(v)
    return jnp.where(col < HALF_LON, own_token(level, kept + row, HALF_LON + WIN_LON + col), -1)


def outer_window_lat(v):
    level, row, col = window_sources(v)
    return jnp.where(col < HALF_LON, level * (HALF_LAT * INNER) + row * INNER + WIN_LON + col, -1)


def outer_window_lon(v):
    level, row, col = window_sources(v)
    return jnp.where(col < HALF_LON, -1, level * (HALF_LAT * HALF_LON) + row * HALF_LON + col - HALF_LON)


def picks(source, rows, columns):
    index = source(lax.broadcasted_iota(jnp.int32, (rows, 1), 0))
    return (index == lax.broadcasted_iota(jnp.int32, (rows, columns), 1)).astype(BF)


def puts(source, rows, columns):
    index = source(lax.broadcasted_iota(jnp.int32, (1, columns), 1))
    return (lax.broadcasted_iota(jnp.int32, (rows, columns), 0) == index).astype(BF)


def pack_kernel(fields, cotangent, lat_out, lon_out, diag_out):
    even = lax.rem(lax.axis_index("lon"), 2) == 0
    sent = jnp.where(even, 0, HALF_LAT)
    kept = HALF_LAT - sent
    for out, pick in (
        (lat_out, picks(lambda s: lat_piece_token(s, sent), LAT_ROWS, TOKENS)),
        (lon_out, picks(lambda s: lon_piece_token(s, sent), LON_ROWS, TOKENS)),
        (diag_out, picks(lambda s: lon_piece_token(s, kept), LON_ROWS, TOKENS)),
    ):
        width = fields.shape[1]
        out[:, :width] = dot(pick, fields[...], NN).astype(BF)
        out[:, width:] = dot(pick, cotangent[...], NN).astype(BF)


def normalise(x):
    mean = jnp.mean(x, -1, keepdims=True)
    centred = x - mean
    variance = jnp.mean(centred * centred, -1, keepdims=True)
    inv_std = lax.rsqrt(variance + epsilon)
    return centred * inv_std, inv_std


def shares(transposed, lon_size, core):
    rows, tokens = transposed.shape
    by_core = transposed.reshape(lon_size // 2, 2, rows // lon_size, tokens)
    first = by_core[:, 0].reshape(rows // 2, tokens)
    second = by_core[:, 1].reshape(rows // 2, tokens)
    return jnp.where(core == 0, first, second), jnp.where(core == 0, second, first)


def transpose_bf16(block):
    return jnp.transpose(block.astype(F32)).astype(BF)


def put_split(out, lanes_from, block):
    width = out.shape[-1]
    for at in range(0, block.shape[1], width):
        out[(lanes_from + at) // width] = block[:, at : at + width].astype(out.dtype)


def attention_kernel(
    fields, cotangent, lat_in, lon_in, diag_in, qkv_weight, proj_weight,
    send_grad, windows_out, grads_out, normed_t_out, grads_t_out, d_projected, mixed,
):
    width = fields.shape[1]
    lat, lon = lax.axis_index("lat"), lax.axis_index("lon")
    lat_size, lon_size = lax.axis_size("lat"), lax.axis_size("lon")
    core = lax.rem(lon, 2)
    even = core == 0
    kept = jnp.where(even, HALF_LAT, 0)
    blocks = []
    for source, mine in ((0, fields), (1, cotangent)):
        lanes = slice(source * width, (source + 1) * width)
        blocks.append(
            jnp.concatenate(
                [
                    dot(picks(lambda v: inner_window_own(v, kept), HALF, TOKENS), mine[...], NN),
                    dot(picks(inner_window_lat, HALF, LAT_ROWS), lat_in[:, lanes], NN),
                    dot(picks(lambda v: outer_window_own(v, kept), HALF, TOKENS), mine[...], NN)
                    + dot(picks(outer_window_lon, HALF, LON_ROWS), lon_in[:, lanes], NN),
                    dot(picks(outer_window_lat, HALF, LAT_ROWS), lat_in[:, lanes], NN)
                    + dot(picks(outer_window_lon, HALF, LON_ROWS), diag_in[:, lanes], NN),
                ],
                axis=0,
            )
        )
    x = blocks[0]
    windows_out[...] = x.astype(BF)
    grads = blocks[1].astype(BF)
    grads_out[...] = grads
    normed, _ = normalise(x)
    normed_b = normed.astype(BF)
    projected = dot(normed_b, qkv_weight[...], NN).astype(BF)
    d_mixed = dot(grads, proj_weight[...], NT).astype(BF)

    head_size = width // HEADS
    factor = head_size ** (-0.5)
    apart = jnp.where(even, lat == lat_size - 1, lat == 0).astype(jnp.int32)
    half_b = (lax.broadcasted_iota(jnp.int32, (WIN, 2 * WIN), 0) >= HALF).astype(jnp.int32)
    at_a = lax.broadcasted_iota(jnp.int32, (WIN, 2 * WIN), 1)
    at_a = jnp.where(at_a >= WIN, at_a - WIN, at_a)
    half_a = (at_a >= HALF).astype(jnp.int32)
    allowed = ((half_a != half_b).astype(jnp.int32) * apart) == 0
    first_head = lax.broadcasted_iota(jnp.int32, (WIN, LANES), 1) < head_size
    zero = jnp.zeros((WIN, LANES), BF)

    def split_heads(block):
        return jnp.concatenate([jnp.where(first_head, block, zero), jnp.where(first_head, zero, block)], axis=0)

    def join_heads(block):
        return jnp.where(first_head, block[:WIN], block[WIN:]).astype(BF)

    for window in range(TOKENS // WIN):
        rows = slice(window * WIN, (window + 1) * WIN)
        for pair in range(width // LANES):
            at = pair * LANES
            q = projected[rows, at : at + LANES]
            k = projected[rows, width + at : width + at + LANES]
            v = projected[rows, 2 * width + at : 2 * width + at + LANES]
            dm = d_mixed[rows, at : at + LANES]
            q2, dm2 = split_heads(q), split_heads(dm)
            scores = dot(k, q2, NT) * factor
            scores = jnp.where(allowed, scores, -1e30)
            exponent = jnp.exp(scores - jnp.max(scores, 0, keepdims=True))
            probs = exponent * (1.0 / jnp.sum(exponent, 0, keepdims=True))
            probs_b = probs.astype(BF)
            mixed[rows, at : at + LANES] = join_heads(dot(probs_b, v, TN))
            d_probs = dot(v, dm2, NT)
            d_projected[rows, 2 * width + at : 2 * width + at + LANES] = dot(probs_b, dm2, NN).astype(BF)
            d_scores = probs * (d_probs - jnp.sum(d_probs * probs, 0, keepdims=True)) * factor
            d_scores = d_scores.astype(BF)
            d_projected[rows, at : at + LANES] = join_heads(dot(d_scores, k, TN))
            d_projected[rows, width + at : width + at + LANES] = dot(d_scores, q2, NN).astype(BF)

    normed_t = transpose_bf16(normed)
    grads_t = transpose_bf16(grads)
    normed_keep, normed_send = shares(normed_t, lon_size, core)
    grads_keep, grads_send = shares(grads_t, lon_size, core)
    normed_t_out[...] = normed_keep
    grads_t_out[...] = grads_keep
    put_split(send_grad, 0, dot(normed_send, d_projected[...], NN))
    put_split(send_grad, 3 * width, dot(grads_send, mixed[...], NN))


def output_kernel(
    windows, grads, normed_t, grads_t, d_projected, mixed, qkv_weight, proj_weight,
    keep_grad, results, lat_out, lon_out, diag_out,
):
    width = windows.shape[1]
    put_split(keep_grad, 0, dot(normed_t[...], d_projected[...], NN))
    put_split(keep_grad, 3 * width, dot(grads_t[...], mixed[...], NN))
    x = windows[...].astype(F32)
    normed, inv_std = normalise(x)
    output = (x + dot(mixed[...], proj_weight[...], NN)).astype(BF)
    d_normed = dot(d_projected[...], qkv_weight[...], NT)
    d_inputs = grads[...].astype(F32) + inv_std * (
        d_normed
        - jnp.mean(d_normed, -1, keepdims=True)
        - normed * jnp.mean(d_normed * normed, -1, keepdims=True)
    )
    results[:, :width] = output
    results[:, width:] = d_inputs.astype(BF)
    inner_y = slice(HALF, WIN)
    outer_x = slice(WIN, WIN + HALF)
    outer_y = slice(WIN + HALF, TOKENS)
    total = jnp.concatenate([output.astype(F32), d_inputs.astype(BF).astype(F32)], axis=1)
    y_inner = total[inner_y].astype(BF)
    y_outer = total[outer_y].astype(BF)
    x_outer = total[outer_x].astype(BF)
    lat_out[...] = (
        dot(puts(inner_window_lat, LAT_ROWS, HALF), y_inner, NN)
        + dot(puts(outer_window_lat, LAT_ROWS, HALF), y_outer, NN)
    ).astype(BF)
    lon_out[...] = dot(puts(outer_window_lon, LON_ROWS, HALF), x_outer, NN).astype(BF)
    diag_out[...] = dot(puts(outer_window_lon, LON_ROWS, HALF), y_outer, NN).astype(BF)


def place_kernel(results, lat_in, lon_in, diag_in, field_out, d_fields):
    width = field_out.shape[1]
    even = lax.rem(lax.axis_index("lon"), 2) == 0
    sent = jnp.where(even, 0, HALF_LAT)
    kept = HALF_LAT - sent
    put_lat = puts(lambda s: lat_piece_token(s, sent), TOKENS, LAT_ROWS)
    put_lon = puts(lambda s: lon_piece_token(s, sent), TOKENS, LON_ROWS)
    put_diag = puts(lambda s: lon_piece_token(s, kept), TOKENS, LON_ROWS)

    def own(t):
        window = (t >= WIN).astype(jnp.int32)
        u = t - window * WIN
        inner = inner_window_own(u, kept)
        outer = outer_window_own(u, kept)
        return jnp.where(u < HALF, jnp.where(window == 0, inner, outer), -1)

    put_own = puts(own, TOKENS, TOKENS)
    for index, out in ((0, field_out), (1, d_fields)):
        lanes = slice(index * width, (index + 1) * width)
        out[...] = (
            dot(put_own, results[:, lanes], NN)
            + dot(put_lat, lat_in[:, lanes], NN)
            + dot(put_lon, lon_in[:, lanes], NN)
            + dot(put_diag, diag_in[:, lanes], NN)
        ).astype(BF)


def add_kernel(a, b, out):
    out[...] = (a[...].astype(F32) + b[...].astype(F32)).astype(out.dtype)


def sum_kernel(parts, out):
    total = parts[0].astype(F32)
    for index in range(1, parts.shape[0]):
        total = total + parts[index].astype(F32)
    out[...] = total.astype(out.dtype)


def finish_kernel(parts, qkv_out, proj_out):
    width = proj_out.shape[0]
    total = jnp.concatenate([parts[i].astype(F32) for i in range(parts.shape[0])], axis=1)
    qkv_out[...] = total[:, : 3 * width]
    proj_out[...] = jnp.transpose(total[:, 3 * width :])


def call(kernel, outs, *args, name, flops=0, limit=32):
    vmem = pl.BlockSpec(memory_space=pltpu.VMEM)
    shapes = [jax.ShapeDtypeStruct(shape, dtype) for shape, dtype in outs]
    nbytes = sum(a.size * a.dtype.itemsize for a in (*args, *shapes))
    return pl.pallas_call(
        kernel,
        out_shape=shapes,
        in_specs=[vmem] * len(args),
        out_specs=[vmem] * len(shapes),
        compiler_params=pltpu.CompilerParams(vmem_limit_bytes=limit * 2**20),
        cost_estimate=pl.CostEstimate(flops=flops, bytes_accessed=nbytes, transcendentals=0),
        name=name,
    )(*args)


def routes(lat_size, lon_size):
    lat, lon, diag = [], [], []
    for i in range(lat_size):
        for j in range(lon_size):
            step = -1 if j % 2 == 0 else 1
            before = (j - 1) % lon_size
            me = i * lon_size + j
            lat.append((me, ((i + step) % lat_size) * lon_size + j))
            lon.append((me, i * lon_size + before))
            diag.append((me, ((i - step) % lat_size) * lon_size + before))
    return lat, lon, diag


def per_device(fields, cotangent, qkv_weight, proj_weight):
    levels, row_count, col_count, width = fields.shape
    lat_size, lon_size = lax.axis_size("lat"), lax.axis_size("lon")
    both = ("lat", "lon")
    lat_route, lon_route, diag_route = routes(lat_size, lon_size)

    def back(route):
        return [(target, source) for source, target in route]

    own_fields = fields.reshape(TOKENS, width)
    own_grads = cotangent.reshape(TOKENS, width)
    piece = [((LAT_ROWS, 2 * width), BF), ((LON_ROWS, 2 * width), BF), ((LON_ROWS, 2 * width), BF)]
    lat_piece, lon_piece, diag_piece = call(pack_kernel, piece, own_fields, own_grads, name="pack")
    lat_in = lax.ppermute(lat_piece, both, lat_route)
    diag_in = lax.ppermute(diag_piece, both, diag_route)
    lon_in = lax.ppermute(lon_piece, both, lon_route)

    split = (lat_size, width // 2, 4 * width // lat_size)
    send_grad, windows, grads, normed_t, grads_t, d_projected, mixed = call(
        attention_kernel,
        [
            (split, BF),
            ((TOKENS, width), BF),
            ((TOKENS, width), BF),
            ((width // 2, TOKENS), BF),
            ((width // 2, TOKENS), BF),
            ((TOKENS, 3 * width), BF),
            ((TOKENS, width), BF),
        ],
        own_fields, own_grads, lat_in, lon_in, diag_in, qkv_weight, proj_weight,
        name="attention", flops=2 * 10**9,
    )
    sibling = [(j, j ^ 1) for j in range(lon_size)]
    received = lax.ppermute(send_grad, "lon", sibling)
    keep_grad, results, lat_back, lon_back, diag_back = call(
        output_kernel,
        [(split, BF), ((TOKENS, 2 * width), BF), *piece],
        windows, grads, normed_t, grads_t, d_projected, mixed, qkv_weight, proj_weight,
        name="outputs", flops=10**9,
    )
    lat_home = lax.ppermute(lat_back, both, back(lat_route))
    diag_home = lax.ppermute(diag_back, both, back(diag_route))
    lon_home = lax.ppermute(lon_back, both, back(lon_route))

    (chip_sum,) = call(add_kernel, [(split, BF)], keep_grad, received, name="chip_sum")
    plane = lax.all_to_all(chip_sum, "lat", 0, 0)
    (plane_sum,) = call(sum_kernel, [(split[1:], BF)], plane, name="plane_sum")
    rows = width // lon_size
    by_chip = plane_sum.reshape(lon_size // 2, rows, split[2])
    groups = [list(range(core, lon_size, 2)) for core in range(2)]
    line = lax.all_to_all(by_chip, "lon", 0, 0, axis_index_groups=groups)
    (line_sum,) = call(sum_kernel, [((rows, split[2]), BF)], line, name="line_sum")
    shared = lax.all_to_all(jnp.broadcast_to(line_sum[None], (lat_size, rows, split[2])), "lat", 0, 0)
    field_out, d_fields = call(
        place_kernel,
        [((TOKENS, width), BF), ((TOKENS, width), BF)],
        results, lat_home, lon_home, diag_home,
        name="place",
    )
    qkv_grad, proj_grad = call(
        finish_kernel, [((rows, 3 * width), F32), ((width, rows), F32)], shared, name="finish"
    )
    return (field_out.reshape(fields.shape), d_fields.reshape(fields.shape), qkv_grad, proj_grad)


def solution(mesh):
    placed = (P(None, "lat", "lon", None), P(None, "lat", "lon", None), P(), P())
    return jax.shard_map(
        per_device,
        mesh=mesh,
        in_specs=placed,
        out_specs=(
            P(None, "lat", "lon", None),
            P(None, "lat", "lon", None),
            P("lon", None),
            P(None, "lon"),
        ),
        check_vma=False,
    )
```

```python
import functools

import jax
import jax.numpy as jnp
from jax import lax
from jax.experimental import pallas as pl
from jax.experimental.pallas import tpu as pltpu
from jax.sharding import PartitionSpec as P

HEADS = 8
WIN_LAT = 6
WIN_LON = 12
LEVELS = 2
COLS = 24
HALF_LAT = WIN_LAT // 2
HALF_LON = WIN_LON // 2
INNER = COLS - HALF_LON
HALF = LEVELS * HALF_LAT * WIN_LON
WIN = 2 * HALF
TOKENS = 2 * WIN
LAT_ROWS = LEVELS * HALF_LAT * INNER
LON_ROWS = LEVELS * HALF_LAT * HALF_LON
LANES = 128

epsilon = 1e-05
BF = jnp.bfloat16
F32 = jnp.float32


def dot(a, b, dims):
    return lax.dot_general(a, b, (dims, ((), ())), preferred_element_type=F32)


NN = ((1,), (0,))
NT = ((1,), (1,))
TN = ((0,), (0,))


def div(x, by):
    return (x * ((65536 + by - 1) // by)) >> 16


def own_token(level, row, col):
    return level * (WIN_LAT * COLS) + row * COLS + col


def lat_piece_token(s, first):
    level = div(s, HALF_LAT * INNER)
    rest = s - level * (HALF_LAT * INNER)
    row = div(rest, INNER)
    return own_token(level, first + row, HALF_LON + rest - row * INNER)


def lon_piece_token(s, first):
    level = div(s, HALF_LAT * HALF_LON)
    rest = s - level * (HALF_LAT * HALF_LON)
    row = div(rest, HALF_LON)
    return own_token(level, first + row, rest - row * HALF_LON)


def window_sources(v):
    level = div(v, HALF_LAT * WIN_LON)
    rest = v - level * (HALF_LAT * WIN_LON)
    row = div(rest, WIN_LON)
    return level, row, rest - row * WIN_LON


def inner_window_own(v, kept):
    level, row, col = window_sources(v)
    return own_token(level, kept + row, HALF_LON + col)


def inner_window_lat(v):
    level, row, col = window_sources(v)
    return level * (HALF_LAT * INNER) + row * INNER + col


def outer_window_own(v, kept):
    level, row, col = window_sources(v)
    return jnp.where(col < HALF_LON, own_token(level, kept + row, HALF_LON + WIN_LON + col), -1)


def outer_window_lat(v):
    level, row, col = window_sources(v)
    return jnp.where(col < HALF_LON, level * (HALF_LAT * INNER) + row * INNER + WIN_LON + col, -1)


def outer_window_lon(v):
    level, row, col = window_sources(v)
    return jnp.where(col < HALF_LON, -1, level * (HALF_LAT * HALF_LON) + row * HALF_LON + col - HALF_LON)


def picks(source, rows, columns):
    index = source(lax.broadcasted_iota(jnp.int32, (rows, 1), 0))
    return (index == lax.broadcasted_iota(jnp.int32, (rows, columns), 1)).astype(BF)


def puts(source, rows, columns):
    index = source(lax.broadcasted_iota(jnp.int32, (1, columns), 1))
    return (lax.broadcasted_iota(jnp.int32, (rows, columns), 0) == index).astype(BF)


def pack_kernel(fields_hbm, cotangent_hbm, lat_out, lon_out, diag_out, own_out, fields, cotangent, arrived):
    loads = [
        pltpu.make_async_copy(fields_hbm, fields, arrived.at[0]),
        pltpu.make_async_copy(cotangent_hbm, cotangent, arrived.at[1]),
    ]
    for load in loads:
        load.start()
    even = lax.rem(lax.axis_index("lon"), 2) == 0
    sent = jnp.where(even, 0, HALF_LAT)
    kept = HALF_LAT - sent
    width = fields.shape[1]
    moves = (
        (lat_out, 0, picks(lambda s: lat_piece_token(s, sent), LAT_ROWS, TOKENS)),
        (lon_out, 0, picks(lambda s: lon_piece_token(s, sent), LON_ROWS, TOKENS)),
        (diag_out, 0, picks(lambda s: lon_piece_token(s, kept), LON_ROWS, TOKENS)),
        (own_out, 0, picks(lambda v: inner_window_own(v, kept), HALF, TOKENS)),
        (own_out, 1, picks(lambda v: outer_window_own(v, kept), HALF, TOKENS)),
    )
    for load in loads:
        load.wait()
    for out, half, pick in moves:
        rows = slice(half * HALF, half * HALF + pick.shape[0])
        out[rows, :width] = dot(pick, fields[...], NN).astype(out.dtype)
        out[rows, width:] = dot(pick, cotangent[...], NN).astype(out.dtype)


def weights_kernel(_, qkv_hbm, proj_hbm, qkv_weight, proj_weight, arrived):
    loads = [
        pltpu.make_async_copy(qkv_hbm, qkv_weight, arrived.at[0]),
        pltpu.make_async_copy(proj_hbm, proj_weight, arrived.at[1]),
    ]
    for load in loads:
        load.start()
    for load in loads:
        load.wait()


def normalise(x):
    mean = jnp.mean(x, -1, keepdims=True)
    centred = x - mean
    variance = jnp.mean(centred * centred, -1, keepdims=True)
    inv_std = lax.rsqrt(variance + epsilon)
    return centred * inv_std, inv_std


def swap_bits(index, size, core):
    bits = size.bit_length() - 1
    turned = sum(((index >> b) & 1) << (bits - 1 - b) for b in range(bits))
    return jnp.where(core == 0, index, turned)


def shares(transposed, out, lon, core_of, lon_size):
    rows = transposed.shape[0] // lon_size
    chip = lon >> 1
    for step in range(lon_size // 2):
        start = pl.multiple_of(((chip ^ step) * 2 + core_of) * rows, rows)
        out[step * rows : (step + 1) * rows, :] = transposed[pl.ds(start, rows), :]


def transpose_bf16(block):
    return jnp.transpose(block.astype(F32)).astype(BF)


def put_split(out, lanes_from, block, lat, core):
    size, _, width = out.shape
    for at in range(0, block.shape[1], width):
        slot = swap_bits(lat ^ ((lanes_from + at) // width), size, core)
        out[slot] = block[:, at : at + width].astype(out.dtype)


def attention_kernel(
    own, lat_in, lon_in, diag_in, qkv_weight, proj_weight,
    send_grad, windows_out, grads_out, normed_t_out, grads_t_out, d_projected, mixed, normed_t, grads_t, send_rows,
):
    width = own.shape[1] // 2
    lat, lon = lax.axis_index("lat"), lax.axis_index("lon")
    lat_size, lon_size = lax.axis_size("lat"), lax.axis_size("lon")
    core = lax.rem(lon, 2)
    even = core == 0
    outer_lon = picks(outer_window_lon, HALF, LON_ROWS)
    both = jnp.concatenate(
        [
            own[:HALF],
            dot(picks(inner_window_lat, HALF, LAT_ROWS), lat_in[...], NN),
            own[HALF:] + dot(outer_lon, lon_in[...], NN),
            dot(picks(outer_window_lat, HALF, LAT_ROWS), lat_in[...], NN) + dot(outer_lon, diag_in[...], NN),
        ],
        axis=0,
    )
    blocks = both[:, :width], both[:, width:]
    x = blocks[0]
    windows_out[...] = x.astype(BF)
    grads = blocks[1].astype(BF)
    grads_out[...] = grads
    normed, _ = normalise(x)
    normed_b = normed.astype(BF)
    projected = dot(normed_b, qkv_weight[...], NN).astype(BF)
    d_mixed = dot(grads, proj_weight[...], NT).astype(BF)

    head_size = width // HEADS
    factor = head_size ** (-0.5)
    apart = jnp.where(even, lat == lat_size - 1, lat == 0).astype(jnp.int32)
    half_b = (lax.broadcasted_iota(jnp.int32, (WIN, 2 * WIN), 0) >= HALF).astype(jnp.int32)
    at_a = lax.broadcasted_iota(jnp.int32, (WIN, 2 * WIN), 1)
    at_a = jnp.where(at_a >= WIN, at_a - WIN, at_a)
    half_a = (at_a >= HALF).astype(jnp.int32)
    allowed = ((half_a != half_b).astype(jnp.int32) * apart) == 0
    first_head = lax.broadcasted_iota(jnp.int32, (WIN, LANES), 1) < head_size
    zero = jnp.zeros((WIN, LANES), BF)

    def split_heads(block):
        return jnp.concatenate([jnp.where(first_head, block, zero), jnp.where(first_head, zero, block)], axis=0)

    def join_heads(block):
        return jnp.where(first_head, block[:WIN], block[WIN:]).astype(BF)

    for window in range(TOKENS // WIN):
        rows = slice(window * WIN, (window + 1) * WIN)
        for pair in range(width // LANES):
            at = pair * LANES
            q = projected[rows, at : at + LANES]
            k = projected[rows, width + at : width + at + LANES]
            v = projected[rows, 2 * width + at : 2 * width + at + LANES]
            dm = d_mixed[rows, at : at + LANES]
            q2, dm2 = split_heads(q), split_heads(dm)
            scores = dot(k, q2, NT) * factor
            scores = jnp.where(allowed, scores, -1e30)
            exponent = jnp.exp(scores - jnp.max(scores, 0, keepdims=True))
            probs = exponent * (1.0 / jnp.sum(exponent, 0, keepdims=True))
            probs_b = probs.astype(BF)
            mixed[rows, at : at + LANES] = join_heads(dot(probs_b, v, TN))
            d_probs = dot(v, dm2, NT)
            d_projected[rows, 2 * width + at : 2 * width + at + LANES] = dot(probs_b, dm2, NN).astype(BF)
            d_scores = probs * (d_probs - jnp.sum(d_probs * probs, 0, keepdims=True)) * factor
            d_scores = d_scores.astype(BF)
            d_projected[rows, at : at + LANES] = join_heads(dot(d_scores, k, TN))
            d_projected[rows, width + at : width + at + LANES] = dot(d_scores, q2, NN).astype(BF)

    normed_t[...] = transpose_bf16(normed)
    grads_t[...] = transpose_bf16(grads)
    shares(normed_t, send_rows, lon, 1 - core, lon_size)
    put_split(send_grad, 0, dot(send_rows[...], d_projected[...], NN), lat, 1 - core)
    shares(grads_t, send_rows, lon, 1 - core, lon_size)
    put_split(send_grad, 3 * width, dot(send_rows[...], mixed[...], NN), lat, 1 - core)
    shares(normed_t, normed_t_out, lon, core, lon_size)
    shares(grads_t, grads_t_out, lon, core, lon_size)


def output_kernel(
    windows, grads, normed_t, grads_t, d_projected, mixed, qkv_weight, proj_weight, keep_grad, results
):
    width = windows.shape[1]
    lat, core = lax.axis_index("lat"), lax.rem(lax.axis_index("lon"), 2)
    put_split(keep_grad, 0, dot(normed_t[...], d_projected[...], NN), lat, core)
    put_split(keep_grad, 3 * width, dot(grads_t[...], mixed[...], NN), lat, core)
    x = windows[...].astype(F32)
    normed, inv_std = normalise(x)
    output = (x + dot(mixed[...], proj_weight[...], NN)).astype(BF)
    d_normed = dot(d_projected[...], qkv_weight[...], NT)
    d_inputs = grads[...].astype(F32) + inv_std * (
        d_normed
        - jnp.mean(d_normed, -1, keepdims=True)
        - normed * jnp.mean(d_normed * normed, -1, keepdims=True)
    )
    results[:, :width] = output
    results[:, width:] = d_inputs.astype(BF)


def pack_back_kernel(_, results, lat_out, lon_out, diag_out):
    total = results[...].astype(F32)
    y_inner = total[HALF:WIN].astype(BF)
    x_outer = total[WIN : WIN + HALF].astype(BF)
    y_outer = total[WIN + HALF :].astype(BF)
    lat_out[...] = (
        dot(puts(inner_window_lat, LAT_ROWS, HALF), y_inner, NN)
        + dot(puts(outer_window_lat, LAT_ROWS, HALF), y_outer, NN)
    ).astype(BF)
    put_lon = puts(outer_window_lon, LON_ROWS, HALF)
    lon_out[...] = dot(put_lon, x_outer, NN).astype(BF)
    diag_out[...] = dot(put_lon, y_outer, NN).astype(BF)


def place_kernel(results, lat_in, lon_in, diag_in, field_out, d_fields):
    width = field_out.shape[1]
    even = lax.rem(lax.axis_index("lon"), 2) == 0
    sent = jnp.where(even, 0, HALF_LAT)
    kept = HALF_LAT - sent
    put_lat = puts(lambda s: lat_piece_token(s, sent), TOKENS, LAT_ROWS)
    put_lon = puts(lambda s: lon_piece_token(s, sent), TOKENS, LON_ROWS)
    put_diag = puts(lambda s: lon_piece_token(s, kept), TOKENS, LON_ROWS)

    def own(t):
        window = (t >= WIN).astype(jnp.int32)
        u = t - window * WIN
        inner = inner_window_own(u, kept)
        outer = outer_window_own(u, kept)
        return jnp.where(u < HALF, jnp.where(window == 0, inner, outer), -1)

    put_own = puts(own, TOKENS, TOKENS)
    for index, out in ((0, field_out), (1, d_fields)):
        lanes = slice(index * width, (index + 1) * width)
        out[...] = (
            dot(put_own, results[:, lanes], NN)
            + dot(put_lat, lat_in[:, lanes], NN)
            + dot(put_lon, lon_in[:, lanes], NN)
            + dot(put_diag, diag_in[:, lanes], NN)
        ).astype(BF)


def halve_kernel(kept, received, send, keep):
    for slot in range(send.shape[0]):
        for out, source in ((send, 2 * slot + 1), (keep, 2 * slot)):
            out[slot] = (kept[source].astype(F32) + received[source].astype(F32)).astype(BF)


def line_parts_kernel(kept, received, keep, *sends):
    rows = keep.shape[0]
    for step, out in enumerate((keep, *sends)):
        at = slice(step * rows, (step + 1) * rows)
        out[...] = (kept[0, at].astype(F32) + received[0, at].astype(F32)).astype(out.dtype)


def sum_kernel(*refs):
    *parts, out = refs
    total = parts[0][...].astype(F32)
    for part in parts[1:]:
        total = total + part[...].astype(F32)
    out[...] = total.astype(out.dtype)


def finish_kernel(*refs):
    *parts, qkv_out, proj_out, shared = refs
    lat = lax.axis_index("lat")
    for step, part in enumerate(parts):
        shared[lat ^ step] = part[...].astype(F32)
    width = shared.shape[2]
    for slot in range(shared.shape[0]):
        at = slot * width
        out, at = (qkv_out, at) if at < qkv_out.shape[1] else (proj_out, at - qkv_out.shape[1])
        out[:, at : at + width] = shared[slot]


def call(kernel, outs, *args, name, flops=0, limit=32, scratch=(), unread=()):
    vmem = pl.BlockSpec(memory_space=pltpu.VMEM)
    anywhere = pl.BlockSpec(memory_space=pltpu.HBM)
    shapes = [jax.ShapeDtypeStruct(shape, dtype) for shape, dtype in outs]
    nbytes = sum(a.size * a.dtype.itemsize for a in (*args, *shapes))
    return pl.pallas_call(
        kernel,
        out_shape=shapes,
        in_specs=[anywhere if i in unread else vmem for i in range(len(args))],
        out_specs=[vmem] * len(shapes),
        scratch_shapes=scratch,
        compiler_params=pltpu.CompilerParams(vmem_limit_bytes=limit * 2**20),
        cost_estimate=pl.CostEstimate(flops=flops, bytes_accessed=nbytes, transcendentals=0),
        name=name,
    )(*args)


def routes(lat_size, lon_size):
    lat, lon, diag = [], [], []
    for i in range(lat_size):
        for j in range(lon_size):
            step = -1 if j % 2 == 0 else 1
            before = (j - 1) % lon_size
            me = i * lon_size + j
            lat.append((me, ((i + step) % lat_size) * lon_size + j))
            lon.append((me, i * lon_size + before))
            diag.append((me, ((i - step) % lat_size) * lon_size + before))
    return lat, lon, diag


def per_device(fields, cotangent, qkv_weight, proj_weight):
    levels, row_count, col_count, width = fields.shape
    lat_size, lon_size = lax.axis_size("lat"), lax.axis_size("lon")
    both = ("lat", "lon")
    lat_route, lon_route, diag_route = routes(lat_size, lon_size)

    def back(route):
        return [(target, source) for source, target in route]

    own_fields = fields.reshape(TOKENS, width)
    own_grads = cotangent.reshape(TOKENS, width)
    piece = [((LAT_ROWS, 2 * width), BF), ((LON_ROWS, 2 * width), BF), ((LON_ROWS, 2 * width), BF)]
    lat_piece, lon_piece, diag_piece, own = call(
        pack_kernel,
        [*piece, ((WIN, 2 * width), F32)],
        own_fields, own_grads,
        name="pack", unread=(0, 1),
        scratch=[pltpu.VMEM((TOKENS, width), BF)] * 2 + [pltpu.SemaphoreType.DMA((2,))],
    )
    lat_in = lax.ppermute(lat_piece, both, lat_route)
    diag_in = lax.ppermute(diag_piece, both, diag_route)
    lon_in = lax.ppermute(lon_piece, both, lon_route)
    qkv_here, proj_here = call(
        weights_kernel,
        [(qkv_weight.shape, BF), (proj_weight.shape, BF)],
        lat_piece, qkv_weight, proj_weight,
        name="weights", unread=(0, 1, 2), scratch=[pltpu.SemaphoreType.DMA((2,))],
    )

    split = (lat_size, width // 2, 4 * width // lat_size)
    send_grad, windows, grads, normed_t, grads_t, d_projected, mixed = call(
        attention_kernel,
        [
            (split, BF),
            ((TOKENS, width), BF),
            ((TOKENS, width), BF),
            ((width // 2, TOKENS), BF),
            ((width // 2, TOKENS), BF),
            ((TOKENS, 3 * width), BF),
            ((TOKENS, width), BF),
        ],
        own, lat_in, lon_in, diag_in, qkv_here, proj_here,
        name="attention", flops=2 * 10**9,
        scratch=[pltpu.VMEM((width, TOKENS), BF)] * 2 + [pltpu.VMEM((width // 2, TOKENS), BF)],
    )
    sibling = [(j, j ^ 1) for j in range(lon_size)]
    received = lax.ppermute(send_grad, "lon", sibling)
    kept, results = call(
        output_kernel,
        [(split, BF), ((TOKENS, 2 * width), BF)],
        windows, grads, normed_t, grads_t, d_projected, mixed, qkv_here, proj_here,
        name="outputs", flops=10**9,
    )

    slots = lat_size
    bits = lat_size.bit_length() - 1
    for phase in range(bits):
        slots //= 2
        half = ((slots, *split[1:]), BF)
        send, kept = call(halve_kernel, [half, half], kept, received, name=f"halve{slots}")
        route = [
            (i * lon_size + j, (i ^ (1 << (phase if j % 2 == 0 else bits - 1 - phase))) * lon_size + j)
            for i in range(lat_size)
            for j in range(lon_size)
        ]
        received = lax.ppermute(send, both, route)

    rows = width // lon_size
    share = ((rows, split[2]), BF)
    parts = call(line_parts_kernel, [share] * (lon_size // 2), kept, received, name="line_parts")
    arrived = [
        lax.ppermute(parts[step], "lon", [(j, j ^ (2 * step)) for j in range(lon_size)])
        for step in range(1, lon_size // 2)
    ]
    lat_back, lon_back, diag_back = call(
        pack_back_kernel, piece, parts[-1], results, name="pack_back", unread=(0,)
    )
    lat_home = lax.ppermute(lat_back, both, back(lat_route))
    diag_home = lax.ppermute(diag_back, both, back(diag_route))
    lon_home = lax.ppermute(lon_back, both, back(lon_route))
    (line_sum,) = call(sum_kernel, [share], parts[0], *arrived, name="line_sum")
    shared = [
        lax.ppermute(line_sum, "lat", [(i, i ^ step) for i in range(lat_size)]) for step in range(1, lat_size)
    ]
    field_out, d_fields = call(
        place_kernel,
        [((TOKENS, width), BF), ((TOKENS, width), BF)],
        results, lat_home, lon_home, diag_home,
        name="place",
    )
    qkv_grad, proj_grad = call(
        finish_kernel,
        [((rows, 3 * width), F32), ((rows, width), F32)],
        line_sum, *shared,
        name="finish", scratch=[pltpu.VMEM((lat_size, *share[0]), F32)],
    )
    return (field_out.reshape(fields.shape), d_fields.reshape(fields.shape), qkv_grad, jnp.transpose(proj_grad))


def solution(mesh):
    placed = (P(None, "lat", "lon", None), P(None, "lat", "lon", None), P(), P())
    return jax.shard_map(
        per_device,
        mesh=mesh,
        in_specs=placed,
        out_specs=(
            P(None, "lat", "lon", None),
            P(None, "lat", "lon", None),
            P("lon", None),
            P(None, "lon"),
        ),
        check_vma=False,
    )
```

```python
import functools

import jax
import jax.numpy as jnp
from jax import lax
from jax.experimental import pallas as pl
from jax.experimental.pallas import tpu as pltpu
from jax.sharding import PartitionSpec as P

HEADS = 8
WIN_LAT = 6
WIN_LON = 12
LEVELS = 2
COLS = 24
HALF_LAT = WIN_LAT // 2
HALF_LON = WIN_LON // 2
HALF = LEVELS * HALF_LAT * WIN_LON
WIN = 2 * HALF
TOKENS = 2 * WIN
QUARTER = HALF // 2
LANES = 128

epsilon = 1e-05
LONG = 5 * 10**10
LOAD = 5 * 10**9
BF = jnp.bfloat16
F32 = jnp.float32


def dot(a, b, dims):
    return lax.dot_general(a, b, (dims, ((), ())), preferred_element_type=F32)


NN = ((1,), (0,))
NT = ((1,), (1,))
TN = ((0,), (0,))


def div(x, by):
    return (x * ((65536 + by - 1) // by)) >> 16


def own_token(level, row, col):
    return level * (WIN_LAT * COLS) + row * COLS + col


def inner_token(v, first):
    level = div(v, HALF_LAT * WIN_LON)
    rest = v - level * (HALF_LAT * WIN_LON)
    row = div(rest, WIN_LON)
    return own_token(level, first + row, HALF_LON + rest - row * WIN_LON)


def half_token(v, first, col):
    level = div(v, HALF_LAT * HALF_LON)
    rest = v - level * (HALF_LAT * HALF_LON)
    row = div(rest, HALF_LON)
    return jnp.where(v < QUARTER, own_token(level, first + row, col + rest - row * HALF_LON), -1)


def sources():
    even = lax.rem(lax.axis_index("lon"), 2) == 0
    sent = jnp.where(even, 0, HALF_LAT)
    kept = HALF_LAT - sent
    outer = HALF_LON + WIN_LON
    return (
        (lambda v: inner_token(v, sent), HALF),
        (lambda v: half_token(v, sent, outer), QUARTER),
        (lambda v: half_token(v, sent, 0), QUARTER),
        (lambda v: half_token(v, kept, 0), QUARTER),
        (lambda v: inner_token(v, kept), HALF),
        (lambda v: half_token(v, kept, outer), HALF),
    )


def picks(source, rows, columns):
    index = source(lax.broadcasted_iota(jnp.int32, (rows, 1), 0))
    return (index == lax.broadcasted_iota(jnp.int32, (rows, columns), 1)).astype(BF)


def puts(source, rows, columns):
    index = source(lax.broadcasted_iota(jnp.int32, (1, columns), 1))
    return (lax.broadcasted_iota(jnp.int32, (rows, columns), 0) == index).astype(BF)


def first_rows(v):
    return v


def last_rows(v):
    return v - QUARTER


def order_kernel(*outs):
    for out, (source, rows) in zip(outs, sources()):
        out[...] = picks(source, rows, TOKENS)


def pack_kernel(fields, cotangent, *refs):
    count = len(refs) // 2
    width = fields.shape[1]
    for pick, out in zip(refs[:count], refs[count:]):
        out[:, :width] = dot(pick[...], fields[...], NN).astype(out.dtype)
        out[:, width:] = dot(pick[...], cotangent[...], NN).astype(out.dtype)


def normalise(x):
    mean = jnp.mean(x, -1, keepdims=True)
    centred = x - mean
    variance = jnp.mean(centred * centred, -1, keepdims=True)
    inv_std = lax.rsqrt(variance + epsilon)
    return centred * inv_std, inv_std


def swap_bits(index, size, core):
    bits = size.bit_length() - 1
    turned = sum(((index >> b) & 1) << (bits - 1 - b) for b in range(bits))
    return jnp.where(core == 0, index, turned)


def shares(transposed, out, lon, core_of, lon_size):
    rows = transposed.shape[0] // lon_size
    chip = lon >> 1
    for step in range(lon_size // 2):
        start = pl.multiple_of(((chip ^ step) * 2 + core_of) * rows, rows)
        out[step * rows : (step + 1) * rows, :] = transposed[pl.ds(start, rows), :]


def transpose_bf16(block):
    return jnp.transpose(block.astype(F32)).astype(BF)


def put_split(out, lanes_from, block, lat, core, so_far=None):
    size, _, width = out.shape
    for at in range(0, block.shape[1], width):
        slot = swap_bits(lat ^ ((lanes_from + at) // width), size, core)
        part = block[:, at : at + width]
        if so_far is not None:
            part = part + so_far[slot]
        out[slot] = part.astype(out.dtype)


def inner_kernel(own, lat_in, qkv_weight, proj_weight, send_grad, *refs):
    both = jnp.concatenate([own[...], lat_in[...].astype(F32)], axis=0)
    one_window(both, qkv_weight, proj_weight, None, send_grad, *refs)


def outer_kernel(own, lat_in, lon_in, diag_in, qkv_weight, proj_weight, grad_so_far, send_grad, *refs):
    last = picks(last_rows, HALF, QUARTER)
    both = jnp.concatenate(
        [
            own[...] + dot(last, lon_in[...], NN),
            dot(picks(first_rows, HALF, QUARTER), lat_in[...], NN) + dot(last, diag_in[...], NN),
        ],
        axis=0,
    )
    one_window(both, qkv_weight, proj_weight, grad_so_far, send_grad, *refs)


def one_window(
    both, qkv_weight, proj_weight, grad_so_far,
    send_grad, windows_out, grads_out, normed_t_out, grads_t_out, d_projected, mixed, normed_t, grads_t, send_rows,
):
    width = both.shape[1] // 2
    lat, lon = lax.axis_index("lat"), lax.axis_index("lon")
    lat_size, lon_size = lax.axis_size("lat"), lax.axis_size("lon")
    core = lax.rem(lon, 2)
    even = core == 0
    blocks = both[:, :width], both[:, width:]
    x = blocks[0]
    windows_out[...] = x.astype(BF)
    grads = blocks[1].astype(BF)
    grads_out[...] = grads
    normed, _ = normalise(x)
    normed_b = normed.astype(BF)
    projected = dot(normed_b, qkv_weight[...], NN).astype(BF)
    d_mixed = dot(grads, proj_weight[...], NT).astype(BF)

    head_size = width // HEADS
    factor = head_size ** (-0.5)
    apart = jnp.where(even, lat == lat_size - 1, lat == 0).astype(jnp.int32)
    half_b = (lax.broadcasted_iota(jnp.int32, (WIN, 2 * WIN), 0) >= HALF).astype(jnp.int32)
    at_a = lax.broadcasted_iota(jnp.int32, (WIN, 2 * WIN), 1)
    at_a = jnp.where(at_a >= WIN, at_a - WIN, at_a)
    half_a = (at_a >= HALF).astype(jnp.int32)
    allowed = ((half_a != half_b).astype(jnp.int32) * apart) == 0
    first_head = lax.broadcasted_iota(jnp.int32, (WIN, LANES), 1) < head_size
    zero = jnp.zeros((WIN, LANES), BF)

    def split_heads(block):
        return jnp.concatenate([jnp.where(first_head, block, zero), jnp.where(first_head, zero, block)], axis=0)

    def join_heads(block):
        return jnp.where(first_head, block[:WIN], block[WIN:]).astype(BF)

    for pair in range(width // LANES):
        at = pair * LANES
        q = projected[:, at : at + LANES]
        k = projected[:, width + at : width + at + LANES]
        v = projected[:, 2 * width + at : 2 * width + at + LANES]
        dm = d_mixed[:, at : at + LANES]
        q2, dm2 = split_heads(q), split_heads(dm)
        scores = dot(k, q2, NT) * factor
        scores = jnp.where(allowed, scores, -1e30)
        exponent = jnp.exp(scores - jnp.max(scores, 0, keepdims=True))
        probs = exponent * (1.0 / jnp.sum(exponent, 0, keepdims=True))
        probs_b = probs.astype(BF)
        mixed[:, at : at + LANES] = join_heads(dot(probs_b, v, TN))
        d_probs = dot(v, dm2, NT)
        d_projected[:, 2 * width + at : 2 * width + at + LANES] = dot(probs_b, dm2, NN).astype(BF)
        d_scores = probs * (d_probs - jnp.sum(d_probs * probs, 0, keepdims=True)) * factor
        d_scores = d_scores.astype(BF)
        d_projected[:, at : at + LANES] = join_heads(dot(d_scores, k, TN))
        d_projected[:, width + at : width + at + LANES] = dot(d_scores, q2, NN).astype(BF)

    normed_t[...] = transpose_bf16(normed)
    grads_t[...] = transpose_bf16(grads)
    shares(normed_t, send_rows, lon, 1 - core, lon_size)
    put_split(send_grad, 0, dot(send_rows[...], d_projected[...], NN), lat, 1 - core, grad_so_far)
    shares(grads_t, send_rows, lon, 1 - core, lon_size)
    put_split(send_grad, 3 * width, dot(send_rows[...], mixed[...], NN), lat, 1 - core, grad_so_far)
    shares(normed_t, normed_t_out, lon, core, lon_size)
    shares(grads_t, grads_t_out, lon, core, lon_size)


def output_kernel(*refs):
    (*windows, qkv_weight, proj_weight, keep_grad, inner_results, outer_results) = refs
    per_window = windows[:6], windows[6:]
    lat, core = lax.axis_index("lat"), lax.rem(lax.axis_index("lon"), 2)
    width = proj_weight.shape[0]
    qkv_grad = sum(dot(w[2][...], w[4][...], NN) for w in per_window)
    proj_grad = sum(dot(w[3][...], w[5][...], NN) for w in per_window)
    put_split(keep_grad, 0, qkv_grad, lat, core)
    put_split(keep_grad, 3 * width, proj_grad, lat, core)
    x, grads, d_projected, mixed = (
        jnp.concatenate([w[i][...] for w in per_window], axis=0) for i in (0, 1, 4, 5)
    )
    x = x.astype(F32)
    normed, inv_std = normalise(x)
    output = (x + dot(mixed, proj_weight[...], NN)).astype(BF)
    d_normed = dot(d_projected, qkv_weight[...], NT)
    d_inputs = grads.astype(F32) + inv_std * (
        d_normed
        - jnp.mean(d_normed, -1, keepdims=True)
        - normed * jnp.mean(d_normed * normed, -1, keepdims=True)
    )
    d_inputs = d_inputs.astype(BF)
    for at, out in ((0, inner_results), (WIN, outer_results)):
        out[:, :width] = output[at : at + WIN]
        out[:, width:] = d_inputs[at : at + WIN]


def pack_back_kernel(_, inner_results, outer_results, lat_out, lon_out, diag_out):
    inner_y = inner_results[...].astype(F32)[HALF:]
    outer = outer_results[...].astype(F32)
    outer_x, outer_y = outer[:HALF].astype(BF), outer[HALF:].astype(BF)
    first, last = puts(first_rows, QUARTER, HALF), puts(last_rows, QUARTER, HALF)
    lat_out[...] = jnp.concatenate([inner_y, dot(first, outer_y, NN)], axis=0).astype(BF)
    lon_out[...] = dot(last, outer_x, NN).astype(BF)
    diag_out[...] = dot(last, outer_y, NN).astype(BF)


def place_kernel(inner_results, outer_results, lat_in, lon_in, diag_in, field_out, d_fields, placed):
    placed[...] = jnp.zeros_like(placed)
    width = field_out.shape[1]
    inner_lat, outer_lat, lon, diag, inner_own, outer_own = (source for source, _ in sources())

    def lat(v):
        return jnp.where(v < HALF, inner_lat(v), outer_lat(v - HALF))

    def only_first(source):
        return lambda v: jnp.where(v < HALF, source(v), -1)

    moves = (
        (puts(only_first(inner_own), TOKENS, WIN), inner_results),
        (puts(only_first(outer_own), TOKENS, WIN), outer_results),
        (puts(lat, TOKENS, HALF + QUARTER), lat_in),
        (puts(lon, TOKENS, QUARTER), lon_in),
        (puts(diag, TOKENS, QUARTER), diag_in),
    )
    for index, out in ((0, field_out), (1, d_fields)):
        lanes = slice(index * width, (index + 1) * width)
        out[...] = sum(dot(put, source[:, lanes], NN) for put, source in moves).astype(BF)


def halve_kernel(kept, received, send, keep):
    for slot in range(send.shape[0]):
        for out, source in ((send, 2 * slot + 1), (keep, 2 * slot)):
            out[slot] = (kept[source].astype(F32) + received[source].astype(F32)).astype(BF)


def line_parts_kernel(kept, received, keep, *sends):
    rows = keep.shape[0]
    for step, out in enumerate((keep, *sends)):
        at = slice(step * rows, (step + 1) * rows)
        out[...] = (kept[0, at].astype(F32) + received[0, at].astype(F32)).astype(out.dtype)


def sum_kernel(*refs):
    *parts, out = refs
    total = parts[0][...].astype(F32)
    for part in parts[1:]:
        total = total + part[...].astype(F32)
    out[...] = total.astype(out.dtype)


def finish_kernel(_, *refs):
    *parts, qkv_out, proj_out, shared = refs
    lat = lax.axis_index("lat")
    for step, part in enumerate(parts):
        shared[lat ^ step] = part[...].astype(F32)
    width = shared.shape[2]
    for slot in range(shared.shape[0]):
        at = slot * width
        out, at = (qkv_out, at) if at < qkv_out.shape[1] else (proj_out, at - qkv_out.shape[1])
        out[:, at : at + width] = shared[slot]


def call(kernel, outs, *args, name, flops=0, limit=32, scratch=(), unread=()):
    vmem = pl.BlockSpec(memory_space=pltpu.VMEM)
    anywhere = pl.BlockSpec(memory_space=pl.ANY)
    shapes = [jax.ShapeDtypeStruct(shape, dtype) for shape, dtype in outs]
    nbytes = sum(a.size * a.dtype.itemsize for a in (*args, *shapes))
    return pl.pallas_call(
        kernel,
        out_shape=shapes,
        in_specs=[anywhere if i in unread else vmem for i in range(len(args))],
        out_specs=[vmem] * len(shapes),
        scratch_shapes=scratch,
        compiler_params=pltpu.CompilerParams(vmem_limit_bytes=limit * 2**20),
        cost_estimate=pl.CostEstimate(flops=flops, bytes_accessed=nbytes, transcendentals=0),
        name=name,
    )(*args)


def routes(lat_size, lon_size):
    lat, lon, diag = [], [], []
    for i in range(lat_size):
        for j in range(lon_size):
            step = -1 if j % 2 == 0 else 1
            before = (j - 1) % lon_size
            me = i * lon_size + j
            lat.append((me, ((i + step) % lat_size) * lon_size + j))
            lon.append((me, i * lon_size + before))
            diag.append((me, ((i - step) % lat_size) * lon_size + before))
    return lat, lon, diag


def per_device(fields, cotangent, qkv_weight, proj_weight):
    levels, row_count, col_count, width = fields.shape
    lat_size, lon_size = lax.axis_size("lat"), lax.axis_size("lon")
    both = ("lat", "lon")
    lat_route, lon_route, diag_route = routes(lat_size, lon_size)

    def back(route):
        return [(target, source) for source, target in route]

    own_fields = fields.reshape(TOKENS, width)
    own_grads = cotangent.reshape(TOKENS, width)
    lengths = (HALF, QUARTER, QUARTER, QUARTER, HALF, HALF)
    picked = call(order_kernel, [((rows, TOKENS), BF) for rows in lengths], name="order", flops=LOAD)
    inner_lat, outer_lat, lon_piece, diag_piece, inner_own, outer_own = call(
        pack_kernel,
        [((rows, 2 * width), BF) for rows in lengths[:4]] + [((HALF, 2 * width), F32)] * 2,
        own_fields, own_grads, *picked,
        name="pack", flops=LOAD,
    )
    inner_in = lax.ppermute(inner_lat, both, lat_route)
    outer_in = lax.ppermute(outer_lat, both, lat_route)
    diag_in = lax.ppermute(diag_piece, both, diag_route)
    lon_in = lax.ppermute(lon_piece, both, lon_route)

    split = (lat_size, width // 2, 4 * width // lat_size)
    per_window = [
        ((WIN, width), BF),
        ((WIN, width), BF),
        ((width // 2, WIN), BF),
        ((width // 2, WIN), BF),
        ((WIN, 3 * width), BF),
        ((WIN, width), BF),
    ]
    scratch = [pltpu.VMEM((width, WIN), BF)] * 2 + [pltpu.VMEM((width // 2, WIN), BF)]
    grad_so_far, *inner = call(
        inner_kernel, [(split, F32), *per_window], inner_own, inner_in, qkv_weight, proj_weight,
        name="inner", flops=10**9, scratch=scratch,
    )
    send_grad, *outer = call(
        outer_kernel, [(split, BF), *per_window],
        outer_own, outer_in, lon_in, diag_in, qkv_weight, proj_weight, grad_so_far,
        name="outer", flops=10**9, scratch=scratch,
    )
    sibling = [(j, j ^ 1) for j in range(lon_size)]
    received = lax.ppermute(send_grad, "lon", sibling)
    kept, *results = call(
        output_kernel, [(split, BF), ((WIN, 2 * width), BF), ((WIN, 2 * width), BF)],
        *inner, *outer, qkv_weight, proj_weight,
        name="outputs", flops=10**9,
    )

    slots = lat_size
    bits = lat_size.bit_length() - 1
    for phase in range(bits):
        slots //= 2
        half = ((slots, *split[1:]), BF)
        send, kept = call(halve_kernel, [half, half], kept, received, name=f"halve{slots}")
        route = [
            (i * lon_size + j, (i ^ (1 << (phase if j % 2 == 0 else bits - 1 - phase))) * lon_size + j)
            for i in range(lat_size)
            for j in range(lon_size)
        ]
        received = lax.ppermute(send, both, route)

    rows = width // lon_size
    share = ((rows, split[2]), BF)
    parts = call(line_parts_kernel, [share] * (lon_size // 2), kept, received, name="line_parts")
    arrived = [
        lax.ppermute(parts[step], "lon", [(j, j ^ (2 * step)) for j in range(lon_size)])
        for step in range(1, lon_size // 2)
    ]
    lat_back, lon_back, diag_back = call(
        pack_back_kernel, [((rows, 2 * width), BF) for rows in (HALF + QUARTER, QUARTER, QUARTER)],
        parts[-1], *results,
        name="pack_back", unread=(0,),
    )
    lat_home = lax.ppermute(lat_back, both, back(lat_route))
    diag_home = lax.ppermute(diag_back, both, back(diag_route))
    lon_home = lax.ppermute(lon_back, both, back(lon_route))
    (line_sum,) = call(sum_kernel, [share], parts[0], *arrived, name="line_sum", flops=LONG)
    shared = [
        lax.ppermute(line_sum, "lat", [(i, i ^ step) for i in range(lat_size)]) for step in range(1, lat_size)
    ]
    field_out, d_fields, placed = call(
        place_kernel,
        [((TOKENS, width), BF), ((TOKENS, width), BF), ((8, LANES), F32)],
        *results, lat_home, lon_home, diag_home,
        name="place",
    )
    qkv_grad, proj_grad = call(
        finish_kernel,
        [((rows, 3 * width), F32), ((rows, width), F32)],
        placed, line_sum, *shared,
        name="finish", unread=(0,), scratch=[pltpu.VMEM((lat_size, *share[0]), F32)],
    )
    return (field_out.reshape(fields.shape), d_fields.reshape(fields.shape), qkv_grad, jnp.transpose(proj_grad))


def solution(mesh):
    placed = (P(None, "lat", "lon", None), P(None, "lat", "lon", None), P(), P())
    return jax.shard_map(
        per_device,
        mesh=mesh,
        in_specs=placed,
        out_specs=(
            P(None, "lat", "lon", None),
            P(None, "lat", "lon", None),
            P("lon", None),
            P(None, "lon"),
        ),
        check_vma=False,
    )
```

```python
import functools

import jax
import jax.numpy as jnp
from jax import lax
from jax.experimental import pallas as pl
from jax.experimental.pallas import tpu as pltpu
from jax.sharding import PartitionSpec as P

HEADS = 8
WIN_LAT = 6
WIN_LON = 12
LEVELS = 2
COLS = 24
HALF_LAT = WIN_LAT // 2
HALF_LON = WIN_LON // 2
HALF = LEVELS * HALF_LAT * WIN_LON
WIN = 2 * HALF
TOKENS = 2 * WIN
QUARTER = HALF // 2
LANES = 128

epsilon = 1e-05
LONG = 5 * 10**10
LOAD = 5 * 10**9
BF = jnp.bfloat16
F32 = jnp.float32


def dot(a, b, dims):
    return lax.dot_general(a, b, (dims, ((), ())), preferred_element_type=F32)


NN = ((1,), (0,))
NT = ((1,), (1,))
TN = ((0,), (0,))


def div(x, by):
    return (x * ((65536 + by - 1) // by)) >> 16


def own_token(level, row, col):
    return level * (WIN_LAT * COLS) + row * COLS + col


def inner_token(v, first):
    level = div(v, HALF_LAT * WIN_LON)
    rest = v - level * (HALF_LAT * WIN_LON)
    row = div(rest, WIN_LON)
    return own_token(level, first + row, HALF_LON + rest - row * WIN_LON)


def half_token(v, first, col):
    level = div(v, HALF_LAT * HALF_LON)
    rest = v - level * (HALF_LAT * HALF_LON)
    row = div(rest, HALF_LON)
    return jnp.where(v < QUARTER, own_token(level, first + row, col + rest - row * HALF_LON), -1)


def sources():
    even = lax.rem(lax.axis_index("lon"), 2) == 0
    sent = jnp.where(even, 0, HALF_LAT)
    kept = HALF_LAT - sent
    outer = HALF_LON + WIN_LON
    return (
        (lambda v: inner_token(v, sent), HALF),
        (lambda v: half_token(v, sent, outer), QUARTER),
        (lambda v: half_token(v, sent, 0), QUARTER),
        (lambda v: half_token(v, kept, 0), QUARTER),
        (lambda v: inner_token(v, kept), HALF),
        (lambda v: half_token(v, kept, outer), HALF),
    )


def picks(source, rows, columns):
    index = source(lax.broadcasted_iota(jnp.int32, (rows, 1), 0))
    return (index == lax.broadcasted_iota(jnp.int32, (rows, columns), 1)).astype(BF)


def puts(source, rows, columns):
    index = source(lax.broadcasted_iota(jnp.int32, (1, columns), 1))
    return (lax.broadcasted_iota(jnp.int32, (rows, columns), 0) == index).astype(BF)


def first_rows(v):
    return v


def last_rows(v):
    return v - QUARTER


def order_kernel(*outs):
    for out, (source, rows) in zip(outs, sources()):
        out[...] = picks(source, rows, TOKENS)


def pack_kernel(fields, cotangent, *refs):
    count = len(refs) // 2
    width = fields.shape[1]
    for pick, out in zip(refs[:count], refs[count:]):
        out[:, :width] = dot(pick[...], fields[...], NN).astype(out.dtype)
        out[:, width:] = dot(pick[...], cotangent[...], NN).astype(out.dtype)


def normalise(x):
    mean = jnp.mean(x, -1, keepdims=True)
    centred = x - mean
    variance = jnp.mean(centred * centred, -1, keepdims=True)
    inv_std = lax.rsqrt(variance + epsilon)
    return centred * inv_std, inv_std


def swap_bits(index, size, core):
    bits = size.bit_length() - 1
    turned = sum(((index >> b) & 1) << (bits - 1 - b) for b in range(bits))
    return jnp.where(core == 0, index, turned)


def shares(transposed, out, lon, core_of, lon_size):
    rows = transposed.shape[0] // lon_size
    chip = lon >> 1
    for step in range(lon_size // 2):
        start = pl.multiple_of(((chip ^ step) * 2 + core_of) * rows, rows)
        out[step * rows : (step + 1) * rows, :] = transposed[pl.ds(start, rows), :]


def transpose_bf16(block):
    return jnp.transpose(block.astype(F32)).astype(BF)


def put_split(out, lanes_from, block, lat, core, so_far=None):
    size, _, width = out.shape
    for at in range(0, block.shape[1], width):
        slot = swap_bits(lat ^ ((lanes_from + at) // width), size, core)
        part = block[:, at : at + width]
        if so_far is not None:
            part = part + so_far[slot]
        out[slot] = part.astype(out.dtype)


def inner_kernel(own, lat_in, qkv_weight, proj_weight, send_grad, *refs):
    both = jnp.concatenate([own[...], lat_in[...].astype(F32)], axis=0)
    one_window(both, qkv_weight, proj_weight, None, send_grad, *refs)


def outer_kernel(own, lon_in, lat_in, diag_in, qkv_weight, proj_weight, grad_so_far, send_grad, *refs):
    last = picks(last_rows, HALF, QUARTER)
    both = jnp.concatenate(
        [
            own[...] + dot(last, lon_in[...], NN),
            dot(picks(first_rows, HALF, QUARTER), lat_in[...], NN) + dot(last, diag_in[...], NN),
        ],
        axis=0,
    )
    one_window(both, qkv_weight, proj_weight, grad_so_far, send_grad, *refs)


def one_window(
    both, qkv_weight, proj_weight, grad_so_far,
    send_grad, windows_out, grads_out, normed_t_out, grads_t_out, d_projected, mixed, normed_t, grads_t, send_rows,
):
    width = both.shape[1] // 2
    lat, lon = lax.axis_index("lat"), lax.axis_index("lon")
    lat_size, lon_size = lax.axis_size("lat"), lax.axis_size("lon")
    core = lax.rem(lon, 2)
    even = core == 0
    blocks = both[:, :width], both[:, width:]
    x = blocks[0]
    windows_out[...] = x.astype(BF)
    grads = blocks[1].astype(BF)
    grads_out[...] = grads
    normed, _ = normalise(x)
    normed_b = normed.astype(BF)
    projected = dot(normed_b, qkv_weight[...], NN).astype(BF)
    d_mixed = dot(grads, proj_weight[...], NT).astype(BF)

    head_size = width // HEADS
    factor = head_size ** (-0.5)
    apart = jnp.where(even, lat == lat_size - 1, lat == 0).astype(jnp.int32)
    half_b = (lax.broadcasted_iota(jnp.int32, (WIN, 2 * WIN), 0) >= HALF).astype(jnp.int32)
    at_a = lax.broadcasted_iota(jnp.int32, (WIN, 2 * WIN), 1)
    at_a = jnp.where(at_a >= WIN, at_a - WIN, at_a)
    half_a = (at_a >= HALF).astype(jnp.int32)
    allowed = ((half_a != half_b).astype(jnp.int32) * apart) == 0
    first_head = lax.broadcasted_iota(jnp.int32, (WIN, LANES), 1) < head_size
    zero = jnp.zeros((WIN, LANES), BF)

    def split_heads(block):
        return jnp.concatenate([jnp.where(first_head, block, zero), jnp.where(first_head, zero, block)], axis=0)

    def join_heads(block):
        return jnp.where(first_head, block[:WIN], block[WIN:]).astype(BF)

    for pair in range(width // LANES):
        at = pair * LANES
        q = projected[:, at : at + LANES]
        k = projected[:, width + at : width + at + LANES]
        v = projected[:, 2 * width + at : 2 * width + at + LANES]
        dm = d_mixed[:, at : at + LANES]
        q2, dm2 = split_heads(q), split_heads(dm)
        scores = dot(k, q2, NT) * factor
        scores = jnp.where(allowed, scores, -1e30)
        exponent = jnp.exp(scores - jnp.max(scores, 0, keepdims=True))
        probs = exponent * (1.0 / jnp.sum(exponent, 0, keepdims=True))
        probs_b = probs.astype(BF)
        mixed[:, at : at + LANES] = join_heads(dot(probs_b, v, TN))
        d_probs = dot(v, dm2, NT)
        d_projected[:, 2 * width + at : 2 * width + at + LANES] = dot(probs_b, dm2, NN).astype(BF)
        d_scores = probs * (d_probs - jnp.sum(d_probs * probs, 0, keepdims=True)) * factor
        d_scores = d_scores.astype(BF)
        d_projected[:, at : at + LANES] = join_heads(dot(d_scores, k, TN))
        d_projected[:, width + at : width + at + LANES] = dot(d_scores, q2, NN).astype(BF)

    normed_t[...] = transpose_bf16(normed)
    grads_t[...] = transpose_bf16(grads)
    shares(normed_t, send_rows, lon, 1 - core, lon_size)
    put_split(send_grad, 0, dot(send_rows[...], d_projected[...], NN), lat, 1 - core, grad_so_far)
    shares(grads_t, send_rows, lon, 1 - core, lon_size)
    put_split(send_grad, 3 * width, dot(send_rows[...], mixed[...], NN), lat, 1 - core, grad_so_far)
    shares(normed_t, normed_t_out, lon, core, lon_size)
    shares(grads_t, grads_t_out, lon, core, lon_size)


def output_kernel(*refs):
    (*windows, qkv_weight, proj_weight, keep_grad, inner_results, outer_results) = refs
    per_window = windows[:6], windows[6:]
    lat, core = lax.axis_index("lat"), lax.rem(lax.axis_index("lon"), 2)
    width = proj_weight.shape[0]
    qkv_grad = sum(dot(w[2][...], w[4][...], NN) for w in per_window)
    proj_grad = sum(dot(w[3][...], w[5][...], NN) for w in per_window)
    put_split(keep_grad, 0, qkv_grad, lat, core)
    put_split(keep_grad, 3 * width, proj_grad, lat, core)
    x, grads, d_projected, mixed = (
        jnp.concatenate([w[i][...] for w in per_window], axis=0) for i in (0, 1, 4, 5)
    )
    x = x.astype(F32)
    normed, inv_std = normalise(x)
    output = (x + dot(mixed, proj_weight[...], NN)).astype(BF)
    d_normed = dot(d_projected, qkv_weight[...], NT)
    d_inputs = grads.astype(F32) + inv_std * (
        d_normed
        - jnp.mean(d_normed, -1, keepdims=True)
        - normed * jnp.mean(d_normed * normed, -1, keepdims=True)
    )
    d_inputs = d_inputs.astype(BF)
    for at, out in ((0, inner_results), (WIN, outer_results)):
        out[:, :width] = output[at : at + WIN]
        out[:, width:] = d_inputs[at : at + WIN]


def pack_back_kernel(_, inner_results, outer_results, lat_out, lon_out, diag_out):
    inner_y = inner_results[...].astype(F32)[HALF:]
    outer = outer_results[...].astype(F32)
    outer_x, outer_y = outer[:HALF].astype(BF), outer[HALF:].astype(BF)
    first, last = puts(first_rows, QUARTER, HALF), puts(last_rows, QUARTER, HALF)
    lat_out[...] = jnp.concatenate([inner_y, dot(first, outer_y, NN)], axis=0).astype(BF)
    lon_out[...] = dot(last, outer_x, NN).astype(BF)
    diag_out[...] = dot(last, outer_y, NN).astype(BF)


def place_kernel(inner_results, outer_results, lat_in, lon_in, diag_in, field_out, d_fields, placed):
    placed[...] = jnp.zeros_like(placed)
    width = field_out.shape[1]
    inner_lat, outer_lat, lon, diag, inner_own, outer_own = (source for source, _ in sources())

    def lat(v):
        return jnp.where(v < HALF, inner_lat(v), outer_lat(v - HALF))

    def only_first(source):
        return lambda v: jnp.where(v < HALF, source(v), -1)

    moves = (
        (puts(only_first(inner_own), TOKENS, WIN), inner_results),
        (puts(only_first(outer_own), TOKENS, WIN), outer_results),
        (puts(lat, TOKENS, HALF + QUARTER), lat_in),
        (puts(lon, TOKENS, QUARTER), lon_in),
        (puts(diag, TOKENS, QUARTER), diag_in),
    )
    for index, out in ((0, field_out), (1, d_fields)):
        lanes = slice(index * width, (index + 1) * width)
        out[...] = sum(dot(put, source[:, lanes], NN) for put, source in moves).astype(BF)


def halve_kernel(kept, received, send, keep):
    for slot in range(send.shape[0]):
        for out, source in ((send, 2 * slot + 1), (keep, 2 * slot)):
            out[slot] = (kept[source].astype(F32) + received[source].astype(F32)).astype(BF)


def line_parts_kernel(kept, received, keep, *sends):
    rows = keep.shape[0]
    for step, out in enumerate((keep, *sends)):
        at = slice(step * rows, (step + 1) * rows)
        out[...] = (kept[0, at].astype(F32) + received[0, at].astype(F32)).astype(out.dtype)


def sum_kernel(_, *refs):
    *parts, out = refs
    total = parts[0][...].astype(F32)
    for part in parts[1:]:
        total = total + part[...].astype(F32)
    out[...] = total.astype(out.dtype)


def finish_kernel(*refs):
    *parts, qkv_out, proj_out, shared = refs
    lat = lax.axis_index("lat")
    for step, part in enumerate(parts):
        shared[lat ^ step] = part[...].astype(F32)
    width = shared.shape[2]
    for slot in range(shared.shape[0]):
        at = slot * width
        out, at = (qkv_out, at) if at < qkv_out.shape[1] else (proj_out, at - qkv_out.shape[1])
        out[:, at : at + width] = shared[slot]


def call(kernel, outs, *args, name, flops=0, limit=32, scratch=(), unread=()):
    vmem = pl.BlockSpec(memory_space=pltpu.VMEM)
    anywhere = pl.BlockSpec(memory_space=pl.ANY)
    shapes = [jax.ShapeDtypeStruct(shape, dtype) for shape, dtype in outs]
    nbytes = sum(a.size * a.dtype.itemsize for a in (*args, *shapes))
    return pl.pallas_call(
        kernel,
        out_shape=shapes,
        in_specs=[anywhere if i in unread else vmem for i in range(len(args))],
        out_specs=[vmem] * len(shapes),
        scratch_shapes=scratch,
        compiler_params=pltpu.CompilerParams(vmem_limit_bytes=limit * 2**20),
        cost_estimate=pl.CostEstimate(flops=flops, bytes_accessed=nbytes, transcendentals=0),
        name=name,
    )(*args)


def routes(lat_size, lon_size):
    lat, lon, diag = [], [], []
    for i in range(lat_size):
        for j in range(lon_size):
            step = -1 if j % 2 == 0 else 1
            before = (j - 1) % lon_size
            me = i * lon_size + j
            lat.append((me, ((i + step) % lat_size) * lon_size + j))
            lon.append((me, i * lon_size + before))
            diag.append((me, ((i - step) % lat_size) * lon_size + before))
    return lat, lon, diag


def per_device(fields, cotangent, qkv_weight, proj_weight):
    levels, row_count, col_count, width = fields.shape
    lat_size, lon_size = lax.axis_size("lat"), lax.axis_size("lon")
    both = ("lat", "lon")
    lat_route, lon_route, diag_route = routes(lat_size, lon_size)

    def back(route):
        return [(target, source) for source, target in route]

    own_fields = fields.reshape(TOKENS, width)
    own_grads = cotangent.reshape(TOKENS, width)
    lengths = (HALF, QUARTER, QUARTER, QUARTER, HALF, HALF)
    picked = call(order_kernel, [((rows, TOKENS), BF) for rows in lengths], name="order", flops=LOAD)
    inner_lat, outer_lat, lon_piece, diag_piece, inner_own, outer_own = call(
        pack_kernel,
        [((rows, 2 * width), BF) for rows in lengths[:4]] + [((HALF, 2 * width), F32)] * 2,
        own_fields, own_grads, *picked,
        name="pack", flops=LOAD,
    )
    inner_in = lax.ppermute(inner_lat, both, lat_route)
    lon_in = lax.ppermute(lon_piece, both, lon_route)
    outer_in = lax.ppermute(outer_lat, both, lat_route)
    diag_in = lax.ppermute(diag_piece, both, diag_route)

    split = (lat_size, width // 2, 4 * width // lat_size)
    per_window = [
        ((WIN, width), BF),
        ((WIN, width), BF),
        ((width // 2, WIN), BF),
        ((width // 2, WIN), BF),
        ((WIN, 3 * width), BF),
        ((WIN, width), BF),
    ]
    scratch = [pltpu.VMEM((width, WIN), BF)] * 2 + [pltpu.VMEM((width // 2, WIN), BF)]
    grad_so_far, *inner = call(
        inner_kernel, [(split, F32), *per_window], inner_own, inner_in, qkv_weight, proj_weight,
        name="inner", flops=10**9, scratch=scratch,
    )
    send_grad, *outer = call(
        outer_kernel, [(split, BF), *per_window],
        outer_own, lon_in, outer_in, diag_in, qkv_weight, proj_weight, grad_so_far,
        name="outer", flops=10**9, scratch=scratch,
    )
    sibling = [(j, j ^ 1) for j in range(lon_size)]
    received = lax.ppermute(send_grad, "lon", sibling)
    kept, *results = call(
        output_kernel, [(split, BF), ((WIN, 2 * width), BF), ((WIN, 2 * width), BF)],
        *inner, *outer, qkv_weight, proj_weight,
        name="outputs", flops=10**9,
    )

    slots = lat_size
    bits = lat_size.bit_length() - 1
    for phase in range(bits):
        slots //= 2
        half = ((slots, *split[1:]), BF)
        send, kept = call(halve_kernel, [half, half], kept, received, name=f"halve{slots}")
        route = [
            (i * lon_size + j, (i ^ (1 << (phase if j % 2 == 0 else bits - 1 - phase))) * lon_size + j)
            for i in range(lat_size)
            for j in range(lon_size)
        ]
        received = lax.ppermute(send, both, route)

    lat_back, lon_back, diag_back = call(
        pack_back_kernel, [((rows, 2 * width), BF) for rows in (HALF + QUARTER, QUARTER, QUARTER)],
        send, *results,
        name="pack_back", unread=(0,),
    )
    lat_home = lax.ppermute(lat_back, both, back(lat_route))
    diag_home = lax.ppermute(diag_back, both, back(diag_route))
    lon_home = lax.ppermute(lon_back, both, back(lon_route))

    rows = width // lon_size
    share = ((rows, split[2]), BF)
    parts = call(line_parts_kernel, [share] * (lon_size // 2), kept, received, name="line_parts", flops=LONG)
    arrived = [
        lax.ppermute(parts[step], "lon", [(j, j ^ (2 * step)) for j in range(lon_size)])
        for step in range(1, lon_size // 2)
    ]
    field_out, d_fields, placed = call(
        place_kernel,
        [((TOKENS, width), BF), ((TOKENS, width), BF), ((8, LANES), F32)],
        *results, lat_home, lon_home, diag_home,
        name="place",
    )
    (line_sum,) = call(sum_kernel, [share], placed, parts[0], *arrived, name="line_sum", unread=(0,))
    shared = [
        lax.ppermute(line_sum, "lat", [(i, i ^ step) for i in range(lat_size)]) for step in range(1, lat_size)
    ]
    qkv_grad, proj_grad = call(
        finish_kernel,
        [((rows, 3 * width), F32), ((rows, width), F32)],
        line_sum, *shared,
        name="finish", scratch=[pltpu.VMEM((lat_size, *share[0]), F32)],
    )
    return (field_out.reshape(fields.shape), d_fields.reshape(fields.shape), qkv_grad, jnp.transpose(proj_grad))


def solution(mesh):
    placed = (P(None, "lat", "lon", None), P(None, "lat", "lon", None), P(), P())
    return jax.shard_map(
        per_device,
        mesh=mesh,
        in_specs=placed,
        out_specs=(
            P(None, "lat", "lon", None),
            P(None, "lat", "lon", None),
            P("lon", None),
            P(None, "lon"),
        ),
        check_vma=False,
    )
```

```python
import functools

import jax
import jax.numpy as jnp
from jax import lax
from jax.experimental import pallas as pl
from jax.experimental.pallas import tpu as pltpu
from jax.sharding import PartitionSpec as P

HEADS = 8
WIN_LAT = 6
WIN_LON = 12
LEVELS = 2
COLS = 24
HALF_LAT = WIN_LAT // 2
HALF_LON = WIN_LON // 2
HALF = LEVELS * HALF_LAT * WIN_LON
WIN = 2 * HALF
TOKENS = 2 * WIN
QUARTER = HALF // 2
LANES = 128

epsilon = 1e-05
LONG = 2 * 10**9
LOAD = 5 * 10**9
BF = jnp.bfloat16
F32 = jnp.float32


def dot(a, b, dims):
    return lax.dot_general(a, b, (dims, ((), ())), preferred_element_type=F32)


NN = ((1,), (0,))
NT = ((1,), (1,))
TN = ((0,), (0,))


def div(x, by):
    return (x * ((65536 + by - 1) // by)) >> 16


def own_token(level, row, col):
    return level * (WIN_LAT * COLS) + row * COLS + col


def inner_token(v, first):
    level = div(v, HALF_LAT * WIN_LON)
    rest = v - level * (HALF_LAT * WIN_LON)
    row = div(rest, WIN_LON)
    return own_token(level, first + row, HALF_LON + rest - row * WIN_LON)


def half_token(v, first, col):
    level = div(v, HALF_LAT * HALF_LON)
    rest = v - level * (HALF_LAT * HALF_LON)
    row = div(rest, HALF_LON)
    return jnp.where(v < QUARTER, own_token(level, first + row, col + rest - row * HALF_LON), -1)


def sources():
    even = lax.rem(lax.axis_index("lon"), 2) == 0
    sent = jnp.where(even, 0, HALF_LAT)
    kept = HALF_LAT - sent
    outer = HALF_LON + WIN_LON
    return (
        (lambda v: inner_token(v, sent), HALF),
        (lambda v: half_token(v, sent, outer), QUARTER),
        (lambda v: half_token(v, sent, 0), QUARTER),
        (lambda v: half_token(v, kept, 0), QUARTER),
        (lambda v: inner_token(v, kept), HALF),
        (lambda v: half_token(v, kept, outer), HALF),
    )


def picks(source, rows, columns):
    index = source(lax.broadcasted_iota(jnp.int32, (rows, 1), 0))
    return (index == lax.broadcasted_iota(jnp.int32, (rows, columns), 1)).astype(BF)


def puts(source, rows, columns):
    index = source(lax.broadcasted_iota(jnp.int32, (1, columns), 1))
    return (lax.broadcasted_iota(jnp.int32, (rows, columns), 0) == index).astype(BF)


def first_rows(v):
    return v


def last_rows(v):
    return v - QUARTER


def order_kernel(*outs):
    for out, (source, rows) in zip(outs, sources()):
        out[...] = picks(source, rows, TOKENS)


def pack_kernel(fields, cotangent, *refs):
    count = len(refs) // 2
    width = fields.shape[1]
    for pick, out in zip(refs[:count], refs[count:]):
        out[:, :width] = dot(pick[...], fields[...], NN).astype(out.dtype)
        out[:, width:] = dot(pick[...], cotangent[...], NN).astype(out.dtype)


def normalise(x):
    mean = jnp.mean(x, -1, keepdims=True)
    centred = x - mean
    variance = jnp.mean(centred * centred, -1, keepdims=True)
    inv_std = lax.rsqrt(variance + epsilon)
    return centred * inv_std, inv_std


def swap_bits(index, size, core):
    bits = size.bit_length() - 1
    turned = sum(((index >> b) & 1) << (bits - 1 - b) for b in range(bits))
    return jnp.where(core == 0, index, turned)


def shares(transposed, out, lon, core_of, lon_size):
    rows = transposed.shape[0] // lon_size
    chip = lon >> 1
    for step in range(lon_size // 2):
        start = pl.multiple_of(((chip ^ step) * 2 + core_of) * rows, rows)
        out[step * rows : (step + 1) * rows, :] = transposed[pl.ds(start, rows), :]


def transpose_bf16(block):
    return jnp.transpose(block.astype(F32)).astype(BF)


def put_split(out, lanes_from, block, lat, core, so_far=None):
    size, _, width = out.shape
    for at in range(0, block.shape[1], width):
        slot = swap_bits(lat ^ ((lanes_from + at) // width), size, core)
        part = block[:, at : at + width]
        if so_far is not None:
            part = part + so_far[slot]
        out[slot] = part.astype(out.dtype)


def inner_kernel(own, lat_in, qkv_weight, proj_weight, send_grad, *refs):
    both = jnp.concatenate([own[...], lat_in[...].astype(F32)], axis=0)
    one_window(both, qkv_weight, proj_weight, None, send_grad, *refs)


def outer_kernel(own, lon_in, lat_in, diag_in, qkv_weight, proj_weight, grad_so_far, send_grad, *refs):
    last = picks(last_rows, HALF, QUARTER)
    both = jnp.concatenate(
        [
            own[...] + dot(last, lon_in[...], NN),
            dot(picks(first_rows, HALF, QUARTER), lat_in[...], NN) + dot(last, diag_in[...], NN),
        ],
        axis=0,
    )
    one_window(both, qkv_weight, proj_weight, grad_so_far, send_grad, *refs)


def one_window(
    both, qkv_weight, proj_weight, grad_so_far,
    send_grad, windows_out, grads_out, normed_t_out, grads_t_out, d_projected, mixed, normed_t, grads_t, send_rows,
):
    width = both.shape[1] // 2
    lat, lon = lax.axis_index("lat"), lax.axis_index("lon")
    lat_size, lon_size = lax.axis_size("lat"), lax.axis_size("lon")
    core = lax.rem(lon, 2)
    even = core == 0
    blocks = both[:, :width], both[:, width:]
    x = blocks[0]
    windows_out[...] = x.astype(BF)
    grads = blocks[1].astype(BF)
    grads_out[...] = grads
    normed, _ = normalise(x)
    normed_b = normed.astype(BF)
    projected = dot(normed_b, qkv_weight[...], NN).astype(BF)
    d_mixed = dot(grads, proj_weight[...], NT).astype(BF)

    head_size = width // HEADS
    factor = head_size ** (-0.5)
    apart = jnp.where(even, lat == lat_size - 1, lat == 0).astype(jnp.int32)
    half_b = (lax.broadcasted_iota(jnp.int32, (WIN, 2 * WIN), 0) >= HALF).astype(jnp.int32)
    at_a = lax.broadcasted_iota(jnp.int32, (WIN, 2 * WIN), 1)
    at_a = jnp.where(at_a >= WIN, at_a - WIN, at_a)
    half_a = (at_a >= HALF).astype(jnp.int32)
    allowed = ((half_a != half_b).astype(jnp.int32) * apart) == 0
    first_head = lax.broadcasted_iota(jnp.int32, (WIN, LANES), 1) < head_size
    zero = jnp.zeros((WIN, LANES), BF)

    def split_heads(block):
        return jnp.concatenate([jnp.where(first_head, block, zero), jnp.where(first_head, zero, block)], axis=0)

    def join_heads(block):
        return jnp.where(first_head, block[:WIN], block[WIN:]).astype(BF)

    for pair in range(width // LANES):
        at = pair * LANES
        q = projected[:, at : at + LANES]
        k = projected[:, width + at : width + at + LANES]
        v = projected[:, 2 * width + at : 2 * width + at + LANES]
        dm = d_mixed[:, at : at + LANES]
        q2, dm2 = split_heads(q), split_heads(dm)
        scores = dot(k, q2, NT) * factor
        scores = jnp.where(allowed, scores, -1e30)
        exponent = jnp.exp(scores - jnp.max(scores, 0, keepdims=True))
        probs = exponent * (1.0 / jnp.sum(exponent, 0, keepdims=True))
        probs_b = probs.astype(BF)
        mixed[:, at : at + LANES] = join_heads(dot(probs_b, v, TN))
        d_probs = dot(v, dm2, NT)
        d_projected[:, 2 * width + at : 2 * width + at + LANES] = dot(probs_b, dm2, NN).astype(BF)
        d_scores = probs * (d_probs - jnp.sum(d_probs * probs, 0, keepdims=True)) * factor
        d_scores = d_scores.astype(BF)
        d_projected[:, at : at + LANES] = join_heads(dot(d_scores, k, TN))
        d_projected[:, width + at : width + at + LANES] = dot(d_scores, q2, NN).astype(BF)

    normed_t[...] = transpose_bf16(normed)
    grads_t[...] = transpose_bf16(grads)
    shares(normed_t, send_rows, lon, 1 - core, lon_size)
    put_split(send_grad, 0, dot(send_rows[...], d_projected[...], NN), lat, 1 - core, grad_so_far)
    shares(grads_t, send_rows, lon, 1 - core, lon_size)
    put_split(send_grad, 3 * width, dot(send_rows[...], mixed[...], NN), lat, 1 - core, grad_so_far)
    shares(normed_t, normed_t_out, lon, core, lon_size)
    shares(grads_t, grads_t_out, lon, core, lon_size)


def output_kernel(*refs):
    (*windows, qkv_weight, proj_weight, keep_grad, inner_results, outer_results) = refs
    per_window = windows[:6], windows[6:]
    lat, core = lax.axis_index("lat"), lax.rem(lax.axis_index("lon"), 2)
    width = proj_weight.shape[0]
    qkv_grad = sum(dot(w[2][...], w[4][...], NN) for w in per_window)
    proj_grad = sum(dot(w[3][...], w[5][...], NN) for w in per_window)
    put_split(keep_grad, 0, qkv_grad, lat, core)
    put_split(keep_grad, 3 * width, proj_grad, lat, core)
    x, grads, d_projected, mixed = (
        jnp.concatenate([w[i][...] for w in per_window], axis=0) for i in (0, 1, 4, 5)
    )
    x = x.astype(F32)
    normed, inv_std = normalise(x)
    output = (x + dot(mixed, proj_weight[...], NN)).astype(BF)
    d_normed = dot(d_projected, qkv_weight[...], NT)
    d_inputs = grads.astype(F32) + inv_std * (
        d_normed
        - jnp.mean(d_normed, -1, keepdims=True)
        - normed * jnp.mean(d_normed * normed, -1, keepdims=True)
    )
    d_inputs = d_inputs.astype(BF)
    for at, out in ((0, inner_results), (WIN, outer_results)):
        out[:, :width] = output[at : at + WIN]
        out[:, width:] = d_inputs[at : at + WIN]


def pack_back_kernel(_, inner_results, outer_results, lat_out, lon_out, diag_out):
    inner_y = inner_results[...].astype(F32)[HALF:]
    outer = outer_results[...].astype(F32)
    outer_x, outer_y = outer[:HALF].astype(BF), outer[HALF:].astype(BF)
    first, last = puts(first_rows, QUARTER, HALF), puts(last_rows, QUARTER, HALF)
    lat_out[...] = jnp.concatenate([inner_y, dot(first, outer_y, NN)], axis=0).astype(BF)
    lon_out[...] = dot(last, outer_x, NN).astype(BF)
    diag_out[...] = dot(last, outer_y, NN).astype(BF)


def place_kernel(inner_results, outer_results, lat_in, placed):
    inner_lat, outer_lat, _, _, inner_own, outer_own = (source for source, _ in sources())

    def lat(v):
        return jnp.where(v < HALF, inner_lat(v), outer_lat(v - HALF))

    def only_first(source):
        return lambda v: jnp.where(v < HALF, source(v), -1)

    placed[...] = (
        dot(puts(only_first(inner_own), TOKENS, WIN), inner_results[...], NN)
        + dot(puts(only_first(outer_own), TOKENS, WIN), outer_results[...], NN)
        + dot(puts(lat, TOKENS, HALF + QUARTER), lat_in[...], NN)
    )


def place_rest_kernel(placed, lon_in, diag_in, field_out, d_fields, done):
    done[...] = jnp.zeros_like(done)
    width = field_out.shape[1]
    _, _, lon, diag, _, _ = (source for source, _ in sources())
    total = (
        placed[...]
        + dot(puts(lon, TOKENS, QUARTER), lon_in[...], NN)
        + dot(puts(diag, TOKENS, QUARTER), diag_in[...], NN)
    ).astype(BF)
    field_out[...] = total[:, :width]
    d_fields[...] = total[:, width:]


def halve_kernel(kept, received, send, keep):
    for slot in range(send.shape[0]):
        for out, source in ((send, 2 * slot + 1), (keep, 2 * slot)):
            out[slot] = (kept[source].astype(F32) + received[source].astype(F32)).astype(BF)


def line_parts_kernel(kept, received, keep, *sends):
    rows = keep.shape[0]
    for step, out in enumerate((keep, *sends)):
        at = slice(step * rows, (step + 1) * rows)
        out[...] = (kept[0, at].astype(F32) + received[0, at].astype(F32)).astype(out.dtype)


def sum_kernel(*refs):
    *parts, out = refs
    total = parts[0][...].astype(F32)
    for part in parts[1:]:
        total = total + part[...].astype(F32)
    out[...] = total.astype(out.dtype)


def finish_kernel(_, *refs):
    *parts, qkv_out, proj_out, shared = refs
    lat = lax.axis_index("lat")
    for step, part in enumerate(parts):
        shared[lat ^ step] = part[...].astype(F32)
    width = shared.shape[2]
    for slot in range(shared.shape[0]):
        at = slot * width
        out, at = (qkv_out, at) if at < qkv_out.shape[1] else (proj_out, at - qkv_out.shape[1])
        out[:, at : at + width] = shared[slot]


def call(kernel, outs, *args, name, flops=0, limit=32, scratch=(), unread=()):
    vmem = pl.BlockSpec(memory_space=pltpu.VMEM)
    anywhere = pl.BlockSpec(memory_space=pl.ANY)
    shapes = [jax.ShapeDtypeStruct(shape, dtype) for shape, dtype in outs]
    nbytes = sum(a.size * a.dtype.itemsize for a in (*args, *shapes))
    return pl.pallas_call(
        kernel,
        out_shape=shapes,
        in_specs=[anywhere if i in unread else vmem for i in range(len(args))],
        out_specs=[vmem] * len(shapes),
        scratch_shapes=scratch,
        compiler_params=pltpu.CompilerParams(vmem_limit_bytes=limit * 2**20),
        cost_estimate=pl.CostEstimate(flops=flops, bytes_accessed=nbytes, transcendentals=0),
        name=name,
    )(*args)


def routes(lat_size, lon_size):
    lat, lon, diag = [], [], []
    for i in range(lat_size):
        for j in range(lon_size):
            step = -1 if j % 2 == 0 else 1
            before = (j - 1) % lon_size
            me = i * lon_size + j
            lat.append((me, ((i + step) % lat_size) * lon_size + j))
            lon.append((me, i * lon_size + before))
            diag.append((me, ((i - step) % lat_size) * lon_size + before))
    return lat, lon, diag


def line_order(chips):
    return [*range(chips // 2, chips), *range(1, chips // 2)]


def per_device(fields, cotangent, qkv_weight, proj_weight):
    levels, row_count, col_count, width = fields.shape
    lat_size, lon_size = lax.axis_size("lat"), lax.axis_size("lon")
    both = ("lat", "lon")
    lat_route, lon_route, diag_route = routes(lat_size, lon_size)

    def back(route):
        return [(target, source) for source, target in route]

    own_fields = fields.reshape(TOKENS, width)
    own_grads = cotangent.reshape(TOKENS, width)
    lengths = (HALF, QUARTER, QUARTER, QUARTER, HALF, HALF)
    picked = call(order_kernel, [((rows, TOKENS), BF) for rows in lengths], name="order", flops=LOAD)
    inner_lat, outer_lat, lon_piece, diag_piece, inner_own, outer_own = call(
        pack_kernel,
        [((rows, 2 * width), BF) for rows in lengths[:4]] + [((HALF, 2 * width), F32)] * 2,
        own_fields, own_grads, *picked,
        name="pack", flops=LOAD,
    )
    inner_in = lax.ppermute(inner_lat, both, lat_route)
    lon_in = lax.ppermute(lon_piece, both, lon_route)
    outer_in = lax.ppermute(outer_lat, both, lat_route)
    diag_in = lax.ppermute(diag_piece, both, diag_route)

    split = (lat_size, width // 2, 4 * width // lat_size)
    per_window = [
        ((WIN, width), BF),
        ((WIN, width), BF),
        ((width // 2, WIN), BF),
        ((width // 2, WIN), BF),
        ((WIN, 3 * width), BF),
        ((WIN, width), BF),
    ]
    scratch = [pltpu.VMEM((width, WIN), BF)] * 2 + [pltpu.VMEM((width // 2, WIN), BF)]
    grad_so_far, *inner = call(
        inner_kernel, [(split, F32), *per_window], inner_own, inner_in, qkv_weight, proj_weight,
        name="inner", flops=10**9, scratch=scratch,
    )
    send_grad, *outer = call(
        outer_kernel, [(split, BF), *per_window],
        outer_own, lon_in, outer_in, diag_in, qkv_weight, proj_weight, grad_so_far,
        name="outer", flops=10**9, scratch=scratch,
    )
    sibling = [(j, j ^ 1) for j in range(lon_size)]
    received = lax.ppermute(send_grad, "lon", sibling)
    kept, *results = call(
        output_kernel, [(split, BF), ((WIN, 2 * width), BF), ((WIN, 2 * width), BF)],
        *inner, *outer, qkv_weight, proj_weight,
        name="outputs", flops=10**9,
    )

    slots = lat_size
    bits = lat_size.bit_length() - 1
    for phase in range(bits):
        slots //= 2
        half = ((slots, *split[1:]), BF)
        send, kept = call(halve_kernel, [half, half], kept, received, name=f"halve{slots}")
        route = [
            (i * lon_size + j, (i ^ (1 << (phase if j % 2 == 0 else bits - 1 - phase))) * lon_size + j)
            for i in range(lat_size)
            for j in range(lon_size)
        ]
        received = lax.ppermute(send, both, route)

    rows = width // lon_size
    share = ((rows, split[2]), BF)
    parts = call(line_parts_kernel, [share] * (lon_size // 2), kept, received, name="line_parts")
    arrived = [
        lax.ppermute(parts[step], "lon", [(j, j ^ (2 * step)) for j in range(lon_size)])
        for step in line_order(lon_size // 2)
    ]
    lat_back, lon_back, diag_back = call(
        pack_back_kernel, [((rows, 2 * width), BF) for rows in (HALF + QUARTER, QUARTER, QUARTER)],
        parts[-1], *results,
        name="pack_back", unread=(0,),
    )
    lat_home = lax.ppermute(lat_back, both, back(lat_route))
    diag_home = lax.ppermute(diag_back, both, back(diag_route))
    lon_home = lax.ppermute(lon_back, both, back(lon_route))
    (line_sum,) = call(sum_kernel, [share], parts[0], *arrived, name="line_sum", flops=LONG)
    shared = [
        lax.ppermute(line_sum, "lat", [(i, i ^ step) for i in range(lat_size)]) for step in range(1, lat_size)
    ]
    (placed,) = call(
        place_kernel, [((TOKENS, 2 * width), F32)], *results, lat_home, name="place"
    )
    field_out, d_fields, done = call(
        place_rest_kernel,
        [((TOKENS, width), BF), ((TOKENS, width), BF), ((8, LANES), F32)],
        placed, lon_home, diag_home,
        name="place_rest",
    )
    qkv_grad, proj_grad = call(
        finish_kernel,
        [((rows, 3 * width), F32), ((rows, width), F32)],
        done, line_sum, *shared,
        name="finish", unread=(0,), scratch=[pltpu.VMEM((lat_size, *share[0]), F32)],
    )
    return (field_out.reshape(fields.shape), d_fields.reshape(fields.shape), qkv_grad, jnp.transpose(proj_grad))


def solution(mesh):
    placed = (P(None, "lat", "lon", None), P(None, "lat", "lon", None), P(), P())
    return jax.shard_map(
        per_device,
        mesh=mesh,
        in_specs=placed,
        out_specs=(
            P(None, "lat", "lon", None),
            P(None, "lat", "lon", None),
            P("lon", None),
            P(None, "lon"),
        ),
        check_vma=False,
    )
```

```python
import functools

import jax
import jax.numpy as jnp
from jax import lax
from jax.experimental import pallas as pl
from jax.experimental.pallas import tpu as pltpu
from jax.sharding import PartitionSpec as P

HEADS = 8
WIN_LAT = 6
WIN_LON = 12
LEVELS = 2
COLS = 24
HALF_LAT = WIN_LAT // 2
HALF_LON = WIN_LON // 2
HALF = LEVELS * HALF_LAT * WIN_LON
WIN = 2 * HALF
TOKENS = 2 * WIN
QUARTER = HALF // 2
LANES = 128

epsilon = 1e-05
LONG = 2 * 10**9
LOAD = 5 * 10**9
BF = jnp.bfloat16
F32 = jnp.float32


def dot(a, b, dims):
    return lax.dot_general(a, b, (dims, ((), ())), preferred_element_type=F32)


NN = ((1,), (0,))
NT = ((1,), (1,))
TN = ((0,), (0,))


def div(x, by):
    return (x * ((65536 + by - 1) // by)) >> 16


def own_token(level, row, col):
    return level * (WIN_LAT * COLS) + row * COLS + col


def inner_token(v, first):
    level = div(v, HALF_LAT * WIN_LON)
    rest = v - level * (HALF_LAT * WIN_LON)
    row = div(rest, WIN_LON)
    return own_token(level, first + row, HALF_LON + rest - row * WIN_LON)


def half_token(v, first, col):
    level = div(v, HALF_LAT * HALF_LON)
    rest = v - level * (HALF_LAT * HALF_LON)
    row = div(rest, HALF_LON)
    return jnp.where(v < QUARTER, own_token(level, first + row, col + rest - row * HALF_LON), -1)


def sources():
    even = lax.rem(lax.axis_index("lon"), 2) == 0
    sent = jnp.where(even, 0, HALF_LAT)
    kept = HALF_LAT - sent
    outer = HALF_LON + WIN_LON
    return (
        (lambda v: inner_token(v, sent), HALF),
        (lambda v: half_token(v, sent, outer), QUARTER),
        (lambda v: half_token(v, sent, 0), QUARTER),
        (lambda v: half_token(v, kept, 0), QUARTER),
        (lambda v: inner_token(v, kept), HALF),
        (lambda v: half_token(v, kept, outer), HALF),
    )


def picks(source, rows, columns):
    index = source(lax.broadcasted_iota(jnp.int32, (rows, 1), 0))
    return (index == lax.broadcasted_iota(jnp.int32, (rows, columns), 1)).astype(BF)


def puts(source, rows, columns):
    index = source(lax.broadcasted_iota(jnp.int32, (1, columns), 1))
    return (lax.broadcasted_iota(jnp.int32, (rows, columns), 0) == index).astype(BF)


def first_rows(v):
    return v


def last_rows(v):
    return v - QUARTER


def order_kernel(*outs):
    for out, (source, rows) in zip(outs, sources()):
        out[...] = picks(source, rows, TOKENS)


def pack_kernel(fields, cotangent, *refs):
    count = len(refs) // 2
    width = fields.shape[1]
    for pick, out in zip(refs[:count], refs[count:]):
        out[:, :width] = dot(pick[...], fields[...], NN).astype(out.dtype)
        out[:, width:] = dot(pick[...], cotangent[...], NN).astype(out.dtype)


def swap_bits(index, size, core):
    bits = size.bit_length() - 1
    turned = sum(((index >> b) & 1) << (bits - 1 - b) for b in range(bits))
    return jnp.where(core == 0, index, turned)


def shares(transposed, out, lon, core_of, lon_size):
    rows = transposed.shape[0] // lon_size
    chip = lon >> 1
    for step in range(lon_size // 2):
        start = pl.multiple_of(((chip ^ step) * 2 + core_of) * rows, rows)
        out[step * rows : (step + 1) * rows, :] = transposed[pl.ds(start, rows), :]


def transpose_bf16(block):
    return jnp.transpose(block.astype(F32)).astype(BF)


def put_split(out, lanes_from, block, lat, core, so_far=None):
    size, _, width = out.shape
    for at in range(0, block.shape[1], width):
        slot = swap_bits(lat ^ ((lanes_from + at) // width), size, core)
        part = block[:, at : at + width]
        if so_far is not None:
            part = part + so_far[slot]
        out[slot] = part.astype(out.dtype)


def normalise(x):
    mean = jnp.mean(x, -1, keepdims=True)
    centred = x - mean
    variance = jnp.mean(centred * centred, -1, keepdims=True)
    inv_std = lax.rsqrt(variance + epsilon)
    return centred * inv_std, inv_std


def project(both, qkv_weight, proj_weight):
    width = both.shape[1] // 2
    normed, _ = normalise(both[:, :width])
    projected = dot(normed.astype(BF), qkv_weight[...], NN)
    return normed, projected, dot(both[:, width:].astype(BF), proj_weight[...], NT)


def own_kernel(
    fields, cotangent, pick_lat, pick_diag, pick_own, inner_own, qkv_weight, proj_weight,
    outer_lat, diag, outer_own, normed, projected, d_mixed,
):
    pack_kernel(fields, cotangent, pick_lat, pick_diag, pick_own, outer_lat, diag, outer_own)
    normed[...], projected[...], d_mixed[...] = project(inner_own[...], qkv_weight, proj_weight)


def inner_kernel(own, own_normed, own_projected, own_d_mixed, lat_in, qkv_weight, proj_weight, send_grad, *refs):
    arrived = lat_in[...].astype(F32)
    parts = project(arrived, qkv_weight, proj_weight)
    both = jnp.concatenate([own[...], arrived], axis=0)
    parts = [jnp.concatenate([mine[...], part], axis=0) for mine, part in zip((own_normed, own_projected, own_d_mixed), parts)]
    one_window(both, *parts, None, send_grad, *refs)


def outer_kernel(own, lon_in, lat_in, diag_in, qkv_weight, proj_weight, grad_so_far, send_grad, *refs):
    last = picks(last_rows, HALF, QUARTER)
    both = jnp.concatenate(
        [
            own[...] + dot(last, lon_in[...], NN),
            dot(picks(first_rows, HALF, QUARTER), lat_in[...], NN) + dot(last, diag_in[...], NN),
        ],
        axis=0,
    )
    one_window(both, *project(both, qkv_weight, proj_weight), grad_so_far, send_grad, *refs)


def one_window(
    both, normed, projected, d_mixed, grad_so_far,
    send_grad, windows_out, grads_out, normed_t_out, grads_t_out, d_projected, mixed, normed_t, grads_t, send_rows,
):
    width = both.shape[1] // 2
    lat, lon = lax.axis_index("lat"), lax.axis_index("lon")
    lat_size, lon_size = lax.axis_size("lat"), lax.axis_size("lon")
    core = lax.rem(lon, 2)
    even = core == 0
    blocks = both[:, :width], both[:, width:]
    x = blocks[0]
    windows_out[...] = x.astype(BF)
    grads = blocks[1].astype(BF)
    grads_out[...] = grads
    projected, d_mixed = projected.astype(BF), d_mixed.astype(BF)

    head_size = width // HEADS
    factor = head_size ** (-0.5)
    apart = jnp.where(even, lat == lat_size - 1, lat == 0).astype(jnp.int32)
    half_b = (lax.broadcasted_iota(jnp.int32, (WIN, 2 * WIN), 0) >= HALF).astype(jnp.int32)
    at_a = lax.broadcasted_iota(jnp.int32, (WIN, 2 * WIN), 1)
    at_a = jnp.where(at_a >= WIN, at_a - WIN, at_a)
    half_a = (at_a >= HALF).astype(jnp.int32)
    allowed = ((half_a != half_b).astype(jnp.int32) * apart) == 0
    first_head = lax.broadcasted_iota(jnp.int32, (WIN, LANES), 1) < head_size
    zero = jnp.zeros((WIN, LANES), BF)

    def split_heads(block):
        return jnp.concatenate([jnp.where(first_head, block, zero), jnp.where(first_head, zero, block)], axis=0)

    def join_heads(block):
        return jnp.where(first_head, block[:WIN], block[WIN:]).astype(BF)

    pairs = range(width // LANES)

    def blocks_of(array, lanes_from):
        return [array[:, lanes_from + pair * LANES : lanes_from + (pair + 1) * LANES] for pair in pairs]

    def store(out, lanes_from, blocks):
        for pair, block in zip(pairs, blocks):
            out[:, lanes_from + pair * LANES : lanes_from + (pair + 1) * LANES] = block.astype(out.dtype)

    k, v = blocks_of(projected, width), blocks_of(projected, 2 * width)
    q2 = [split_heads(block) for block in blocks_of(projected, 0)]
    dm2 = [split_heads(block) for block in blocks_of(d_mixed, 0)]
    scores = [jnp.where(allowed, dot(k[p], q2[p], NT) * factor, -1e30) for p in pairs]
    d_probs = [dot(v[p], dm2[p], NT) for p in pairs]
    exponents = [jnp.exp(s - jnp.max(s, 0, keepdims=True)) for s in scores]
    probs = [e * (1.0 / jnp.sum(e, 0, keepdims=True)) for e in exponents]
    probs_b = [p.astype(BF) for p in probs]
    store(mixed, 0, [join_heads(dot(probs_b[p], v[p], TN)) for p in pairs])
    store(d_projected, 2 * width, [dot(probs_b[p], dm2[p], NN) for p in pairs])
    d_scores = [
        (probs[p] * (d_probs[p] - jnp.sum(d_probs[p] * probs[p], 0, keepdims=True)) * factor).astype(BF)
        for p in pairs
    ]
    store(d_projected, 0, [join_heads(dot(d_scores[p], k[p], TN)) for p in pairs])
    store(d_projected, width, [dot(d_scores[p], q2[p], NN) for p in pairs])

    normed_t[...] = transpose_bf16(normed)
    grads_t[...] = transpose_bf16(grads)
    shares(normed_t, send_rows, lon, 1 - core, lon_size)
    put_split(send_grad, 0, dot(send_rows[...], d_projected[...], NN), lat, 1 - core, grad_so_far)
    shares(grads_t, send_rows, lon, 1 - core, lon_size)
    put_split(send_grad, 3 * width, dot(send_rows[...], mixed[...], NN), lat, 1 - core, grad_so_far)
    shares(normed_t, normed_t_out, lon, core, lon_size)
    shares(grads_t, grads_t_out, lon, core, lon_size)


def output_kernel(*refs):
    (*windows, qkv_weight, proj_weight, keep_grad, inner_results, outer_results) = refs
    per_window = windows[:6], windows[6:]
    lat, core = lax.axis_index("lat"), lax.rem(lax.axis_index("lon"), 2)
    width = proj_weight.shape[0]
    qkv_grad = sum(dot(w[2][...], w[4][...], NN) for w in per_window)
    proj_grad = sum(dot(w[3][...], w[5][...], NN) for w in per_window)
    put_split(keep_grad, 0, qkv_grad, lat, core)
    put_split(keep_grad, 3 * width, proj_grad, lat, core)
    x, grads, d_projected, mixed = (
        jnp.concatenate([w[i][...] for w in per_window], axis=0) for i in (0, 1, 4, 5)
    )
    x = x.astype(F32)
    normed, inv_std = normalise(x)
    output = (x + dot(mixed, proj_weight[...], NN)).astype(BF)
    d_normed = dot(d_projected, qkv_weight[...], NT)
    d_inputs = grads.astype(F32) + inv_std * (
        d_normed
        - jnp.mean(d_normed, -1, keepdims=True)
        - normed * jnp.mean(d_normed * normed, -1, keepdims=True)
    )
    d_inputs = d_inputs.astype(BF)
    for at, out in ((0, inner_results), (WIN, outer_results)):
        out[:, :width] = output[at : at + WIN]
        out[:, width:] = d_inputs[at : at + WIN]


def pack_back_kernel(_, inner_results, outer_results, lat_out, lon_out, diag_out):
    inner_y = inner_results[...].astype(F32)[HALF:]
    outer = outer_results[...].astype(F32)
    outer_x, outer_y = outer[:HALF].astype(BF), outer[HALF:].astype(BF)
    first, last = puts(first_rows, QUARTER, HALF), puts(last_rows, QUARTER, HALF)
    lat_out[...] = jnp.concatenate([inner_y, dot(first, outer_y, NN)], axis=0).astype(BF)
    lon_out[...] = dot(last, outer_x, NN).astype(BF)
    diag_out[...] = dot(last, outer_y, NN).astype(BF)


def place_kernel(inner_results, outer_results, lat_in, placed):
    inner_lat, outer_lat, _, _, inner_own, outer_own = (source for source, _ in sources())

    def lat(v):
        return jnp.where(v < HALF, inner_lat(v), outer_lat(v - HALF))

    def only_first(source):
        return lambda v: jnp.where(v < HALF, source(v), -1)

    placed[...] = (
        dot(puts(only_first(inner_own), TOKENS, WIN), inner_results[...], NN)
        + dot(puts(only_first(outer_own), TOKENS, WIN), outer_results[...], NN)
        + dot(puts(lat, TOKENS, HALF + QUARTER), lat_in[...], NN)
    )


def place_rest_kernel(placed, lon_in, diag_in, field_out, d_fields, done):
    done[...] = jnp.zeros_like(done)
    width = field_out.shape[1]
    _, _, lon, diag, _, _ = (source for source, _ in sources())
    total = (
        placed[...]
        + dot(puts(lon, TOKENS, QUARTER), lon_in[...], NN)
        + dot(puts(diag, TOKENS, QUARTER), diag_in[...], NN)
    ).astype(BF)
    field_out[...] = total[:, :width]
    d_fields[...] = total[:, width:]


def halve_kernel(kept, received, send, keep):
    for slot in range(send.shape[0]):
        for out, source in ((send, 2 * slot + 1), (keep, 2 * slot)):
            out[slot] = (kept[source].astype(F32) + received[source].astype(F32)).astype(BF)


def line_parts_kernel(kept, received, keep, *sends):
    rows = keep.shape[0]
    for step, out in enumerate((keep, *sends)):
        at = slice(step * rows, (step + 1) * rows)
        out[...] = (kept[0, at].astype(F32) + received[0, at].astype(F32)).astype(out.dtype)


def sum_kernel(*refs):
    *parts, out = refs
    total = parts[0][...].astype(F32)
    for part in parts[1:]:
        total = total + part[...].astype(F32)
    out[...] = total.astype(out.dtype)


def finish_kernel(_, *refs):
    *parts, qkv_out, proj_out, shared = refs
    lat = lax.axis_index("lat")
    for step, part in enumerate(parts):
        shared[lat ^ step] = part[...].astype(F32)
    width = shared.shape[2]
    for slot in range(shared.shape[0]):
        at = slot * width
        out, at = (qkv_out, at) if at < qkv_out.shape[1] else (proj_out, at - qkv_out.shape[1])
        out[:, at : at + width] = shared[slot]


def call(kernel, outs, *args, name, flops=0, limit=32, scratch=(), unread=()):
    vmem = pl.BlockSpec(memory_space=pltpu.VMEM)
    anywhere = pl.BlockSpec(memory_space=pl.ANY)
    shapes = [jax.ShapeDtypeStruct(shape, dtype) for shape, dtype in outs]
    nbytes = sum(a.size * a.dtype.itemsize for a in (*args, *shapes))
    return pl.pallas_call(
        kernel,
        out_shape=shapes,
        in_specs=[anywhere if i in unread else vmem for i in range(len(args))],
        out_specs=[vmem] * len(shapes),
        scratch_shapes=scratch,
        compiler_params=pltpu.CompilerParams(vmem_limit_bytes=limit * 2**20),
        cost_estimate=pl.CostEstimate(flops=flops, bytes_accessed=nbytes, transcendentals=0),
        name=name,
    )(*args)


def routes(lat_size, lon_size):
    lat, lon, diag = [], [], []
    for i in range(lat_size):
        for j in range(lon_size):
            step = -1 if j % 2 == 0 else 1
            before = (j - 1) % lon_size
            me = i * lon_size + j
            lat.append((me, ((i + step) % lat_size) * lon_size + j))
            lon.append((me, i * lon_size + before))
            diag.append((me, ((i - step) % lat_size) * lon_size + before))
    return lat, lon, diag


def per_device(fields, cotangent, qkv_weight, proj_weight):
    levels, row_count, col_count, width = fields.shape
    lat_size, lon_size = lax.axis_size("lat"), lax.axis_size("lon")
    both = ("lat", "lon")
    lat_route, lon_route, diag_route = routes(lat_size, lon_size)

    def back(route):
        return [(target, source) for source, target in route]

    own_fields = fields.reshape(TOKENS, width)
    own_grads = cotangent.reshape(TOKENS, width)
    lengths = (HALF, QUARTER, QUARTER, QUARTER, HALF, HALF)
    picked = call(order_kernel, [((rows, TOKENS), BF) for rows in lengths], name="order", flops=LOAD)
    pick_inner, pick_outer, pick_lon, pick_diag, pick_own, pick_outer_own = picked
    whole, half = ((HALF, 2 * width), F32), ((HALF, 2 * width), BF)
    quarter = ((QUARTER, 2 * width), BF)
    inner_lat, lon_piece, inner_own = call(
        pack_kernel, [half, quarter, whole], own_fields, own_grads, pick_inner, pick_lon, pick_own,
        name="pack", flops=LOAD,
    )
    outer_lat, diag_piece, outer_own, *own_parts = call(
        own_kernel,
        [quarter, quarter, whole, *(((HALF, lanes), F32) for lanes in (width, 3 * width, width))],
        own_fields, own_grads, pick_outer, pick_diag, pick_outer_own, inner_own, qkv_weight, proj_weight,
        name="own", flops=5 * 10**8,
    )
    inner_in = lax.ppermute(inner_lat, both, lat_route)
    lon_in = lax.ppermute(lon_piece, both, lon_route)
    outer_in = lax.ppermute(outer_lat, both, lat_route)
    diag_in = lax.ppermute(diag_piece, both, diag_route)

    split = (lat_size, width // 2, 4 * width // lat_size)
    per_window = [
        ((WIN, width), BF),
        ((WIN, width), BF),
        ((width // 2, WIN), BF),
        ((width // 2, WIN), BF),
        ((WIN, 3 * width), BF),
        ((WIN, width), BF),
    ]
    scratch = [pltpu.VMEM((width, WIN), BF)] * 2 + [pltpu.VMEM((width // 2, WIN), BF)]
    grad_so_far, *inner = call(
        inner_kernel, [(split, F32), *per_window], inner_own, *own_parts, inner_in, qkv_weight, proj_weight,
        name="inner", flops=10**9, scratch=scratch,
    )
    send_grad, *outer = call(
        outer_kernel, [(split, BF), *per_window],
        outer_own, lon_in, outer_in, diag_in, qkv_weight, proj_weight, grad_so_far,
        name="outer", flops=10**9, scratch=scratch,
    )
    sibling = [(j, j ^ 1) for j in range(lon_size)]
    received = lax.ppermute(send_grad, "lon", sibling)
    kept, *results = call(
        output_kernel, [(split, BF), ((WIN, 2 * width), BF), ((WIN, 2 * width), BF)],
        *inner, *outer, qkv_weight, proj_weight,
        name="outputs", flops=10**9,
    )

    slots = lat_size
    bits = lat_size.bit_length() - 1
    for phase in range(bits):
        slots //= 2
        half = ((slots, *split[1:]), BF)
        send, kept = call(halve_kernel, [half, half], kept, received, name=f"halve{slots}")
        route = [
            (i * lon_size + j, (i ^ (1 << (phase if j % 2 == 0 else bits - 1 - phase))) * lon_size + j)
            for i in range(lat_size)
            for j in range(lon_size)
        ]
        received = lax.ppermute(send, both, route)

    rows = width // lon_size
    share = ((rows, split[2]), BF)
    parts = call(line_parts_kernel, [share] * (lon_size // 2), kept, received, name="line_parts")
    arrived = [
        lax.ppermute(parts[step], "lon", [(j, j ^ (2 * step)) for j in range(lon_size)])
        for step in range(lon_size // 2 - 1, 0, -1)
    ]
    lat_back, lon_back, diag_back = call(
        pack_back_kernel, [((rows, 2 * width), BF) for rows in (HALF + QUARTER, QUARTER, QUARTER)],
        parts[-1], *results,
        name="pack_back", unread=(0,),
    )
    lat_home = lax.ppermute(lat_back, both, back(lat_route))
    diag_home = lax.ppermute(diag_back, both, back(diag_route))
    lon_home = lax.ppermute(lon_back, both, back(lon_route))
    (line_sum,) = call(sum_kernel, [share], parts[0], *arrived, name="line_sum", flops=LONG)
    shared = [
        lax.ppermute(line_sum, "lat", [(i, i ^ step) for i in range(lat_size)]) for step in range(1, lat_size)
    ]
    (placed,) = call(
        place_kernel, [((TOKENS, 2 * width), F32)], *results, lat_home, name="place"
    )
    field_out, d_fields, done = call(
        place_rest_kernel,
        [((TOKENS, width), BF), ((TOKENS, width), BF), ((8, LANES), F32)],
        placed, lon_home, diag_home,
        name="place_rest",
    )
    qkv_grad, proj_grad = call(
        finish_kernel,
        [((rows, 3 * width), F32), ((rows, width), F32)],
        done, line_sum, *shared,
        name="finish", unread=(0,), scratch=[pltpu.VMEM((lat_size, *share[0]), F32)],
    )
    return (field_out.reshape(fields.shape), d_fields.reshape(fields.shape), qkv_grad, jnp.transpose(proj_grad))


def solution(mesh):
    placed = (P(None, "lat", "lon", None), P(None, "lat", "lon", None), P(), P())
    return jax.shard_map(
        per_device,
        mesh=mesh,
        in_specs=placed,
        out_specs=(
            P(None, "lat", "lon", None),
            P(None, "lat", "lon", None),
            P("lon", None),
            P(None, "lon"),
        ),
        check_vma=False,
    )
```

```python
import functools

import jax
import jax.numpy as jnp
from jax import lax
from jax.experimental import pallas as pl
from jax.experimental.pallas import tpu as pltpu
from jax.sharding import PartitionSpec as P

HEADS = 8
WIN_LAT = 6
WIN_LON = 12
LEVELS = 2
COLS = 24
HALF_LAT = WIN_LAT // 2
HALF_LON = WIN_LON // 2
HALF = LEVELS * HALF_LAT * WIN_LON
WIN = 2 * HALF
TOKENS = 2 * WIN
QUARTER = HALF // 2
LANES = 128

epsilon = 1e-05
LONG = 13 * 10**8
LOAD = 5 * 10**9
BF = jnp.bfloat16
F32 = jnp.float32


def dot(a, b, dims):
    return lax.dot_general(a, b, (dims, ((), ())), preferred_element_type=F32)


NN = ((1,), (0,))
NT = ((1,), (1,))
TN = ((0,), (0,))


def div(x, by):
    return (x * ((65536 + by - 1) // by)) >> 16


def own_token(level, row, col):
    return level * (WIN_LAT * COLS) + row * COLS + col


def inner_token(v, first):
    level = div(v, HALF_LAT * WIN_LON)
    rest = v - level * (HALF_LAT * WIN_LON)
    row = div(rest, WIN_LON)
    return own_token(level, first + row, HALF_LON + rest - row * WIN_LON)


def half_token(v, first, col):
    level = div(v, HALF_LAT * HALF_LON)
    rest = v - level * (HALF_LAT * HALF_LON)
    row = div(rest, HALF_LON)
    return jnp.where(v < QUARTER, own_token(level, first + row, col + rest - row * HALF_LON), -1)


def sources():
    even = lax.rem(lax.axis_index("lon"), 2) == 0
    sent = jnp.where(even, 0, HALF_LAT)
    kept = HALF_LAT - sent
    outer = HALF_LON + WIN_LON
    return (
        (lambda v: inner_token(v, sent), HALF),
        (lambda v: half_token(v, sent, outer), QUARTER),
        (lambda v: half_token(v, sent, 0), QUARTER),
        (lambda v: half_token(v, kept, 0), QUARTER),
        (lambda v: inner_token(v, kept), HALF),
        (lambda v: half_token(v, kept, outer), HALF),
    )


def picks(source, rows, columns):
    index = source(lax.broadcasted_iota(jnp.int32, (rows, 1), 0))
    return (index == lax.broadcasted_iota(jnp.int32, (rows, columns), 1)).astype(BF)


def puts(source, rows, columns):
    index = source(lax.broadcasted_iota(jnp.int32, (1, columns), 1))
    return (lax.broadcasted_iota(jnp.int32, (rows, columns), 0) == index).astype(BF)


def first_rows(v):
    return v


def last_rows(v):
    return v - QUARTER


def order_kernel(*outs):
    for out, (source, rows) in zip(outs, sources()):
        out[...] = picks(source, rows, TOKENS)


def pack_kernel(fields, cotangent, *refs):
    count = len(refs) // 2
    width = fields.shape[1]
    for pick, out in zip(refs[:count], refs[count:]):
        out[:, :width] = dot(pick[...], fields[...], NN).astype(out.dtype)
        out[:, width:] = dot(pick[...], cotangent[...], NN).astype(out.dtype)


def swap_bits(index, size, core):
    bits = size.bit_length() - 1
    turned = sum(((index >> b) & 1) << (bits - 1 - b) for b in range(bits))
    return jnp.where(core == 0, index, turned)


def shares(transposed, out, lon, core_of, lon_size):
    rows = transposed.shape[0] // lon_size
    chip = lon >> 1
    for step in range(lon_size // 2):
        start = pl.multiple_of(((chip ^ step) * 2 + core_of) * rows, rows)
        out[step * rows : (step + 1) * rows, :] = transposed[pl.ds(start, rows), :]


def transpose_bf16(block):
    return jnp.transpose(block.astype(F32)).astype(BF)


def slot_product(slot, size, lat, core, windows):
    share = lat ^ swap_bits(slot, size, core)
    total = None
    for left, right in windows:
        lanes = right.shape[1] // size
        of_proj = (share >= 3 * size // 4).astype(jnp.int32)
        part = dot(left[of_proj], right[:, pl.ds(pl.multiple_of(share * lanes, lanes), lanes)], NN)
        total = part if total is None else total + part
    return total


def normalise(x):
    mean = jnp.mean(x, -1, keepdims=True)
    centred = x - mean
    variance = jnp.mean(centred * centred, -1, keepdims=True)
    inv_std = lax.rsqrt(variance + epsilon)
    return centred * inv_std, inv_std


def project(both, qkv_weight, proj_weight):
    width = both.shape[1] // 2
    normed, _ = normalise(both[:, :width])
    projected = dot(normed.astype(BF), qkv_weight[...], NN)
    return normed, projected, dot(both[:, width:].astype(BF), proj_weight[...], NT)


def own_kernel(
    fields, cotangent, pick_lat, pick_diag, pick_own, inner_own, qkv_weight, proj_weight,
    outer_lat, diag, outer_own, normed, projected, d_mixed,
):
    pack_kernel(fields, cotangent, pick_lat, pick_diag, pick_own, outer_lat, diag, outer_own)
    normed[...], projected[...], d_mixed[...] = project(inner_own[...], qkv_weight, proj_weight)


def inner_kernel(own, own_normed, own_projected, own_d_mixed, lat_in, qkv_weight, proj_weight, send_grad, *refs):
    arrived = lat_in[...].astype(F32)
    parts = project(arrived, qkv_weight, proj_weight)
    both = jnp.concatenate([own[...], arrived], axis=0)
    mine = own_normed, own_projected, own_d_mixed
    parts = [jnp.concatenate([first[...], second], axis=0) for first, second in zip(mine, parts)]
    one_window(both, *parts, *refs)
    *_, right, left, _, _ = refs
    lat, core, size = place()
    for slot in range(size):
        send_grad[slot] = slot_product(slot, size, lat, 1 - core, [(left, right)])


def outer_kernel(own, lon_in, lat_in, diag_in, qkv_weight, proj_weight, grad_so_far, send_first, send_rest, *refs):
    last = picks(last_rows, HALF, QUARTER)
    both = jnp.concatenate(
        [
            own[...] + dot(last, lon_in[...], NN),
            dot(picks(first_rows, HALF, QUARTER), lat_in[...], NN) + dot(last, diag_in[...], NN),
        ],
        axis=0,
    )
    one_window(both, *project(both, qkv_weight, proj_weight), *refs)
    *_, right, left, _, _ = refs
    lat, core, size = place()
    for slot in first_order(size):
        total = grad_so_far[slot] + slot_product(slot, size, lat, 1 - core, [(left, right)])
        (send_first if slot % 2 else send_rest)[slot // 2] = total.astype(BF)


def place():
    return lax.axis_index("lat"), lax.rem(lax.axis_index("lon"), 2), lax.axis_size("lat")


def first_order(size):
    return [*range(1, size, 2), *range(0, size, 2)]


def one_window(
    both, normed, projected, d_mixed,
    windows_out, grads_out, left_keep, right, left_send, normed_t, grads_t,
):
    width = both.shape[1] // 2
    lat, core, lat_size = place()
    lon, lon_size = lax.axis_index("lon"), lax.axis_size("lon")
    even = core == 0
    blocks = both[:, :width], both[:, width:]
    x = blocks[0]
    windows_out[...] = x.astype(BF)
    grads = blocks[1].astype(BF)
    grads_out[...] = grads
    projected, d_mixed = projected.astype(BF), d_mixed.astype(BF)

    head_size = width // HEADS
    factor = head_size ** (-0.5)
    apart = jnp.where(even, lat == lat_size - 1, lat == 0).astype(jnp.int32)
    half_b = (lax.broadcasted_iota(jnp.int32, (WIN, 2 * WIN), 0) >= HALF).astype(jnp.int32)
    at_a = lax.broadcasted_iota(jnp.int32, (WIN, 2 * WIN), 1)
    at_a = jnp.where(at_a >= WIN, at_a - WIN, at_a)
    half_a = (at_a >= HALF).astype(jnp.int32)
    allowed = ((half_a != half_b).astype(jnp.int32) * apart) == 0
    first_head = lax.broadcasted_iota(jnp.int32, (WIN, LANES), 1) < head_size
    zero = jnp.zeros((WIN, LANES), BF)

    def split_heads(block):
        return jnp.concatenate([jnp.where(first_head, block, zero), jnp.where(first_head, zero, block)], axis=0)

    def join_heads(block):
        return jnp.where(first_head, block[:WIN], block[WIN:]).astype(BF)

    pairs = range(width // LANES)

    def blocks_of(array, lanes_from):
        return [array[:, lanes_from + pair * LANES : lanes_from + (pair + 1) * LANES] for pair in pairs]

    def store(out, lanes_from, blocks):
        for pair, block in zip(pairs, blocks):
            out[:, lanes_from + pair * LANES : lanes_from + (pair + 1) * LANES] = block.astype(out.dtype)

    k, v = blocks_of(projected, width), blocks_of(projected, 2 * width)
    q2 = [split_heads(block) for block in blocks_of(projected, 0)]
    dm2 = [split_heads(block) for block in blocks_of(d_mixed, 0)]
    scores = [jnp.where(allowed, dot(k[p], q2[p], NT) * factor, -1e30) for p in pairs]
    d_probs = [dot(v[p], dm2[p], NT) for p in pairs]
    exponents = [jnp.exp(s - jnp.max(s, 0, keepdims=True)) for s in scores]
    probs = [e * (1.0 / jnp.sum(e, 0, keepdims=True)) for e in exponents]
    probs_b = [p.astype(BF) for p in probs]
    store(right, 3 * width, [join_heads(dot(probs_b[p], v[p], TN)) for p in pairs])
    store(right, 2 * width, [dot(probs_b[p], dm2[p], NN) for p in pairs])
    d_scores = [
        (probs[p] * (d_probs[p] - jnp.sum(d_probs[p] * probs[p], 0, keepdims=True)) * factor).astype(BF)
        for p in pairs
    ]
    store(right, 0, [join_heads(dot(d_scores[p], k[p], TN)) for p in pairs])
    store(right, width, [dot(d_scores[p], q2[p], NN) for p in pairs])

    normed_t[...] = transpose_bf16(normed)
    grads_t[...] = transpose_bf16(grads)
    for index, source in enumerate((normed_t, grads_t)):
        shares(source, left_send.at[index], lon, 1 - core, lon_size)
        shares(source, left_keep.at[index], lon, core, lon_size)


def keep_kernel(inner_left, inner_right, outer_left, outer_right, keep_first):
    lat, core, size = place()
    windows = [(inner_left, inner_right), (outer_left, outer_right)]
    for slot in range(1, size, 2):
        keep_first[slot // 2] = slot_product(slot, size, lat, core, windows).astype(BF)


def output_kernel(_, *refs):
    (*windows, qkv_weight, proj_weight, keep_rest, inner_results, outer_results) = refs
    per_window = windows[:4], windows[4:]
    lat, core, size = place()
    width = proj_weight.shape[0]
    for slot in range(0, size, 2):
        keep_rest[slot // 2] = slot_product(slot, size, lat, core, [w[2:] for w in per_window]).astype(BF)
    x, grads, right = (jnp.concatenate([w[i][...] for w in per_window], axis=0) for i in (0, 1, 3))
    d_projected, mixed = right[:, : 3 * width], right[:, 3 * width :]
    x = x.astype(F32)
    normed, inv_std = normalise(x)
    output = (x + dot(mixed, proj_weight[...], NN)).astype(BF)
    d_normed = dot(d_projected, qkv_weight[...], NT)
    d_inputs = grads.astype(F32) + inv_std * (
        d_normed
        - jnp.mean(d_normed, -1, keepdims=True)
        - normed * jnp.mean(d_normed * normed, -1, keepdims=True)
    )
    d_inputs = d_inputs.astype(BF)
    for at, out in ((0, inner_results), (WIN, outer_results)):
        out[:, :width] = output[at : at + WIN]
        out[:, width:] = d_inputs[at : at + WIN]


def pack_lon_kernel(outer_results, lon_out):
    outer_x = outer_results[...].astype(F32)[:HALF].astype(BF)
    lon_out[...] = dot(puts(last_rows, QUARTER, HALF), outer_x, NN).astype(BF)


def pack_back_kernel(_, inner_results, outer_results, lat_out, diag_out):
    inner_y = inner_results[...].astype(F32)[HALF:]
    outer_y = outer_results[...].astype(F32)[HALF:].astype(BF)
    lat_out[...] = jnp.concatenate([inner_y, dot(puts(first_rows, QUARTER, HALF), outer_y, NN)], axis=0).astype(BF)
    diag_out[...] = dot(puts(last_rows, QUARTER, HALF), outer_y, NN).astype(BF)


def place_kernel(inner_results, outer_results, lat_in, placed):
    inner_lat, outer_lat, _, _, inner_own, outer_own = (source for source, _ in sources())

    def lat(v):
        return jnp.where(v < HALF, inner_lat(v), outer_lat(v - HALF))

    def only_first(source):
        return lambda v: jnp.where(v < HALF, source(v), -1)

    placed[...] = (
        dot(puts(only_first(inner_own), TOKENS, WIN), inner_results[...], NN)
        + dot(puts(only_first(outer_own), TOKENS, WIN), outer_results[...], NN)
        + dot(puts(lat, TOKENS, HALF + QUARTER), lat_in[...], NN)
    )


def place_rest_kernel(placed, lon_in, diag_in, field_out, d_fields, done):
    done[...] = jnp.zeros_like(done)
    width = field_out.shape[1]
    _, _, lon, diag, _, _ = (source for source, _ in sources())
    total = (
        placed[...]
        + dot(puts(lon, TOKENS, QUARTER), lon_in[...], NN)
        + dot(puts(diag, TOKENS, QUARTER), diag_in[...], NN)
    ).astype(BF)
    field_out[...] = total[:, :width]
    d_fields[...] = total[:, width:]


def halve_kernel(_, *refs):
    *parts, send, keep = refs
    for slot in range(send.shape[0]):
        for out, source in ((send, 2 * slot + 1), (keep, 2 * slot)):
            out[slot] = sum(part[source].astype(F32) for part in parts).astype(BF)


def line_parts_kernel(count, *refs):
    parts, (keep, *sends) = refs[:count], refs[count:]
    rows = keep.shape[0]
    for step, out in enumerate((keep, *sends)):
        at = slice(step * rows, (step + 1) * rows)
        out[...] = sum(part[0, at].astype(F32) for part in parts).astype(out.dtype)


def sum_kernel(*refs):
    *parts, out = refs
    total = parts[0][...].astype(F32)
    for part in parts[1:]:
        total = total + part[...].astype(F32)
    out[...] = total.astype(out.dtype)


def finish_kernel(_, *refs):
    *parts, qkv_out, proj_out, shared = refs
    lat = lax.axis_index("lat")
    for step, part in enumerate(parts):
        shared[lat ^ step] = part[...].astype(F32)
    width = shared.shape[2]
    for slot in range(shared.shape[0]):
        at = slot * width
        out, at = (qkv_out, at) if at < qkv_out.shape[1] else (proj_out, at - qkv_out.shape[1])
        out[:, at : at + width] = shared[slot]


def call(kernel, outs, *args, name, flops=0, limit=32, scratch=(), unread=()):
    vmem = pl.BlockSpec(memory_space=pltpu.VMEM)
    anywhere = pl.BlockSpec(memory_space=pl.ANY)
    shapes = [jax.ShapeDtypeStruct(shape, dtype) for shape, dtype in outs]
    nbytes = sum(a.size * a.dtype.itemsize for a in (*args, *shapes))
    return pl.pallas_call(
        kernel,
        out_shape=shapes,
        in_specs=[anywhere if i in unread else vmem for i in range(len(args))],
        out_specs=[vmem] * len(shapes),
        scratch_shapes=scratch,
        compiler_params=pltpu.CompilerParams(vmem_limit_bytes=limit * 2**20),
        cost_estimate=pl.CostEstimate(flops=flops, bytes_accessed=nbytes, transcendentals=0),
        name=name,
    )(*args)


def routes(lat_size, lon_size):
    lat, lon, diag = [], [], []
    for i in range(lat_size):
        for j in range(lon_size):
            step = -1 if j % 2 == 0 else 1
            before = (j - 1) % lon_size
            me = i * lon_size + j
            lat.append((me, ((i + step) % lat_size) * lon_size + j))
            lon.append((me, i * lon_size + before))
            diag.append((me, ((i - step) % lat_size) * lon_size + before))
    return lat, lon, diag


def per_device(fields, cotangent, qkv_weight, proj_weight):
    levels, row_count, col_count, width = fields.shape
    lat_size, lon_size = lax.axis_size("lat"), lax.axis_size("lon")
    both = ("lat", "lon")
    lat_route, lon_route, diag_route = routes(lat_size, lon_size)

    def back(route):
        return [(target, source) for source, target in route]

    own_fields = fields.reshape(TOKENS, width)
    own_grads = cotangent.reshape(TOKENS, width)
    lengths = (HALF, QUARTER, QUARTER, QUARTER, HALF, HALF)
    picked = call(order_kernel, [((rows, TOKENS), BF) for rows in lengths], name="order", flops=LOAD)
    pick_inner, pick_outer, pick_lon, pick_diag, pick_own, pick_outer_own = picked
    whole, half = ((HALF, 2 * width), F32), ((HALF, 2 * width), BF)
    quarter = ((QUARTER, 2 * width), BF)
    inner_lat, lon_piece, inner_own = call(
        pack_kernel, [half, quarter, whole], own_fields, own_grads, pick_inner, pick_lon, pick_own,
        name="pack", flops=LOAD,
    )
    outer_lat, diag_piece, outer_own, *own_parts = call(
        own_kernel,
        [quarter, quarter, whole, *(((HALF, lanes), F32) for lanes in (width, 3 * width, width))],
        own_fields, own_grads, pick_outer, pick_diag, pick_outer_own, inner_own, qkv_weight, proj_weight,
        name="own", flops=5 * 10**8,
    )
    inner_in = lax.ppermute(inner_lat, both, lat_route)
    lon_in = lax.ppermute(lon_piece, both, lon_route)
    outer_in = lax.ppermute(outer_lat, both, lat_route)
    diag_in = lax.ppermute(diag_piece, both, diag_route)

    split = (lat_size, width // 2, 4 * width // lat_size)
    halves = ((lat_size // 2, *split[1:]), BF)
    per_window = [
        ((WIN, width), BF),
        ((WIN, width), BF),
        ((2, width // 2, WIN), BF),
        ((WIN, 4 * width), BF),
    ]
    scratch = [pltpu.VMEM((2, width // 2, WIN), BF)] + [pltpu.VMEM((width, WIN), BF)] * 2
    grad_so_far, *inner = call(
        inner_kernel, [(split, F32), *per_window], inner_own, *own_parts, inner_in, qkv_weight, proj_weight,
        name="inner", flops=10**9, scratch=scratch,
    )
    send_first, send_rest, *outer = call(
        outer_kernel, [halves, halves, *per_window],
        outer_own, lon_in, outer_in, diag_in, qkv_weight, proj_weight, grad_so_far,
        name="outer", flops=10**9, scratch=scratch,
    )
    sibling = [(j, j ^ 1) for j in range(lon_size)]
    received_first = lax.ppermute(send_first, "lon", sibling)
    received_rest = lax.ppermute(send_rest, "lon", sibling)
    (keep_first,) = call(keep_kernel, [halves], *inner[2:], *outer[2:], name="keep", flops=10**9)

    def halving(phase, send):
        route = [
            (i * lon_size + j, (i ^ (1 << (phase if j % 2 == 0 else bits - 1 - phase))) * lon_size + j)
            for i in range(lat_size)
            for j in range(lon_size)
        ]
        return lax.ppermute(send, both, route)

    bits = lat_size.bit_length() - 1
    (send,) = call(sum_kernel, [halves], keep_first, received_first, name="chip_sum")
    received = halving(0, send)
    keep_rest, *results = call(
        output_kernel, [halves, ((WIN, 2 * width), BF), ((WIN, 2 * width), BF)],
        send, *inner, *outer, qkv_weight, proj_weight,
        name="outputs", flops=10**9, unread=(0,),
    )
    (lon_back,) = call(pack_lon_kernel, [quarter], results[1], name="pack_lon")
    lon_home = lax.ppermute(lon_back, both, back(lon_route))
    kept = [keep_rest, received_rest, received]
    slots = lat_size // 2
    for phase in range(1, bits):
        slots //= 2
        stay = ((slots, *split[1:]), BF)
        send, keep = call(halve_kernel, [stay, stay], lon_home, *kept, name=f"halve{slots}", unread=(0,))
        kept = [keep, halving(phase, send)]

    rows = width // lon_size
    share = ((rows, split[2]), BF)
    parts = call(
        functools.partial(line_parts_kernel, len(kept)), [share] * (lon_size // 2), *kept, name="line_parts"
    )
    arrived = [
        lax.ppermute(parts[step], "lon", [(j, j ^ (2 * step)) for j in range(lon_size)])
        for step in range(lon_size // 2 - 1, 0, -1)
    ]
    lat_back, diag_back = call(
        pack_back_kernel, [((HALF + QUARTER, 2 * width), BF), quarter],
        parts[1], *results,
        name="pack_back", unread=(0,),
    )
    lat_home = lax.ppermute(lat_back, both, back(lat_route))
    diag_home = lax.ppermute(diag_back, both, back(diag_route))
    (line_sum,) = call(sum_kernel, [share], parts[0], *arrived, name="line_sum", flops=LONG)
    shared = [
        lax.ppermute(line_sum, "lat", [(i, i ^ step) for i in range(lat_size)]) for step in range(1, lat_size)
    ]
    (placed,) = call(
        place_kernel, [((TOKENS, 2 * width), F32)], *results, lat_home, name="place"
    )
    field_out, d_fields, done = call(
        place_rest_kernel,
        [((TOKENS, width), BF), ((TOKENS, width), BF), ((8, LANES), F32)],
        placed, lon_home, diag_home,
        name="place_rest",
    )
    qkv_grad, proj_grad = call(
        finish_kernel,
        [((rows, 3 * width), F32), ((rows, width), F32)],
        done, line_sum, *shared,
        name="finish", unread=(0,), scratch=[pltpu.VMEM((lat_size, *share[0]), F32)],
    )
    return (field_out.reshape(fields.shape), d_fields.reshape(fields.shape), qkv_grad, jnp.transpose(proj_grad))


def solution(mesh):
    placed = (P(None, "lat", "lon", None), P(None, "lat", "lon", None), P(), P())
    return jax.shard_map(
        per_device,
        mesh=mesh,
        in_specs=placed,
        out_specs=(
            P(None, "lat", "lon", None),
            P(None, "lat", "lon", None),
            P("lon", None),
            P(None, "lon"),
        ),
        check_vma=False,
    )
```

```python
import functools

import jax
import jax.numpy as jnp
from jax import lax
from jax.experimental import pallas as pl
from jax.experimental.pallas import tpu as pltpu
from jax.sharding import PartitionSpec as P

HEADS = 8
WIN_LAT = 6
WIN_LON = 12
LEVELS = 2
COLS = 24
HALF_LAT = WIN_LAT // 2
HALF_LON = WIN_LON // 2
HALF = LEVELS * HALF_LAT * WIN_LON
WIN = 2 * HALF
TOKENS = 2 * WIN
QUARTER = HALF // 2
LANES = 128

epsilon = 1e-05
LONG = 13 * 10**8
LOAD = 5 * 10**9
BF = jnp.bfloat16
F32 = jnp.float32


def dot(a, b, dims):
    return lax.dot_general(a, b, (dims, ((), ())), preferred_element_type=F32)


NN = ((1,), (0,))
NT = ((1,), (1,))
TN = ((0,), (0,))


def div(x, by):
    return (x * ((65536 + by - 1) // by)) >> 16


def own_token(level, row, col):
    return level * (WIN_LAT * COLS) + row * COLS + col


def inner_token(v, first):
    level = div(v, HALF_LAT * WIN_LON)
    rest = v - level * (HALF_LAT * WIN_LON)
    row = div(rest, WIN_LON)
    return own_token(level, first + row, HALF_LON + rest - row * WIN_LON)


def half_token(v, first, col):
    level = div(v, HALF_LAT * HALF_LON)
    rest = v - level * (HALF_LAT * HALF_LON)
    row = div(rest, HALF_LON)
    return jnp.where(v < QUARTER, own_token(level, first + row, col + rest - row * HALF_LON), -1)


def sources():
    even = lax.rem(lax.axis_index("lon"), 2) == 0
    sent = jnp.where(even, 0, HALF_LAT)
    kept = HALF_LAT - sent
    outer = HALF_LON + WIN_LON
    return (
        (lambda v: inner_token(v, sent), HALF),
        (lambda v: half_token(v, sent, outer), QUARTER),
        (lambda v: half_token(v, sent, 0), QUARTER),
        (lambda v: half_token(v, kept, 0), QUARTER),
        (lambda v: inner_token(v, kept), HALF),
        (lambda v: half_token(v, kept, outer), HALF),
    )


def picks(source, rows, columns):
    index = source(lax.broadcasted_iota(jnp.int32, (rows, 1), 0))
    return (index == lax.broadcasted_iota(jnp.int32, (rows, columns), 1)).astype(BF)


def puts(source, rows, columns):
    index = source(lax.broadcasted_iota(jnp.int32, (1, columns), 1))
    return (lax.broadcasted_iota(jnp.int32, (rows, columns), 0) == index).astype(BF)


def first_rows(v):
    return v


def last_rows(v):
    return v - QUARTER


def order_kernel(*outs):
    for out, (source, rows) in zip(outs, sources()):
        out[...] = picks(source, rows, TOKENS)


def pack_kernel(fields, cotangent, *refs):
    count = len(refs) // 2
    width = fields.shape[1]
    for pick, out in zip(refs[:count], refs[count:]):
        out[:, :width] = dot(pick[...], fields[...], NN).astype(out.dtype)
        out[:, width:] = dot(pick[...], cotangent[...], NN).astype(out.dtype)


def swap_bits(index, size, core):
    bits = size.bit_length() - 1
    turned = sum(((index >> b) & 1) << (bits - 1 - b) for b in range(bits))
    return jnp.where(core == 0, index, turned)


def shares(transposed, out, lon, core_of, lon_size):
    rows = transposed.shape[0] // lon_size
    chip = lon >> 1
    for step in range(lon_size // 2):
        start = pl.multiple_of(((chip ^ step) * 2 + core_of) * rows, rows)
        out[step * rows : (step + 1) * rows, :] = transposed[pl.ds(start, rows), :]


def transpose_bf16(block):
    return jnp.transpose(block.astype(F32)).astype(BF)


def slot_product(slot, size, lat, core, windows):
    share = lat ^ swap_bits(slot, size, core)
    total = None
    for left, right in windows:
        lanes = right.shape[1] // size
        of_proj = (share >= 3 * size // 4).astype(jnp.int32)
        part = dot(left[of_proj], right[:, pl.ds(pl.multiple_of(share * lanes, lanes), lanes)], NN)
        total = part if total is None else total + part
    return total


def normalise(x):
    mean = jnp.mean(x, -1, keepdims=True)
    centred = x - mean
    variance = jnp.mean(centred * centred, -1, keepdims=True)
    inv_std = lax.rsqrt(variance + epsilon)
    return centred * inv_std, inv_std


def project(both, qkv_weight, proj_weight):
    width = both.shape[1] // 2
    normed, _ = normalise(both[:, :width])
    projected = dot(normed.astype(BF), qkv_weight[...], NN)
    return normed, projected, dot(both[:, width:].astype(BF), proj_weight[...], NT)


def own_kernel(
    _, fields, cotangent, pick_lat, pick_diag, pick_outer, pick_inner, qkv_weight, proj_weight,
    outer_lat, diag, outer_own, inner_own, normed, projected, d_mixed,
):
    picked = pick_lat, pick_diag, pick_outer, pick_inner
    pack_kernel(fields, cotangent, *picked, outer_lat, diag, outer_own, inner_own)
    normed[...], projected[...], d_mixed[...] = project(inner_own[...], qkv_weight, proj_weight)


def inner_kernel(own, own_normed, own_projected, own_d_mixed, lat_in, qkv_weight, proj_weight, send_grad, *refs):
    arrived = lat_in[...].astype(F32)
    parts = project(arrived, qkv_weight, proj_weight)
    both = jnp.concatenate([own[...], arrived], axis=0)
    mine = own_normed, own_projected, own_d_mixed
    parts = [jnp.concatenate([first[...], second], axis=0) for first, second in zip(mine, parts)]
    one_window(both, *parts, *refs)
    *_, right, left, _, _ = refs
    lat, core, size = place()
    for slot in range(1, size, 2):
        send_grad[slot // 2] = slot_product(slot, size, lat, 1 - core, [(left, right)])


def outer_kernel(own, lon_in, lat_in, diag_in, qkv_weight, proj_weight, grad_so_far, send_first, *refs):
    last = picks(last_rows, HALF, QUARTER)
    both = jnp.concatenate(
        [
            own[...] + dot(last, lon_in[...], NN),
            dot(picks(first_rows, HALF, QUARTER), lat_in[...], NN) + dot(last, diag_in[...], NN),
        ],
        axis=0,
    )
    one_window(both, *project(both, qkv_weight, proj_weight), *refs)
    *_, right, left, _, _ = refs
    lat, core, size = place()
    for slot in range(1, size, 2):
        total = grad_so_far[slot // 2] + slot_product(slot, size, lat, 1 - core, [(left, right)])
        send_first[slot // 2] = total.astype(BF)


def place():
    return lax.axis_index("lat"), lax.rem(lax.axis_index("lon"), 2), lax.axis_size("lat")


def one_window(
    both, normed, projected, d_mixed,
    windows_out, grads_out, left_keep, right, left_send, normed_t, grads_t,
):
    width = both.shape[1] // 2
    lat, core, lat_size = place()
    lon, lon_size = lax.axis_index("lon"), lax.axis_size("lon")
    even = core == 0
    blocks = both[:, :width], both[:, width:]
    x = blocks[0]
    windows_out[...] = x.astype(BF)
    grads = blocks[1].astype(BF)
    grads_out[...] = grads
    projected, d_mixed = projected.astype(BF), d_mixed.astype(BF)

    head_size = width // HEADS
    factor = head_size ** (-0.5)
    apart = jnp.where(even, lat == lat_size - 1, lat == 0).astype(jnp.int32)
    half_b = (lax.broadcasted_iota(jnp.int32, (WIN, 2 * WIN), 0) >= HALF).astype(jnp.int32)
    at_a = lax.broadcasted_iota(jnp.int32, (WIN, 2 * WIN), 1)
    at_a = jnp.where(at_a >= WIN, at_a - WIN, at_a)
    half_a = (at_a >= HALF).astype(jnp.int32)
    allowed = ((half_a != half_b).astype(jnp.int32) * apart) == 0
    first_head = lax.broadcasted_iota(jnp.int32, (WIN, LANES), 1) < head_size
    zero = jnp.zeros((WIN, LANES), BF)

    def split_heads(block):
        return jnp.concatenate([jnp.where(first_head, block, zero), jnp.where(first_head, zero, block)], axis=0)

    def join_heads(block):
        return jnp.where(first_head, block[:WIN], block[WIN:]).astype(BF)

    pairs = range(width // LANES)

    def blocks_of(array, lanes_from):
        return [array[:, lanes_from + pair * LANES : lanes_from + (pair + 1) * LANES] for pair in pairs]

    def store(out, lanes_from, blocks):
        for pair, block in zip(pairs, blocks):
            out[:, lanes_from + pair * LANES : lanes_from + (pair + 1) * LANES] = block.astype(out.dtype)

    k, v = blocks_of(projected, width), blocks_of(projected, 2 * width)
    q2 = [split_heads(block) for block in blocks_of(projected, 0)]
    dm2 = [split_heads(block) for block in blocks_of(d_mixed, 0)]
    scores = [jnp.where(allowed, dot(k[p], q2[p], NT) * factor, -1e30) for p in pairs]
    d_probs = [dot(v[p], dm2[p], NT) for p in pairs]
    exponents = [jnp.exp(s - jnp.max(s, 0, keepdims=True)) for s in scores]
    probs = [e * (1.0 / jnp.sum(e, 0, keepdims=True)) for e in exponents]
    probs_b = [p.astype(BF) for p in probs]
    store(right, 3 * width, [join_heads(dot(probs_b[p], v[p], TN)) for p in pairs])
    store(right, 2 * width, [dot(probs_b[p], dm2[p], NN) for p in pairs])
    d_scores = [
        (probs[p] * (d_probs[p] - jnp.sum(d_probs[p] * probs[p], 0, keepdims=True)) * factor).astype(BF)
        for p in pairs
    ]
    store(right, 0, [join_heads(dot(d_scores[p], k[p], TN)) for p in pairs])
    store(right, width, [dot(d_scores[p], q2[p], NN) for p in pairs])

    normed_t[...] = transpose_bf16(normed)
    grads_t[...] = transpose_bf16(grads)
    for index, source in enumerate((normed_t, grads_t)):
        shares(source, left_send.at[index], lon, 1 - core, lon_size)
        shares(source, left_keep.at[index], lon, core, lon_size)


def keep_kernel(*refs):
    *windows, send_rest, keep_first = refs
    windows = windows[:3], windows[3:]
    lat, core, size = place()
    for slot in range(0, size, 2):
        send_rest[slot // 2] = slot_product(slot, size, lat, 1 - core, [(w[2], w[1]) for w in windows]).astype(BF)
    for slot in range(1, size, 2):
        keep_first[slot // 2] = slot_product(slot, size, lat, core, [(w[0], w[1]) for w in windows]).astype(BF)


def output_kernel(_, *refs):
    (*windows, qkv_weight, proj_weight, keep_rest, inner_results, outer_results) = refs
    per_window = windows[:4], windows[4:]
    lat, core, size = place()
    width = proj_weight.shape[0]
    for slot in range(0, size, 2):
        keep_rest[slot // 2] = slot_product(slot, size, lat, core, [w[2:] for w in per_window]).astype(BF)
    x, grads, right = (jnp.concatenate([w[i][...] for w in per_window], axis=0) for i in (0, 1, 3))
    d_projected, mixed = right[:, : 3 * width], right[:, 3 * width :]
    x = x.astype(F32)
    normed, inv_std = normalise(x)
    output = (x + dot(mixed, proj_weight[...], NN)).astype(BF)
    d_normed = dot(d_projected, qkv_weight[...], NT)
    d_inputs = grads.astype(F32) + inv_std * (
        d_normed
        - jnp.mean(d_normed, -1, keepdims=True)
        - normed * jnp.mean(d_normed * normed, -1, keepdims=True)
    )
    d_inputs = d_inputs.astype(BF)
    for at, out in ((0, inner_results), (WIN, outer_results)):
        out[:, :width] = output[at : at + WIN]
        out[:, width:] = d_inputs[at : at + WIN]


def pack_lon_kernel(outer_results, lon_out):
    outer_x = outer_results[...].astype(F32)[:HALF].astype(BF)
    lon_out[...] = dot(puts(last_rows, QUARTER, HALF), outer_x, NN).astype(BF)


def pack_back_kernel(_, inner_results, outer_results, lat_out, diag_out):
    inner_y = inner_results[...].astype(F32)[HALF:]
    outer_y = outer_results[...].astype(F32)[HALF:].astype(BF)
    lat_out[...] = jnp.concatenate([inner_y, dot(puts(first_rows, QUARTER, HALF), outer_y, NN)], axis=0).astype(BF)
    diag_out[...] = dot(puts(last_rows, QUARTER, HALF), outer_y, NN).astype(BF)


def place_kernel(inner_results, outer_results, lat_in, placed):
    inner_lat, outer_lat, _, _, inner_own, outer_own = (source for source, _ in sources())

    def lat(v):
        return jnp.where(v < HALF, inner_lat(v), outer_lat(v - HALF))

    def only_first(source):
        return lambda v: jnp.where(v < HALF, source(v), -1)

    placed[...] = (
        dot(puts(only_first(inner_own), TOKENS, WIN), inner_results[...], NN)
        + dot(puts(only_first(outer_own), TOKENS, WIN), outer_results[...], NN)
        + dot(puts(lat, TOKENS, HALF + QUARTER), lat_in[...], NN)
    )


def place_rest_kernel(placed, lon_in, diag_in, field_out, d_fields, done):
    done[...] = jnp.zeros_like(done)
    width = field_out.shape[1]
    _, _, lon, diag, _, _ = (source for source, _ in sources())
    total = (
        placed[...]
        + dot(puts(lon, TOKENS, QUARTER), lon_in[...], NN)
        + dot(puts(diag, TOKENS, QUARTER), diag_in[...], NN)
    ).astype(BF)
    field_out[...] = total[:, :width]
    d_fields[...] = total[:, width:]


def halve_kernel(_, *refs):
    *parts, send, keep = refs
    for slot in range(send.shape[0]):
        for out, source in ((send, 2 * slot + 1), (keep, 2 * slot)):
            out[slot] = sum(part[source].astype(F32) for part in parts).astype(BF)


def line_parts_kernel(count, *refs):
    parts, (keep, *sends) = refs[:count], refs[count:]
    rows = keep.shape[0]
    for step, out in enumerate((keep, *sends)):
        at = slice(step * rows, (step + 1) * rows)
        out[...] = sum(part[0, at].astype(F32) for part in parts).astype(out.dtype)


def sum_kernel(*refs):
    *parts, out = refs
    total = parts[0][...].astype(F32)
    for part in parts[1:]:
        total = total + part[...].astype(F32)
    out[...] = total.astype(out.dtype)


def finish_kernel(_, *refs):
    *parts, qkv_out, proj_out = refs
    lat, _, size = place()
    width = parts[0].shape[1]
    for step, part in enumerate(parts):
        share = lat ^ step
        total = part[...].astype(F32)
        of_qkv = 3 * size // 4

        @pl.when(share < of_qkv)
        def _():
            qkv_out[:, pl.ds(pl.multiple_of(share * width, width), width)] = total

        @pl.when(share >= of_qkv)
        def _():
            proj_out[:, pl.ds(pl.multiple_of((share - of_qkv) * width, width), width)] = total


def call(kernel, outs, *args, name, flops=0, limit=32, scratch=(), unread=()):
    vmem = pl.BlockSpec(memory_space=pltpu.VMEM)
    anywhere = pl.BlockSpec(memory_space=pl.ANY)
    shapes = [jax.ShapeDtypeStruct(shape, dtype) for shape, dtype in outs]
    nbytes = sum(a.size * a.dtype.itemsize for a in (*args, *shapes))
    return pl.pallas_call(
        kernel,
        out_shape=shapes,
        in_specs=[anywhere if i in unread else vmem for i in range(len(args))],
        out_specs=[vmem] * len(shapes),
        scratch_shapes=scratch,
        compiler_params=pltpu.CompilerParams(vmem_limit_bytes=limit * 2**20),
        cost_estimate=pl.CostEstimate(flops=flops, bytes_accessed=nbytes, transcendentals=0),
        name=name,
    )(*args)


def routes(lat_size, lon_size):
    lat, lon, diag = [], [], []
    for i in range(lat_size):
        for j in range(lon_size):
            step = -1 if j % 2 == 0 else 1
            before = (j - 1) % lon_size
            me = i * lon_size + j
            lat.append((me, ((i + step) % lat_size) * lon_size + j))
            lon.append((me, i * lon_size + before))
            diag.append((me, ((i - step) % lat_size) * lon_size + before))
    return lat, lon, diag


def per_device(fields, cotangent, qkv_weight, proj_weight):
    levels, row_count, col_count, width = fields.shape
    lat_size, lon_size = lax.axis_size("lat"), lax.axis_size("lon")
    both = ("lat", "lon")
    lat_route, lon_route, diag_route = routes(lat_size, lon_size)

    def back(route):
        return [(target, source) for source, target in route]

    own_fields = fields.reshape(TOKENS, width)
    own_grads = cotangent.reshape(TOKENS, width)
    lengths = (HALF, QUARTER, QUARTER, QUARTER, HALF, HALF)
    picked = call(order_kernel, [((rows, TOKENS), BF) for rows in lengths], name="order", flops=LOAD)
    pick_inner, pick_outer, pick_lon, pick_diag, pick_own, pick_outer_own = picked
    whole, half = ((HALF, 2 * width), F32), ((HALF, 2 * width), BF)
    quarter = ((QUARTER, 2 * width), BF)
    inner_lat, lon_piece = call(
        pack_kernel, [half, quarter], own_fields, own_grads, pick_inner, pick_lon, name="pack", flops=LOAD
    )
    outer_lat, diag_piece, outer_own, inner_own, *own_parts = call(
        own_kernel,
        [quarter, quarter, whole, whole, *(((HALF, lanes), F32) for lanes in (width, 3 * width, width))],
        lon_piece, own_fields, own_grads, pick_outer, pick_diag, pick_outer_own, pick_own, qkv_weight, proj_weight,
        name="own", flops=5 * 10**8, unread=(0,),
    )
    inner_in = lax.ppermute(inner_lat, both, lat_route)
    lon_in = lax.ppermute(lon_piece, both, lon_route)
    outer_in = lax.ppermute(outer_lat, both, lat_route)
    diag_in = lax.ppermute(diag_piece, both, diag_route)

    split = (lat_size, width // 2, 4 * width // lat_size)
    halves = ((lat_size // 2, *split[1:]), BF)
    per_window = [
        ((WIN, width), BF),
        ((WIN, width), BF),
        ((2, width // 2, WIN), BF),
        ((WIN, 4 * width), BF),
        ((2, width // 2, WIN), BF),
    ]
    scratch = [pltpu.VMEM((width, WIN), BF)] * 2
    grad_so_far, *inner = call(
        inner_kernel, [(halves[0], F32), *per_window], inner_own, *own_parts, inner_in, qkv_weight, proj_weight,
        name="inner", flops=10**9, scratch=scratch,
    )
    send_first, *outer = call(
        outer_kernel, [halves, *per_window],
        outer_own, lon_in, outer_in, diag_in, qkv_weight, proj_weight, grad_so_far,
        name="outer", flops=10**9, scratch=scratch,
    )
    sibling = [(j, j ^ 1) for j in range(lon_size)]
    received_first = lax.ppermute(send_first, "lon", sibling)
    send_rest, keep_first = call(keep_kernel, [halves, halves], *inner[2:], *outer[2:], name="keep", flops=10**9)
    received_rest = lax.ppermute(send_rest, "lon", sibling)

    def halving(phase, send):
        route = [
            (i * lon_size + j, (i ^ (1 << (phase if j % 2 == 0 else bits - 1 - phase))) * lon_size + j)
            for i in range(lat_size)
            for j in range(lon_size)
        ]
        return lax.ppermute(send, both, route)

    bits = lat_size.bit_length() - 1
    (send,) = call(sum_kernel, [halves], keep_first, received_first, name="chip_sum")
    received = halving(0, send)
    keep_rest, *results = call(
        output_kernel, [halves, ((WIN, 2 * width), BF), ((WIN, 2 * width), BF)],
        send, *inner[:4], *outer[:4], qkv_weight, proj_weight,
        name="outputs", flops=10**9, unread=(0,),
    )
    (lon_back,) = call(pack_lon_kernel, [quarter], results[1], name="pack_lon")
    lon_home = lax.ppermute(lon_back, both, back(lon_route))
    kept = [keep_rest, received_rest, received]
    slots = lat_size // 2
    for phase in range(1, bits):
        slots //= 2
        stay = ((slots, *split[1:]), BF)
        send, keep = call(halve_kernel, [stay, stay], lon_home, *kept, name=f"halve{slots}", unread=(0,))
        kept = [keep, halving(phase, send)]

    rows = width // lon_size
    share = ((rows, split[2]), BF)
    parts = call(
        functools.partial(line_parts_kernel, len(kept)), [share] * (lon_size // 2), *kept, name="line_parts"
    )
    arrived = [
        lax.ppermute(parts[step], "lon", [(j, j ^ (2 * step)) for j in range(lon_size)])
        for step in range(lon_size // 2 - 1, 0, -1)
    ]
    lat_back, diag_back = call(
        pack_back_kernel, [((HALF + QUARTER, 2 * width), BF), quarter],
        parts[1], *results,
        name="pack_back", unread=(0,),
    )
    lat_home = lax.ppermute(lat_back, both, back(lat_route))
    diag_home = lax.ppermute(diag_back, both, back(diag_route))
    (line_sum,) = call(sum_kernel, [share], parts[0], *arrived, name="line_sum", flops=LONG)
    shared = [
        lax.ppermute(line_sum, "lat", [(i, i ^ step) for i in range(lat_size)]) for step in range(1, lat_size)
    ]
    (placed,) = call(
        place_kernel, [((TOKENS, 2 * width), F32)], *results, lat_home, name="place"
    )
    field_out, d_fields, done = call(
        place_rest_kernel,
        [((TOKENS, width), BF), ((TOKENS, width), BF), ((8, LANES), F32)],
        placed, lon_home, diag_home,
        name="place_rest",
    )
    qkv_grad, proj_grad = call(
        finish_kernel,
        [((rows, 3 * width), F32), ((rows, width), F32)],
        done, line_sum, *shared,
        name="finish", unread=(0,),
    )
    return (field_out.reshape(fields.shape), d_fields.reshape(fields.shape), qkv_grad, jnp.transpose(proj_grad))


def solution(mesh):
    placed = (P(None, "lat", "lon", None), P(None, "lat", "lon", None), P(), P())
    return jax.shard_map(
        per_device,
        mesh=mesh,
        in_specs=placed,
        out_specs=(
            P(None, "lat", "lon", None),
            P(None, "lat", "lon", None),
            P("lon", None),
            P(None, "lon"),
        ),
        check_vma=False,
    )
```

```python
import functools

import jax
import jax.numpy as jnp
from jax import lax
from jax.experimental import pallas as pl
from jax.experimental.pallas import tpu as pltpu
from jax.sharding import PartitionSpec as P

HEADS = 8
WIN_LAT = 6
WIN_LON = 12
LEVELS = 2
COLS = 24
HALF_LAT = WIN_LAT // 2
HALF_LON = WIN_LON // 2
HALF = LEVELS * HALF_LAT * WIN_LON
WIN = 2 * HALF
TOKENS = 2 * WIN
QUARTER = HALF // 2
LANES = 128

epsilon = 1e-05
LONG = 13 * 10**8
LOAD = 5 * 10**9
BF = jnp.bfloat16
F32 = jnp.float32


def dot(a, b, dims):
    return lax.dot_general(a, b, (dims, ((), ())), preferred_element_type=F32)


NN = ((1,), (0,))
NT = ((1,), (1,))
TN = ((0,), (0,))


def div(x, by):
    return (x * ((65536 + by - 1) // by)) >> 16


def own_token(level, row, col):
    return level * (WIN_LAT * COLS) + row * COLS + col


def inner_token(v, first):
    level = div(v, HALF_LAT * WIN_LON)
    rest = v - level * (HALF_LAT * WIN_LON)
    row = div(rest, WIN_LON)
    return own_token(level, first + row, HALF_LON + rest - row * WIN_LON)


def half_token(v, first, col):
    level = div(v, HALF_LAT * HALF_LON)
    rest = v - level * (HALF_LAT * HALF_LON)
    row = div(rest, HALF_LON)
    return jnp.where(v < QUARTER, own_token(level, first + row, col + rest - row * HALF_LON), -1)


def sources():
    even = lax.rem(lax.axis_index("lon"), 2) == 0
    sent = jnp.where(even, 0, HALF_LAT)
    kept = HALF_LAT - sent
    outer = HALF_LON + WIN_LON
    return (
        (lambda v: inner_token(v, sent), HALF),
        (lambda v: half_token(v, sent, outer), QUARTER),
        (lambda v: half_token(v, sent, 0), QUARTER),
        (lambda v: half_token(v, kept, 0), QUARTER),
        (lambda v: inner_token(v, kept), HALF),
        (lambda v: half_token(v, kept, outer), HALF),
    )


def picks(source, rows, columns):
    index = source(lax.broadcasted_iota(jnp.int32, (rows, 1), 0))
    return (index == lax.broadcasted_iota(jnp.int32, (rows, columns), 1)).astype(BF)


def puts(source, rows, columns):
    index = source(lax.broadcasted_iota(jnp.int32, (1, columns), 1))
    return (lax.broadcasted_iota(jnp.int32, (rows, columns), 0) == index).astype(BF)


def first_rows(v):
    return v


def last_rows(v):
    return v - QUARTER


def order_kernel(*outs):
    for out, (source, rows) in zip(outs, sources()):
        out[...] = picks(source, rows, TOKENS)


def pack_kernel(fields, cotangent, *refs):
    count = len(refs) // 2
    width = fields.shape[1]
    for pick, out in zip(refs[:count], refs[count:]):
        out[:, :width] = dot(pick[...], fields[...], NN).astype(out.dtype)
        out[:, width:] = dot(pick[...], cotangent[...], NN).astype(out.dtype)


def swap_bits(index, size, core):
    bits = size.bit_length() - 1
    turned = sum(((index >> b) & 1) << (bits - 1 - b) for b in range(bits))
    return jnp.where(core == 0, index, turned)


def shares(transposed, out, lon, core_of, lon_size):
    rows = transposed.shape[0] // lon_size
    chip = lon >> 1
    for step in range(lon_size // 2):
        start = pl.multiple_of(((chip ^ step) * 2 + core_of) * rows, rows)
        out[step * rows : (step + 1) * rows, :] = transposed[pl.ds(start, rows), :]


def transpose_bf16(block):
    return jnp.transpose(block.astype(F32)).astype(BF)


def slot_product(slot, size, lat, core, windows):
    share = lat ^ swap_bits(slot, size, core)
    total = None
    for left, right in windows:
        lanes = right.shape[1] // size
        of_proj = (share >= 3 * size // 4).astype(jnp.int32)
        part = dot(left[of_proj], right[:, pl.ds(pl.multiple_of(share * lanes, lanes), lanes)], NN)
        total = part if total is None else total + part
    return total


def normalise(x):
    mean = jnp.mean(x, -1, keepdims=True)
    centred = x - mean
    variance = jnp.mean(centred * centred, -1, keepdims=True)
    inv_std = lax.rsqrt(variance + epsilon)
    return centred * inv_std, inv_std


def project(both, qkv_weight, proj_weight):
    width = both.shape[1] // 2
    normed, _ = normalise(both[:, :width])
    projected = dot(normed.astype(BF), qkv_weight[...], NN)
    return normed, projected, dot(both[:, width:].astype(BF), proj_weight[...], NT)


def pack_rest_kernel(_, *refs):
    pack_kernel(*refs)


def own_kernel(inner_own, qkv_weight, proj_weight, normed, projected, d_mixed):
    normed[...], projected[...], d_mixed[...] = project(inner_own[...], qkv_weight, proj_weight)


def inner_kernel(own, own_normed, own_projected, own_d_mixed, lat_in, qkv_weight, proj_weight, send_grad, *refs):
    arrived = lat_in[...].astype(F32)
    parts = project(arrived, qkv_weight, proj_weight)
    both = jnp.concatenate([own[...], arrived], axis=0)
    mine = own_normed, own_projected, own_d_mixed
    parts = [jnp.concatenate([first[...], second], axis=0) for first, second in zip(mine, parts)]
    one_window(both, *parts, *refs)
    *_, right, left, _, _ = refs
    lat, core, size = place()
    for slot in range(1, size, 2):
        send_grad[slot // 2] = slot_product(slot, size, lat, 1 - core, [(left, right)])


def outer_kernel(own, lon_in, lat_in, diag_in, qkv_weight, proj_weight, grad_so_far, send_first, *refs):
    last = picks(last_rows, HALF, QUARTER)
    both = jnp.concatenate(
        [
            own[...] + dot(last, lon_in[...], NN),
            dot(picks(first_rows, HALF, QUARTER), lat_in[...], NN) + dot(last, diag_in[...], NN),
        ],
        axis=0,
    )
    one_window(both, *project(both, qkv_weight, proj_weight), *refs)
    *_, right, left, _, _ = refs
    lat, core, size = place()
    for slot in range(1, size, 2):
        total = grad_so_far[slot // 2] + slot_product(slot, size, lat, 1 - core, [(left, right)])
        send_first[slot // 2] = total.astype(BF)


def place():
    return lax.axis_index("lat"), lax.rem(lax.axis_index("lon"), 2), lax.axis_size("lat")


def one_window(
    both, normed, projected, d_mixed,
    windows_out, grads_out, left_keep, right, left_send, normed_t, grads_t,
):
    width = both.shape[1] // 2
    lat, core, lat_size = place()
    lon, lon_size = lax.axis_index("lon"), lax.axis_size("lon")
    even = core == 0
    blocks = both[:, :width], both[:, width:]
    x = blocks[0]
    windows_out[...] = x.astype(BF)
    grads = blocks[1].astype(BF)
    grads_out[...] = grads
    projected, d_mixed = projected.astype(BF), d_mixed.astype(BF)

    head_size = width // HEADS
    factor = head_size ** (-0.5)
    apart = jnp.where(even, lat == lat_size - 1, lat == 0).astype(jnp.int32)
    half_b = (lax.broadcasted_iota(jnp.int32, (WIN, 2 * WIN), 0) >= HALF).astype(jnp.int32)
    at_a = lax.broadcasted_iota(jnp.int32, (WIN, 2 * WIN), 1)
    at_a = jnp.where(at_a >= WIN, at_a - WIN, at_a)
    half_a = (at_a >= HALF).astype(jnp.int32)
    allowed = ((half_a != half_b).astype(jnp.int32) * apart) == 0
    first_head = lax.broadcasted_iota(jnp.int32, (WIN, LANES), 1) < head_size
    zero = jnp.zeros((WIN, LANES), BF)

    def split_heads(block):
        return jnp.concatenate([jnp.where(first_head, block, zero), jnp.where(first_head, zero, block)], axis=0)

    def join_heads(block):
        return jnp.where(first_head, block[:WIN], block[WIN:]).astype(BF)

    pairs = range(width // LANES)

    def blocks_of(array, lanes_from):
        return [array[:, lanes_from + pair * LANES : lanes_from + (pair + 1) * LANES] for pair in pairs]

    def store(out, lanes_from, blocks):
        for pair, block in zip(pairs, blocks):
            out[:, lanes_from + pair * LANES : lanes_from + (pair + 1) * LANES] = block.astype(out.dtype)

    k, v = blocks_of(projected, width), blocks_of(projected, 2 * width)
    q2 = [split_heads(block) for block in blocks_of(projected, 0)]
    dm2 = [split_heads(block) for block in blocks_of(d_mixed, 0)]
    scores = [jnp.where(allowed, dot(k[p], q2[p], NT) * factor, -1e30) for p in pairs]
    d_probs = [dot(v[p], dm2[p], NT) for p in pairs]
    exponents = [jnp.exp(s - jnp.max(s, 0, keepdims=True)) for s in scores]
    probs = [e * (1.0 / jnp.sum(e, 0, keepdims=True)) for e in exponents]
    probs_b = [p.astype(BF) for p in probs]
    store(right, 3 * width, [join_heads(dot(probs_b[p], v[p], TN)) for p in pairs])
    store(right, 2 * width, [dot(probs_b[p], dm2[p], NN) for p in pairs])
    d_scores = [
        (probs[p] * (d_probs[p] - jnp.sum(d_probs[p] * probs[p], 0, keepdims=True)) * factor).astype(BF)
        for p in pairs
    ]
    store(right, 0, [join_heads(dot(d_scores[p], k[p], TN)) for p in pairs])
    store(right, width, [dot(d_scores[p], q2[p], NN) for p in pairs])

    normed_t[...] = transpose_bf16(normed)
    grads_t[...] = transpose_bf16(grads)
    for index, source in enumerate((normed_t, grads_t)):
        shares(source, left_send.at[index], lon, 1 - core, lon_size)
        shares(source, left_keep.at[index], lon, core, lon_size)


def keep_kernel(*refs):
    *windows, send_rest, keep_first = refs
    windows = windows[:3], windows[3:]
    lat, core, size = place()
    for slot in range(0, size, 2):
        send_rest[slot // 2] = slot_product(slot, size, lat, 1 - core, [(w[2], w[1]) for w in windows]).astype(BF)
    for slot in range(1, size, 2):
        keep_first[slot // 2] = slot_product(slot, size, lat, core, [(w[0], w[1]) for w in windows]).astype(BF)


def output_kernel(_, *refs):
    (*windows, qkv_weight, proj_weight, keep_rest, inner_results, outer_results) = refs
    per_window = windows[:4], windows[4:]
    lat, core, size = place()
    width = proj_weight.shape[0]
    for slot in range(0, size, 2):
        keep_rest[slot // 2] = slot_product(slot, size, lat, core, [w[2:] for w in per_window]).astype(BF)
    x, grads, right = (jnp.concatenate([w[i][...] for w in per_window], axis=0) for i in (0, 1, 3))
    d_projected, mixed = right[:, : 3 * width], right[:, 3 * width :]
    x = x.astype(F32)
    normed, inv_std = normalise(x)
    output = (x + dot(mixed, proj_weight[...], NN)).astype(BF)
    d_normed = dot(d_projected, qkv_weight[...], NT)
    d_inputs = grads.astype(F32) + inv_std * (
        d_normed
        - jnp.mean(d_normed, -1, keepdims=True)
        - normed * jnp.mean(d_normed * normed, -1, keepdims=True)
    )
    d_inputs = d_inputs.astype(BF)
    for at, out in ((0, inner_results), (WIN, outer_results)):
        out[:, :width] = output[at : at + WIN]
        out[:, width:] = d_inputs[at : at + WIN]


def pack_lon_kernel(outer_results, lon_out):
    outer_x = outer_results[...].astype(F32)[:HALF].astype(BF)
    lon_out[...] = dot(puts(last_rows, QUARTER, HALF), outer_x, NN).astype(BF)


def pack_back_kernel(_, inner_results, outer_results, lat_out, diag_out):
    inner_y = inner_results[...].astype(F32)[HALF:]
    outer_y = outer_results[...].astype(F32)[HALF:].astype(BF)
    lat_out[...] = jnp.concatenate([inner_y, dot(puts(first_rows, QUARTER, HALF), outer_y, NN)], axis=0).astype(BF)
    diag_out[...] = dot(puts(last_rows, QUARTER, HALF), outer_y, NN).astype(BF)


def place_kernel(inner_results, outer_results, lat_in, placed):
    inner_lat, outer_lat, _, _, inner_own, outer_own = (source for source, _ in sources())

    def lat(v):
        return jnp.where(v < HALF, inner_lat(v), outer_lat(v - HALF))

    def only_first(source):
        return lambda v: jnp.where(v < HALF, source(v), -1)

    placed[...] = (
        dot(puts(only_first(inner_own), TOKENS, WIN), inner_results[...], NN)
        + dot(puts(only_first(outer_own), TOKENS, WIN), outer_results[...], NN)
        + dot(puts(lat, TOKENS, HALF + QUARTER), lat_in[...], NN)
    )


def place_rest_kernel(placed, lon_in, diag_in, field_out, d_fields, done):
    done[...] = jnp.zeros_like(done)
    width = field_out.shape[1]
    _, _, lon, diag, _, _ = (source for source, _ in sources())
    total = (
        placed[...]
        + dot(puts(lon, TOKENS, QUARTER), lon_in[...], NN)
        + dot(puts(diag, TOKENS, QUARTER), diag_in[...], NN)
    ).astype(BF)
    field_out[...] = total[:, :width]
    d_fields[...] = total[:, width:]


def halve_kernel(_, *refs):
    *parts, send, keep = refs
    for slot in range(send.shape[0]):
        for out, source in ((send, 2 * slot + 1), (keep, 2 * slot)):
            out[slot] = sum(part[source].astype(F32) for part in parts).astype(BF)


def line_parts_kernel(count, *refs):
    parts, (keep, *sends) = refs[:count], refs[count:]
    rows = keep.shape[0]
    for step, out in enumerate((keep, *sends)):
        at = slice(step * rows, (step + 1) * rows)
        out[...] = sum(part[0, at].astype(F32) for part in parts).astype(out.dtype)


def sum_kernel(*refs):
    *parts, out = refs
    total = parts[0][...].astype(F32)
    for part in parts[1:]:
        total = total + part[...].astype(F32)
    out[...] = total.astype(out.dtype)


def finish_kernel(_, *refs):
    *parts, qkv_out, proj_out = refs
    lat, _, size = place()
    width = parts[0].shape[1]
    for step, part in enumerate(parts):
        share = lat ^ step
        total = part[...].astype(F32)
        of_qkv = 3 * size // 4

        @pl.when(share < of_qkv)
        def _():
            qkv_out[:, pl.ds(pl.multiple_of(share * width, width), width)] = total

        @pl.when(share >= of_qkv)
        def _():
            proj_out[:, pl.ds(pl.multiple_of((share - of_qkv) * width, width), width)] = total


def call(kernel, outs, *args, name, flops=0, limit=32, scratch=(), unread=()):
    vmem = pl.BlockSpec(memory_space=pltpu.VMEM)
    anywhere = pl.BlockSpec(memory_space=pl.ANY)
    shapes = [jax.ShapeDtypeStruct(shape, dtype) for shape, dtype in outs]
    nbytes = sum(a.size * a.dtype.itemsize for a in (*args, *shapes))
    return pl.pallas_call(
        kernel,
        out_shape=shapes,
        in_specs=[anywhere if i in unread else vmem for i in range(len(args))],
        out_specs=[vmem] * len(shapes),
        scratch_shapes=scratch,
        compiler_params=pltpu.CompilerParams(vmem_limit_bytes=limit * 2**20),
        cost_estimate=pl.CostEstimate(flops=flops, bytes_accessed=nbytes, transcendentals=0),
        name=name,
    )(*args)


def routes(lat_size, lon_size):
    lat, lon, diag = [], [], []
    for i in range(lat_size):
        for j in range(lon_size):
            step = -1 if j % 2 == 0 else 1
            before = (j - 1) % lon_size
            me = i * lon_size + j
            lat.append((me, ((i + step) % lat_size) * lon_size + j))
            lon.append((me, i * lon_size + before))
            diag.append((me, ((i - step) % lat_size) * lon_size + before))
    return lat, lon, diag


def per_device(fields, cotangent, qkv_weight, proj_weight):
    levels, row_count, col_count, width = fields.shape
    lat_size, lon_size = lax.axis_size("lat"), lax.axis_size("lon")
    both = ("lat", "lon")
    lat_route, lon_route, diag_route = routes(lat_size, lon_size)

    def back(route):
        return [(target, source) for source, target in route]

    own_fields = fields.reshape(TOKENS, width)
    own_grads = cotangent.reshape(TOKENS, width)
    lengths = (HALF, QUARTER, QUARTER, QUARTER, HALF, HALF)
    picked = call(order_kernel, [((rows, TOKENS), BF) for rows in lengths], name="order", flops=LOAD)
    pick_inner, pick_outer, pick_lon, pick_diag, pick_own, pick_outer_own = picked
    whole, half = ((HALF, 2 * width), F32), ((HALF, 2 * width), BF)
    quarter = ((QUARTER, 2 * width), BF)
    inner_lat, lon_piece = call(
        pack_kernel, [half, quarter], own_fields, own_grads, pick_inner, pick_lon, name="pack", flops=LOAD
    )
    outer_lat, diag_piece, outer_own, inner_own = call(
        pack_rest_kernel, [quarter, quarter, whole, whole],
        lon_piece, own_fields, own_grads, pick_outer, pick_diag, pick_outer_own, pick_own,
        name="pack_rest", flops=5 * 10**8, unread=(0,),
    )
    own_parts = call(
        own_kernel, [((HALF, lanes), F32) for lanes in (width, 3 * width, width)],
        inner_own, qkv_weight, proj_weight,
        name="own", flops=5 * 10**8,
    )
    inner_in = lax.ppermute(inner_lat, both, lat_route)
    lon_in = lax.ppermute(lon_piece, both, lon_route)
    outer_in = lax.ppermute(outer_lat, both, lat_route)
    diag_in = lax.ppermute(diag_piece, both, diag_route)

    split = (lat_size, width // 2, 4 * width // lat_size)
    halves = ((lat_size // 2, *split[1:]), BF)
    per_window = [
        ((WIN, width), BF),
        ((WIN, width), BF),
        ((2, width // 2, WIN), BF),
        ((WIN, 4 * width), BF),
        ((2, width // 2, WIN), BF),
    ]
    scratch = [pltpu.VMEM((width, WIN), BF)] * 2
    grad_so_far, *inner = call(
        inner_kernel, [(halves[0], F32), *per_window], inner_own, *own_parts, inner_in, qkv_weight, proj_weight,
        name="inner", flops=10**9, scratch=scratch,
    )
    send_first, *outer = call(
        outer_kernel, [halves, *per_window],
        outer_own, lon_in, outer_in, diag_in, qkv_weight, proj_weight, grad_so_far,
        name="outer", flops=10**9, scratch=scratch,
    )
    sibling = [(j, j ^ 1) for j in range(lon_size)]
    received_first = lax.ppermute(send_first, "lon", sibling)
    send_rest, keep_first = call(keep_kernel, [halves, halves], *inner[2:], *outer[2:], name="keep", flops=10**9)
    received_rest = lax.ppermute(send_rest, "lon", sibling)

    def halving(phase, send):
        route = [
            (i * lon_size + j, (i ^ (1 << (phase if j % 2 == 0 else bits - 1 - phase))) * lon_size + j)
            for i in range(lat_size)
            for j in range(lon_size)
        ]
        return lax.ppermute(send, both, route)

    bits = lat_size.bit_length() - 1
    (send,) = call(sum_kernel, [halves], keep_first, received_first, name="chip_sum")
    received = halving(0, send)
    keep_rest, *results = call(
        output_kernel, [halves, ((WIN, 2 * width), BF), ((WIN, 2 * width), BF)],
        send, *inner[:4], *outer[:4], qkv_weight, proj_weight,
        name="outputs", flops=10**9, unread=(0,),
    )
    (lon_back,) = call(pack_lon_kernel, [quarter], results[1], name="pack_lon")
    lon_home = lax.ppermute(lon_back, both, back(lon_route))
    kept = [keep_rest, received_rest, received]
    slots = lat_size // 2
    for phase in range(1, bits):
        slots //= 2
        stay = ((slots, *split[1:]), BF)
        send, keep = call(halve_kernel, [stay, stay], lon_home, *kept, name=f"halve{slots}", unread=(0,))
        kept = [keep, halving(phase, send)]

    rows = width // lon_size
    share = ((rows, split[2]), BF)
    parts = call(
        functools.partial(line_parts_kernel, len(kept)), [share] * (lon_size // 2), *kept, name="line_parts"
    )
    arrived = [
        lax.ppermute(parts[step], "lon", [(j, j ^ (2 * step)) for j in range(lon_size)])
        for step in range(lon_size // 2 - 1, 0, -1)
    ]
    lat_back, diag_back = call(
        pack_back_kernel, [((HALF + QUARTER, 2 * width), BF), quarter],
        parts[1], *results,
        name="pack_back", unread=(0,),
    )
    lat_home = lax.ppermute(lat_back, both, back(lat_route))
    diag_home = lax.ppermute(diag_back, both, back(diag_route))
    (line_sum,) = call(sum_kernel, [share], parts[0], *arrived, name="line_sum", flops=LONG)
    shared = [
        lax.ppermute(line_sum, "lat", [(i, i ^ step) for i in range(lat_size)]) for step in range(1, lat_size)
    ]
    (placed,) = call(
        place_kernel, [((TOKENS, 2 * width), F32)], *results, lat_home, name="place"
    )
    field_out, d_fields, done = call(
        place_rest_kernel,
        [((TOKENS, width), BF), ((TOKENS, width), BF), ((8, LANES), F32)],
        placed, lon_home, diag_home,
        name="place_rest",
    )
    qkv_grad, proj_grad = call(
        finish_kernel,
        [((rows, 3 * width), F32), ((rows, width), F32)],
        done, line_sum, *shared,
        name="finish", unread=(0,),
    )
    return (field_out.reshape(fields.shape), d_fields.reshape(fields.shape), qkv_grad, jnp.transpose(proj_grad))


def solution(mesh):
    placed = (P(None, "lat", "lon", None), P(None, "lat", "lon", None), P(), P())
    return jax.shard_map(
        per_device,
        mesh=mesh,
        in_specs=placed,
        out_specs=(
            P(None, "lat", "lon", None),
            P(None, "lat", "lon", None),
            P("lon", None),
            P(None, "lon"),
        ),
        check_vma=False,
    )
```

```python
import functools

import jax
import jax.numpy as jnp
from jax import lax
from jax.experimental import pallas as pl
from jax.experimental.pallas import tpu as pltpu
from jax.sharding import PartitionSpec as P

HEADS = 8
WIN_LAT = 6
WIN_LON = 12
LEVELS = 2
COLS = 24
HALF_LAT = WIN_LAT // 2
HALF_LON = WIN_LON // 2
HALF = LEVELS * HALF_LAT * WIN_LON
WIN = 2 * HALF
TOKENS = 2 * WIN
QUARTER = HALF // 2
LANES = 128

epsilon = 1e-05
LONG = 13 * 10**8
LOAD = 5 * 10**9
BF = jnp.bfloat16
F32 = jnp.float32


def dot(a, b, dims):
    return lax.dot_general(a, b, (dims, ((), ())), preferred_element_type=F32)


NN = ((1,), (0,))
NT = ((1,), (1,))
TN = ((0,), (0,))


def div(x, by):
    return (x * ((65536 + by - 1) // by)) >> 16


def own_token(level, row, col):
    return level * (WIN_LAT * COLS) + row * COLS + col


def inner_token(v, first):
    level = div(v, HALF_LAT * WIN_LON)
    rest = v - level * (HALF_LAT * WIN_LON)
    row = div(rest, WIN_LON)
    return own_token(level, first + row, HALF_LON + rest - row * WIN_LON)


def half_token(v, first, col):
    level = div(v, HALF_LAT * HALF_LON)
    rest = v - level * (HALF_LAT * HALF_LON)
    row = div(rest, HALF_LON)
    return jnp.where(v < QUARTER, own_token(level, first + row, col + rest - row * HALF_LON), -1)


def sources():
    even = lax.rem(lax.axis_index("lon"), 2) == 0
    sent = jnp.where(even, 0, HALF_LAT)
    kept = HALF_LAT - sent
    outer = HALF_LON + WIN_LON
    return (
        (lambda v: inner_token(v, sent), HALF),
        (lambda v: half_token(v, sent, outer), QUARTER),
        (lambda v: half_token(v, sent, 0), QUARTER),
        (lambda v: half_token(v, kept, 0), QUARTER),
        (lambda v: inner_token(v, kept), HALF),
        (lambda v: half_token(v, kept, outer), HALF),
    )


def picks(source, rows, columns):
    index = source(lax.broadcasted_iota(jnp.int32, (rows, 1), 0))
    return (index == lax.broadcasted_iota(jnp.int32, (rows, columns), 1)).astype(BF)


def puts(source, rows, columns):
    index = source(lax.broadcasted_iota(jnp.int32, (1, columns), 1))
    return (lax.broadcasted_iota(jnp.int32, (rows, columns), 0) == index).astype(BF)


def first_rows(v):
    return v


def last_rows(v):
    return v - QUARTER


def order_kernel(*outs):
    for out, (source, rows) in zip(outs, sources()):
        out[...] = picks(source, rows, TOKENS)


def pack_kernel(fields, cotangent, *refs):
    count = len(refs) // 2
    width = fields.shape[1]
    for pick, out in zip(refs[:count], refs[count:]):
        out[:, :width] = dot(pick[...], fields[...], NN).astype(out.dtype)
        out[:, width:] = dot(pick[...], cotangent[...], NN).astype(out.dtype)


def swap_bits(index, size, core):
    bits = size.bit_length() - 1
    turned = sum(((index >> b) & 1) << (bits - 1 - b) for b in range(bits))
    return jnp.where(core == 0, index, turned)


def shares(transposed, out, lon, core_of, lon_size):
    rows = transposed.shape[0] // lon_size
    chip = lon >> 1
    for step in range(lon_size // 2):
        start = pl.multiple_of(((chip ^ step) * 2 + core_of) * rows, rows)
        out[step * rows : (step + 1) * rows, :] = transposed[pl.ds(start, rows), :]


def transpose_bf16(block):
    return jnp.transpose(block.astype(F32)).astype(BF)


def slot_product(slot, size, lat, core, windows):
    share = lat ^ swap_bits(slot, size, core)
    total = None
    for left, right in windows:
        lanes = right.shape[1] // size
        of_proj = (share >= 3 * size // 4).astype(jnp.int32)
        part = dot(left[of_proj], right[:, pl.ds(pl.multiple_of(share * lanes, lanes), lanes)], NN)
        total = part if total is None else total + part
    return total


def normalise(x):
    mean = jnp.mean(x, -1, keepdims=True)
    centred = x - mean
    variance = jnp.mean(centred * centred, -1, keepdims=True)
    inv_std = lax.rsqrt(variance + epsilon)
    return centred * inv_std, inv_std


def project(both, qkv_weight, proj_weight):
    width = both.shape[1] // 2
    normed, _ = normalise(both[:, :width])
    projected = dot(normed.astype(BF), qkv_weight[...], NN)
    return normed, projected, dot(both[:, width:].astype(BF), proj_weight[...], NT)


def pack_rest_kernel(_, *refs):
    pack_kernel(*refs)


def own_kernel(inner_own, qkv_weight, proj_weight, normed, projected, d_mixed):
    normed[...], projected[...], d_mixed[...] = project(inner_own[...], qkv_weight, proj_weight)


def inner_kernel(own, own_normed, own_projected, own_d_mixed, lat_in, qkv_weight, proj_weight, send_grad, *refs):
    arrived = lat_in[...].astype(F32)
    parts = project(arrived, qkv_weight, proj_weight)
    both = jnp.concatenate([own[...], arrived], axis=0)
    mine = own_normed, own_projected, own_d_mixed
    parts = [jnp.concatenate([first[...], second], axis=0) for first, second in zip(mine, parts)]
    one_window(both, *parts, *refs)
    *_, right, left, _, _ = refs
    lat, core, size = place()
    for slot in range(1, size, 2):
        send_grad[slot // 2] = slot_product(slot, size, lat, 1 - core, [(left, right)])


def outer_kernel(own, lon_in, diag_in, lat_in, qkv_weight, proj_weight, grad_so_far, send_first, *refs):
    last = picks(last_rows, HALF, QUARTER)
    both = jnp.concatenate(
        [
            own[...] + dot(last, lon_in[...], NN),
            dot(picks(first_rows, HALF, QUARTER), lat_in[...], NN) + dot(last, diag_in[...], NN),
        ],
        axis=0,
    )
    one_window(both, *project(both, qkv_weight, proj_weight), *refs)
    *_, right, left, _, _ = refs
    lat, core, size = place()
    for slot in range(1, size, 2):
        total = grad_so_far[slot // 2] + slot_product(slot, size, lat, 1 - core, [(left, right)])
        send_first[slot // 2] = total.astype(BF)


def place():
    return lax.axis_index("lat"), lax.rem(lax.axis_index("lon"), 2), lax.axis_size("lat")


def one_window(
    both, normed, projected, d_mixed,
    windows_out, grads_out, left_keep, right, left_send, normed_t, grads_t,
):
    width = both.shape[1] // 2
    lat, core, lat_size = place()
    lon, lon_size = lax.axis_index("lon"), lax.axis_size("lon")
    even = core == 0
    blocks = both[:, :width], both[:, width:]
    x = blocks[0]
    windows_out[...] = x.astype(BF)
    grads = blocks[1].astype(BF)
    grads_out[...] = grads
    projected, d_mixed = projected.astype(BF), d_mixed.astype(BF)

    head_size = width // HEADS
    factor = head_size ** (-0.5)
    apart = jnp.where(even, lat == lat_size - 1, lat == 0).astype(jnp.int32)
    half_b = (lax.broadcasted_iota(jnp.int32, (WIN, 2 * WIN), 0) >= HALF).astype(jnp.int32)
    at_a = lax.broadcasted_iota(jnp.int32, (WIN, 2 * WIN), 1)
    at_a = jnp.where(at_a >= WIN, at_a - WIN, at_a)
    half_a = (at_a >= HALF).astype(jnp.int32)
    allowed = ((half_a != half_b).astype(jnp.int32) * apart) == 0
    first_head = lax.broadcasted_iota(jnp.int32, (WIN, LANES), 1) < head_size
    zero = jnp.zeros((WIN, LANES), BF)

    def split_heads(block):
        return jnp.concatenate([jnp.where(first_head, block, zero), jnp.where(first_head, zero, block)], axis=0)

    def join_heads(block):
        return jnp.where(first_head, block[:WIN], block[WIN:]).astype(BF)

    pairs = range(width // LANES)

    def blocks_of(array, lanes_from):
        return [array[:, lanes_from + pair * LANES : lanes_from + (pair + 1) * LANES] for pair in pairs]

    def store(out, lanes_from, blocks):
        for pair, block in zip(pairs, blocks):
            out[:, lanes_from + pair * LANES : lanes_from + (pair + 1) * LANES] = block.astype(out.dtype)

    k, v = blocks_of(projected, width), blocks_of(projected, 2 * width)
    q2 = [split_heads(block) for block in blocks_of(projected, 0)]
    dm2 = [split_heads(block) for block in blocks_of(d_mixed, 0)]
    scores = [jnp.where(allowed, dot(k[p], q2[p], NT) * factor, -1e30) for p in pairs]
    d_probs = [dot(v[p], dm2[p], NT) for p in pairs]
    exponents = [jnp.exp(s - jnp.max(s, 0, keepdims=True)) for s in scores]
    probs = [e * (1.0 / jnp.sum(e, 0, keepdims=True)) for e in exponents]
    probs_b = [p.astype(BF) for p in probs]
    store(right, 3 * width, [join_heads(dot(probs_b[p], v[p], TN)) for p in pairs])
    store(right, 2 * width, [dot(probs_b[p], dm2[p], NN) for p in pairs])
    d_scores = [
        (probs[p] * (d_probs[p] - jnp.sum(d_probs[p] * probs[p], 0, keepdims=True)) * factor).astype(BF)
        for p in pairs
    ]
    store(right, 0, [join_heads(dot(d_scores[p], k[p], TN)) for p in pairs])
    store(right, width, [dot(d_scores[p], q2[p], NN) for p in pairs])

    normed_t[...] = transpose_bf16(normed)
    grads_t[...] = transpose_bf16(grads)
    for index, source in enumerate((normed_t, grads_t)):
        shares(source, left_send.at[index], lon, 1 - core, lon_size)
        shares(source, left_keep.at[index], lon, core, lon_size)


def keep_kernel(*refs):
    *windows, send_rest, keep_first = refs
    windows = windows[:3], windows[3:]
    lat, core, size = place()
    for slot in range(0, size, 2):
        send_rest[slot // 2] = slot_product(slot, size, lat, 1 - core, [(w[2], w[1]) for w in windows]).astype(BF)
    for slot in range(1, size, 2):
        keep_first[slot // 2] = slot_product(slot, size, lat, core, [(w[0], w[1]) for w in windows]).astype(BF)


def output_kernel(_, *refs):
    (*windows, qkv_weight, proj_weight, keep_rest, inner_results, outer_results) = refs
    per_window = windows[:4], windows[4:]
    lat, core, size = place()
    width = proj_weight.shape[0]
    for slot in range(0, size, 2):
        keep_rest[slot // 2] = slot_product(slot, size, lat, core, [w[2:] for w in per_window]).astype(BF)
    x, grads, right = (jnp.concatenate([w[i][...] for w in per_window], axis=0) for i in (0, 1, 3))
    d_projected, mixed = right[:, : 3 * width], right[:, 3 * width :]
    x = x.astype(F32)
    normed, inv_std = normalise(x)
    output = (x + dot(mixed, proj_weight[...], NN)).astype(BF)
    d_normed = dot(d_projected, qkv_weight[...], NT)
    d_inputs = grads.astype(F32) + inv_std * (
        d_normed
        - jnp.mean(d_normed, -1, keepdims=True)
        - normed * jnp.mean(d_normed * normed, -1, keepdims=True)
    )
    d_inputs = d_inputs.astype(BF)
    for at, out in ((0, inner_results), (WIN, outer_results)):
        out[:, :width] = output[at : at + WIN]
        out[:, width:] = d_inputs[at : at + WIN]


def pack_lon_kernel(outer_results, lon_out):
    outer_x = outer_results[...].astype(F32)[:HALF].astype(BF)
    lon_out[...] = dot(puts(last_rows, QUARTER, HALF), outer_x, NN).astype(BF)


def pack_back_kernel(_, inner_results, outer_results, lat_out, diag_out):
    inner_y = inner_results[...].astype(F32)[HALF:]
    outer_y = outer_results[...].astype(F32)[HALF:].astype(BF)
    lat_out[...] = jnp.concatenate([inner_y, dot(puts(first_rows, QUARTER, HALF), outer_y, NN)], axis=0).astype(BF)
    diag_out[...] = dot(puts(last_rows, QUARTER, HALF), outer_y, NN).astype(BF)


def place_kernel(inner_results, outer_results, lat_in, placed):
    inner_lat, outer_lat, _, _, inner_own, outer_own = (source for source, _ in sources())

    def lat(v):
        return jnp.where(v < HALF, inner_lat(v), outer_lat(v - HALF))

    def only_first(source):
        return lambda v: jnp.where(v < HALF, source(v), -1)

    placed[...] = (
        dot(puts(only_first(inner_own), TOKENS, WIN), inner_results[...], NN)
        + dot(puts(only_first(outer_own), TOKENS, WIN), outer_results[...], NN)
        + dot(puts(lat, TOKENS, HALF + QUARTER), lat_in[...], NN)
    )


def place_rest_kernel(placed, lon_in, diag_in, field_out, d_fields, done):
    done[...] = jnp.zeros_like(done)
    width = field_out.shape[1]
    _, _, lon, diag, _, _ = (source for source, _ in sources())
    total = (
        placed[...]
        + dot(puts(lon, TOKENS, QUARTER), lon_in[...], NN)
        + dot(puts(diag, TOKENS, QUARTER), diag_in[...], NN)
    ).astype(BF)
    field_out[...] = total[:, :width]
    d_fields[...] = total[:, width:]


def halve_kernel(_, *refs):
    *parts, send, keep = refs
    for slot in range(send.shape[0]):
        for out, source in ((send, 2 * slot + 1), (keep, 2 * slot)):
            out[slot] = sum(part[source].astype(F32) for part in parts).astype(BF)


def line_parts_kernel(count, *refs):
    parts, (keep, *sends) = refs[:count], refs[count:]
    rows = keep.shape[0]
    for step, out in enumerate((keep, *sends)):
        at = slice(step * rows, (step + 1) * rows)
        out[...] = sum(part[0, at].astype(F32) for part in parts).astype(out.dtype)


def sum_kernel(*refs):
    *parts, out = refs
    total = parts[0][...].astype(F32)
    for part in parts[1:]:
        total = total + part[...].astype(F32)
    out[...] = total.astype(out.dtype)


def at_share(share, size, width, qkv_out, proj_out, write):
    of_qkv = 3 * size // 4

    @pl.when(share < of_qkv)
    def _():
        write(qkv_out.at[:, pl.ds(pl.multiple_of(share * width, width), width)])

    @pl.when(share >= of_qkv)
    def _():
        write(proj_out.at[:, pl.ds(pl.multiple_of((share - of_qkv) * width, width), width)])


def finish_kernel(_, *refs):
    *parts, qkv_out, proj_out = refs
    lat, _, size = place()
    for step, part in zip((0, *range(2, size)), parts):
        total = part[...].astype(F32)

        def write(out):
            out[...] = total

        at_share(lat ^ step, size, part.shape[1], qkv_out, proj_out, write)


def last_share_kernel(part, qkv_in, proj_in, qkv_out, proj_out, total, done):
    lat, _, size = place()
    total[...] = part[...].astype(F32)

    def write(out):
        copy = pltpu.make_async_copy(total, out, done)
        copy.start()
        copy.wait()

    at_share(lat ^ 1, size, part.shape[1], qkv_out, proj_out, write)


def call(kernel, outs, *args, name, flops=0, limit=32, scratch=(), unread=()):
    vmem = pl.BlockSpec(memory_space=pltpu.VMEM)
    anywhere = pl.BlockSpec(memory_space=pl.ANY)
    shapes = [jax.ShapeDtypeStruct(shape, dtype) for shape, dtype in outs]
    nbytes = sum(a.size * a.dtype.itemsize for a in (*args, *shapes))
    return pl.pallas_call(
        kernel,
        out_shape=shapes,
        in_specs=[anywhere if i in unread else vmem for i in range(len(args))],
        out_specs=[vmem] * len(shapes),
        scratch_shapes=scratch,
        compiler_params=pltpu.CompilerParams(vmem_limit_bytes=limit * 2**20),
        cost_estimate=pl.CostEstimate(flops=flops, bytes_accessed=nbytes, transcendentals=0),
        name=name,
    )(*args)


def routes(lat_size, lon_size):
    lat, lon, diag = [], [], []
    for i in range(lat_size):
        for j in range(lon_size):
            step = -1 if j % 2 == 0 else 1
            before = (j - 1) % lon_size
            me = i * lon_size + j
            lat.append((me, ((i + step) % lat_size) * lon_size + j))
            lon.append((me, i * lon_size + before))
            diag.append((me, ((i - step) % lat_size) * lon_size + before))
    return lat, lon, diag


def per_device(fields, cotangent, qkv_weight, proj_weight):
    levels, row_count, col_count, width = fields.shape
    lat_size, lon_size = lax.axis_size("lat"), lax.axis_size("lon")
    both = ("lat", "lon")
    lat_route, lon_route, diag_route = routes(lat_size, lon_size)

    def back(route):
        return [(target, source) for source, target in route]

    own_fields = fields.reshape(TOKENS, width)
    own_grads = cotangent.reshape(TOKENS, width)
    lengths = (HALF, QUARTER, QUARTER, QUARTER, HALF, HALF)
    picked = call(order_kernel, [((rows, TOKENS), BF) for rows in lengths], name="order", flops=LOAD)
    pick_inner, pick_outer, pick_lon, pick_diag, pick_own, pick_outer_own = picked
    whole, half = ((HALF, 2 * width), F32), ((HALF, 2 * width), BF)
    quarter = ((QUARTER, 2 * width), BF)
    inner_lat, lon_piece = call(
        pack_kernel, [half, quarter], own_fields, own_grads, pick_inner, pick_lon, name="pack", flops=LOAD
    )
    outer_lat, diag_piece, outer_own, inner_own = call(
        pack_rest_kernel, [quarter, quarter, whole, whole],
        lon_piece, own_fields, own_grads, pick_outer, pick_diag, pick_outer_own, pick_own,
        name="pack_rest", flops=5 * 10**8, unread=(0,),
    )
    own_parts = call(
        own_kernel, [((HALF, lanes), F32) for lanes in (width, 3 * width, width)],
        inner_own, qkv_weight, proj_weight,
        name="own", flops=5 * 10**8,
    )
    inner_in = lax.ppermute(inner_lat, both, lat_route)
    lon_in = lax.ppermute(lon_piece, both, lon_route)
    outer_in = lax.ppermute(outer_lat, both, lat_route)
    diag_in = lax.ppermute(diag_piece, both, diag_route)

    split = (lat_size, width // 2, 4 * width // lat_size)
    halves = ((lat_size // 2, *split[1:]), BF)
    per_window = [
        ((WIN, width), BF),
        ((WIN, width), BF),
        ((2, width // 2, WIN), BF),
        ((WIN, 4 * width), BF),
        ((2, width // 2, WIN), BF),
    ]
    scratch = [pltpu.VMEM((width, WIN), BF)] * 2
    grad_so_far, *inner = call(
        inner_kernel, [(halves[0], F32), *per_window], inner_own, *own_parts, inner_in, qkv_weight, proj_weight,
        name="inner", flops=10**9, scratch=scratch,
    )
    send_first, *outer = call(
        outer_kernel, [halves, *per_window],
        outer_own, lon_in, diag_in, outer_in, qkv_weight, proj_weight, grad_so_far,
        name="outer", flops=10**9, scratch=scratch,
    )
    sibling = [(j, j ^ 1) for j in range(lon_size)]
    received_first = lax.ppermute(send_first, "lon", sibling)
    send_rest, keep_first = call(keep_kernel, [halves, halves], *inner[2:], *outer[2:], name="keep", flops=10**9)
    received_rest = lax.ppermute(send_rest, "lon", sibling)

    def halving(phase, send):
        route = [
            (i * lon_size + j, (i ^ (1 << (phase if j % 2 == 0 else bits - 1 - phase))) * lon_size + j)
            for i in range(lat_size)
            for j in range(lon_size)
        ]
        return lax.ppermute(send, both, route)

    bits = lat_size.bit_length() - 1
    (send,) = call(sum_kernel, [halves], keep_first, received_first, name="chip_sum")
    received = halving(0, send)
    keep_rest, *results = call(
        output_kernel, [halves, ((WIN, 2 * width), BF), ((WIN, 2 * width), BF)],
        send, *inner[:4], *outer[:4], qkv_weight, proj_weight,
        name="outputs", flops=10**9, unread=(0,),
    )
    (lon_back,) = call(pack_lon_kernel, [quarter], results[1], name="pack_lon")
    lon_home = lax.ppermute(lon_back, both, back(lon_route))
    kept = [keep_rest, received_rest, received]
    slots = lat_size // 2
    for phase in range(1, bits):
        slots //= 2
        stay = ((slots, *split[1:]), BF)
        send, keep = call(halve_kernel, [stay, stay], lon_home, *kept, name=f"halve{slots}", unread=(0,))
        kept = [keep, halving(phase, send)]

    rows = width // lon_size
    share = ((rows, split[2]), BF)
    parts = call(
        functools.partial(line_parts_kernel, len(kept)), [share] * (lon_size // 2), *kept, name="line_parts"
    )
    arrived = [
        lax.ppermute(parts[step], "lon", [(j, j ^ (2 * step)) for j in range(lon_size)])
        for step in range(lon_size // 2 - 1, 0, -1)
    ]
    lat_back, diag_back = call(
        pack_back_kernel, [((HALF + QUARTER, 2 * width), BF), quarter],
        parts[1], *results,
        name="pack_back", unread=(0,),
    )
    lat_home = lax.ppermute(lat_back, both, back(lat_route))
    diag_home = lax.ppermute(diag_back, both, back(diag_route))
    (line_sum,) = call(sum_kernel, [share], parts[0], *arrived, name="line_sum", flops=LONG)
    shared = [
        lax.ppermute(line_sum, "lat", [(i, i ^ step) for i in range(lat_size)]) for step in range(1, lat_size)
    ]
    (placed,) = call(
        place_kernel, [((TOKENS, 2 * width), F32)], *results, lat_home, name="place"
    )
    field_out, d_fields, done = call(
        place_rest_kernel,
        [((TOKENS, width), BF), ((TOKENS, width), BF), ((8, LANES), F32)],
        placed, lon_home, diag_home,
        name="place_rest",
    )
    grads_so_far = call(
        finish_kernel,
        [((rows, 3 * width), F32), ((rows, width), F32)],
        done, line_sum, *shared[1:],
        name="finish", unread=(0,),
    )
    anywhere = pl.BlockSpec(memory_space=pl.ANY)
    qkv_grad, proj_grad = pl.pallas_call(
        last_share_kernel,
        out_shape=[jax.ShapeDtypeStruct(part.shape, part.dtype) for part in grads_so_far],
        in_specs=[pl.BlockSpec(memory_space=pltpu.VMEM), anywhere, anywhere],
        out_specs=[anywhere, anywhere],
        scratch_shapes=[pltpu.VMEM(share[0], F32), pltpu.SemaphoreType.DMA],
        input_output_aliases={1: 0, 2: 1},
        name="last_share",
    )(shared[0], *grads_so_far)
    return (field_out.reshape(fields.shape), d_fields.reshape(fields.shape), qkv_grad, jnp.transpose(proj_grad))


def solution(mesh):
    placed = (P(None, "lat", "lon", None), P(None, "lat", "lon", None), P(), P())
    return jax.shard_map(
        per_device,
        mesh=mesh,
        in_specs=placed,
        out_specs=(
            P(None, "lat", "lon", None),
            P(None, "lat", "lon", None),
            P("lon", None),
            P(None, "lon"),
        ),
        check_vma=False,
    )
```

```python
import functools

import jax
import jax.numpy as jnp
from jax import lax
from jax.experimental import pallas as pl
from jax.experimental.pallas import tpu as pltpu
from jax.sharding import PartitionSpec as P

HEADS = 8
WIN_LAT = 6
WIN_LON = 12
LEVELS = 2
COLS = 24
HALF_LAT = WIN_LAT // 2
HALF_LON = WIN_LON // 2
HALF = LEVELS * HALF_LAT * WIN_LON
WIN = 2 * HALF
TOKENS = 2 * WIN
QUARTER = HALF // 2
LANES = 128

epsilon = 1e-05
LONG = 5 * 10**9
LOAD = 5 * 10**9
BF = jnp.bfloat16
F32 = jnp.float32


def dot(a, b, dims):
    return lax.dot_general(a, b, (dims, ((), ())), preferred_element_type=F32)


NN = ((1,), (0,))
NT = ((1,), (1,))
TN = ((0,), (0,))


def div(x, by):
    return (x * ((65536 + by - 1) // by)) >> 16


def own_token(level, row, col):
    return level * (WIN_LAT * COLS) + row * COLS + col


def inner_token(v, first):
    level = div(v, HALF_LAT * WIN_LON)
    rest = v - level * (HALF_LAT * WIN_LON)
    row = div(rest, WIN_LON)
    return own_token(level, first + row, HALF_LON + rest - row * WIN_LON)


def half_token(v, first, col):
    level = div(v, HALF_LAT * HALF_LON)
    rest = v - level * (HALF_LAT * HALF_LON)
    row = div(rest, HALF_LON)
    return jnp.where(v < QUARTER, own_token(level, first + row, col + rest - row * HALF_LON), -1)


def sources():
    even = lax.rem(lax.axis_index("lon"), 2) == 0
    sent = jnp.where(even, 0, HALF_LAT)
    kept = HALF_LAT - sent
    outer = HALF_LON + WIN_LON
    return (
        (lambda v: inner_token(v, sent), HALF),
        (lambda v: half_token(v, sent, outer), QUARTER),
        (lambda v: half_token(v, sent, 0), QUARTER),
        (lambda v: half_token(v, kept, 0), QUARTER),
        (lambda v: inner_token(v, kept), HALF),
        (lambda v: half_token(v, kept, outer), HALF),
    )


def picks(source, rows, columns):
    index = source(lax.broadcasted_iota(jnp.int32, (rows, 1), 0))
    return (index == lax.broadcasted_iota(jnp.int32, (rows, columns), 1)).astype(BF)


def puts(source, rows, columns):
    index = source(lax.broadcasted_iota(jnp.int32, (1, columns), 1))
    return (lax.broadcasted_iota(jnp.int32, (rows, columns), 0) == index).astype(BF)


def first_rows(v):
    return v


def last_rows(v):
    return v - QUARTER


def order_kernel(*outs):
    for out, (source, rows) in zip(outs, sources()):
        out[...] = picks(source, rows, TOKENS)


def pack_kernel(fields, cotangent, *refs):
    count = len(refs) // 2
    width = fields.shape[1]
    for pick, out in zip(refs[:count], refs[count:]):
        out[:, :width] = dot(pick[...], fields[...], NN).astype(out.dtype)
        out[:, width:] = dot(pick[...], cotangent[...], NN).astype(out.dtype)


def swap_bits(index, size, core):
    bits = size.bit_length() - 1
    turned = sum(((index >> b) & 1) << (bits - 1 - b) for b in range(bits))
    return jnp.where(core == 0, index, turned)


def shares(transposed, out, lon, core_of, lon_size):
    rows = transposed.shape[0] // lon_size
    chip = lon >> 1
    for step in range(lon_size // 2):
        start = pl.multiple_of(((chip ^ step) * 2 + core_of) * rows, rows)
        out[step * rows : (step + 1) * rows, :] = transposed[pl.ds(start, rows), :]


def transpose_bf16(block):
    return jnp.transpose(block.astype(F32)).astype(BF)


def slot_product(slot, size, lat, core, windows):
    share = lat ^ swap_bits(slot, size, core)
    total = None
    for left, right in windows:
        lanes = right.shape[1] // size
        of_proj = (share >= 3 * size // 4).astype(jnp.int32)
        part = dot(left[of_proj], right[:, pl.ds(pl.multiple_of(share * lanes, lanes), lanes)], NN)
        total = part if total is None else total + part
    return total


def normalise(x):
    mean = jnp.mean(x, -1, keepdims=True)
    centred = x - mean
    variance = jnp.mean(centred * centred, -1, keepdims=True)
    inv_std = lax.rsqrt(variance + epsilon)
    return centred * inv_std, inv_std


def project(both, qkv_weight, proj_weight):
    width = both.shape[1] // 2
    normed, _ = normalise(both[:, :width])
    projected = dot(normed.astype(BF), qkv_weight[...], NN)
    return normed, projected, dot(both[:, width:].astype(BF), proj_weight[...], NT)


def pack_rest_kernel(_, *refs):
    pack_kernel(*refs)


def own_kernel(inner_own, qkv_weight, proj_weight, normed, projected, d_mixed):
    normed[...], projected[...], d_mixed[...] = project(inner_own[...], qkv_weight, proj_weight)


def inner_kernel(own, own_normed, own_projected, own_d_mixed, lat_in, qkv_weight, proj_weight, send_grad, *refs):
    arrived = lat_in[...].astype(F32)
    parts = project(arrived, qkv_weight, proj_weight)
    both = jnp.concatenate([own[...], arrived], axis=0)
    mine = own_normed, own_projected, own_d_mixed
    parts = [jnp.concatenate([first[...], second], axis=0) for first, second in zip(mine, parts)]
    one_window(both, *parts, *refs)
    *_, right, left, _, _ = refs
    lat, core, size = place()
    for slot in range(1, size, 2):
        send_grad[slot // 2] = slot_product(slot, size, lat, 1 - core, [(left, right)])


def outer_kernel(own, lon_in, lat_in, diag_in, qkv_weight, proj_weight, grad_so_far, send_first, *refs):
    last = picks(last_rows, HALF, QUARTER)
    both = jnp.concatenate(
        [
            own[...] + dot(last, lon_in[...], NN),
            dot(picks(first_rows, HALF, QUARTER), lat_in[...], NN) + dot(last, diag_in[...], NN),
        ],
        axis=0,
    )
    one_window(both, *project(both, qkv_weight, proj_weight), *refs)
    *_, right, left, _, _ = refs
    lat, core, size = place()
    for slot in range(1, size, 2):
        total = grad_so_far[slot // 2] + slot_product(slot, size, lat, 1 - core, [(left, right)])
        send_first[slot // 2] = total.astype(BF)


def place():
    return lax.axis_index("lat"), lax.rem(lax.axis_index("lon"), 2), lax.axis_size("lat")


def one_window(
    both, normed, projected, d_mixed,
    windows_out, grads_out, left_keep, right, left_send, normed_t, grads_t,
):
    width = both.shape[1] // 2
    lat, core, lat_size = place()
    lon, lon_size = lax.axis_index("lon"), lax.axis_size("lon")
    even = core == 0
    blocks = both[:, :width], both[:, width:]
    x = blocks[0]
    windows_out[...] = x.astype(BF)
    grads = blocks[1].astype(BF)
    grads_out[...] = grads
    projected, d_mixed = projected.astype(BF), d_mixed.astype(BF)

    head_size = width // HEADS
    factor = head_size ** (-0.5)
    apart = jnp.where(even, lat == lat_size - 1, lat == 0).astype(jnp.int32)
    half_b = (lax.broadcasted_iota(jnp.int32, (WIN, 2 * WIN), 0) >= HALF).astype(jnp.int32)
    at_a = lax.broadcasted_iota(jnp.int32, (WIN, 2 * WIN), 1)
    at_a = jnp.where(at_a >= WIN, at_a - WIN, at_a)
    half_a = (at_a >= HALF).astype(jnp.int32)
    allowed = ((half_a != half_b).astype(jnp.int32) * apart) == 0
    first_head = lax.broadcasted_iota(jnp.int32, (WIN, LANES), 1) < head_size
    zero = jnp.zeros((WIN, LANES), BF)

    def split_heads(block):
        return jnp.concatenate([jnp.where(first_head, block, zero), jnp.where(first_head, zero, block)], axis=0)

    def join_heads(block):
        return jnp.where(first_head, block[:WIN], block[WIN:]).astype(BF)

    pairs = range(width // LANES)

    def blocks_of(array, lanes_from):
        return [array[:, lanes_from + pair * LANES : lanes_from + (pair + 1) * LANES] for pair in pairs]

    def store(out, lanes_from, blocks):
        for pair, block in zip(pairs, blocks):
            out[:, lanes_from + pair * LANES : lanes_from + (pair + 1) * LANES] = block.astype(out.dtype)

    k, v = blocks_of(projected, width), blocks_of(projected, 2 * width)
    q2 = [split_heads(block) for block in blocks_of(projected, 0)]
    dm2 = [split_heads(block) for block in blocks_of(d_mixed, 0)]
    scores = [jnp.where(allowed, dot(k[p], q2[p], NT) * factor, -1e30) for p in pairs]
    d_probs = [dot(v[p], dm2[p], NT) for p in pairs]
    exponents = [jnp.exp(s - jnp.max(s, 0, keepdims=True)) for s in scores]
    probs = [e * (1.0 / jnp.sum(e, 0, keepdims=True)) for e in exponents]
    probs_b = [p.astype(BF) for p in probs]
    store(right, 3 * width, [join_heads(dot(probs_b[p], v[p], TN)) for p in pairs])
    store(right, 2 * width, [dot(probs_b[p], dm2[p], NN) for p in pairs])
    d_scores = [
        (probs[p] * (d_probs[p] - jnp.sum(d_probs[p] * probs[p], 0, keepdims=True)) * factor).astype(BF)
        for p in pairs
    ]
    store(right, 0, [join_heads(dot(d_scores[p], k[p], TN)) for p in pairs])
    store(right, width, [dot(d_scores[p], q2[p], NN) for p in pairs])

    normed_t[...] = transpose_bf16(normed)
    grads_t[...] = transpose_bf16(grads)
    for index, source in enumerate((normed_t, grads_t)):
        shares(source, left_send.at[index], lon, 1 - core, lon_size)
        shares(source, left_keep.at[index], lon, core, lon_size)


def keep_kernel(*refs):
    *windows, send_rest, keep_first = refs
    windows = windows[:3], windows[3:]
    lat, core, size = place()
    for slot in range(0, size, 2):
        send_rest[slot // 2] = slot_product(slot, size, lat, 1 - core, [(w[2], w[1]) for w in windows]).astype(BF)
    for slot in range(1, size, 2):
        keep_first[slot // 2] = slot_product(slot, size, lat, core, [(w[0], w[1]) for w in windows]).astype(BF)


def output_kernel(_, *refs):
    (*windows, qkv_weight, proj_weight, keep_rest, inner_results, outer_results) = refs
    per_window = windows[:4], windows[4:]
    lat, core, size = place()
    width = proj_weight.shape[0]
    for slot in range(0, size, 2):
        keep_rest[slot // 2] = slot_product(slot, size, lat, core, [w[2:] for w in per_window]).astype(BF)
    x, grads, right = (jnp.concatenate([w[i][...] for w in per_window], axis=0) for i in (0, 1, 3))
    d_projected, mixed = right[:, : 3 * width], right[:, 3 * width :]
    x = x.astype(F32)
    normed, inv_std = normalise(x)
    output = (x + dot(mixed, proj_weight[...], NN)).astype(BF)
    d_normed = dot(d_projected, qkv_weight[...], NT)
    d_inputs = grads.astype(F32) + inv_std * (
        d_normed
        - jnp.mean(d_normed, -1, keepdims=True)
        - normed * jnp.mean(d_normed * normed, -1, keepdims=True)
    )
    d_inputs = d_inputs.astype(BF)
    for at, out in ((0, inner_results), (WIN, outer_results)):
        out[:, :width] = output[at : at + WIN]
        out[:, width:] = d_inputs[at : at + WIN]


def pack_lon_kernel(outer_results, lon_out):
    outer_x = outer_results[...].astype(F32)[:HALF].astype(BF)
    lon_out[...] = dot(puts(last_rows, QUARTER, HALF), outer_x, NN).astype(BF)


def place_own_kernel(_, inner_results, outer_results, placed, lat_out):
    _, _, _, _, inner_own, outer_own = (source for source, _ in sources())

    def only_first(source):
        return lambda v: jnp.where(v < HALF, source(v), -1)

    placed[...] = dot(puts(only_first(inner_own), TOKENS, WIN), inner_results[...], NN) + dot(
        puts(only_first(outer_own), TOKENS, WIN), outer_results[...], NN
    )
    inner_y = inner_results[...].astype(F32)[HALF:]
    outer_y = outer_results[...].astype(F32)[HALF:].astype(BF)
    lat_out[...] = jnp.concatenate([inner_y, dot(puts(first_rows, QUARTER, HALF), outer_y, NN)], axis=0).astype(BF)


def pack_diag_kernel(_, outer_results, diag_out):
    outer_y = outer_results[...].astype(F32)[HALF:].astype(BF)
    diag_out[...] = dot(puts(last_rows, QUARTER, HALF), outer_y, NN).astype(BF)


def place_lat_kernel(so_far, lat_in, placed):
    inner_lat, outer_lat, _, _, _, _ = (source for source, _ in sources())

    def lat(v):
        return jnp.where(v < HALF, inner_lat(v), outer_lat(v - HALF))

    placed[...] = so_far[...] + dot(puts(lat, TOKENS, HALF + QUARTER), lat_in[...], NN)


def place_rest_kernel(placed, lon_in, diag_in, field_out, d_fields, done):
    done[...] = jnp.zeros_like(done)
    width = field_out.shape[1]
    _, _, lon, diag, _, _ = (source for source, _ in sources())
    total = (
        placed[...]
        + dot(puts(lon, TOKENS, QUARTER), lon_in[...], NN)
        + dot(puts(diag, TOKENS, QUARTER), diag_in[...], NN)
    ).astype(BF)
    field_out[...] = total[:, :width]
    d_fields[...] = total[:, width:]


def halve_kernel(_, *refs):
    *parts, send, keep = refs
    for slot in range(send.shape[0]):
        for out, source in ((send, 2 * slot + 1), (keep, 2 * slot)):
            out[slot] = sum(part[source].astype(F32) for part in parts).astype(BF)


def line_parts_kernel(count, *refs):
    parts, (keep, *sends) = refs[:count], refs[count:]
    rows = keep.shape[0]
    for step, out in enumerate((keep, *sends)):
        at = slice(step * rows, (step + 1) * rows)
        out[...] = sum(part[0, at].astype(F32) for part in parts).astype(out.dtype)


def line_sum_kernel(_, *refs):
    sum_kernel(*refs)


def sum_kernel(*refs):
    *parts, out = refs
    total = parts[0][...].astype(F32)
    for part in parts[1:]:
        total = total + part[...].astype(F32)
    out[...] = total.astype(out.dtype)


def finish_kernel(_, *refs):
    *parts, qkv_out, proj_out = refs
    lat, _, size = place()
    width = parts[0].shape[1]
    for step, part in enumerate(parts):
        share = lat ^ step
        total = part[...].astype(F32)
        of_qkv = 3 * size // 4

        @pl.when(share < of_qkv)
        def _():
            qkv_out[:, pl.ds(pl.multiple_of(share * width, width), width)] = total

        @pl.when(share >= of_qkv)
        def _():
            proj_out[:, pl.ds(pl.multiple_of((share - of_qkv) * width, width), width)] = total


def call(kernel, outs, *args, name, flops=0, limit=32, scratch=(), unread=()):
    vmem = pl.BlockSpec(memory_space=pltpu.VMEM)
    anywhere = pl.BlockSpec(memory_space=pl.ANY)
    shapes = [jax.ShapeDtypeStruct(shape, dtype) for shape, dtype in outs]
    nbytes = sum(a.size * a.dtype.itemsize for a in (*args, *shapes))
    return pl.pallas_call(
        kernel,
        out_shape=shapes,
        in_specs=[anywhere if i in unread else vmem for i in range(len(args))],
        out_specs=[vmem] * len(shapes),
        scratch_shapes=scratch,
        compiler_params=pltpu.CompilerParams(vmem_limit_bytes=limit * 2**20),
        cost_estimate=pl.CostEstimate(flops=flops, bytes_accessed=nbytes, transcendentals=0),
        name=name,
    )(*args)


def routes(lat_size, lon_size):
    lat, lon, diag = [], [], []
    for i in range(lat_size):
        for j in range(lon_size):
            step = -1 if j % 2 == 0 else 1
            before = (j - 1) % lon_size
            me = i * lon_size + j
            lat.append((me, ((i + step) % lat_size) * lon_size + j))
            lon.append((me, i * lon_size + before))
            diag.append((me, ((i - step) % lat_size) * lon_size + before))
    return lat, lon, diag


def per_device(fields, cotangent, qkv_weight, proj_weight):
    levels, row_count, col_count, width = fields.shape
    lat_size, lon_size = lax.axis_size("lat"), lax.axis_size("lon")
    both = ("lat", "lon")
    lat_route, lon_route, diag_route = routes(lat_size, lon_size)

    def back(route):
        return [(target, source) for source, target in route]

    own_fields = fields.reshape(TOKENS, width)
    own_grads = cotangent.reshape(TOKENS, width)
    lengths = (HALF, QUARTER, QUARTER, QUARTER, HALF, HALF)
    picked = call(order_kernel, [((rows, TOKENS), BF) for rows in lengths], name="order", flops=LOAD)
    pick_inner, pick_outer, pick_lon, pick_diag, pick_own, pick_outer_own = picked
    whole, half = ((HALF, 2 * width), F32), ((HALF, 2 * width), BF)
    quarter = ((QUARTER, 2 * width), BF)
    inner_lat, lon_piece = call(
        pack_kernel, [half, quarter], own_fields, own_grads, pick_inner, pick_lon, name="pack", flops=LOAD
    )
    outer_lat, diag_piece, outer_own, inner_own = call(
        pack_rest_kernel, [quarter, quarter, whole, whole],
        lon_piece, own_fields, own_grads, pick_outer, pick_diag, pick_outer_own, pick_own,
        name="pack_rest", flops=5 * 10**8, unread=(0,),
    )
    own_parts = call(
        own_kernel, [((HALF, lanes), F32) for lanes in (width, 3 * width, width)],
        inner_own, qkv_weight, proj_weight,
        name="own", flops=5 * 10**8,
    )
    inner_in = lax.ppermute(inner_lat, both, lat_route)
    lon_in = lax.ppermute(lon_piece, both, lon_route)
    outer_in = lax.ppermute(outer_lat, both, lat_route)
    diag_in = lax.ppermute(diag_piece, both, diag_route)

    split = (lat_size, width // 2, 4 * width // lat_size)
    halves = ((lat_size // 2, *split[1:]), BF)
    per_window = [
        ((WIN, width), BF),
        ((WIN, width), BF),
        ((2, width // 2, WIN), BF),
        ((WIN, 4 * width), BF),
        ((2, width // 2, WIN), BF),
    ]
    scratch = [pltpu.VMEM((width, WIN), BF)] * 2
    grad_so_far, *inner = call(
        inner_kernel, [(halves[0], F32), *per_window], inner_own, *own_parts, inner_in, qkv_weight, proj_weight,
        name="inner", flops=10**9, scratch=scratch,
    )
    send_first, *outer = call(
        outer_kernel, [halves, *per_window],
        outer_own, lon_in, outer_in, diag_in, qkv_weight, proj_weight, grad_so_far,
        name="outer", flops=10**9, scratch=scratch,
    )
    sibling = [(j, j ^ 1) for j in range(lon_size)]
    received_first = lax.ppermute(send_first, "lon", sibling)
    send_rest, keep_first = call(keep_kernel, [halves, halves], *inner[2:], *outer[2:], name="keep", flops=10**9)
    received_rest = lax.ppermute(send_rest, "lon", sibling)

    def halving(phase, send):
        route = [
            (i * lon_size + j, (i ^ (1 << (phase if j % 2 == 0 else bits - 1 - phase))) * lon_size + j)
            for i in range(lat_size)
            for j in range(lon_size)
        ]
        return lax.ppermute(send, both, route)

    bits = lat_size.bit_length() - 1
    (send,) = call(sum_kernel, [halves], keep_first, received_first, name="chip_sum")
    received = halving(0, send)
    keep_rest, *results = call(
        output_kernel, [halves, ((WIN, 2 * width), BF), ((WIN, 2 * width), BF)],
        send, *inner[:4], *outer[:4], qkv_weight, proj_weight,
        name="outputs", flops=10**9, unread=(0,),
    )
    (lon_back,) = call(pack_lon_kernel, [quarter], results[1], name="pack_lon")
    lon_home = lax.ppermute(lon_back, both, back(lon_route))
    kept = [keep_rest, received_rest, received]
    slots = lat_size // 2
    for phase in range(1, bits):
        slots //= 2
        stay = ((slots, *split[1:]), BF)
        send, keep = call(halve_kernel, [stay, stay], lon_home, *kept, name=f"halve{slots}", unread=(0,))
        kept = [keep, halving(phase, send)]

    placed, lat_back = call(
        place_own_kernel, [((TOKENS, 2 * width), F32), ((HALF + QUARTER, 2 * width), BF)], send, *results,
        name="place_own", unread=(0,),
    )
    lat_home = lax.ppermute(lat_back, both, back(lat_route))

    rows = width // lon_size
    share = ((rows, split[2]), BF)
    parts = call(
        functools.partial(line_parts_kernel, len(kept)), [share] * (lon_size // 2), *kept, name="line_parts", flops=LONG
    )
    arrived = [
        lax.ppermute(parts[step], "lon", [(j, j ^ (2 * step)) for j in range(lon_size)])
        for step in range(lon_size // 2 - 1, 0, -1)
    ]
    (diag_back,) = call(pack_diag_kernel, [quarter], parts[1], results[1], name="pack_diag", unread=(0,))
    diag_home = lax.ppermute(diag_back, both, back(diag_route))
    (placed,) = call(place_lat_kernel, [((TOKENS, 2 * width), F32)], placed, lat_home, name="place_lat")
    (line_sum,) = call(
        line_sum_kernel, [share], placed, parts[0], *arrived, name="line_sum", unread=(0,)
    )
    shared = [
        lax.ppermute(line_sum, "lat", [(i, i ^ step) for i in range(lat_size)]) for step in range(1, lat_size)
    ]
    field_out, d_fields, done = call(
        place_rest_kernel,
        [((TOKENS, width), BF), ((TOKENS, width), BF), ((8, LANES), F32)],
        placed, lon_home, diag_home,
        name="place_rest",
    )
    qkv_grad, proj_grad = call(
        finish_kernel,
        [((rows, 3 * width), F32), ((rows, width), F32)],
        done, line_sum, *shared,
        name="finish", unread=(0,),
    )
    return (field_out.reshape(fields.shape), d_fields.reshape(fields.shape), qkv_grad, jnp.transpose(proj_grad))


def solution(mesh):
    placed = (P(None, "lat", "lon", None), P(None, "lat", "lon", None), P(), P())
    return jax.shard_map(
        per_device,
        mesh=mesh,
        in_specs=placed,
        out_specs=(
            P(None, "lat", "lon", None),
            P(None, "lat", "lon", None),
            P("lon", None),
            P(None, "lon"),
        ),
        check_vma=False,
    )
```

```python
import functools

import jax
import jax.numpy as jnp
from jax import lax
from jax.experimental import pallas as pl
from jax.experimental.pallas import tpu as pltpu
from jax.sharding import PartitionSpec as P

HEADS = 8
WIN_LAT = 6
WIN_LON = 12
LEVELS = 2
COLS = 24
HALF_LAT = WIN_LAT // 2
HALF_LON = WIN_LON // 2
HALF = LEVELS * HALF_LAT * WIN_LON
WIN = 2 * HALF
TOKENS = 2 * WIN
QUARTER = HALF // 2
LANES = 128

epsilon = 1e-05
LONG = 13 * 10**8
LOAD = 5 * 10**9
BF = jnp.bfloat16
F32 = jnp.float32


def dot(a, b, dims):
    return lax.dot_general(a, b, (dims, ((), ())), preferred_element_type=F32)


NN = ((1,), (0,))
NT = ((1,), (1,))
TN = ((0,), (0,))


def div(x, by):
    return (x * ((65536 + by - 1) // by)) >> 16


def own_token(level, row, col):
    return level * (WIN_LAT * COLS) + row * COLS + col


def inner_token(v, first):
    level = div(v, HALF_LAT * WIN_LON)
    rest = v - level * (HALF_LAT * WIN_LON)
    row = div(rest, WIN_LON)
    return own_token(level, first + row, HALF_LON + rest - row * WIN_LON)


def half_token(v, first, col):
    level = div(v, HALF_LAT * HALF_LON)
    rest = v - level * (HALF_LAT * HALF_LON)
    row = div(rest, HALF_LON)
    return jnp.where(v < QUARTER, own_token(level, first + row, col + rest - row * HALF_LON), -1)


def sources():
    even = lax.rem(lax.axis_index("lon"), 2) == 0
    sent = jnp.where(even, 0, HALF_LAT)
    kept = HALF_LAT - sent
    outer = HALF_LON + WIN_LON
    return (
        (lambda v: inner_token(v, sent), HALF),
        (lambda v: half_token(v, sent, outer), QUARTER),
        (lambda v: half_token(v, sent, 0), QUARTER),
        (lambda v: half_token(v, kept, 0), QUARTER),
        (lambda v: inner_token(v, kept), HALF),
        (lambda v: half_token(v, kept, outer), HALF),
    )


def picks(source, rows, columns):
    index = source(lax.broadcasted_iota(jnp.int32, (rows, 1), 0))
    return (index == lax.broadcasted_iota(jnp.int32, (rows, columns), 1)).astype(BF)


def puts(source, rows, columns):
    index = source(lax.broadcasted_iota(jnp.int32, (1, columns), 1))
    return (lax.broadcasted_iota(jnp.int32, (rows, columns), 0) == index).astype(BF)


def first_rows(v):
    return v


def last_rows(v):
    return v - QUARTER


def order_kernel(*outs):
    for out, (source, rows) in zip(outs, sources()):
        out[...] = picks(source, rows, TOKENS)


def pack_kernel(fields, cotangent, *refs):
    count = len(refs) // 2
    width = fields.shape[1]
    for pick, out in zip(refs[:count], refs[count:]):
        out[:, :width] = dot(pick[...], fields[...], NN).astype(out.dtype)
        out[:, width:] = dot(pick[...], cotangent[...], NN).astype(out.dtype)


def swap_bits(index, size, core):
    bits = size.bit_length() - 1
    turned = sum(((index >> b) & 1) << (bits - 1 - b) for b in range(bits))
    return jnp.where(core == 0, index, turned)


def shares(transposed, out, lon, core_of, lon_size):
    rows = transposed.shape[0] // lon_size
    chip = lon >> 1
    for step in range(lon_size // 2):
        start = pl.multiple_of(((chip ^ step) * 2 + core_of) * rows, rows)
        out[step * rows : (step + 1) * rows, :] = transposed[pl.ds(start, rows), :]


def transpose_bf16(block):
    return jnp.transpose(block.astype(BF))


def slot_product(slot, size, lat, core, windows):
    share = lat ^ swap_bits(slot, size, core)
    total = None
    for left, right in windows:
        rows = right.shape[0] // size
        of_proj = (share >= 3 * size // 4).astype(jnp.int32)
        part = dot(left[of_proj], right[pl.ds(pl.multiple_of(share * rows, rows), rows), :], NT)
        total = part if total is None else total + part
    return total


def normalise(x):
    mean = jnp.mean(x, -1, keepdims=True)
    centred = x - mean
    variance = jnp.mean(centred * centred, -1, keepdims=True)
    inv_std = lax.rsqrt(variance + epsilon)
    return centred * inv_std, inv_std


def project(both, qkv_weight, proj_weight):
    width = both.shape[1] // 2
    normed, _ = normalise(both[:, :width])
    projected = dot(normed.astype(BF), qkv_weight[...], NN)
    return normed, projected, dot(both[:, width:].astype(BF), proj_weight[...], NT)


def pack_rest_kernel(_, *refs):
    pack_kernel(*refs)


def own_kernel(inner_own, qkv_weight, proj_weight, normed, projected, d_mixed):
    normed[...], projected[...], d_mixed[...] = project(inner_own[...], qkv_weight, proj_weight)


def inner_kernel(own, own_normed, own_projected, own_d_mixed, lat_in, qkv_weight, proj_weight, send_grad, *refs):
    arrived = lat_in[...].astype(F32)
    parts = project(arrived, qkv_weight, proj_weight)
    both = jnp.concatenate([own[...], arrived], axis=0)
    mine = own_normed, own_projected, own_d_mixed
    parts = [jnp.concatenate([first[...], second], axis=0) for first, second in zip(mine, parts)]
    one_window(both, *parts, *refs)
    *_, right, left, _, _ = refs
    lat, core, size = place()
    for slot in range(1, size, 2):
        send_grad[slot // 2] = slot_product(slot, size, lat, 1 - core, [(left, right)])


def outer_kernel(own, lon_in, lat_in, diag_in, qkv_weight, proj_weight, grad_so_far, send_first, *refs):
    last = picks(last_rows, HALF, QUARTER)
    both = jnp.concatenate(
        [
            own[...] + dot(last, lon_in[...], NN),
            dot(picks(first_rows, HALF, QUARTER), lat_in[...], NN) + dot(last, diag_in[...], NN),
        ],
        axis=0,
    )
    one_window(both, *project(both, qkv_weight, proj_weight), *refs)
    *_, right, left, _, _ = refs
    lat, core, size = place()
    for slot in range(1, size, 2):
        total = grad_so_far[slot // 2] + slot_product(slot, size, lat, 1 - core, [(left, right)])
        send_first[slot // 2] = total.astype(BF)


def place():
    return lax.axis_index("lat"), lax.rem(lax.axis_index("lon"), 2), lax.axis_size("lat")


def one_window(
    both, normed, projected, d_mixed,
    windows_out, grads_out, left_keep, right, left_send, normed_t, grads_t,
):
    width = both.shape[1] // 2
    lat, core, lat_size = place()
    lon, lon_size = lax.axis_index("lon"), lax.axis_size("lon")
    even = core == 0
    blocks = both[:, :width], both[:, width:]
    x = blocks[0]
    windows_out[...] = x.astype(BF)
    grads = blocks[1].astype(BF)
    grads_out[...] = grads
    projected, d_mixed = projected.astype(BF), d_mixed.astype(BF)

    head_size = width // HEADS
    factor = head_size ** (-0.5)
    apart = jnp.where(even, lat == lat_size - 1, lat == 0).astype(jnp.int32)
    half_b = (lax.broadcasted_iota(jnp.int32, (WIN, WIN), 0) >= HALF).astype(jnp.int32)
    half_a = (lax.broadcasted_iota(jnp.int32, (WIN, WIN), 1) >= HALF).astype(jnp.int32)
    allowed = ((half_a != half_b).astype(jnp.int32) * apart) == 0
    first_head = lax.broadcasted_iota(jnp.int32, (WIN, LANES), 1) < head_size
    zero = jnp.zeros((WIN, LANES), BF)

    pairs = range(width // LANES)
    heads = range(HEADS)

    def blocks_of(array, lanes_from):
        return [array[:, lanes_from + pair * LANES : lanes_from + (pair + 1) * LANES] for pair in pairs]

    def head_lanes(blocks):
        return [
            jnp.where(first_head, block, zero) if half == 0 else jnp.where(first_head, zero, block)
            for block in blocks
            for half in range(2)
        ]

    def head_rows(blocks):
        turned = [jnp.transpose(block) for block in blocks]
        return [block[half * head_size : (half + 1) * head_size] for block in turned for half in range(2)]

    def store(rows_from, blocks):
        for head, block in zip(heads, blocks):
            right[rows_from + head * head_size : rows_from + (head + 1) * head_size, :] = block.astype(BF)

    q, k, v = (blocks_of(projected, at * width) for at in range(3))
    dm = blocks_of(d_mixed, 0)
    q_lanes, dm_lanes = head_lanes(q), head_lanes(dm)
    scores = [jnp.where(allowed, dot(k[h // 2], q_lanes[h], NT) * factor, -1e30) for h in heads]
    d_probs = [dot(v[h // 2], dm_lanes[h], NT) for h in heads]
    q_rows, k_rows, v_rows, dm_rows = (head_rows(blocks) for blocks in (q, k, v, dm))
    exponents = [jnp.exp(s - jnp.max(s, 0, keepdims=True)) for s in scores]
    probs = [e * (1.0 / jnp.sum(e, 0, keepdims=True)) for e in exponents]
    probs_b = [p.astype(BF) for p in probs]
    store(3 * width, [dot(v_rows[h], probs_b[h], NN) for h in heads])
    store(2 * width, [dot(dm_rows[h], probs_b[h], NT) for h in heads])
    d_scores = [
        (probs[h] * (d_probs[h] - jnp.sum(d_probs[h] * probs[h], 0, keepdims=True)) * factor).astype(BF)
        for h in heads
    ]
    store(0, [dot(k_rows[h], d_scores[h], NN) for h in heads])
    store(width, [dot(q_rows[h], d_scores[h], NT) for h in heads])

    normed_t[...] = transpose_bf16(normed)
    grads_t[...] = transpose_bf16(grads)
    for index, source in enumerate((normed_t, grads_t)):
        shares(source, left_send.at[index], lon, 1 - core, lon_size)
        shares(source, left_keep.at[index], lon, core, lon_size)


def keep_kernel(*refs):
    *windows, send_rest, keep_first = refs
    windows = windows[:3], windows[3:]
    lat, core, size = place()
    for slot in range(0, size, 2):
        send_rest[slot // 2] = slot_product(slot, size, lat, 1 - core, [(w[2], w[1]) for w in windows]).astype(BF)
    for slot in range(1, size, 2):
        keep_first[slot // 2] = slot_product(slot, size, lat, core, [(w[0], w[1]) for w in windows]).astype(BF)


def output_kernel(_, *refs):
    (*windows, qkv_weight, proj_weight, keep_rest, inner_results, outer_results) = refs
    per_window = windows[:4], windows[4:]
    lat, core, size = place()
    width = proj_weight.shape[0]
    for slot in range(0, size, 2):
        keep_rest[slot // 2] = slot_product(slot, size, lat, core, [w[2:] for w in per_window]).astype(BF)
    x, grads = (jnp.concatenate([w[i][...] for w in per_window], axis=0) for i in (0, 1))

    def times(rows, weight, dims):
        return jnp.concatenate([dot(w[3][rows, :], weight[...], dims) for w in per_window], axis=0)

    x = x.astype(F32)
    normed, inv_std = normalise(x)
    output = (x + times(slice(3 * width, 4 * width), proj_weight, TN)).astype(BF)
    d_normed = times(slice(0, 3 * width), qkv_weight, ((0,), (1,)))
    d_inputs = grads.astype(F32) + inv_std * (
        d_normed
        - jnp.mean(d_normed, -1, keepdims=True)
        - normed * jnp.mean(d_normed * normed, -1, keepdims=True)
    )
    d_inputs = d_inputs.astype(BF)
    for at, out in ((0, inner_results), (WIN, outer_results)):
        out[:, :width] = output[at : at + WIN]
        out[:, width:] = d_inputs[at : at + WIN]


def pack_lon_kernel(outer_results, lon_out):
    outer_x = outer_results[...].astype(F32)[:HALF].astype(BF)
    lon_out[...] = dot(puts(last_rows, QUARTER, HALF), outer_x, NN).astype(BF)


def pack_back_kernel(_, inner_results, outer_results, lat_out, diag_out):
    inner_y = inner_results[...].astype(F32)[HALF:]
    outer_y = outer_results[...].astype(F32)[HALF:].astype(BF)
    lat_out[...] = jnp.concatenate([inner_y, dot(puts(first_rows, QUARTER, HALF), outer_y, NN)], axis=0).astype(BF)
    diag_out[...] = dot(puts(last_rows, QUARTER, HALF), outer_y, NN).astype(BF)


def place_kernel(inner_results, outer_results, lat_in, placed):
    inner_lat, outer_lat, _, _, inner_own, outer_own = (source for source, _ in sources())

    def lat(v):
        return jnp.where(v < HALF, inner_lat(v), outer_lat(v - HALF))

    def only_first(source):
        return lambda v: jnp.where(v < HALF, source(v), -1)

    placed[...] = (
        dot(puts(only_first(inner_own), TOKENS, WIN), inner_results[...], NN)
        + dot(puts(only_first(outer_own), TOKENS, WIN), outer_results[...], NN)
        + dot(puts(lat, TOKENS, HALF + QUARTER), lat_in[...], NN)
    )


def place_rest_kernel(placed, lon_in, diag_in, field_out, d_fields, done):
    done[...] = jnp.zeros_like(done)
    width = field_out.shape[1]
    _, _, lon, diag, _, _ = (source for source, _ in sources())
    total = (
        placed[...]
        + dot(puts(lon, TOKENS, QUARTER), lon_in[...], NN)
        + dot(puts(diag, TOKENS, QUARTER), diag_in[...], NN)
    ).astype(BF)
    field_out[...] = total[:, :width]
    d_fields[...] = total[:, width:]


def halve_kernel(_, *refs):
    *parts, send, keep = refs
    for slot in range(send.shape[0]):
        for out, source in ((send, 2 * slot + 1), (keep, 2 * slot)):
            out[slot] = sum(part[source].astype(F32) for part in parts).astype(BF)


def line_parts_kernel(count, *refs):
    parts, (keep, *sends) = refs[:count], refs[count:]
    rows = keep.shape[0]
    for step, out in enumerate((keep, *sends)):
        at = slice(step * rows, (step + 1) * rows)
        out[...] = sum(part[0, at].astype(F32) for part in parts).astype(out.dtype)


def sum_kernel(*refs):
    *parts, out = refs
    total = parts[0][...].astype(F32)
    for part in parts[1:]:
        total = total + part[...].astype(F32)
    out[...] = total.astype(out.dtype)


def finish_kernel(_, *refs):
    *parts, qkv_out, proj_out = refs
    lat, _, size = place()
    width = parts[0].shape[1]
    for step, part in enumerate(parts):
        share = lat ^ step
        total = part[...].astype(F32)
        of_qkv = 3 * size // 4

        @pl.when(share < of_qkv)
        def _():
            qkv_out[:, pl.ds(pl.multiple_of(share * width, width), width)] = total

        @pl.when(share >= of_qkv)
        def _():
            proj_out[:, pl.ds(pl.multiple_of((share - of_qkv) * width, width), width)] = total


def call(kernel, outs, *args, name, flops=0, limit=32, scratch=(), unread=()):
    vmem = pl.BlockSpec(memory_space=pltpu.VMEM)
    anywhere = pl.BlockSpec(memory_space=pl.ANY)
    shapes = [jax.ShapeDtypeStruct(shape, dtype) for shape, dtype in outs]
    nbytes = sum(a.size * a.dtype.itemsize for a in (*args, *shapes))
    return pl.pallas_call(
        kernel,
        out_shape=shapes,
        in_specs=[anywhere if i in unread else vmem for i in range(len(args))],
        out_specs=[vmem] * len(shapes),
        scratch_shapes=scratch,
        compiler_params=pltpu.CompilerParams(vmem_limit_bytes=limit * 2**20),
        cost_estimate=pl.CostEstimate(flops=flops, bytes_accessed=nbytes, transcendentals=0),
        name=name,
    )(*args)


def routes(lat_size, lon_size):
    lat, lon, diag = [], [], []
    for i in range(lat_size):
        for j in range(lon_size):
            step = -1 if j % 2 == 0 else 1
            before = (j - 1) % lon_size
            me = i * lon_size + j
            lat.append((me, ((i + step) % lat_size) * lon_size + j))
            lon.append((me, i * lon_size + before))
            diag.append((me, ((i - step) % lat_size) * lon_size + before))
    return lat, lon, diag


def per_device(fields, cotangent, qkv_weight, proj_weight):
    levels, row_count, col_count, width = fields.shape
    lat_size, lon_size = lax.axis_size("lat"), lax.axis_size("lon")
    both = ("lat", "lon")
    lat_route, lon_route, diag_route = routes(lat_size, lon_size)

    def back(route):
        return [(target, source) for source, target in route]

    own_fields = fields.reshape(TOKENS, width)
    own_grads = cotangent.reshape(TOKENS, width)
    lengths = (HALF, QUARTER, QUARTER, QUARTER, HALF, HALF)
    picked = call(order_kernel, [((rows, TOKENS), BF) for rows in lengths], name="order", flops=LOAD)
    pick_inner, pick_outer, pick_lon, pick_diag, pick_own, pick_outer_own = picked
    whole, half = ((HALF, 2 * width), F32), ((HALF, 2 * width), BF)
    quarter = ((QUARTER, 2 * width), BF)
    inner_lat, lon_piece = call(
        pack_kernel, [half, quarter], own_fields, own_grads, pick_inner, pick_lon, name="pack", flops=LOAD
    )
    outer_lat, diag_piece, outer_own, inner_own = call(
        pack_rest_kernel, [quarter, quarter, whole, whole],
        lon_piece, own_fields, own_grads, pick_outer, pick_diag, pick_outer_own, pick_own,
        name="pack_rest", flops=5 * 10**8, unread=(0,),
    )
    own_parts = call(
        own_kernel, [((HALF, lanes), F32) for lanes in (width, 3 * width, width)],
        inner_own, qkv_weight, proj_weight,
        name="own", flops=5 * 10**8,
    )
    inner_in = lax.ppermute(inner_lat, both, lat_route)
    lon_in = lax.ppermute(lon_piece, both, lon_route)
    outer_in = lax.ppermute(outer_lat, both, lat_route)
    diag_in = lax.ppermute(diag_piece, both, diag_route)

    split = (lat_size, width // 2, 4 * width // lat_size)
    halves = ((lat_size // 2, *split[1:]), BF)
    per_window = [
        ((WIN, width), BF),
        ((WIN, width), BF),
        ((2, width // 2, WIN), BF),
        ((4 * width, WIN), BF),
        ((2, width // 2, WIN), BF),
    ]
    scratch = [pltpu.VMEM((width, WIN), BF)] * 2
    grad_so_far, *inner = call(
        inner_kernel, [(halves[0], F32), *per_window], inner_own, *own_parts, inner_in, qkv_weight, proj_weight,
        name="inner", flops=10**9, scratch=scratch,
    )
    send_first, *outer = call(
        outer_kernel, [halves, *per_window],
        outer_own, lon_in, outer_in, diag_in, qkv_weight, proj_weight, grad_so_far,
        name="outer", flops=10**9, scratch=scratch,
    )
    sibling = [(j, j ^ 1) for j in range(lon_size)]
    received_first = lax.ppermute(send_first, "lon", sibling)
    send_rest, keep_first = call(keep_kernel, [halves, halves], *inner[2:], *outer[2:], name="keep", flops=10**9)
    received_rest = lax.ppermute(send_rest, "lon", sibling)

    def halving(phase, send):
        route = [
            (i * lon_size + j, (i ^ (1 << (phase if j % 2 == 0 else bits - 1 - phase))) * lon_size + j)
            for i in range(lat_size)
            for j in range(lon_size)
        ]
        return lax.ppermute(send, both, route)

    bits = lat_size.bit_length() - 1
    (send,) = call(sum_kernel, [halves], keep_first, received_first, name="chip_sum")
    received = halving(0, send)
    keep_rest, *results = call(
        output_kernel, [halves, ((WIN, 2 * width), BF), ((WIN, 2 * width), BF)],
        send, *inner[:4], *outer[:4], qkv_weight, proj_weight,
        name="outputs", flops=10**9, unread=(0,),
    )
    (lon_back,) = call(pack_lon_kernel, [quarter], results[1], name="pack_lon")
    lon_home = lax.ppermute(lon_back, both, back(lon_route))
    kept = [keep_rest, received_rest, received]
    slots = lat_size // 2
    for phase in range(1, bits):
        slots //= 2
        stay = ((slots, *split[1:]), BF)
        send, keep = call(halve_kernel, [stay, stay], lon_home, *kept, name=f"halve{slots}", unread=(0,))
        kept = [keep, halving(phase, send)]

    rows = width // lon_size
    share = ((rows, split[2]), BF)
    parts = call(
        functools.partial(line_parts_kernel, len(kept)), [share] * (lon_size // 2), *kept, name="line_parts"
    )
    arrived = [
        lax.ppermute(parts[step], "lon", [(j, j ^ (2 * step)) for j in range(lon_size)])
        for step in range(lon_size // 2 - 1, 0, -1)
    ]
    lat_back, diag_back = call(
        pack_back_kernel, [((HALF + QUARTER, 2 * width), BF), quarter],
        parts[1], *results,
        name="pack_back", unread=(0,),
    )
    lat_home = lax.ppermute(lat_back, both, back(lat_route))
    diag_home = lax.ppermute(diag_back, both, back(diag_route))
    (line_sum,) = call(sum_kernel, [share], parts[0], *arrived, name="line_sum", flops=LONG)
    shared = [
        lax.ppermute(line_sum, "lat", [(i, i ^ step) for i in range(lat_size)]) for step in range(1, lat_size)
    ]
    (placed,) = call(
        place_kernel, [((TOKENS, 2 * width), F32)], *results, lat_home, name="place"
    )
    field_out, d_fields, done = call(
        place_rest_kernel,
        [((TOKENS, width), BF), ((TOKENS, width), BF), ((8, LANES), F32)],
        placed, lon_home, diag_home,
        name="place_rest",
    )
    qkv_grad, proj_grad = call(
        finish_kernel,
        [((rows, 3 * width), F32), ((rows, width), F32)],
        done, line_sum, *shared,
        name="finish", unread=(0,),
    )
    return (field_out.reshape(fields.shape), d_fields.reshape(fields.shape), qkv_grad, jnp.transpose(proj_grad))


def solution(mesh):
    placed = (P(None, "lat", "lon", None), P(None, "lat", "lon", None), P(), P())
    return jax.shard_map(
        per_device,
        mesh=mesh,
        in_specs=placed,
        out_specs=(
            P(None, "lat", "lon", None),
            P(None, "lat", "lon", None),
            P("lon", None),
            P(None, "lon"),
        ),
        check_vma=False,
    )
```

```python
import functools
import math

import jax
import jax.numpy as jnp
from jax import lax
from jax.experimental import pallas as pl
from jax.experimental.pallas import tpu as pltpu
from jax.sharding import PartitionSpec as P

HEADS = 8
WIN_LAT = 6
WIN_LON = 12
LEVELS = 2
COLS = 24
HALF_LAT = WIN_LAT // 2
HALF_LON = WIN_LON // 2
HALF = LEVELS * HALF_LAT * WIN_LON
WIN = 2 * HALF
TOKENS = 2 * WIN
QUARTER = HALF // 2
LANES = 128

epsilon = 1e-05
LONG = 13 * 10**8
LOAD = 5 * 10**9
BF = jnp.bfloat16
F32 = jnp.float32


def dot(a, b, dims):
    return lax.dot_general(a, b, (dims, ((), ())), preferred_element_type=F32)


NN = ((1,), (0,))
NT = ((1,), (1,))
TN = ((0,), (0,))


def div(x, by):
    return (x * ((65536 + by - 1) // by)) >> 16


def own_token(level, row, col):
    return level * (WIN_LAT * COLS) + row * COLS + col


def inner_token(v, first):
    level = div(v, HALF_LAT * WIN_LON)
    rest = v - level * (HALF_LAT * WIN_LON)
    row = div(rest, WIN_LON)
    return own_token(level, first + row, HALF_LON + rest - row * WIN_LON)


def half_token(v, first, col):
    level = div(v, HALF_LAT * HALF_LON)
    rest = v - level * (HALF_LAT * HALF_LON)
    row = div(rest, HALF_LON)
    return jnp.where(v < QUARTER, own_token(level, first + row, col + rest - row * HALF_LON), -1)


def sources():
    even = lax.rem(lax.axis_index("lon"), 2) == 0
    sent = jnp.where(even, 0, HALF_LAT)
    kept = HALF_LAT - sent
    outer = HALF_LON + WIN_LON
    return (
        (lambda v: inner_token(v, sent), HALF),
        (lambda v: half_token(v, sent, outer), QUARTER),
        (lambda v: half_token(v, sent, 0), QUARTER),
        (lambda v: half_token(v, kept, 0), QUARTER),
        (lambda v: inner_token(v, kept), HALF),
        (lambda v: half_token(v, kept, outer), HALF),
    )


def picks(source, rows, columns):
    index = source(lax.broadcasted_iota(jnp.int32, (rows, 1), 0))
    return (index == lax.broadcasted_iota(jnp.int32, (rows, columns), 1)).astype(BF)


def puts(source, rows, columns):
    index = source(lax.broadcasted_iota(jnp.int32, (1, columns), 1))
    return (lax.broadcasted_iota(jnp.int32, (rows, columns), 0) == index).astype(BF)


def first_rows(v):
    return v


def last_rows(v):
    return v - QUARTER


def order_kernel(*outs):
    for out, (source, rows) in zip(outs, sources()):
        out[...] = picks(source, rows, TOKENS)


def pack_kernel(fields, cotangent, *refs):
    count = len(refs) // 2
    width = fields.shape[1]
    for pick, out in zip(refs[:count], refs[count:]):
        out[:, :width] = dot(pick[...], fields[...], NN).astype(out.dtype)
        out[:, width:] = dot(pick[...], cotangent[...], NN).astype(out.dtype)


def swap_bits(index, size, core):
    bits = size.bit_length() - 1
    turned = sum(((index >> b) & 1) << (bits - 1 - b) for b in range(bits))
    return jnp.where(core == 0, index, turned)


def shares(transposed, out, lon, core_of, lon_size):
    rows = transposed.shape[0] // lon_size
    chip = lon >> 1
    for step in range(lon_size // 2):
        start = pl.multiple_of(((chip ^ step) * 2 + core_of) * rows, rows)
        out[step * rows : (step + 1) * rows, :] = transposed[pl.ds(start, rows), :]


def transpose_bf16(block):
    return jnp.transpose(block.astype(BF))


def slot_product(slot, size, lat, core, windows):
    share = lat ^ swap_bits(slot, size, core)
    total = None
    for left, right in windows:
        lanes = right.shape[1] // size
        of_proj = (share >= 3 * size // 4).astype(jnp.int32)
        part = dot(left[of_proj], right[:, pl.ds(pl.multiple_of(share * lanes, lanes), lanes)], NN)
        total = part if total is None else total + part
    return total


def normalise(x):
    mean = jnp.mean(x, -1, keepdims=True)
    centred = x - mean
    variance = jnp.mean(centred * centred, -1, keepdims=True)
    inv_std = lax.rsqrt(variance + epsilon)
    return centred * inv_std, inv_std


def project(both, qkv_weight, proj_weight):
    width = both.shape[1] // 2
    normed, _ = normalise(both[:, :width])
    projected = dot(normed.astype(BF), qkv_weight[...], NN)
    return normed, projected, dot(both[:, width:].astype(BF), proj_weight[...], NT)


def pack_rest_kernel(_, *refs):
    pack_kernel(*refs)


def own_kernel(inner_own, qkv_weight, proj_weight, normed, projected, d_mixed):
    normed[...], projected[...], d_mixed[...] = project(inner_own[...], qkv_weight, proj_weight)


def inner_kernel(own, own_normed, own_projected, own_d_mixed, lat_in, qkv_weight, proj_weight, send_grad, *refs):
    arrived = lat_in[...].astype(F32)
    parts = project(arrived, qkv_weight, proj_weight)
    both = jnp.concatenate([own[...], arrived], axis=0)
    mine = own_normed, own_projected, own_d_mixed
    parts = [jnp.concatenate([first[...], second], axis=0) for first, second in zip(mine, parts)]
    one_window(both, *parts, *refs)
    *_, right, left, _, _ = refs
    lat, core, size = place()
    for slot in range(1, size, 2):
        send_grad[slot // 2] = slot_product(slot, size, lat, 1 - core, [(left, right)])


def outer_kernel(own, lon_in, lat_in, diag_in, qkv_weight, proj_weight, grad_so_far, send_first, *refs):
    last = picks(last_rows, HALF, QUARTER)
    both = jnp.concatenate(
        [
            own[...] + dot(last, lon_in[...], NN),
            dot(picks(first_rows, HALF, QUARTER), lat_in[...], NN) + dot(last, diag_in[...], NN),
        ],
        axis=0,
    )
    one_window(both, *project(both, qkv_weight, proj_weight), *refs)
    *_, right, left, _, _ = refs
    lat, core, size = place()
    for slot in range(1, size, 2):
        total = grad_so_far[slot // 2] + slot_product(slot, size, lat, 1 - core, [(left, right)])
        send_first[slot // 2] = total.astype(BF)


def place():
    return lax.axis_index("lat"), lax.rem(lax.axis_index("lon"), 2), lax.axis_size("lat")


def one_window(
    both, normed, projected, d_mixed,
    windows_out, grads_out, left_keep, right, left_send, normed_t, grads_t,
):
    width = both.shape[1] // 2
    lat, core, lat_size = place()
    lon, lon_size = lax.axis_index("lon"), lax.axis_size("lon")
    even = core == 0
    blocks = both[:, :width], both[:, width:]
    x = blocks[0]
    windows_out[...] = x.astype(BF)
    grads = blocks[1].astype(BF)
    grads_out[...] = grads
    projected, d_mixed = projected.astype(BF), d_mixed.astype(BF)

    head_size = width // HEADS
    factor = head_size ** (-0.5)
    apart = jnp.where(even, lat == lat_size - 1, lat == 0).astype(jnp.int32)
    half_b = (lax.broadcasted_iota(jnp.int32, (WIN, 2 * WIN), 0) >= HALF).astype(jnp.int32)
    at_a = lax.broadcasted_iota(jnp.int32, (WIN, 2 * WIN), 1)
    at_a = jnp.where(at_a >= WIN, at_a - WIN, at_a)
    half_a = (at_a >= HALF).astype(jnp.int32)
    allowed = ((half_a != half_b).astype(jnp.int32) * apart) == 0
    first_head = lax.broadcasted_iota(jnp.int32, (WIN, LANES), 1) < head_size
    zero = jnp.zeros((WIN, LANES), BF)

    def split_heads(block):
        return jnp.concatenate([jnp.where(first_head, block, zero), jnp.where(first_head, zero, block)], axis=0)

    def join_heads(block):
        return jnp.where(first_head, block[:WIN], block[WIN:]).astype(BF)

    pairs = range(width // LANES)

    def blocks_of(array, lanes_from):
        return [array[:, lanes_from + pair * LANES : lanes_from + (pair + 1) * LANES] for pair in pairs]

    def store(out, lanes_from, blocks):
        for pair, block in zip(pairs, blocks):
            out[:, lanes_from + pair * LANES : lanes_from + (pair + 1) * LANES] = block.astype(out.dtype)

    k, v = blocks_of(projected, width), blocks_of(projected, 2 * width)
    q2 = [split_heads(block) for block in blocks_of(projected, 0)]
    dm2 = [split_heads(block) for block in blocks_of(d_mixed, 0)]
    to_power = factor * math.log2(math.e)
    scores = [jnp.where(allowed, dot(k[p], q2[p], NT), -1e30) for p in pairs]
    d_probs = [dot(v[p], dm2[p] * jnp.asarray(factor, BF), NT) for p in pairs]
    exponents = [jnp.exp2((s - jnp.max(s, 0, keepdims=True)) * to_power) for s in scores]
    probs = [e * (1.0 / jnp.sum(e, 0, keepdims=True)) for e in exponents]
    probs_b = [p.astype(BF) for p in probs]
    store(right, 3 * width, [join_heads(dot(probs_b[p], v[p], TN)) for p in pairs])
    store(right, 2 * width, [dot(probs_b[p], dm2[p], NN) for p in pairs])
    d_scores = [
        (probs[p] * (d_probs[p] - jnp.sum(d_probs[p] * probs[p], 0, keepdims=True))).astype(BF)
        for p in pairs
    ]
    store(right, 0, [join_heads(dot(d_scores[p], k[p], TN)) for p in pairs])
    store(right, width, [dot(d_scores[p], q2[p], NN) for p in pairs])

    normed_t[...] = transpose_bf16(normed)
    grads_t[...] = transpose_bf16(grads)
    for index, source in enumerate((normed_t, grads_t)):
        shares(source, left_send.at[index], lon, 1 - core, lon_size)
        shares(source, left_keep.at[index], lon, core, lon_size)


def keep_kernel(*refs):
    *windows, send_rest, keep_first = refs
    windows = windows[:3], windows[3:]
    lat, core, size = place()
    for slot in range(0, size, 2):
        send_rest[slot // 2] = slot_product(slot, size, lat, 1 - core, [(w[2], w[1]) for w in windows]).astype(BF)
    for slot in range(1, size, 2):
        keep_first[slot // 2] = slot_product(slot, size, lat, core, [(w[0], w[1]) for w in windows]).astype(BF)


def output_kernel(_, *refs):
    (*windows, qkv_weight, proj_weight, keep_rest, inner_results, outer_results) = refs
    per_window = windows[:4], windows[4:]
    lat, core, size = place()
    width = proj_weight.shape[0]
    for slot in range(0, size, 2):
        keep_rest[slot // 2] = slot_product(slot, size, lat, core, [w[2:] for w in per_window]).astype(BF)
    x, grads, right = (jnp.concatenate([w[i][...] for w in per_window], axis=0) for i in (0, 1, 3))
    d_projected, mixed = right[:, : 3 * width], right[:, 3 * width :]
    x = x.astype(F32)
    normed, inv_std = normalise(x)
    output = (x + dot(mixed, proj_weight[...], NN)).astype(BF)
    d_normed = dot(d_projected, qkv_weight[...], NT)
    d_inputs = grads.astype(F32) + inv_std * (
        d_normed
        - jnp.mean(d_normed, -1, keepdims=True)
        - normed * jnp.mean(d_normed * normed, -1, keepdims=True)
    )
    d_inputs = d_inputs.astype(BF)
    for at, out in ((0, inner_results), (WIN, outer_results)):
        out[:, :width] = output[at : at + WIN]
        out[:, width:] = d_inputs[at : at + WIN]


def pack_lon_kernel(outer_results, lon_out):
    outer_x = outer_results[...].astype(F32)[:HALF].astype(BF)
    lon_out[...] = dot(puts(last_rows, QUARTER, HALF), outer_x, NN).astype(BF)


def pack_back_kernel(_, inner_results, outer_results, lat_out, diag_out):
    inner_y = inner_results[...].astype(F32)[HALF:]
    outer_y = outer_results[...].astype(F32)[HALF:].astype(BF)
    lat_out[...] = jnp.concatenate([inner_y, dot(puts(first_rows, QUARTER, HALF), outer_y, NN)], axis=0).astype(BF)
    diag_out[...] = dot(puts(last_rows, QUARTER, HALF), outer_y, NN).astype(BF)


def place_kernel(inner_results, outer_results, lat_in, placed):
    inner_lat, outer_lat, _, _, inner_own, outer_own = (source for source, _ in sources())

    def lat(v):
        return jnp.where(v < HALF, inner_lat(v), outer_lat(v - HALF))

    def only_first(source):
        return lambda v: jnp.where(v < HALF, source(v), -1)

    placed[...] = (
        dot(puts(only_first(inner_own), TOKENS, WIN), inner_results[...], NN)
        + dot(puts(only_first(outer_own), TOKENS, WIN), outer_results[...], NN)
        + dot(puts(lat, TOKENS, HALF + QUARTER), lat_in[...], NN)
    )


def place_rest_kernel(placed, lon_in, diag_in, field_out, d_fields, done):
    done[...] = jnp.zeros_like(done)
    width = field_out.shape[1]
    _, _, lon, diag, _, _ = (source for source, _ in sources())
    total = (
        placed[...]
        + dot(puts(lon, TOKENS, QUARTER), lon_in[...], NN)
        + dot(puts(diag, TOKENS, QUARTER), diag_in[...], NN)
    ).astype(BF)
    field_out[...] = total[:, :width]
    d_fields[...] = total[:, width:]


def halve_kernel(_, *refs):
    *parts, send, keep = refs
    for slot in range(send.shape[0]):
        for out, source in ((send, 2 * slot + 1), (keep, 2 * slot)):
            out[slot] = sum(part[source].astype(F32) for part in parts).astype(BF)


def line_parts_kernel(count, *refs):
    parts, (keep, *sends) = refs[:count], refs[count:]
    rows = keep.shape[0]
    for step, out in enumerate((keep, *sends)):
        at = slice(step * rows, (step + 1) * rows)
        out[...] = sum(part[0, at].astype(F32) for part in parts).astype(out.dtype)


def sum_kernel(*refs):
    *parts, out = refs
    total = parts[0][...].astype(F32)
    for part in parts[1:]:
        total = total + part[...].astype(F32)
    out[...] = total.astype(out.dtype)


def finish_kernel(_, *refs):
    *parts, qkv_out, proj_out = refs
    lat, _, size = place()
    width = parts[0].shape[1]
    for step, part in enumerate(parts):
        share = lat ^ step
        total = part[...].astype(F32)
        of_qkv = 3 * size // 4

        @pl.when(share < of_qkv)
        def _():
            qkv_out[:, pl.ds(pl.multiple_of(share * width, width), width)] = total

        @pl.when(share >= of_qkv)
        def _():
            proj_out[:, pl.ds(pl.multiple_of((share - of_qkv) * width, width), width)] = total


def call(kernel, outs, *args, name, flops=0, limit=32, scratch=(), unread=()):
    vmem = pl.BlockSpec(memory_space=pltpu.VMEM)
    anywhere = pl.BlockSpec(memory_space=pl.ANY)
    shapes = [jax.ShapeDtypeStruct(shape, dtype) for shape, dtype in outs]
    nbytes = sum(a.size * a.dtype.itemsize for a in (*args, *shapes))
    return pl.pallas_call(
        kernel,
        out_shape=shapes,
        in_specs=[anywhere if i in unread else vmem for i in range(len(args))],
        out_specs=[vmem] * len(shapes),
        scratch_shapes=scratch,
        compiler_params=pltpu.CompilerParams(vmem_limit_bytes=limit * 2**20),
        cost_estimate=pl.CostEstimate(flops=flops, bytes_accessed=nbytes, transcendentals=0),
        name=name,
    )(*args)


def routes(lat_size, lon_size):
    lat, lon, diag = [], [], []
    for i in range(lat_size):
        for j in range(lon_size):
            step = -1 if j % 2 == 0 else 1
            before = (j - 1) % lon_size
            me = i * lon_size + j
            lat.append((me, ((i + step) % lat_size) * lon_size + j))
            lon.append((me, i * lon_size + before))
            diag.append((me, ((i - step) % lat_size) * lon_size + before))
    return lat, lon, diag


def per_device(fields, cotangent, qkv_weight, proj_weight):
    levels, row_count, col_count, width = fields.shape
    lat_size, lon_size = lax.axis_size("lat"), lax.axis_size("lon")
    both = ("lat", "lon")
    lat_route, lon_route, diag_route = routes(lat_size, lon_size)

    def back(route):
        return [(target, source) for source, target in route]

    own_fields = fields.reshape(TOKENS, width)
    own_grads = cotangent.reshape(TOKENS, width)
    lengths = (HALF, QUARTER, QUARTER, QUARTER, HALF, HALF)
    picked = call(order_kernel, [((rows, TOKENS), BF) for rows in lengths], name="order", flops=LOAD)
    pick_inner, pick_outer, pick_lon, pick_diag, pick_own, pick_outer_own = picked
    whole, half = ((HALF, 2 * width), F32), ((HALF, 2 * width), BF)
    quarter = ((QUARTER, 2 * width), BF)
    inner_lat, lon_piece = call(
        pack_kernel, [half, quarter], own_fields, own_grads, pick_inner, pick_lon, name="pack", flops=LOAD
    )
    outer_lat, diag_piece, outer_own, inner_own = call(
        pack_rest_kernel, [quarter, quarter, whole, whole],
        lon_piece, own_fields, own_grads, pick_outer, pick_diag, pick_outer_own, pick_own,
        name="pack_rest", flops=5 * 10**8, unread=(0,),
    )
    own_parts = call(
        own_kernel, [((HALF, lanes), F32) for lanes in (width, 3 * width, width)],
        inner_own, qkv_weight, proj_weight,
        name="own", flops=5 * 10**8,
    )
    inner_in = lax.ppermute(inner_lat, both, lat_route)
    lon_in = lax.ppermute(lon_piece, both, lon_route)
    outer_in = lax.ppermute(outer_lat, both, lat_route)
    diag_in = lax.ppermute(diag_piece, both, diag_route)

    split = (lat_size, width // 2, 4 * width // lat_size)
    halves = ((lat_size // 2, *split[1:]), BF)
    per_window = [
        ((WIN, width), BF),
        ((WIN, width), BF),
        ((2, width // 2, WIN), BF),
        ((WIN, 4 * width), BF),
        ((2, width // 2, WIN), BF),
    ]
    scratch = [pltpu.VMEM((width, WIN), BF)] * 2
    grad_so_far, *inner = call(
        inner_kernel, [(halves[0], F32), *per_window], inner_own, *own_parts, inner_in, qkv_weight, proj_weight,
        name="inner", flops=10**9, scratch=scratch,
    )
    send_first, *outer = call(
        outer_kernel, [halves, *per_window],
        outer_own, lon_in, outer_in, diag_in, qkv_weight, proj_weight, grad_so_far,
        name="outer", flops=10**9, scratch=scratch,
    )
    sibling = [(j, j ^ 1) for j in range(lon_size)]
    received_first = lax.ppermute(send_first, "lon", sibling)
    send_rest, keep_first = call(keep_kernel, [halves, halves], *inner[2:], *outer[2:], name="keep", flops=10**9)
    received_rest = lax.ppermute(send_rest, "lon", sibling)

    def halving(phase, send):
        route = [
            (i * lon_size + j, (i ^ (1 << (phase if j % 2 == 0 else bits - 1 - phase))) * lon_size + j)
            for i in range(lat_size)
            for j in range(lon_size)
        ]
        return lax.ppermute(send, both, route)

    bits = lat_size.bit_length() - 1
    (send,) = call(sum_kernel, [halves], keep_first, received_first, name="chip_sum")
    received = halving(0, send)
    keep_rest, *results = call(
        output_kernel, [halves, ((WIN, 2 * width), BF), ((WIN, 2 * width), BF)],
        send, *inner[:4], *outer[:4], qkv_weight, proj_weight,
        name="outputs", flops=10**9, unread=(0,),
    )
    (lon_back,) = call(pack_lon_kernel, [quarter], results[1], name="pack_lon")
    lon_home = lax.ppermute(lon_back, both, back(lon_route))
    kept = [keep_rest, received_rest, received]
    slots = lat_size // 2
    for phase in range(1, bits):
        slots //= 2
        stay = ((slots, *split[1:]), BF)
        send, keep = call(halve_kernel, [stay, stay], lon_home, *kept, name=f"halve{slots}", unread=(0,))
        kept = [keep, halving(phase, send)]

    rows = width // lon_size
    share = ((rows, split[2]), BF)
    parts = call(
        functools.partial(line_parts_kernel, len(kept)), [share] * (lon_size // 2), *kept, name="line_parts"
    )
    arrived = [
        lax.ppermute(parts[step], "lon", [(j, j ^ (2 * step)) for j in range(lon_size)])
        for step in range(lon_size // 2 - 1, 0, -1)
    ]
    lat_back, diag_back = call(
        pack_back_kernel, [((HALF + QUARTER, 2 * width), BF), quarter],
        parts[1], *results,
        name="pack_back", unread=(0,),
    )
    lat_home = lax.ppermute(lat_back, both, back(lat_route))
    diag_home = lax.ppermute(diag_back, both, back(diag_route))
    (line_sum,) = call(sum_kernel, [share], parts[0], *arrived, name="line_sum", flops=LONG)
    shared = [
        lax.ppermute(line_sum, "lat", [(i, i ^ step) for i in range(lat_size)]) for step in range(1, lat_size)
    ]
    (placed,) = call(
        place_kernel, [((TOKENS, 2 * width), F32)], *results, lat_home, name="place"
    )
    field_out, d_fields, done = call(
        place_rest_kernel,
        [((TOKENS, width), BF), ((TOKENS, width), BF), ((8, LANES), F32)],
        placed, lon_home, diag_home,
        name="place_rest",
    )
    qkv_grad, proj_grad = call(
        finish_kernel,
        [((rows, 3 * width), F32), ((rows, width), F32)],
        done, line_sum, *shared,
        name="finish", unread=(0,),
    )
    return (field_out.reshape(fields.shape), d_fields.reshape(fields.shape), qkv_grad, jnp.transpose(proj_grad))


def solution(mesh):
    placed = (P(None, "lat", "lon", None), P(None, "lat", "lon", None), P(), P())
    return jax.shard_map(
        per_device,
        mesh=mesh,
        in_specs=placed,
        out_specs=(
            P(None, "lat", "lon", None),
            P(None, "lat", "lon", None),
            P("lon", None),
            P(None, "lon"),
        ),
        check_vma=False,
    )
```

```python
import functools

import jax
import jax.numpy as jnp
from jax import lax
from jax.experimental import pallas as pl
from jax.experimental.pallas import tpu as pltpu
from jax.sharding import PartitionSpec as P

HEADS = 8
WIN_LAT = 6
WIN_LON = 12
LEVELS = 2
COLS = 24
HALF_LAT = WIN_LAT // 2
HALF_LON = WIN_LON // 2
HALF = LEVELS * HALF_LAT * WIN_LON
WIN = 2 * HALF
TOKENS = 2 * WIN
QUARTER = HALF // 2
LANES = 128

epsilon = 1e-05
LONG = 13 * 10**8
LOAD = 5 * 10**9
BF = jnp.bfloat16
F32 = jnp.float32


def dot(a, b, dims):
    return lax.dot_general(a, b, (dims, ((), ())), preferred_element_type=F32)


NN = ((1,), (0,))
NT = ((1,), (1,))
TN = ((0,), (0,))


def div(x, by):
    return (x * ((65536 + by - 1) // by)) >> 16


def own_token(level, row, col):
    return level * (WIN_LAT * COLS) + row * COLS + col


def inner_token(v, first):
    level = div(v, HALF_LAT * WIN_LON)
    rest = v - level * (HALF_LAT * WIN_LON)
    row = div(rest, WIN_LON)
    return own_token(level, first + row, HALF_LON + rest - row * WIN_LON)


def half_token(v, first, col):
    level = div(v, HALF_LAT * HALF_LON)
    rest = v - level * (HALF_LAT * HALF_LON)
    row = div(rest, HALF_LON)
    return jnp.where(v < QUARTER, own_token(level, first + row, col + rest - row * HALF_LON), -1)


def sources():
    even = lax.rem(lax.axis_index("lon"), 2) == 0
    sent = jnp.where(even, 0, HALF_LAT)
    kept = HALF_LAT - sent
    outer = HALF_LON + WIN_LON
    return (
        (lambda v: inner_token(v, sent), HALF),
        (lambda v: half_token(v, sent, outer), QUARTER),
        (lambda v: half_token(v, sent, 0), QUARTER),
        (lambda v: half_token(v, kept, 0), QUARTER),
        (lambda v: inner_token(v, kept), HALF),
        (lambda v: half_token(v, kept, outer), HALF),
    )


def picks(source, rows, columns):
    index = source(lax.broadcasted_iota(jnp.int32, (rows, 1), 0))
    return (index == lax.broadcasted_iota(jnp.int32, (rows, columns), 1)).astype(BF)


def puts(source, rows, columns):
    index = source(lax.broadcasted_iota(jnp.int32, (1, columns), 1))
    return (lax.broadcasted_iota(jnp.int32, (rows, columns), 0) == index).astype(BF)


def first_rows(v):
    return v


def last_rows(v):
    return v - QUARTER


def order_kernel(*outs):
    for out, (source, rows) in zip(outs, sources()):
        out[...] = picks(source, rows, TOKENS)


def pack_kernel(fields, cotangent, *refs):
    count = len(refs) // 2
    width = fields.shape[1]
    for pick, out in zip(refs[:count], refs[count:]):
        out[:, :width] = dot(pick[...], fields[...], NN).astype(out.dtype)
        out[:, width:] = dot(pick[...], cotangent[...], NN).astype(out.dtype)


def swap_bits(index, size, core):
    bits = size.bit_length() - 1
    turned = sum(((index >> b) & 1) << (bits - 1 - b) for b in range(bits))
    return jnp.where(core == 0, index, turned)


def shares(transposed, out, lon, core_of, lon_size):
    rows = transposed.shape[0] // lon_size
    chip = lon >> 1
    for step in range(lon_size // 2):
        start = pl.multiple_of(((chip ^ step) * 2 + core_of) * rows, rows)
        out[step * rows : (step + 1) * rows, :] = transposed[pl.ds(start, rows), :]


def transpose_bf16(block):
    return jnp.transpose(block.astype(F32)).astype(BF)


def slot_product(slot, size, lat, core, windows):
    share = lat ^ swap_bits(slot, size, core)
    total = None
    for left, right in windows:
        lanes = right.shape[1] // size
        of_proj = (share >= 3 * size // 4).astype(jnp.int32)
        part = dot(left[of_proj], right[:, pl.ds(pl.multiple_of(share * lanes, lanes), lanes)], NN)
        total = part if total is None else total + part
    return total


def normalise(x):
    mean = jnp.mean(x, -1, keepdims=True)
    centred = x - mean
    variance = jnp.mean(centred * centred, -1, keepdims=True)
    inv_std = lax.rsqrt(variance + epsilon)
    return centred * inv_std, inv_std


def project(both, qkv_weight, proj_weight):
    width = both.shape[1] // 2
    normed, _ = normalise(both[:, :width])
    projected = dot(normed.astype(BF), qkv_weight[...], NN)
    return normed, projected, dot(both[:, width:].astype(BF), proj_weight[...], NT)


def pack_rest_kernel(_, *refs):
    pack_kernel(*refs)


def own_kernel(inner_own, qkv_weight, proj_weight, normed, projected, d_mixed):
    normed[...], projected[...], d_mixed[...] = project(inner_own[...], qkv_weight, proj_weight)


def inner_kernel(own, own_normed, own_projected, own_d_mixed, lat_in, qkv_weight, proj_weight, send_grad, *refs):
    arrived = lat_in[...].astype(F32)
    parts = project(arrived, qkv_weight, proj_weight)
    both = jnp.concatenate([own[...], arrived], axis=0)
    mine = own_normed, own_projected, own_d_mixed
    parts = [jnp.concatenate([first[...], second], axis=0) for first, second in zip(mine, parts)]
    one_window(both, *parts, *refs)
    *_, right, left, _, _ = refs
    lat, core, size = place()
    for slot in range(1, size, 2):
        send_grad[slot // 2] = slot_product(slot, size, lat, 1 - core, [(left, right)])


def outer_kernel(own, lon_in, lat_in, diag_in, qkv_weight, proj_weight, grad_so_far, send_a, send_b, *refs):
    last = picks(last_rows, HALF, QUARTER)
    both = jnp.concatenate(
        [
            own[...] + dot(last, lon_in[...], NN),
            dot(picks(first_rows, HALF, QUARTER), lat_in[...], NN) + dot(last, diag_in[...], NN),
        ],
        axis=0,
    )
    one_window(both, *project(both, qkv_weight, proj_weight), *refs)
    *_, right, left, _, _ = refs
    lat, core, size = place()
    for slot in range(1, size, 2):
        total = grad_so_far[slot // 2] + slot_product(slot, size, lat, 1 - core, [(left, right)])
        put_chunks((send_a, send_b), slot // 2, total)


def put_chunks(outs, slot, total):
    width = outs[0].shape[2]
    for chunk, out in enumerate(outs):
        out[slot] = total[:, chunk * width : (chunk + 1) * width].astype(BF)


def place():
    return lax.axis_index("lat"), lax.rem(lax.axis_index("lon"), 2), lax.axis_size("lat")


def one_window(
    both, normed, projected, d_mixed,
    windows_out, grads_out, left_keep, right, left_send, normed_t, grads_t,
):
    width = both.shape[1] // 2
    lat, core, lat_size = place()
    lon, lon_size = lax.axis_index("lon"), lax.axis_size("lon")
    even = core == 0
    blocks = both[:, :width], both[:, width:]
    x = blocks[0]
    windows_out[...] = x.astype(BF)
    grads = blocks[1].astype(BF)
    grads_out[...] = grads
    projected, d_mixed = projected.astype(BF), d_mixed.astype(BF)

    head_size = width // HEADS
    factor = head_size ** (-0.5)
    apart = jnp.where(even, lat == lat_size - 1, lat == 0).astype(jnp.int32)
    half_b = (lax.broadcasted_iota(jnp.int32, (WIN, 2 * WIN), 0) >= HALF).astype(jnp.int32)
    at_a = lax.broadcasted_iota(jnp.int32, (WIN, 2 * WIN), 1)
    at_a = jnp.where(at_a >= WIN, at_a - WIN, at_a)
    half_a = (at_a >= HALF).astype(jnp.int32)
    allowed = ((half_a != half_b).astype(jnp.int32) * apart) == 0
    first_head = lax.broadcasted_iota(jnp.int32, (WIN, LANES), 1) < head_size
    zero = jnp.zeros((WIN, LANES), BF)

    def split_heads(block):
        return jnp.concatenate([jnp.where(first_head, block, zero), jnp.where(first_head, zero, block)], axis=0)

    def join_heads(block):
        return jnp.where(first_head, block[:WIN], block[WIN:]).astype(BF)

    pairs = range(width // LANES)

    def blocks_of(array, lanes_from):
        return [array[:, lanes_from + pair * LANES : lanes_from + (pair + 1) * LANES] for pair in pairs]

    def store(out, lanes_from, blocks):
        for pair, block in zip(pairs, blocks):
            out[:, lanes_from + pair * LANES : lanes_from + (pair + 1) * LANES] = block.astype(out.dtype)

    k, v = blocks_of(projected, width), blocks_of(projected, 2 * width)
    q2 = [split_heads(block) for block in blocks_of(projected, 0)]
    dm2 = [split_heads(block) for block in blocks_of(d_mixed, 0)]
    scores = [jnp.where(allowed, dot(k[p], q2[p], NT) * factor, -1e30) for p in pairs]
    d_probs = [dot(v[p], dm2[p], NT) for p in pairs]
    exponents = [jnp.exp(s - jnp.max(s, 0, keepdims=True)) for s in scores]
    probs = [e * (1.0 / jnp.sum(e, 0, keepdims=True)) for e in exponents]
    probs_b = [p.astype(BF) for p in probs]
    store(right, 3 * width, [join_heads(dot(probs_b[p], v[p], TN)) for p in pairs])
    store(right, 2 * width, [dot(probs_b[p], dm2[p], NN) for p in pairs])
    d_scores = [
        (probs[p] * (d_probs[p] - jnp.sum(d_probs[p] * probs[p], 0, keepdims=True)) * factor).astype(BF)
        for p in pairs
    ]
    store(right, 0, [join_heads(dot(d_scores[p], k[p], TN)) for p in pairs])
    store(right, width, [dot(d_scores[p], q2[p], NN) for p in pairs])

    normed_t[...] = transpose_bf16(normed)
    grads_t[...] = transpose_bf16(grads)
    for index, source in enumerate((normed_t, grads_t)):
        shares(source, left_send.at[index], lon, 1 - core, lon_size)
        shares(source, left_keep.at[index], lon, core, lon_size)


def keep_kernel(*refs):
    *windows, keep_a, keep_b = refs
    windows = [windows[:2], windows[2:]]
    lat, core, size = place()
    for slot in range(1, size, 2):
        put_chunks((keep_a, keep_b), slot // 2, slot_product(slot, size, lat, core, windows))


def rest_kernel(_, __, *refs):
    *windows, send_rest, keep_rest = refs
    windows = windows[:3], windows[3:]
    lat, core, size = place()
    for slot in range(0, size, 2):
        send_rest[slot // 2] = slot_product(slot, size, lat, 1 - core, [(w[2], w[1]) for w in windows]).astype(BF)
    for slot in range(0, size, 2):
        keep_rest[slot // 2] = slot_product(slot, size, lat, core, [(w[0], w[1]) for w in windows]).astype(BF)


def output_kernel(_, *refs):
    (*windows, qkv_weight, proj_weight, inner_results, outer_results) = refs
    per_window = windows[:3], windows[3:]
    width = proj_weight.shape[0]
    x, grads, right = (jnp.concatenate([w[i][...] for w in per_window], axis=0) for i in range(3))
    d_projected, mixed = right[:, : 3 * width], right[:, 3 * width :]
    x = x.astype(F32)
    normed, inv_std = normalise(x)
    output = (x + dot(mixed, proj_weight[...], NN)).astype(BF)
    d_normed = dot(d_projected, qkv_weight[...], NT)
    d_inputs = grads.astype(F32) + inv_std * (
        d_normed
        - jnp.mean(d_normed, -1, keepdims=True)
        - normed * jnp.mean(d_normed * normed, -1, keepdims=True)
    )
    d_inputs = d_inputs.astype(BF)
    for at, out in ((0, inner_results), (WIN, outer_results)):
        out[:, :width] = output[at : at + WIN]
        out[:, width:] = d_inputs[at : at + WIN]


def pack_lon_kernel(outer_results, lon_out):
    outer_x = outer_results[...].astype(F32)[:HALF].astype(BF)
    lon_out[...] = dot(puts(last_rows, QUARTER, HALF), outer_x, NN).astype(BF)


def pack_back_kernel(_, inner_results, outer_results, lat_out, diag_out):
    inner_y = inner_results[...].astype(F32)[HALF:]
    outer_y = outer_results[...].astype(F32)[HALF:].astype(BF)
    lat_out[...] = jnp.concatenate([inner_y, dot(puts(first_rows, QUARTER, HALF), outer_y, NN)], axis=0).astype(BF)
    diag_out[...] = dot(puts(last_rows, QUARTER, HALF), outer_y, NN).astype(BF)


def place_kernel(inner_results, outer_results, lat_in, placed):
    inner_lat, outer_lat, _, _, inner_own, outer_own = (source for source, _ in sources())

    def lat(v):
        return jnp.where(v < HALF, inner_lat(v), outer_lat(v - HALF))

    def only_first(source):
        return lambda v: jnp.where(v < HALF, source(v), -1)

    placed[...] = (
        dot(puts(only_first(inner_own), TOKENS, WIN), inner_results[...], NN)
        + dot(puts(only_first(outer_own), TOKENS, WIN), outer_results[...], NN)
        + dot(puts(lat, TOKENS, HALF + QUARTER), lat_in[...], NN)
    )


def place_rest_kernel(placed, lon_in, diag_in, field_out, d_fields, done):
    done[...] = jnp.zeros_like(done)
    width = field_out.shape[1]
    _, _, lon, diag, _, _ = (source for source, _ in sources())
    total = (
        placed[...]
        + dot(puts(lon, TOKENS, QUARTER), lon_in[...], NN)
        + dot(puts(diag, TOKENS, QUARTER), diag_in[...], NN)
    ).astype(BF)
    field_out[...] = total[:, :width]
    d_fields[...] = total[:, width:]


def halve_kernel(chunk, _, *refs):
    *parts, send, keep = refs
    width = send.shape[2]

    def lanes(part):
        return slice(None) if part.shape[2] == width else slice(chunk * width, (chunk + 1) * width)

    for slot in range(send.shape[0]):
        for out, source in ((send, 2 * slot + 1), (keep, 2 * slot)):
            out[slot] = sum(part[source, :, lanes(part)].astype(F32) for part in parts).astype(BF)


def line_parts_kernel(count, *refs):
    chunks, (keep, *sends) = (refs[:count], refs[count : 2 * count]), refs[2 * count :]
    rows = keep.shape[0]
    for step, out in enumerate((keep, *sends)):
        at = slice(step * rows, (step + 1) * rows)
        totals = [sum(part[0, at].astype(F32) for part in parts) for parts in chunks]
        out[...] = jnp.concatenate(totals, axis=1).astype(out.dtype)


def sum_kernel(*refs):
    *parts, out = refs
    total = parts[0][...].astype(F32)
    for part in parts[1:]:
        total = total + part[...].astype(F32)
    out[...] = total.astype(out.dtype)


def finish_kernel(_, *refs):
    *parts, qkv_out, proj_out = refs
    lat, _, size = place()
    width = parts[0].shape[1]
    for step, part in enumerate(parts):
        share = lat ^ step
        total = part[...].astype(F32)
        of_qkv = 3 * size // 4

        @pl.when(share < of_qkv)
        def _():
            qkv_out[:, pl.ds(pl.multiple_of(share * width, width), width)] = total

        @pl.when(share >= of_qkv)
        def _():
            proj_out[:, pl.ds(pl.multiple_of((share - of_qkv) * width, width), width)] = total


def call(kernel, outs, *args, name, flops=0, limit=32, scratch=(), unread=(), beside=False):
    vmem = pl.BlockSpec(memory_space=pltpu.VMEM)
    anywhere = pl.BlockSpec(memory_space=pl.ANY)
    shapes = [jax.ShapeDtypeStruct(shape, dtype) for shape, dtype in outs]
    nbytes = 0 if beside else sum(a.size * a.dtype.itemsize for a in (*args, *shapes))
    return pl.pallas_call(
        kernel,
        out_shape=shapes,
        in_specs=[anywhere if i in unread else vmem for i in range(len(args))],
        out_specs=[vmem] * len(shapes),
        scratch_shapes=scratch,
        compiler_params=pltpu.CompilerParams(vmem_limit_bytes=limit * 2**20),
        cost_estimate=pl.CostEstimate(flops=flops, bytes_accessed=nbytes, transcendentals=0),
        name=name,
    )(*args)


def routes(lat_size, lon_size):
    lat, lon, diag = [], [], []
    for i in range(lat_size):
        for j in range(lon_size):
            step = -1 if j % 2 == 0 else 1
            before = (j - 1) % lon_size
            me = i * lon_size + j
            lat.append((me, ((i + step) % lat_size) * lon_size + j))
            lon.append((me, i * lon_size + before))
            diag.append((me, ((i - step) % lat_size) * lon_size + before))
    return lat, lon, diag


def per_device(fields, cotangent, qkv_weight, proj_weight):
    levels, row_count, col_count, width = fields.shape
    lat_size, lon_size = lax.axis_size("lat"), lax.axis_size("lon")
    both = ("lat", "lon")
    lat_route, lon_route, diag_route = routes(lat_size, lon_size)

    def back(route):
        return [(target, source) for source, target in route]

    own_fields = fields.reshape(TOKENS, width)
    own_grads = cotangent.reshape(TOKENS, width)
    lengths = (HALF, QUARTER, QUARTER, QUARTER, HALF, HALF)
    picked = call(order_kernel, [((rows, TOKENS), BF) for rows in lengths], name="order", flops=LOAD)
    pick_inner, pick_outer, pick_lon, pick_diag, pick_own, pick_outer_own = picked
    whole, half = ((HALF, 2 * width), F32), ((HALF, 2 * width), BF)
    quarter = ((QUARTER, 2 * width), BF)
    inner_lat, lon_piece = call(
        pack_kernel, [half, quarter], own_fields, own_grads, pick_inner, pick_lon, name="pack", flops=LOAD
    )
    outer_lat, diag_piece, outer_own, inner_own = call(
        pack_rest_kernel, [quarter, quarter, whole, whole],
        lon_piece, own_fields, own_grads, pick_outer, pick_diag, pick_outer_own, pick_own,
        name="pack_rest", flops=5 * 10**8, unread=(0,),
    )
    own_parts = call(
        own_kernel, [((HALF, lanes), F32) for lanes in (width, 3 * width, width)],
        inner_own, qkv_weight, proj_weight,
        name="own", flops=5 * 10**8,
    )
    inner_in = lax.ppermute(inner_lat, both, lat_route)
    lon_in = lax.ppermute(lon_piece, both, lon_route)
    outer_in = lax.ppermute(outer_lat, both, lat_route)
    diag_in = lax.ppermute(diag_piece, both, diag_route)

    split = (lat_size, width // 2, 4 * width // lat_size)
    halves = ((lat_size // 2, *split[1:]), BF)
    chunk = ((lat_size // 2, split[1], split[2] // 2), BF)
    per_window = [
        ((WIN, width), BF),
        ((WIN, width), BF),
        ((2, width // 2, WIN), BF),
        ((WIN, 4 * width), BF),
        ((2, width // 2, WIN), BF),
    ]
    scratch = [pltpu.VMEM((width, WIN), BF)] * 2
    grad_so_far, *inner = call(
        inner_kernel, [(halves[0], F32), *per_window], inner_own, *own_parts, inner_in, qkv_weight, proj_weight,
        name="inner", flops=10**9, scratch=scratch,
    )
    send_a, send_b, *outer = call(
        outer_kernel, [chunk, chunk, *per_window],
        outer_own, lon_in, outer_in, diag_in, qkv_weight, proj_weight, grad_so_far,
        name="outer", flops=10**9, scratch=scratch,
    )
    sibling = [(j, j ^ 1) for j in range(lon_size)]
    arrived = [lax.ppermute(send, "lon", sibling) for send in (send_a, send_b)]
    keep = call(keep_kernel, [chunk, chunk], *inner[2:4], *outer[2:4], name="keep", flops=10**9)

    def halving(phase, send):
        route = [
            (i * lon_size + j, (i ^ (1 << (phase if j % 2 == 0 else bits - 1 - phase))) * lon_size + j)
            for i in range(lat_size)
            for j in range(lon_size)
        ]
        return lax.ppermute(send, both, route)

    bits = lat_size.bit_length() - 1
    sends = [
        call(sum_kernel, [chunk], mine, theirs, name="chip_sum")[0] for mine, theirs in zip(keep, arrived)
    ]
    received = [halving(0, send) for send in sends]
    send_rest, keep_rest = call(
        rest_kernel, [halves, halves], *sends, *inner[2:], *outer[2:], name="rest", unread=(0, 1), beside=True
    )
    received_rest = lax.ppermute(send_rest, "lon", sibling)
    results = call(
        output_kernel, [((WIN, 2 * width), BF)] * 2,
        keep_rest, *inner[:2], inner[3], *outer[:2], outer[3], qkv_weight, proj_weight,
        name="outputs", unread=(0,), flops=10**10,
    )
    (lon_back,) = call(pack_lon_kernel, [quarter], results[1], name="pack_lon", beside=True)
    lon_home = lax.ppermute(lon_back, both, back(lon_route))
    kept = [[keep_rest, received_rest, part] for part in received]
    slots = lat_size // 2
    for phase in range(1, bits):
        slots //= 2
        stay = ((slots, *chunk[0][1:]), BF)
        for index, after in enumerate((lon_home, sends[1])):
            send, keep = call(
                functools.partial(halve_kernel, index), [stay, stay], after, *kept[index],
                name=f"halve{slots}", unread=(0,),
            )
            kept[index] = [keep, halving(phase, send)]

    rows = width // lon_size
    share = ((rows, split[2]), BF)
    parts = call(
        functools.partial(line_parts_kernel, len(kept[0])), [share] * (lon_size // 2), *kept[0], *kept[1],
        name="line_parts",
    )
    arrived = [
        lax.ppermute(parts[step], "lon", [(j, j ^ (2 * step)) for j in range(lon_size)])
        for step in range(lon_size // 2 - 1, 0, -1)
    ]
    lat_back, diag_back = call(
        pack_back_kernel, [((HALF + QUARTER, 2 * width), BF), quarter],
        parts[1], *results,
        name="pack_back", unread=(0,),
    )
    lat_home = lax.ppermute(lat_back, both, back(lat_route))
    diag_home = lax.ppermute(diag_back, both, back(diag_route))
    (line_sum,) = call(sum_kernel, [share], parts[0], *arrived, name="line_sum", flops=LONG)
    shared = [
        lax.ppermute(line_sum, "lat", [(i, i ^ step) for i in range(lat_size)]) for step in range(1, lat_size)
    ]
    (placed,) = call(
        place_kernel, [((TOKENS, 2 * width), F32)], *results, lat_home, name="place"
    )
    field_out, d_fields, done = call(
        place_rest_kernel,
        [((TOKENS, width), BF), ((TOKENS, width), BF), ((8, LANES), F32)],
        placed, lon_home, diag_home,
        name="place_rest",
    )
    qkv_grad, proj_grad = call(
        finish_kernel,
        [((rows, 3 * width), F32), ((rows, width), F32)],
        done, line_sum, *shared,
        name="finish", unread=(0,),
    )
    return (field_out.reshape(fields.shape), d_fields.reshape(fields.shape), qkv_grad, jnp.transpose(proj_grad))


def solution(mesh):
    placed = (P(None, "lat", "lon", None), P(None, "lat", "lon", None), P(), P())
    return jax.shard_map(
        per_device,
        mesh=mesh,
        in_specs=placed,
        out_specs=(
            P(None, "lat", "lon", None),
            P(None, "lat", "lon", None),
            P("lon", None),
            P(None, "lon"),
        ),
        check_vma=False,
    )
```

```python
import functools

import jax
import jax.numpy as jnp
from jax import lax
from jax.experimental import pallas as pl
from jax.experimental.pallas import tpu as pltpu
from jax.sharding import PartitionSpec as P

HEADS = 8
WIN_LAT = 6
WIN_LON = 12
LEVELS = 2
COLS = 24
HALF_LAT = WIN_LAT // 2
HALF_LON = WIN_LON // 2
HALF = LEVELS * HALF_LAT * WIN_LON
WIN = 2 * HALF
TOKENS = 2 * WIN
QUARTER = HALF // 2
LANES = 128

epsilon = 1e-05
LONG = 13 * 10**8
LOAD = 5 * 10**9
BF = jnp.bfloat16
F32 = jnp.float32


def dot(a, b, dims):
    return lax.dot_general(a, b, (dims, ((), ())), preferred_element_type=F32)


NN = ((1,), (0,))
NT = ((1,), (1,))
TN = ((0,), (0,))


def div(x, by):
    return (x * ((65536 + by - 1) // by)) >> 16


def own_token(level, row, col):
    return level * (WIN_LAT * COLS) + row * COLS + col


def inner_token(v, first):
    level = div(v, HALF_LAT * WIN_LON)
    rest = v - level * (HALF_LAT * WIN_LON)
    row = div(rest, WIN_LON)
    return own_token(level, first + row, HALF_LON + rest - row * WIN_LON)


def half_token(v, first, col):
    level = div(v, HALF_LAT * HALF_LON)
    rest = v - level * (HALF_LAT * HALF_LON)
    row = div(rest, HALF_LON)
    return jnp.where(v < QUARTER, own_token(level, first + row, col + rest - row * HALF_LON), -1)


def sources():
    even = lax.rem(lax.axis_index("lon"), 2) == 0
    sent = jnp.where(even, 0, HALF_LAT)
    kept = HALF_LAT - sent
    outer = HALF_LON + WIN_LON
    return (
        (lambda v: inner_token(v, sent), HALF),
        (lambda v: half_token(v, sent, outer), QUARTER),
        (lambda v: half_token(v, sent, 0), QUARTER),
        (lambda v: half_token(v, kept, 0), QUARTER),
        (lambda v: inner_token(v, kept), HALF),
        (lambda v: half_token(v, kept, outer), HALF),
    )


def picks(source, rows, columns):
    index = source(lax.broadcasted_iota(jnp.int32, (rows, 1), 0))
    return (index == lax.broadcasted_iota(jnp.int32, (rows, columns), 1)).astype(BF)


def puts(source, rows, columns):
    index = source(lax.broadcasted_iota(jnp.int32, (1, columns), 1))
    return (lax.broadcasted_iota(jnp.int32, (rows, columns), 0) == index).astype(BF)


def first_rows(v):
    return v


def last_rows(v):
    return v - QUARTER


def order_kernel(*outs):
    for out, (source, rows) in zip(outs, sources()):
        out[...] = picks(source, rows, TOKENS)


def pack_kernel(fields, cotangent, *refs):
    count = len(refs) // 2
    width = fields.shape[1]
    for pick, out in zip(refs[:count], refs[count:]):
        out[:, :width] = dot(pick[...], fields[...], NN).astype(out.dtype)
        out[:, width:] = dot(pick[...], cotangent[...], NN).astype(out.dtype)


def swap_bits(index, size, core):
    bits = size.bit_length() - 1
    turned = sum(((index >> b) & 1) << (bits - 1 - b) for b in range(bits))
    return jnp.where(core == 0, index, turned)


def shares(transposed, out, lon, core_of, lon_size):
    rows = transposed.shape[0] // lon_size
    chip = lon >> 1
    for step in range(lon_size // 2):
        start = pl.multiple_of(((chip ^ step) * 2 + core_of) * rows, rows)
        out[step * rows : (step + 1) * rows, :] = transposed[pl.ds(start, rows), :]


def transpose_bf16(block):
    return jnp.transpose(block.astype(F32)).astype(BF)


def slot_product(slot, size, lat, core, windows):
    share = lat ^ swap_bits(slot, size, core)
    total = None
    for left, right in windows:
        lanes = right.shape[1] // size
        of_proj = (share >= 3 * size // 4).astype(jnp.int32)
        part = dot(left[of_proj], right[:, pl.ds(pl.multiple_of(share * lanes, lanes), lanes)], NN)
        total = part if total is None else total + part
    return total


def normalise(x):
    mean = jnp.mean(x, -1, keepdims=True)
    centred = x - mean
    variance = jnp.mean(centred * centred, -1, keepdims=True)
    inv_std = lax.rsqrt(variance + epsilon)
    return centred * inv_std, inv_std


def project(both, qkv_weight, proj_weight):
    width = both.shape[1] // 2
    normed, _ = normalise(both[:, :width])
    projected = dot(normed.astype(BF), qkv_weight[...], NN)
    return normed, projected, dot(both[:, width:].astype(BF), proj_weight[...], NT)


def pack_rest_kernel(_, *refs):
    pack_kernel(*refs)


def own_kernel(inner_own, qkv_weight, proj_weight, normed, projected, d_mixed):
    normed[...], projected[...], d_mixed[...] = project(inner_own[...], qkv_weight, proj_weight)


def inner_kernel(own, own_normed, own_projected, own_d_mixed, lat_in, qkv_weight, proj_weight, send_grad, *refs):
    arrived = lat_in[...].astype(F32)
    parts = project(arrived, qkv_weight, proj_weight)
    both = jnp.concatenate([own[...], arrived], axis=0)
    mine = own_normed, own_projected, own_d_mixed
    parts = [jnp.concatenate([first[...], second], axis=0) for first, second in zip(mine, parts)]
    one_window(both, *parts, *refs)
    *_, right, left, _, _ = refs
    lat, core, size = place()
    for slot in range(1, size, 2):
        send_grad[slot // 2] = slot_product(slot, size, lat, 1 - core, [(left, right)])


def outer_kernel(own, lon_in, lat_in, diag_in, qkv_weight, proj_weight, grad_so_far, *refs):
    count = len(chunk_widths(proj_weight.shape[0] * 4 // lax.axis_size("lat")))
    sends, refs = refs[:count], refs[count:]
    last = picks(last_rows, HALF, QUARTER)
    both = jnp.concatenate(
        [
            own[...] + dot(last, lon_in[...], NN),
            dot(picks(first_rows, HALF, QUARTER), lat_in[...], NN) + dot(last, diag_in[...], NN),
        ],
        axis=0,
    )
    one_window(both, *project(both, qkv_weight, proj_weight), *refs)
    *_, right, left, _, _ = refs
    lat, core, size = place()
    for slot in range(1, size, 2):
        total = grad_so_far[slot // 2] + slot_product(slot, size, lat, 1 - core, [(left, right)])
        put_chunks(sends, slot // 2, total)


def chunk_widths(lanes):
    return (lanes // 2, lanes // 4, lanes // 4) if lanes % 512 == 0 else (lanes // 2,) * 2


def put_chunks(outs, slot, total):
    at = 0
    for out in outs:
        out[slot] = total[:, at : at + out.shape[2]].astype(BF)
        at += out.shape[2]


def place():
    return lax.axis_index("lat"), lax.rem(lax.axis_index("lon"), 2), lax.axis_size("lat")


def one_window(
    both, normed, projected, d_mixed,
    windows_out, grads_out, left_keep, right, left_send, normed_t, grads_t,
):
    width = both.shape[1] // 2
    lat, core, lat_size = place()
    lon, lon_size = lax.axis_index("lon"), lax.axis_size("lon")
    even = core == 0
    blocks = both[:, :width], both[:, width:]
    x = blocks[0]
    windows_out[...] = x.astype(BF)
    grads = blocks[1].astype(BF)
    grads_out[...] = grads
    projected, d_mixed = projected.astype(BF), d_mixed.astype(BF)

    head_size = width // HEADS
    factor = head_size ** (-0.5)
    apart = jnp.where(even, lat == lat_size - 1, lat == 0).astype(jnp.int32)
    half_b = (lax.broadcasted_iota(jnp.int32, (WIN, 2 * WIN), 0) >= HALF).astype(jnp.int32)
    at_a = lax.broadcasted_iota(jnp.int32, (WIN, 2 * WIN), 1)
    at_a = jnp.where(at_a >= WIN, at_a - WIN, at_a)
    half_a = (at_a >= HALF).astype(jnp.int32)
    allowed = ((half_a != half_b).astype(jnp.int32) * apart) == 0
    first_head = lax.broadcasted_iota(jnp.int32, (WIN, LANES), 1) < head_size
    zero = jnp.zeros((WIN, LANES), BF)

    def split_heads(block):
        return jnp.concatenate([jnp.where(first_head, block, zero), jnp.where(first_head, zero, block)], axis=0)

    def join_heads(block):
        return jnp.where(first_head, block[:WIN], block[WIN:]).astype(BF)

    pairs = range(width // LANES)

    def blocks_of(array, lanes_from):
        return [array[:, lanes_from + pair * LANES : lanes_from + (pair + 1) * LANES] for pair in pairs]

    def store(out, lanes_from, blocks):
        for pair, block in zip(pairs, blocks):
            out[:, lanes_from + pair * LANES : lanes_from + (pair + 1) * LANES] = block.astype(out.dtype)

    k, v = blocks_of(projected, width), blocks_of(projected, 2 * width)
    q2 = [split_heads(block) for block in blocks_of(projected, 0)]
    dm2 = [split_heads(block) for block in blocks_of(d_mixed, 0)]
    scores = [jnp.where(allowed, dot(k[p], q2[p], NT) * factor, -1e30) for p in pairs]
    d_probs = [dot(v[p], dm2[p], NT) for p in pairs]
    exponents = [jnp.exp(s - jnp.max(s, 0, keepdims=True)) for s in scores]
    probs = [e * (1.0 / jnp.sum(e, 0, keepdims=True)) for e in exponents]
    probs_b = [p.astype(BF) for p in probs]
    store(right, 3 * width, [join_heads(dot(probs_b[p], v[p], TN)) for p in pairs])
    store(right, 2 * width, [dot(probs_b[p], dm2[p], NN) for p in pairs])
    d_scores = [
        (probs[p] * (d_probs[p] - jnp.sum(d_probs[p] * probs[p], 0, keepdims=True)) * factor).astype(BF)
        for p in pairs
    ]
    store(right, 0, [join_heads(dot(d_scores[p], k[p], TN)) for p in pairs])
    store(right, width, [dot(d_scores[p], q2[p], NN) for p in pairs])

    normed_t[...] = transpose_bf16(normed)
    grads_t[...] = transpose_bf16(grads)
    for index, source in enumerate((normed_t, grads_t)):
        shares(source, left_send.at[index], lon, 1 - core, lon_size)
        shares(source, left_keep.at[index], lon, core, lon_size)


def keep_kernel(*refs):
    windows, keeps = [refs[:2], refs[2:4]], refs[4:]
    lat, core, size = place()
    for slot in range(1, size, 2):
        put_chunks(keeps, slot // 2, slot_product(slot, size, lat, core, windows))


def rest_kernel(count, *refs):
    *windows, send_rest, keep_rest = refs[count:]
    windows = windows[:3], windows[3:]
    lat, core, size = place()
    for slot in range(0, size, 2):
        send_rest[slot // 2] = slot_product(slot, size, lat, 1 - core, [(w[2], w[1]) for w in windows]).astype(BF)
    for slot in range(0, size, 2):
        keep_rest[slot // 2] = slot_product(slot, size, lat, core, [(w[0], w[1]) for w in windows]).astype(BF)


def output_kernel(_, *refs):
    (*windows, qkv_weight, proj_weight, inner_results, outer_results) = refs
    per_window = windows[:3], windows[3:]
    width = proj_weight.shape[0]
    x, grads, right = (jnp.concatenate([w[i][...] for w in per_window], axis=0) for i in range(3))
    d_projected, mixed = right[:, : 3 * width], right[:, 3 * width :]
    x = x.astype(F32)
    normed, inv_std = normalise(x)
    output = (x + dot(mixed, proj_weight[...], NN)).astype(BF)
    d_normed = dot(d_projected, qkv_weight[...], NT)
    d_inputs = grads.astype(F32) + inv_std * (
        d_normed
        - jnp.mean(d_normed, -1, keepdims=True)
        - normed * jnp.mean(d_normed * normed, -1, keepdims=True)
    )
    d_inputs = d_inputs.astype(BF)
    for at, out in ((0, inner_results), (WIN, outer_results)):
        out[:, :width] = output[at : at + WIN]
        out[:, width:] = d_inputs[at : at + WIN]


def pack_lon_kernel(outer_results, lon_out):
    outer_x = outer_results[...].astype(F32)[:HALF].astype(BF)
    lon_out[...] = dot(puts(last_rows, QUARTER, HALF), outer_x, NN).astype(BF)


def pack_back_kernel(_, inner_results, outer_results, lat_out, diag_out):
    inner_y = inner_results[...].astype(F32)[HALF:]
    outer_y = outer_results[...].astype(F32)[HALF:].astype(BF)
    lat_out[...] = jnp.concatenate([inner_y, dot(puts(first_rows, QUARTER, HALF), outer_y, NN)], axis=0).astype(BF)
    diag_out[...] = dot(puts(last_rows, QUARTER, HALF), outer_y, NN).astype(BF)


def place_kernel(inner_results, outer_results, lat_in, placed):
    inner_lat, outer_lat, _, _, inner_own, outer_own = (source for source, _ in sources())

    def lat(v):
        return jnp.where(v < HALF, inner_lat(v), outer_lat(v - HALF))

    def only_first(source):
        return lambda v: jnp.where(v < HALF, source(v), -1)

    placed[...] = (
        dot(puts(only_first(inner_own), TOKENS, WIN), inner_results[...], NN)
        + dot(puts(only_first(outer_own), TOKENS, WIN), outer_results[...], NN)
        + dot(puts(lat, TOKENS, HALF + QUARTER), lat_in[...], NN)
    )


def place_rest_kernel(placed, lon_in, diag_in, field_out, d_fields, done):
    done[...] = jnp.zeros_like(done)
    width = field_out.shape[1]
    _, _, lon, diag, _, _ = (source for source, _ in sources())
    total = (
        placed[...]
        + dot(puts(lon, TOKENS, QUARTER), lon_in[...], NN)
        + dot(puts(diag, TOKENS, QUARTER), diag_in[...], NN)
    ).astype(BF)
    field_out[...] = total[:, :width]
    d_fields[...] = total[:, width:]


def halve_kernel(first_lane, _, *refs):
    *parts, send, keep = refs
    width = send.shape[2]

    def lanes(part):
        return slice(None) if part.shape[2] == width else slice(first_lane, first_lane + width)

    for slot in range(send.shape[0]):
        for out, source in ((send, 2 * slot + 1), (keep, 2 * slot)):
            out[slot] = sum(part[source, :, lanes(part)].astype(F32) for part in parts).astype(BF)


def line_parts_kernel(counts, *refs):
    chunks = []
    for count in counts:
        chunks.append(refs[:count])
        refs = refs[count:]
    rows = refs[0].shape[0]
    for step, out in enumerate(refs):
        at = slice(step * rows, (step + 1) * rows)
        totals = [sum(part[0, at].astype(F32) for part in parts) for parts in chunks]
        out[...] = jnp.concatenate(totals, axis=1).astype(out.dtype)


def sum_kernel(*refs):
    *parts, out = refs
    total = parts[0][...].astype(F32)
    for part in parts[1:]:
        total = total + part[...].astype(F32)
    out[...] = total.astype(out.dtype)


def next_sum_kernel(_, *refs):
    sum_kernel(*refs)


def finish_kernel(_, *refs):
    *parts, qkv_out, proj_out = refs
    lat, _, size = place()
    width = parts[0].shape[1]
    for step, part in enumerate(parts):
        share = lat ^ step
        total = part[...].astype(F32)
        of_qkv = 3 * size // 4

        @pl.when(share < of_qkv)
        def _():
            qkv_out[:, pl.ds(pl.multiple_of(share * width, width), width)] = total

        @pl.when(share >= of_qkv)
        def _():
            proj_out[:, pl.ds(pl.multiple_of((share - of_qkv) * width, width), width)] = total


def call(kernel, outs, *args, name, flops=0, limit=32, scratch=(), unread=(), beside=False):
    vmem = pl.BlockSpec(memory_space=pltpu.VMEM)
    anywhere = pl.BlockSpec(memory_space=pl.ANY)
    shapes = [jax.ShapeDtypeStruct(shape, dtype) for shape, dtype in outs]
    nbytes = 0 if beside else sum(a.size * a.dtype.itemsize for a in (*args, *shapes))
    return pl.pallas_call(
        kernel,
        out_shape=shapes,
        in_specs=[anywhere if i in unread else vmem for i in range(len(args))],
        out_specs=[vmem] * len(shapes),
        scratch_shapes=scratch,
        compiler_params=pltpu.CompilerParams(vmem_limit_bytes=limit * 2**20),
        cost_estimate=pl.CostEstimate(flops=flops, bytes_accessed=nbytes, transcendentals=0),
        name=name,
    )(*args)


def routes(lat_size, lon_size):
    lat, lon, diag = [], [], []
    for i in range(lat_size):
        for j in range(lon_size):
            step = -1 if j % 2 == 0 else 1
            before = (j - 1) % lon_size
            me = i * lon_size + j
            lat.append((me, ((i + step) % lat_size) * lon_size + j))
            lon.append((me, i * lon_size + before))
            diag.append((me, ((i - step) % lat_size) * lon_size + before))
    return lat, lon, diag


def per_device(fields, cotangent, qkv_weight, proj_weight):
    levels, row_count, col_count, width = fields.shape
    lat_size, lon_size = lax.axis_size("lat"), lax.axis_size("lon")
    both = ("lat", "lon")
    lat_route, lon_route, diag_route = routes(lat_size, lon_size)

    def back(route):
        return [(target, source) for source, target in route]

    own_fields = fields.reshape(TOKENS, width)
    own_grads = cotangent.reshape(TOKENS, width)
    lengths = (HALF, QUARTER, QUARTER, QUARTER, HALF, HALF)
    picked = call(order_kernel, [((rows, TOKENS), BF) for rows in lengths], name="order", flops=LOAD)
    pick_inner, pick_outer, pick_lon, pick_diag, pick_own, pick_outer_own = picked
    whole, half = ((HALF, 2 * width), F32), ((HALF, 2 * width), BF)
    quarter = ((QUARTER, 2 * width), BF)
    inner_lat, lon_piece = call(
        pack_kernel, [half, quarter], own_fields, own_grads, pick_inner, pick_lon, name="pack", flops=LOAD
    )
    outer_lat, diag_piece, outer_own, inner_own = call(
        pack_rest_kernel, [quarter, quarter, whole, whole],
        lon_piece, own_fields, own_grads, pick_outer, pick_diag, pick_outer_own, pick_own,
        name="pack_rest", flops=5 * 10**8, unread=(0,),
    )
    own_parts = call(
        own_kernel, [((HALF, lanes), F32) for lanes in (width, 3 * width, width)],
        inner_own, qkv_weight, proj_weight,
        name="own", flops=5 * 10**8,
    )
    inner_in = lax.ppermute(inner_lat, both, lat_route)
    lon_in = lax.ppermute(lon_piece, both, lon_route)
    outer_in = lax.ppermute(outer_lat, both, lat_route)
    diag_in = lax.ppermute(diag_piece, both, diag_route)

    split = (lat_size, width // 2, 4 * width // lat_size)
    halves = ((lat_size // 2, *split[1:]), BF)
    widths = chunk_widths(split[2])
    chunks = [((lat_size // 2, split[1], lanes), BF) for lanes in widths]
    per_window = [
        ((WIN, width), BF),
        ((WIN, width), BF),
        ((2, width // 2, WIN), BF),
        ((WIN, 4 * width), BF),
        ((2, width // 2, WIN), BF),
    ]
    scratch = [pltpu.VMEM((width, WIN), BF)] * 2
    grad_so_far, *inner = call(
        inner_kernel, [(halves[0], F32), *per_window], inner_own, *own_parts, inner_in, qkv_weight, proj_weight,
        name="inner", flops=10**9, scratch=scratch,
    )
    outer = call(
        outer_kernel, [*chunks, *per_window],
        outer_own, lon_in, outer_in, diag_in, qkv_weight, proj_weight, grad_so_far,
        name="outer", flops=10**9, scratch=scratch,
    )
    sibling = [(j, j ^ 1) for j in range(lon_size)]
    first, outer = outer[: len(widths)], outer[len(widths) :]
    arrived = [lax.ppermute(send, "lon", sibling) for send in first]
    keep = call(keep_kernel, chunks, *inner[2:4], *outer[2:4], name="keep", flops=10**9)

    def halving(phase, send):
        route = [
            (i * lon_size + j, (i ^ (1 << (phase if j % 2 == 0 else bits - 1 - phase))) * lon_size + j)
            for i in range(lat_size)
            for j in range(lon_size)
        ]
        return lax.ppermute(send, both, route)

    bits = lat_size.bit_length() - 1
    sends = [keep[0]]
    for part, mine, theirs in zip(chunks, keep, arrived):
        sends += call(next_sum_kernel, [part], sends[-1], mine, theirs, name="chip_sum", unread=(0,))
    sends = sends[1:]
    received = [halving(0, send) for send in sends]
    send_rest, keep_rest = call(
        functools.partial(rest_kernel, len(sends)), [halves, halves], *sends, *inner[2:], *outer[2:],
        name="rest", unread=range(len(sends)), beside=True,
    )
    received_rest = lax.ppermute(send_rest, "lon", sibling)
    results = call(
        output_kernel, [((WIN, 2 * width), BF)] * 2,
        keep_rest, *inner[:2], inner[3], *outer[:2], outer[3], qkv_weight, proj_weight,
        name="outputs", unread=(0,), flops=10**10,
    )
    (lon_back,) = call(pack_lon_kernel, [quarter], results[1], name="pack_lon", beside=True)
    lon_home = lax.ppermute(lon_back, both, back(lon_route))
    kept = [[keep_rest, received_rest, part] for part in received]
    slots = lat_size // 2
    for phase in range(1, bits):
        slots //= 2
        after = sends[-1]
        for index, lanes in enumerate(widths):
            stay = ((slots, split[1], lanes), BF)
            send, keep = call(
                functools.partial(halve_kernel, sum(widths[:index])), [stay, stay], lon_home if index == len(widths) - 1 else after, *kept[index],
                name=f"halve{slots}", unread=(0,),
            )
            kept[index] = [keep, halving(phase, send)]
            after = send

    rows = width // lon_size
    share = ((rows, split[2]), BF)
    parts = call(
        functools.partial(line_parts_kernel, [len(parts) for parts in kept]), [share] * (lon_size // 2),
        *sum(kept, []), name="line_parts",
    )
    arrived = [
        lax.ppermute(parts[step], "lon", [(j, j ^ (2 * step)) for j in range(lon_size)])
        for step in range(lon_size // 2 - 1, 0, -1)
    ]
    lat_back, diag_back = call(
        pack_back_kernel, [((HALF + QUARTER, 2 * width), BF), quarter],
        parts[1], *results,
        name="pack_back", unread=(0,),
    )
    lat_home = lax.ppermute(lat_back, both, back(lat_route))
    diag_home = lax.ppermute(diag_back, both, back(diag_route))
    (line_sum,) = call(sum_kernel, [share], parts[0], *arrived, name="line_sum", flops=LONG)
    shared = [
        lax.ppermute(line_sum, "lat", [(i, i ^ step) for i in range(lat_size)]) for step in range(1, lat_size)
    ]
    (placed,) = call(
        place_kernel, [((TOKENS, 2 * width), F32)], *results, lat_home, name="place"
    )
    field_out, d_fields, done = call(
        place_rest_kernel,
        [((TOKENS, width), BF), ((TOKENS, width), BF), ((8, LANES), F32)],
        placed, lon_home, diag_home,
        name="place_rest",
    )
    qkv_grad, proj_grad = call(
        finish_kernel,
        [((rows, 3 * width), F32), ((rows, width), F32)],
        done, line_sum, *shared,
        name="finish", unread=(0,),
    )
    return (field_out.reshape(fields.shape), d_fields.reshape(fields.shape), qkv_grad, jnp.transpose(proj_grad))


def solution(mesh):
    placed = (P(None, "lat", "lon", None), P(None, "lat", "lon", None), P(), P())
    return jax.shard_map(
        per_device,
        mesh=mesh,
        in_specs=placed,
        out_specs=(
            P(None, "lat", "lon", None),
            P(None, "lat", "lon", None),
            P("lon", None),
            P(None, "lon"),
        ),
        check_vma=False,
    )
```

```python
import functools

import jax
import jax.numpy as jnp
from jax import lax
from jax.experimental import pallas as pl
from jax.experimental.pallas import tpu as pltpu
from jax.sharding import PartitionSpec as P

HEADS = 8
WIN_LAT = 6
WIN_LON = 12
LEVELS = 2
COLS = 24
HALF_LAT = WIN_LAT // 2
HALF_LON = WIN_LON // 2
HALF = LEVELS * HALF_LAT * WIN_LON
WIN = 2 * HALF
TOKENS = 2 * WIN
QUARTER = HALF // 2
LANES = 128

epsilon = 1e-05
LONG = 8 * 10**8
LOAD = 5 * 10**9
LATER = 10**9
BF = jnp.bfloat16
F32 = jnp.float32


def dot(a, b, dims):
    return lax.dot_general(a, b, (dims, ((), ())), preferred_element_type=F32)


NN = ((1,), (0,))
NT = ((1,), (1,))
TN = ((0,), (0,))


def div(x, by):
    return (x * ((65536 + by - 1) // by)) >> 16


def own_token(level, row, col):
    return level * (WIN_LAT * COLS) + row * COLS + col


def inner_token(v, first):
    level = div(v, HALF_LAT * WIN_LON)
    rest = v - level * (HALF_LAT * WIN_LON)
    row = div(rest, WIN_LON)
    return own_token(level, first + row, HALF_LON + rest - row * WIN_LON)


def half_token(v, first, col):
    level = div(v, HALF_LAT * HALF_LON)
    rest = v - level * (HALF_LAT * HALF_LON)
    row = div(rest, HALF_LON)
    return jnp.where(v < QUARTER, own_token(level, first + row, col + rest - row * HALF_LON), -1)


def sources():
    even = lax.rem(lax.axis_index("lon"), 2) == 0
    sent = jnp.where(even, 0, HALF_LAT)
    kept = HALF_LAT - sent
    outer = HALF_LON + WIN_LON
    return (
        (lambda v: inner_token(v, sent), HALF),
        (lambda v: half_token(v, sent, outer), QUARTER),
        (lambda v: half_token(v, sent, 0), QUARTER),
        (lambda v: half_token(v, kept, 0), QUARTER),
        (lambda v: inner_token(v, kept), HALF),
        (lambda v: half_token(v, kept, outer), HALF),
    )


def picks(source, rows, columns):
    index = source(lax.broadcasted_iota(jnp.int32, (rows, 1), 0))
    return (index == lax.broadcasted_iota(jnp.int32, (rows, columns), 1)).astype(BF)


def puts(source, rows, columns):
    index = source(lax.broadcasted_iota(jnp.int32, (1, columns), 1))
    return (lax.broadcasted_iota(jnp.int32, (rows, columns), 0) == index).astype(BF)


def first_rows(v):
    return v


def last_rows(v):
    return v - QUARTER


def order_kernel(*outs):
    for out, (source, rows) in zip(outs, sources()):
        out[...] = picks(source, rows, TOKENS)


def pack_kernel(fields, cotangent, *refs):
    count = len(refs) // 2
    width = fields.shape[1]
    for pick, out in zip(refs[:count], refs[count:]):
        out[:, :width] = dot(pick[...], fields[...], NN).astype(out.dtype)
        out[:, width:] = dot(pick[...], cotangent[...], NN).astype(out.dtype)


def swap_bits(index, size, core):
    bits = size.bit_length() - 1
    turned = sum(((index >> b) & 1) << (bits - 1 - b) for b in range(bits))
    return jnp.where(core == 0, index, turned)


def shares(transposed, out, lon, core_of, lon_size):
    rows = transposed.shape[0] // lon_size
    chip = lon >> 1
    for step in range(lon_size // 2):
        start = pl.multiple_of(((chip ^ step) * 2 + core_of) * rows, rows)
        out[step * rows : (step + 1) * rows, :] = transposed[pl.ds(start, rows), :]


def transpose_bf16(block):
    return jnp.transpose(block.astype(F32)).astype(BF)


def slot_product(slot, size, lat, core, windows):
    share = lat ^ swap_bits(slot, size, core)
    total = None
    for left, right in windows:
        lanes = right.shape[1] // size
        of_proj = (share >= 3 * size // 4).astype(jnp.int32)
        part = dot(left[of_proj], right[:, pl.ds(pl.multiple_of(share * lanes, lanes), lanes)], NN)
        total = part if total is None else total + part
    return total


def normalise(x):
    mean = jnp.mean(x, -1, keepdims=True)
    centred = x - mean
    variance = jnp.mean(centred * centred, -1, keepdims=True)
    inv_std = lax.rsqrt(variance + epsilon)
    return centred * inv_std, inv_std


def project(both, qkv_weight, proj_weight):
    width = both.shape[1] // 2
    normed, _ = normalise(both[:, :width])
    projected = dot(normed.astype(BF), qkv_weight[...], NN)
    return normed, projected, dot(both[:, width:].astype(BF), proj_weight[...], NT)


def pack_rest_kernel(_, *refs):
    pack_kernel(*refs)


def own_kernel(inner_own, qkv_weight, proj_weight, normed, projected, d_mixed):
    normed[...], projected[...], d_mixed[...] = project(inner_own[...], qkv_weight, proj_weight)


def inner_kernel(own, own_normed, own_projected, own_d_mixed, lat_in, qkv_weight, proj_weight, send_grad, *refs):
    arrived = lat_in[...].astype(F32)
    parts = project(arrived, qkv_weight, proj_weight)
    both = jnp.concatenate([own[...], arrived], axis=0)
    mine = own_normed, own_projected, own_d_mixed
    parts = [jnp.concatenate([first[...], second], axis=0) for first, second in zip(mine, parts)]
    one_window(both, *parts, *refs)
    *_, right, left, _, _ = refs
    lat, core, size = place()
    for slot in range(1, size, 2):
        send_grad[slot // 2] = slot_product(slot, size, lat, 1 - core, [(left, right)])


def outer_kernel(own, lon_in, lat_in, diag_in, qkv_weight, proj_weight, grad_so_far, *refs):
    count = len(chunk_widths(proj_weight.shape[0] * 4 // lax.axis_size("lat")))
    sends, refs = refs[:count], refs[count:]
    last = picks(last_rows, HALF, QUARTER)
    both = jnp.concatenate(
        [
            own[...] + dot(last, lon_in[...], NN),
            dot(picks(first_rows, HALF, QUARTER), lat_in[...], NN) + dot(last, diag_in[...], NN),
        ],
        axis=0,
    )
    one_window(both, *project(both, qkv_weight, proj_weight), *refs)
    *_, right, left, _, _ = refs
    lat, core, size = place()
    for slot in range(1, size, 2):
        total = grad_so_far[slot // 2] + slot_product(slot, size, lat, 1 - core, [(left, right)])
        put_chunks(sends, slot // 2, total)


def chunk_widths(lanes):
    return (lanes // 2, lanes // 4, lanes // 4) if lanes % 512 == 0 else (lanes // 2,) * 2


def put_chunks(outs, slot, total):
    at = 0
    for out in outs:
        out[slot] = total[:, at : at + out.shape[2]].astype(BF)
        at += out.shape[2]


def place():
    return lax.axis_index("lat"), lax.rem(lax.axis_index("lon"), 2), lax.axis_size("lat")


def one_window(
    both, normed, projected, d_mixed,
    windows_out, grads_out, left_keep, right, left_send, normed_t, grads_t,
):
    width = both.shape[1] // 2
    lat, core, lat_size = place()
    lon, lon_size = lax.axis_index("lon"), lax.axis_size("lon")
    even = core == 0
    blocks = both[:, :width], both[:, width:]
    x = blocks[0]
    windows_out[...] = x.astype(BF)
    grads = blocks[1].astype(BF)
    grads_out[...] = grads
    projected, d_mixed = projected.astype(BF), d_mixed.astype(BF)

    head_size = width // HEADS
    factor = head_size ** (-0.5)
    apart = jnp.where(even, lat == lat_size - 1, lat == 0).astype(jnp.int32)
    half_b = (lax.broadcasted_iota(jnp.int32, (WIN, 2 * WIN), 0) >= HALF).astype(jnp.int32)
    at_a = lax.broadcasted_iota(jnp.int32, (WIN, 2 * WIN), 1)
    at_a = jnp.where(at_a >= WIN, at_a - WIN, at_a)
    half_a = (at_a >= HALF).astype(jnp.int32)
    allowed = ((half_a != half_b).astype(jnp.int32) * apart) == 0
    first_head = lax.broadcasted_iota(jnp.int32, (WIN, LANES), 1) < head_size
    zero = jnp.zeros((WIN, LANES), BF)

    def split_heads(block):
        return jnp.concatenate([jnp.where(first_head, block, zero), jnp.where(first_head, zero, block)], axis=0)

    def join_heads(block):
        return jnp.where(first_head, block[:WIN], block[WIN:]).astype(BF)

    pairs = range(width // LANES)

    def blocks_of(array, lanes_from):
        return [array[:, lanes_from + pair * LANES : lanes_from + (pair + 1) * LANES] for pair in pairs]

    def store(out, lanes_from, blocks):
        for pair, block in zip(pairs, blocks):
            out[:, lanes_from + pair * LANES : lanes_from + (pair + 1) * LANES] = block.astype(out.dtype)

    k, v = blocks_of(projected, width), blocks_of(projected, 2 * width)
    q2 = [split_heads(block) for block in blocks_of(projected, 0)]
    dm2 = [split_heads(block) for block in blocks_of(d_mixed, 0)]
    scores = [jnp.where(allowed, dot(k[p], q2[p], NT) * factor, -1e30) for p in pairs]
    d_probs = [dot(v[p], dm2[p], NT) for p in pairs]
    exponents = [jnp.exp(s - jnp.max(s, 0, keepdims=True)) for s in scores]
    probs = [e * (1.0 / jnp.sum(e, 0, keepdims=True)) for e in exponents]
    probs_b = [p.astype(BF) for p in probs]
    store(right, 3 * width, [join_heads(dot(probs_b[p], v[p], TN)) for p in pairs])
    store(right, 2 * width, [dot(probs_b[p], dm2[p], NN) for p in pairs])
    d_scores = [
        (probs[p] * (d_probs[p] - jnp.sum(d_probs[p] * probs[p], 0, keepdims=True)) * factor).astype(BF)
        for p in pairs
    ]
    store(right, 0, [join_heads(dot(d_scores[p], k[p], TN)) for p in pairs])
    store(right, width, [dot(d_scores[p], q2[p], NN) for p in pairs])

    normed_t[...] = transpose_bf16(normed)
    grads_t[...] = transpose_bf16(grads)
    for index, source in enumerate((normed_t, grads_t)):
        shares(source, left_send.at[index], lon, 1 - core, lon_size)
        shares(source, left_keep.at[index], lon, core, lon_size)


def keep_kernel(*refs):
    windows, keeps = [refs[:2], refs[2:4]], refs[4:]
    lat, core, size = place()
    for slot in range(1, size, 2):
        put_chunks(keeps, slot // 2, slot_product(slot, size, lat, core, windows))


def rest_kernel(count, *refs):
    *windows, send_rest, keep_rest = refs[count:]
    windows = windows[:3], windows[3:]
    lat, core, size = place()
    for slot in range(0, size, 2):
        send_rest[slot // 2] = slot_product(slot, size, lat, 1 - core, [(w[2], w[1]) for w in windows]).astype(BF)
    for slot in range(0, size, 2):
        keep_rest[slot // 2] = slot_product(slot, size, lat, core, [(w[0], w[1]) for w in windows]).astype(BF)


def output_kernel(_, *refs):
    (*windows, qkv_weight, proj_weight, inner_results, outer_results) = refs
    per_window = windows[:3], windows[3:]
    width = proj_weight.shape[0]
    x, grads, right = (jnp.concatenate([w[i][...] for w in per_window], axis=0) for i in range(3))
    d_projected, mixed = right[:, : 3 * width], right[:, 3 * width :]
    x = x.astype(F32)
    normed, inv_std = normalise(x)
    output = (x + dot(mixed, proj_weight[...], NN)).astype(BF)
    d_normed = dot(d_projected, qkv_weight[...], NT)
    d_inputs = grads.astype(F32) + inv_std * (
        d_normed
        - jnp.mean(d_normed, -1, keepdims=True)
        - normed * jnp.mean(d_normed * normed, -1, keepdims=True)
    )
    d_inputs = d_inputs.astype(BF)
    for at, out in ((0, inner_results), (WIN, outer_results)):
        out[:, :width] = output[at : at + WIN]
        out[:, width:] = d_inputs[at : at + WIN]


def pack_lon_kernel(outer_results, lon_out):
    outer_x = outer_results[...].astype(F32)[:HALF].astype(BF)
    lon_out[...] = dot(puts(last_rows, QUARTER, HALF), outer_x, NN).astype(BF)


def pack_back_kernel(_, inner_results, outer_results, lat_out, diag_out):
    inner_y = inner_results[...].astype(F32)[HALF:]
    outer_y = outer_results[...].astype(F32)[HALF:].astype(BF)
    lat_out[...] = jnp.concatenate([inner_y, dot(puts(first_rows, QUARTER, HALF), outer_y, NN)], axis=0).astype(BF)
    diag_out[...] = dot(puts(last_rows, QUARTER, HALF), outer_y, NN).astype(BF)


def place_kernel(inner_results, outer_results, lat_in, placed):
    inner_lat, outer_lat, _, _, inner_own, outer_own = (source for source, _ in sources())

    def lat(v):
        return jnp.where(v < HALF, inner_lat(v), outer_lat(v - HALF))

    def only_first(source):
        return lambda v: jnp.where(v < HALF, source(v), -1)

    placed[...] = (
        dot(puts(only_first(inner_own), TOKENS, WIN), inner_results[...], NN)
        + dot(puts(only_first(outer_own), TOKENS, WIN), outer_results[...], NN)
        + dot(puts(lat, TOKENS, HALF + QUARTER), lat_in[...], NN)
    )


def place_rest_kernel(placed, lon_in, diag_in, field_out, d_fields, done):
    done[...] = jnp.zeros_like(done)
    width = field_out.shape[1]
    _, _, lon, diag, _, _ = (source for source, _ in sources())
    total = (
        placed[...]
        + dot(puts(lon, TOKENS, QUARTER), lon_in[...], NN)
        + dot(puts(diag, TOKENS, QUARTER), diag_in[...], NN)
    ).astype(BF)
    field_out[...] = total[:, :width]
    d_fields[...] = total[:, width:]


def halve_kernel(first_lane, _, *refs):
    *parts, send, keep = refs
    width = send.shape[2]

    def lanes(part):
        return slice(None) if part.shape[2] == width else slice(first_lane, first_lane + width)

    for slot in range(send.shape[0]):
        for out, source in ((send, 2 * slot + 1), (keep, 2 * slot)):
            out[slot] = sum(part[source, :, lanes(part)].astype(F32) for part in parts).astype(BF)


def line_parts_kernel(counts, first_step, after, *refs):
    chunks, refs = [], refs[after:]
    for count in counts:
        chunks.append(refs[:count])
        refs = refs[count:]
    rows = refs[0].shape[0]
    for step, out in enumerate(refs, first_step):
        at = slice(step * rows, (step + 1) * rows)
        totals = [sum(part[0, at].astype(F32) for part in parts) for parts in chunks]
        out[...] = jnp.concatenate(totals, axis=1).astype(out.dtype)


def sum_kernel(*refs):
    *parts, out = refs
    total = parts[0][...].astype(F32)
    for part in parts[1:]:
        total = total + part[...].astype(F32)
    out[...] = total.astype(out.dtype)


def next_sum_kernel(_, *refs):
    sum_kernel(*refs)


def finish_kernel(_, *refs):
    *parts, qkv_out, proj_out = refs
    lat, _, size = place()
    width = parts[0].shape[1]
    for step, part in enumerate(parts):
        share = lat ^ step
        total = part[...].astype(F32)
        of_qkv = 3 * size // 4

        @pl.when(share < of_qkv)
        def _():
            qkv_out[:, pl.ds(pl.multiple_of(share * width, width), width)] = total

        @pl.when(share >= of_qkv)
        def _():
            proj_out[:, pl.ds(pl.multiple_of((share - of_qkv) * width, width), width)] = total


def call(kernel, outs, *args, name, flops=0, limit=32, scratch=(), unread=(), beside=False):
    vmem = pl.BlockSpec(memory_space=pltpu.VMEM)
    anywhere = pl.BlockSpec(memory_space=pl.ANY)
    shapes = [jax.ShapeDtypeStruct(shape, dtype) for shape, dtype in outs]
    nbytes = 0 if beside else sum(a.size * a.dtype.itemsize for a in (*args, *shapes))
    return pl.pallas_call(
        kernel,
        out_shape=shapes,
        in_specs=[anywhere if i in unread else vmem for i in range(len(args))],
        out_specs=[vmem] * len(shapes),
        scratch_shapes=scratch,
        compiler_params=pltpu.CompilerParams(vmem_limit_bytes=limit * 2**20),
        cost_estimate=pl.CostEstimate(flops=flops, bytes_accessed=nbytes, transcendentals=0),
        name=name,
    )(*args)


def routes(lat_size, lon_size):
    lat, lon, diag = [], [], []
    for i in range(lat_size):
        for j in range(lon_size):
            step = -1 if j % 2 == 0 else 1
            before = (j - 1) % lon_size
            me = i * lon_size + j
            lat.append((me, ((i + step) % lat_size) * lon_size + j))
            lon.append((me, i * lon_size + before))
            diag.append((me, ((i - step) % lat_size) * lon_size + before))
    return lat, lon, diag


def per_device(fields, cotangent, qkv_weight, proj_weight):
    levels, row_count, col_count, width = fields.shape
    lat_size, lon_size = lax.axis_size("lat"), lax.axis_size("lon")
    both = ("lat", "lon")
    lat_route, lon_route, diag_route = routes(lat_size, lon_size)

    def back(route):
        return [(target, source) for source, target in route]

    own_fields = fields.reshape(TOKENS, width)
    own_grads = cotangent.reshape(TOKENS, width)
    lengths = (HALF, QUARTER, QUARTER, QUARTER, HALF, HALF)
    picked = call(order_kernel, [((rows, TOKENS), BF) for rows in lengths], name="order", flops=LOAD)
    pick_inner, pick_outer, pick_lon, pick_diag, pick_own, pick_outer_own = picked
    whole, half = ((HALF, 2 * width), F32), ((HALF, 2 * width), BF)
    quarter = ((QUARTER, 2 * width), BF)
    inner_lat, lon_piece = call(
        pack_kernel, [half, quarter], own_fields, own_grads, pick_inner, pick_lon, name="pack", flops=LOAD
    )
    outer_lat, diag_piece, outer_own, inner_own = call(
        pack_rest_kernel, [quarter, quarter, whole, whole],
        lon_piece, own_fields, own_grads, pick_outer, pick_diag, pick_outer_own, pick_own,
        name="pack_rest", flops=5 * 10**8, unread=(0,),
    )
    own_parts = call(
        own_kernel, [((HALF, lanes), F32) for lanes in (width, 3 * width, width)],
        inner_own, qkv_weight, proj_weight,
        name="own", flops=5 * 10**8,
    )
    inner_in = lax.ppermute(inner_lat, both, lat_route)
    lon_in = lax.ppermute(lon_piece, both, lon_route)
    outer_in = lax.ppermute(outer_lat, both, lat_route)
    diag_in = lax.ppermute(diag_piece, both, diag_route)

    split = (lat_size, width // 2, 4 * width // lat_size)
    halves = ((lat_size // 2, *split[1:]), BF)
    widths = chunk_widths(split[2])
    chunks = [((lat_size // 2, split[1], lanes), BF) for lanes in widths]
    per_window = [
        ((WIN, width), BF),
        ((WIN, width), BF),
        ((2, width // 2, WIN), BF),
        ((WIN, 4 * width), BF),
        ((2, width // 2, WIN), BF),
    ]
    scratch = [pltpu.VMEM((width, WIN), BF)] * 2
    grad_so_far, *inner = call(
        inner_kernel, [(halves[0], F32), *per_window], inner_own, *own_parts, inner_in, qkv_weight, proj_weight,
        name="inner", flops=10**9, scratch=scratch,
    )
    outer = call(
        outer_kernel, [*chunks, *per_window],
        outer_own, lon_in, outer_in, diag_in, qkv_weight, proj_weight, grad_so_far,
        name="outer", flops=10**9, scratch=scratch,
    )
    sibling = [(j, j ^ 1) for j in range(lon_size)]
    first, outer = outer[: len(widths)], outer[len(widths) :]
    arrived = [lax.ppermute(send, "lon", sibling) for send in first]
    keep = call(keep_kernel, chunks, *inner[2:4], *outer[2:4], name="keep", flops=10**9)

    def halving(phase, send):
        route = [
            (i * lon_size + j, (i ^ (1 << (phase if j % 2 == 0 else bits - 1 - phase))) * lon_size + j)
            for i in range(lat_size)
            for j in range(lon_size)
        ]
        return lax.ppermute(send, both, route)

    bits = lat_size.bit_length() - 1
    sends = [keep[0]]
    for part, mine, theirs in zip(chunks, keep, arrived):
        sends += call(next_sum_kernel, [part], sends[-1], mine, theirs, name="chip_sum", unread=(0,))
    sends = sends[1:]
    received = [halving(0, send) for send in sends]
    send_rest, keep_rest = call(
        functools.partial(rest_kernel, len(sends)), [halves, halves], *sends, *inner[2:], *outer[2:],
        name="rest", unread=range(len(sends)), beside=True,
    )
    received_rest = lax.ppermute(send_rest, "lon", sibling)
    results = call(
        output_kernel, [((WIN, 2 * width), BF)] * 2,
        keep_rest, *inner[:2], inner[3], *outer[:2], outer[3], qkv_weight, proj_weight,
        name="outputs", unread=(0,), flops=10**10,
    )
    (lon_back,) = call(pack_lon_kernel, [quarter], results[1], name="pack_lon", beside=True)
    lon_home = lax.ppermute(lon_back, both, back(lon_route))
    kept = [[keep_rest, received_rest, part] for part in received]
    slots = lat_size // 2
    for phase in range(1, bits):
        slots //= 2
        after = sends[-1]
        for index, lanes in enumerate(widths):
            stay = ((slots, split[1], lanes), BF)
            send, keep = call(
                functools.partial(halve_kernel, sum(widths[:index])), [stay, stay], lon_home if index == len(widths) - 1 else after, *kept[index],
                name=f"halve{slots}", unread=(0,),
            )
            kept[index] = [keep, halving(phase, send)]
            after = send

    rows = width // lon_size
    share = ((rows, split[2]), BF)
    counts, chips = [len(parts) for parts in kept], lon_size // 2

    def line_parts(first, last, *after):
        return call(
            functools.partial(line_parts_kernel, counts, first, len(after)), [share] * (last - first),
            *after, *sum(kept, []), name="line_parts", unread=range(len(after)),
        )

    def along(part, step):
        return lax.ppermute(part, "lon", [(j, j ^ (2 * step)) for j in range(lon_size)])

    (farthest,) = line_parts(chips - 1, chips)
    arrived = [along(farthest, chips - 1)]
    lat_back, diag_back = call(
        pack_back_kernel, [((HALF + QUARTER, 2 * width), BF), quarter],
        farthest, *results,
        name="pack_back", unread=(0,),
    )
    lat_home = lax.ppermute(lat_back, both, back(lat_route))
    diag_home = lax.ppermute(diag_back, both, back(diag_route))
    parts = line_parts(0, chips - 1, lat_back)
    arrived += [along(parts[step], step) for step in range(chips - 2, 0, -1)]
    (far_sum,) = call(sum_kernel, [((rows, split[2]), F32)], parts[0], arrived[0], name="far_sum", flops=LATER)
    (line_sum,) = call(sum_kernel, [share], far_sum, *arrived[1:], name="line_sum", flops=LONG)
    shared = [
        lax.ppermute(line_sum, "lat", [(i, i ^ step) for i in range(lat_size)]) for step in range(1, lat_size)
    ]
    (placed,) = call(
        place_kernel, [((TOKENS, 2 * width), F32)], *results, lat_home, name="place"
    )
    field_out, d_fields, done = call(
        place_rest_kernel,
        [((TOKENS, width), BF), ((TOKENS, width), BF), ((8, LANES), F32)],
        placed, lon_home, diag_home,
        name="place_rest",
    )
    qkv_grad, proj_grad = call(
        finish_kernel,
        [((rows, 3 * width), F32), ((rows, width), F32)],
        done, line_sum, *shared,
        name="finish", unread=(0,),
    )
    return (field_out.reshape(fields.shape), d_fields.reshape(fields.shape), qkv_grad, jnp.transpose(proj_grad))


def solution(mesh):
    placed = (P(None, "lat", "lon", None), P(None, "lat", "lon", None), P(), P())
    return jax.shard_map(
        per_device,
        mesh=mesh,
        in_specs=placed,
        out_specs=(
            P(None, "lat", "lon", None),
            P(None, "lat", "lon", None),
            P("lon", None),
            P(None, "lon"),
        ),
        check_vma=False,
    )
```

```python
import functools

import jax
import jax.numpy as jnp
from jax import lax
from jax.experimental import pallas as pl
from jax.experimental.pallas import tpu as pltpu
from jax.sharding import PartitionSpec as P

HEADS = 8
WIN_LAT = 6
WIN_LON = 12
LEVELS = 2
COLS = 24
HALF_LAT = WIN_LAT // 2
HALF_LON = WIN_LON // 2
HALF = LEVELS * HALF_LAT * WIN_LON
WIN = 2 * HALF
TOKENS = 2 * WIN
QUARTER = HALF // 2
LANES = 128

epsilon = 1e-05
LONG = 13 * 10**8
LOAD = 5 * 10**9
PARTS = 5 * 10**9
BF = jnp.bfloat16
F32 = jnp.float32


def dot(a, b, dims):
    return lax.dot_general(a, b, (dims, ((), ())), preferred_element_type=F32)


NN = ((1,), (0,))
NT = ((1,), (1,))
TN = ((0,), (0,))


def div(x, by):
    return (x * ((65536 + by - 1) // by)) >> 16


def own_token(level, row, col):
    return level * (WIN_LAT * COLS) + row * COLS + col


def inner_token(v, first):
    level = div(v, HALF_LAT * WIN_LON)
    rest = v - level * (HALF_LAT * WIN_LON)
    row = div(rest, WIN_LON)
    return own_token(level, first + row, HALF_LON + rest - row * WIN_LON)


def half_token(v, first, col):
    level = div(v, HALF_LAT * HALF_LON)
    rest = v - level * (HALF_LAT * HALF_LON)
    row = div(rest, HALF_LON)
    return jnp.where(v < QUARTER, own_token(level, first + row, col + rest - row * HALF_LON), -1)


def sources():
    even = lax.rem(lax.axis_index("lon"), 2) == 0
    sent = jnp.where(even, 0, HALF_LAT)
    kept = HALF_LAT - sent
    outer = HALF_LON + WIN_LON
    return (
        (lambda v: inner_token(v, sent), HALF),
        (lambda v: half_token(v, sent, outer), QUARTER),
        (lambda v: half_token(v, sent, 0), QUARTER),
        (lambda v: half_token(v, kept, 0), QUARTER),
        (lambda v: inner_token(v, kept), HALF),
        (lambda v: half_token(v, kept, outer), HALF),
    )


def picks(source, rows, columns):
    index = source(lax.broadcasted_iota(jnp.int32, (rows, 1), 0))
    return (index == lax.broadcasted_iota(jnp.int32, (rows, columns), 1)).astype(BF)


def puts(source, rows, columns):
    index = source(lax.broadcasted_iota(jnp.int32, (1, columns), 1))
    return (lax.broadcasted_iota(jnp.int32, (rows, columns), 0) == index).astype(BF)


def first_rows(v):
    return v


def last_rows(v):
    return v - QUARTER


def order_kernel(*outs):
    for out, (source, rows) in zip(outs, sources()):
        out[...] = picks(source, rows, TOKENS)


def pack_kernel(fields, cotangent, *refs):
    count = len(refs) // 2
    width = fields.shape[1]
    for pick, out in zip(refs[:count], refs[count:]):
        out[:, :width] = dot(pick[...], fields[...], NN).astype(out.dtype)
        out[:, width:] = dot(pick[...], cotangent[...], NN).astype(out.dtype)


def swap_bits(index, size, core):
    bits = size.bit_length() - 1
    turned = sum(((index >> b) & 1) << (bits - 1 - b) for b in range(bits))
    return jnp.where(core == 0, index, turned)


def shares(transposed, out, lon, core_of, lon_size):
    rows = transposed.shape[0] // lon_size
    chip = lon >> 1
    for step in range(lon_size // 2):
        start = pl.multiple_of(((chip ^ step) * 2 + core_of) * rows, rows)
        out[step * rows : (step + 1) * rows, :] = transposed[pl.ds(start, rows), :]


def transpose_bf16(block):
    return jnp.transpose(block.astype(F32)).astype(BF)


def slot_product(slot, size, lat, core, windows):
    share = lat ^ swap_bits(slot, size, core)
    total = None
    for left, right in windows:
        lanes = right.shape[1] // size
        of_proj = (share >= 3 * size // 4).astype(jnp.int32)
        part = dot(left[of_proj], right[:, pl.ds(pl.multiple_of(share * lanes, lanes), lanes)], NN)
        total = part if total is None else total + part
    return total


def normalise(x):
    mean = jnp.mean(x, -1, keepdims=True)
    centred = x - mean
    variance = jnp.mean(centred * centred, -1, keepdims=True)
    inv_std = lax.rsqrt(variance + epsilon)
    return centred * inv_std, inv_std


def project(both, qkv_weight, proj_weight):
    width = both.shape[1] // 2
    normed, _ = normalise(both[:, :width])
    projected = dot(normed.astype(BF), qkv_weight[...], NN)
    return normed, projected, dot(both[:, width:].astype(BF), proj_weight[...], NT)


def pack_rest_kernel(_, *refs):
    pack_kernel(*refs)


def own_kernel(inner_own, qkv_weight, proj_weight, normed, projected, d_mixed):
    normed[...], projected[...], d_mixed[...] = project(inner_own[...], qkv_weight, proj_weight)


def inner_kernel(own, own_normed, own_projected, own_d_mixed, lat_in, qkv_weight, proj_weight, send_grad, *refs):
    arrived = lat_in[...].astype(F32)
    parts = project(arrived, qkv_weight, proj_weight)
    both = jnp.concatenate([own[...], arrived], axis=0)
    mine = own_normed, own_projected, own_d_mixed
    parts = [jnp.concatenate([first[...], second], axis=0) for first, second in zip(mine, parts)]
    one_window(both, *parts, *refs)
    *_, right, left, _, _ = refs
    lat, core, size = place()
    for slot in range(1, size, 2):
        send_grad[slot // 2] = slot_product(slot, size, lat, 1 - core, [(left, right)])


def outer_kernel(own, lon_in, lat_in, diag_in, qkv_weight, proj_weight, grad_so_far, send_a, send_b, *refs):
    last = picks(last_rows, HALF, QUARTER)
    both = jnp.concatenate(
        [
            own[...] + dot(last, lon_in[...], NN),
            dot(picks(first_rows, HALF, QUARTER), lat_in[...], NN) + dot(last, diag_in[...], NN),
        ],
        axis=0,
    )
    one_window(both, *project(both, qkv_weight, proj_weight), *refs)
    *_, right, left, _, _ = refs
    lat, core, size = place()
    for slot in range(1, size, 2):
        total = grad_so_far[slot // 2] + slot_product(slot, size, lat, 1 - core, [(left, right)])
        put_chunks((send_a, send_b), slot // 2, total)


def put_chunks(outs, slot, total):
    width = outs[0].shape[2]
    for chunk, out in enumerate(outs):
        out[slot] = total[:, chunk * width : (chunk + 1) * width].astype(BF)


def place():
    return lax.axis_index("lat"), lax.rem(lax.axis_index("lon"), 2), lax.axis_size("lat")


def one_window(
    both, normed, projected, d_mixed,
    windows_out, grads_out, left_keep, right, left_send, normed_t, grads_t,
):
    width = both.shape[1] // 2
    lat, core, lat_size = place()
    lon, lon_size = lax.axis_index("lon"), lax.axis_size("lon")
    even = core == 0
    blocks = both[:, :width], both[:, width:]
    x = blocks[0]
    windows_out[...] = x.astype(BF)
    grads = blocks[1].astype(BF)
    grads_out[...] = grads
    projected, d_mixed = projected.astype(BF), d_mixed.astype(BF)

    head_size = width // HEADS
    factor = head_size ** (-0.5)
    apart = jnp.where(even, lat == lat_size - 1, lat == 0).astype(jnp.int32)
    half_b = (lax.broadcasted_iota(jnp.int32, (WIN, 2 * WIN), 0) >= HALF).astype(jnp.int32)
    at_a = lax.broadcasted_iota(jnp.int32, (WIN, 2 * WIN), 1)
    at_a = jnp.where(at_a >= WIN, at_a - WIN, at_a)
    half_a = (at_a >= HALF).astype(jnp.int32)
    allowed = ((half_a != half_b).astype(jnp.int32) * apart) == 0
    first_head = lax.broadcasted_iota(jnp.int32, (WIN, LANES), 1) < head_size
    zero = jnp.zeros((WIN, LANES), BF)

    def split_heads(block):
        return jnp.concatenate([jnp.where(first_head, block, zero), jnp.where(first_head, zero, block)], axis=0)

    def join_heads(block):
        return jnp.where(first_head, block[:WIN], block[WIN:]).astype(BF)

    pairs = range(width // LANES)

    def blocks_of(array, lanes_from):
        return [array[:, lanes_from + pair * LANES : lanes_from + (pair + 1) * LANES] for pair in pairs]

    def store(out, lanes_from, blocks):
        for pair, block in zip(pairs, blocks):
            out[:, lanes_from + pair * LANES : lanes_from + (pair + 1) * LANES] = block.astype(out.dtype)

    k, v = blocks_of(projected, width), blocks_of(projected, 2 * width)
    q2 = [split_heads(block) for block in blocks_of(projected, 0)]
    dm2 = [split_heads(block) for block in blocks_of(d_mixed, 0)]
    scores = [jnp.where(allowed, dot(k[p], q2[p], NT) * factor, -1e30) for p in pairs]
    d_probs = [dot(v[p], dm2[p], NT) for p in pairs]
    exponents = [jnp.exp(s - jnp.max(s, 0, keepdims=True)) for s in scores]
    probs = [e * (1.0 / jnp.sum(e, 0, keepdims=True)) for e in exponents]
    probs_b = [p.astype(BF) for p in probs]
    store(right, 3 * width, [join_heads(dot(probs_b[p], v[p], TN)) for p in pairs])
    store(right, 2 * width, [dot(probs_b[p], dm2[p], NN) for p in pairs])
    d_scores = [
        (probs[p] * (d_probs[p] - jnp.sum(d_probs[p] * probs[p], 0, keepdims=True)) * factor).astype(BF)
        for p in pairs
    ]
    store(right, 0, [join_heads(dot(d_scores[p], k[p], TN)) for p in pairs])
    store(right, width, [dot(d_scores[p], q2[p], NN) for p in pairs])

    normed_t[...] = transpose_bf16(normed)
    grads_t[...] = transpose_bf16(grads)
    for index, source in enumerate((normed_t, grads_t)):
        shares(source, left_send.at[index], lon, 1 - core, lon_size)
        shares(source, left_keep.at[index], lon, core, lon_size)


def keep_kernel(*refs):
    *windows, keep_a, keep_b = refs
    windows = [windows[:2], windows[2:]]
    lat, core, size = place()
    for slot in range(1, size, 2):
        put_chunks((keep_a, keep_b), slot // 2, slot_product(slot, size, lat, core, windows))


def rest_kernel(_, __, *refs):
    *windows, send_rest, keep_rest = refs
    windows = windows[:3], windows[3:]
    lat, core, size = place()
    for slot in range(0, size, 2):
        send_rest[slot // 2] = slot_product(slot, size, lat, 1 - core, [(w[2], w[1]) for w in windows]).astype(BF)
    for slot in range(0, size, 2):
        keep_rest[slot // 2] = slot_product(slot, size, lat, core, [(w[0], w[1]) for w in windows]).astype(BF)


def output_kernel(_, *refs):
    (*windows, qkv_weight, proj_weight, inner_results, outer_results) = refs
    per_window = windows[:3], windows[3:]
    width = proj_weight.shape[0]
    x, grads, right = (jnp.concatenate([w[i][...] for w in per_window], axis=0) for i in range(3))
    d_projected, mixed = right[:, : 3 * width], right[:, 3 * width :]
    x = x.astype(F32)
    normed, inv_std = normalise(x)
    output = (x + dot(mixed, proj_weight[...], NN)).astype(BF)
    d_normed = dot(d_projected, qkv_weight[...], NT)
    d_inputs = grads.astype(F32) + inv_std * (
        d_normed
        - jnp.mean(d_normed, -1, keepdims=True)
        - normed * jnp.mean(d_normed * normed, -1, keepdims=True)
    )
    d_inputs = d_inputs.astype(BF)
    for at, out in ((0, inner_results), (WIN, outer_results)):
        out[:, :width] = output[at : at + WIN]
        out[:, width:] = d_inputs[at : at + WIN]


def pack_lon_kernel(outer_results, lon_out):
    outer_x = outer_results[...].astype(F32)[:HALF].astype(BF)
    lon_out[...] = dot(puts(last_rows, QUARTER, HALF), outer_x, NN).astype(BF)


def pack_diag_kernel(_, outer_results, diag_out):
    outer_y = outer_results[...].astype(F32)[HALF:].astype(BF)
    diag_out[...] = dot(puts(last_rows, QUARTER, HALF), outer_y, NN).astype(BF)


def pack_lat_kernel(_, inner_results, outer_results, lat_out):
    inner_y = inner_results[...].astype(F32)[HALF:]
    outer_y = outer_results[...].astype(F32)[HALF:].astype(BF)
    lat_out[...] = jnp.concatenate([inner_y, dot(puts(first_rows, QUARTER, HALF), outer_y, NN)], axis=0).astype(BF)


def place_kernel(inner_results, outer_results, lon_in, diag_in, placed):
    _, _, lon, diag, inner_own, outer_own = (source for source, _ in sources())

    def only_first(source):
        return lambda v: jnp.where(v < HALF, source(v), -1)

    placed[...] = (
        dot(puts(only_first(inner_own), TOKENS, WIN), inner_results[...], NN)
        + dot(puts(only_first(outer_own), TOKENS, WIN), outer_results[...], NN)
        + dot(puts(lon, TOKENS, QUARTER), lon_in[...], NN)
        + dot(puts(diag, TOKENS, QUARTER), diag_in[...], NN)
    )


def place_rest_kernel(placed, lat_in, field_out, d_fields, done):
    done[...] = jnp.zeros_like(done)
    width = field_out.shape[1]
    inner_lat, outer_lat, *_ = (source for source, _ in sources())

    def lat(v):
        return jnp.where(v < HALF, inner_lat(v), outer_lat(v - HALF))

    total = (placed[...] + dot(puts(lat, TOKENS, HALF + QUARTER), lat_in[...], NN)).astype(BF)
    field_out[...] = total[:, :width]
    d_fields[...] = total[:, width:]


def halve_kernel(chunk, _, *refs):
    *parts, send, keep = refs
    width = send.shape[2]

    def lanes(part):
        return slice(None) if part.shape[2] == width else slice(chunk * width, (chunk + 1) * width)

    for slot in range(send.shape[0]):
        for out, source in ((send, 2 * slot + 1), (keep, 2 * slot)):
            out[slot] = sum(part[source, :, lanes(part)].astype(F32) for part in parts).astype(BF)


def line_parts_kernel(count, *refs):
    chunks, (keep, *sends) = (refs[:count], refs[count : 2 * count]), refs[2 * count :]
    rows = keep.shape[0]
    for step, out in enumerate((keep, *sends)):
        at = slice(step * rows, (step + 1) * rows)
        totals = [sum(part[0, at].astype(F32) for part in parts) for parts in chunks]
        out[...] = jnp.concatenate(totals, axis=1).astype(out.dtype)


def line_sum_kernel(_, *refs):
    sum_kernel(*refs)


def sum_kernel(*refs):
    *parts, out = refs
    total = parts[0][...].astype(F32)
    for part in parts[1:]:
        total = total + part[...].astype(F32)
    out[...] = total.astype(out.dtype)


def finish_kernel(_, *refs):
    *parts, qkv_out, proj_out = refs
    lat, _, size = place()
    width = parts[0].shape[1]
    for step, part in enumerate(parts):
        share = lat ^ step
        total = part[...].astype(F32)
        of_qkv = 3 * size // 4

        @pl.when(share < of_qkv)
        def _():
            qkv_out[:, pl.ds(pl.multiple_of(share * width, width), width)] = total

        @pl.when(share >= of_qkv)
        def _():
            proj_out[:, pl.ds(pl.multiple_of((share - of_qkv) * width, width), width)] = total


def call(kernel, outs, *args, name, flops=0, limit=32, scratch=(), unread=(), beside=False):
    vmem = pl.BlockSpec(memory_space=pltpu.VMEM)
    anywhere = pl.BlockSpec(memory_space=pl.ANY)
    shapes = [jax.ShapeDtypeStruct(shape, dtype) for shape, dtype in outs]
    nbytes = 0 if beside else sum(a.size * a.dtype.itemsize for a in (*args, *shapes))
    return pl.pallas_call(
        kernel,
        out_shape=shapes,
        in_specs=[anywhere if i in unread else vmem for i in range(len(args))],
        out_specs=[vmem] * len(shapes),
        scratch_shapes=scratch,
        compiler_params=pltpu.CompilerParams(vmem_limit_bytes=limit * 2**20),
        cost_estimate=pl.CostEstimate(flops=flops, bytes_accessed=nbytes, transcendentals=0),
        name=name,
    )(*args)


def routes(lat_size, lon_size):
    lat, lon, diag = [], [], []
    for i in range(lat_size):
        for j in range(lon_size):
            step = -1 if j % 2 == 0 else 1
            before = (j - 1) % lon_size
            me = i * lon_size + j
            lat.append((me, ((i + step) % lat_size) * lon_size + j))
            lon.append((me, i * lon_size + before))
            diag.append((me, ((i - step) % lat_size) * lon_size + before))
    return lat, lon, diag


def per_device(fields, cotangent, qkv_weight, proj_weight):
    levels, row_count, col_count, width = fields.shape
    lat_size, lon_size = lax.axis_size("lat"), lax.axis_size("lon")
    both = ("lat", "lon")
    lat_route, lon_route, diag_route = routes(lat_size, lon_size)

    def back(route):
        return [(target, source) for source, target in route]

    own_fields = fields.reshape(TOKENS, width)
    own_grads = cotangent.reshape(TOKENS, width)
    lengths = (HALF, QUARTER, QUARTER, QUARTER, HALF, HALF)
    picked = call(order_kernel, [((rows, TOKENS), BF) for rows in lengths], name="order", flops=LOAD)
    pick_inner, pick_outer, pick_lon, pick_diag, pick_own, pick_outer_own = picked
    whole, half = ((HALF, 2 * width), F32), ((HALF, 2 * width), BF)
    quarter = ((QUARTER, 2 * width), BF)
    inner_lat, lon_piece = call(
        pack_kernel, [half, quarter], own_fields, own_grads, pick_inner, pick_lon, name="pack", flops=LOAD
    )
    outer_lat, diag_piece, outer_own, inner_own = call(
        pack_rest_kernel, [quarter, quarter, whole, whole],
        lon_piece, own_fields, own_grads, pick_outer, pick_diag, pick_outer_own, pick_own,
        name="pack_rest", flops=5 * 10**8, unread=(0,),
    )
    own_parts = call(
        own_kernel, [((HALF, lanes), F32) for lanes in (width, 3 * width, width)],
        inner_own, qkv_weight, proj_weight,
        name="own", flops=5 * 10**8,
    )
    inner_in = lax.ppermute(inner_lat, both, lat_route)
    lon_in = lax.ppermute(lon_piece, both, lon_route)
    outer_in = lax.ppermute(outer_lat, both, lat_route)
    diag_in = lax.ppermute(diag_piece, both, diag_route)

    split = (lat_size, width // 2, 4 * width // lat_size)
    halves = ((lat_size // 2, *split[1:]), BF)
    chunk = ((lat_size // 2, split[1], split[2] // 2), BF)
    per_window = [
        ((WIN, width), BF),
        ((WIN, width), BF),
        ((2, width // 2, WIN), BF),
        ((WIN, 4 * width), BF),
        ((2, width // 2, WIN), BF),
    ]
    scratch = [pltpu.VMEM((width, WIN), BF)] * 2
    grad_so_far, *inner = call(
        inner_kernel, [(halves[0], F32), *per_window], inner_own, *own_parts, inner_in, qkv_weight, proj_weight,
        name="inner", flops=10**9, scratch=scratch,
    )
    send_a, send_b, *outer = call(
        outer_kernel, [chunk, chunk, *per_window],
        outer_own, lon_in, outer_in, diag_in, qkv_weight, proj_weight, grad_so_far,
        name="outer", flops=10**9, scratch=scratch,
    )
    sibling = [(j, j ^ 1) for j in range(lon_size)]
    arrived = [lax.ppermute(send, "lon", sibling) for send in (send_a, send_b)]
    keep = call(keep_kernel, [chunk, chunk], *inner[2:4], *outer[2:4], name="keep", flops=10**9)

    def halving(phase, send):
        route = [
            (i * lon_size + j, (i ^ (1 << (phase if j % 2 == 0 else bits - 1 - phase))) * lon_size + j)
            for i in range(lat_size)
            for j in range(lon_size)
        ]
        return lax.ppermute(send, both, route)

    bits = lat_size.bit_length() - 1
    sends = [
        call(sum_kernel, [chunk], mine, theirs, name="chip_sum")[0] for mine, theirs in zip(keep, arrived)
    ]
    received = [halving(0, send) for send in sends]
    send_rest, keep_rest = call(
        rest_kernel, [halves, halves], *sends, *inner[2:], *outer[2:], name="rest", unread=(0, 1), beside=True
    )
    received_rest = lax.ppermute(send_rest, "lon", sibling)
    results = call(
        output_kernel, [((WIN, 2 * width), BF)] * 2,
        keep_rest, *inner[:2], inner[3], *outer[:2], outer[3], qkv_weight, proj_weight,
        name="outputs", unread=(0,), flops=10**10,
    )
    (lon_back,) = call(pack_lon_kernel, [quarter], results[1], name="pack_lon", beside=True)
    lon_home = lax.ppermute(lon_back, both, back(lon_route))
    kept = [[keep_rest, received_rest, part] for part in received]
    slots = lat_size // 2
    for phase in range(1, bits):
        slots //= 2
        stay = ((slots, *chunk[0][1:]), BF)
        for index, after in enumerate((lon_home, sends[1])):
            send, keep = call(
                functools.partial(halve_kernel, index), [stay, stay], after, *kept[index],
                name=f"halve{slots}", unread=(0,),
            )
            kept[index] = [keep, halving(phase, send)]

    (diag_back,) = call(pack_diag_kernel, [quarter], send, results[1], name="pack_diag", unread=(0,))
    diag_home = lax.ppermute(diag_back, both, back(diag_route))

    rows = width // lon_size
    share = ((rows, split[2]), BF)
    parts = call(
        functools.partial(line_parts_kernel, len(kept[0])), [share] * (lon_size // 2), *kept[0], *kept[1],
        name="line_parts", flops=PARTS,
    )
    arrived = [
        lax.ppermute(parts[step], "lon", [(j, j ^ (2 * step)) for j in range(lon_size)])
        for step in range(lon_size // 2 - 1, 0, -1)
    ]
    (lat_back,) = call(
        pack_lat_kernel, [((HALF + QUARTER, 2 * width), BF)], parts[1], *results, name="pack_lat", unread=(0,)
    )
    lat_home = lax.ppermute(lat_back, both, back(lat_route))
    (placed,) = call(
        place_kernel, [((TOKENS, 2 * width), F32)], *results, lon_home, diag_home, name="place"
    )
    (line_sum,) = call(
        line_sum_kernel, [share], placed, parts[0], *arrived, name="line_sum", flops=LONG, unread=(0,)
    )
    shared = [
        lax.ppermute(line_sum, "lat", [(i, i ^ step) for i in range(lat_size)]) for step in range(1, lat_size)
    ]
    field_out, d_fields, done = call(
        place_rest_kernel,
        [((TOKENS, width), BF), ((TOKENS, width), BF), ((8, LANES), F32)],
        placed, lat_home,
        name="place_rest",
    )
    qkv_grad, proj_grad = call(
        finish_kernel,
        [((rows, 3 * width), F32), ((rows, width), F32)],
        done, line_sum, *shared,
        name="finish", unread=(0,),
    )
    return (field_out.reshape(fields.shape), d_fields.reshape(fields.shape), qkv_grad, jnp.transpose(proj_grad))


def solution(mesh):
    placed = (P(None, "lat", "lon", None), P(None, "lat", "lon", None), P(), P())
    return jax.shard_map(
        per_device,
        mesh=mesh,
        in_specs=placed,
        out_specs=(
            P(None, "lat", "lon", None),
            P(None, "lat", "lon", None),
            P("lon", None),
            P(None, "lon"),
        ),
        check_vma=False,
    )
```

```python
import functools

import jax
import jax.numpy as jnp
from jax import lax
from jax.experimental import pallas as pl
from jax.experimental.pallas import tpu as pltpu
from jax.sharding import PartitionSpec as P

HEADS = 8
WIN_LAT = 6
WIN_LON = 12
LEVELS = 2
COLS = 24
HALF_LAT = WIN_LAT // 2
HALF_LON = WIN_LON // 2
HALF = LEVELS * HALF_LAT * WIN_LON
WIN = 2 * HALF
TOKENS = 2 * WIN
QUARTER = HALF // 2
LANES = 128

epsilon = 1e-05
LONG = 13 * 10**8
LOAD = 5 * 10**9
LATER = 10**9
PARTS = 5 * 10**9
BF = jnp.bfloat16
F32 = jnp.float32


def dot(a, b, dims):
    return lax.dot_general(a, b, (dims, ((), ())), preferred_element_type=F32)


NN = ((1,), (0,))
NT = ((1,), (1,))
TN = ((0,), (0,))


def div(x, by):
    return (x * ((65536 + by - 1) // by)) >> 16


def own_token(level, row, col):
    return level * (WIN_LAT * COLS) + row * COLS + col


def inner_token(v, first):
    level = div(v, HALF_LAT * WIN_LON)
    rest = v - level * (HALF_LAT * WIN_LON)
    row = div(rest, WIN_LON)
    return own_token(level, first + row, HALF_LON + rest - row * WIN_LON)


def half_token(v, first, col):
    level = div(v, HALF_LAT * HALF_LON)
    rest = v - level * (HALF_LAT * HALF_LON)
    row = div(rest, HALF_LON)
    return jnp.where(v < QUARTER, own_token(level, first + row, col + rest - row * HALF_LON), -1)


def sources():
    even = lax.rem(lax.axis_index("lon"), 2) == 0
    sent = jnp.where(even, 0, HALF_LAT)
    kept = HALF_LAT - sent
    outer = HALF_LON + WIN_LON
    return (
        (lambda v: inner_token(v, sent), HALF),
        (lambda v: half_token(v, sent, outer), QUARTER),
        (lambda v: half_token(v, sent, 0), QUARTER),
        (lambda v: half_token(v, kept, 0), QUARTER),
        (lambda v: inner_token(v, kept), HALF),
        (lambda v: half_token(v, kept, outer), HALF),
    )


def picks(source, rows, columns):
    index = source(lax.broadcasted_iota(jnp.int32, (rows, 1), 0))
    return (index == lax.broadcasted_iota(jnp.int32, (rows, columns), 1)).astype(BF)


def puts(source, rows, columns):
    index = source(lax.broadcasted_iota(jnp.int32, (1, columns), 1))
    return (lax.broadcasted_iota(jnp.int32, (rows, columns), 0) == index).astype(BF)


def first_rows(v):
    return v


def last_rows(v):
    return v - QUARTER


def order_kernel(*outs):
    for out, (source, rows) in zip(outs, sources()):
        out[...] = picks(source, rows, TOKENS)


def pack_kernel(fields, cotangent, *refs):
    count = len(refs) // 2
    width = fields.shape[1]
    for pick, out in zip(refs[:count], refs[count:]):
        out[:, :width] = dot(pick[...], fields[...], NN).astype(out.dtype)
        out[:, width:] = dot(pick[...], cotangent[...], NN).astype(out.dtype)


def swap_bits(index, size, core):
    bits = size.bit_length() - 1
    turned = sum(((index >> b) & 1) << (bits - 1 - b) for b in range(bits))
    return jnp.where(core == 0, index, turned)


def shares(transposed, out, lon, core_of, lon_size):
    rows = transposed.shape[0] // lon_size
    chip = lon >> 1
    for step in range(lon_size // 2):
        start = pl.multiple_of(((chip ^ step) * 2 + core_of) * rows, rows)
        out[step * rows : (step + 1) * rows, :] = transposed[pl.ds(start, rows), :]


def transpose_bf16(block):
    return jnp.transpose(block.astype(F32)).astype(BF)


def slot_product(slot, size, lat, core, windows):
    share = lat ^ swap_bits(slot, size, core)
    total = None
    for left, right in windows:
        lanes = right.shape[1] // size
        of_proj = (share >= 3 * size // 4).astype(jnp.int32)
        part = dot(left[of_proj], right[:, pl.ds(pl.multiple_of(share * lanes, lanes), lanes)], NN)
        total = part if total is None else total + part
    return total


def normalise(x):
    mean = jnp.mean(x, -1, keepdims=True)
    centred = x - mean
    variance = jnp.mean(centred * centred, -1, keepdims=True)
    inv_std = lax.rsqrt(variance + epsilon)
    return centred * inv_std, inv_std


def project(both, qkv_weight, proj_weight):
    width = both.shape[1] // 2
    normed, _ = normalise(both[:, :width])
    projected = dot(normed.astype(BF), qkv_weight[...], NN)
    return normed, projected, dot(both[:, width:].astype(BF), proj_weight[...], NT)


def pack_rest_kernel(_, *refs):
    pack_kernel(*refs)


def own_kernel(inner_own, qkv_weight, proj_weight, normed, projected, d_mixed):
    normed[...], projected[...], d_mixed[...] = project(inner_own[...], qkv_weight, proj_weight)


def inner_kernel(own, own_normed, own_projected, own_d_mixed, lat_in, qkv_weight, proj_weight, send_grad, *refs):
    arrived = lat_in[...].astype(F32)
    parts = project(arrived, qkv_weight, proj_weight)
    both = jnp.concatenate([own[...], arrived], axis=0)
    mine = own_normed, own_projected, own_d_mixed
    parts = [jnp.concatenate([first[...], second], axis=0) for first, second in zip(mine, parts)]
    one_window(both, *parts, *refs)
    *_, right, left, _, _ = refs
    lat, core, size = place()
    for slot in range(1, size, 2):
        send_grad[slot // 2] = slot_product(slot, size, lat, 1 - core, [(left, right)])


def outer_kernel(own, lon_in, lat_in, diag_in, qkv_weight, proj_weight, grad_so_far, send_a, send_b, *refs):
    last = picks(last_rows, HALF, QUARTER)
    both = jnp.concatenate(
        [
            own[...] + dot(last, lon_in[...], NN),
            dot(picks(first_rows, HALF, QUARTER), lat_in[...], NN) + dot(last, diag_in[...], NN),
        ],
        axis=0,
    )
    one_window(both, *project(both, qkv_weight, proj_weight), *refs)
    *_, right, left, _, _ = refs
    lat, core, size = place()
    for slot in range(1, size, 2):
        total = grad_so_far[slot // 2] + slot_product(slot, size, lat, 1 - core, [(left, right)])
        put_chunks((send_a, send_b), slot // 2, total)


def put_chunks(outs, slot, total):
    width = outs[0].shape[2]
    for chunk, out in enumerate(outs):
        out[slot] = total[:, chunk * width : (chunk + 1) * width].astype(BF)


def place():
    return lax.axis_index("lat"), lax.rem(lax.axis_index("lon"), 2), lax.axis_size("lat")


def one_window(
    both, normed, projected, d_mixed,
    windows_out, grads_out, left_keep, right, left_send, normed_t, grads_t,
):
    width = both.shape[1] // 2
    lat, core, lat_size = place()
    lon, lon_size = lax.axis_index("lon"), lax.axis_size("lon")
    even = core == 0
    blocks = both[:, :width], both[:, width:]
    x = blocks[0]
    windows_out[...] = x.astype(BF)
    grads = blocks[1].astype(BF)
    grads_out[...] = grads
    projected, d_mixed = projected.astype(BF), d_mixed.astype(BF)

    head_size = width // HEADS
    factor = head_size ** (-0.5)
    apart = jnp.where(even, lat == lat_size - 1, lat == 0).astype(jnp.int32)
    half_b = (lax.broadcasted_iota(jnp.int32, (WIN, 2 * WIN), 0) >= HALF).astype(jnp.int32)
    at_a = lax.broadcasted_iota(jnp.int32, (WIN, 2 * WIN), 1)
    at_a = jnp.where(at_a >= WIN, at_a - WIN, at_a)
    half_a = (at_a >= HALF).astype(jnp.int32)
    allowed = ((half_a != half_b).astype(jnp.int32) * apart) == 0
    first_head = lax.broadcasted_iota(jnp.int32, (WIN, LANES), 1) < head_size
    zero = jnp.zeros((WIN, LANES), BF)

    def split_heads(block):
        return jnp.concatenate([jnp.where(first_head, block, zero), jnp.where(first_head, zero, block)], axis=0)

    def join_heads(block):
        return jnp.where(first_head, block[:WIN], block[WIN:]).astype(BF)

    pairs = range(width // LANES)

    def blocks_of(array, lanes_from):
        return [array[:, lanes_from + pair * LANES : lanes_from + (pair + 1) * LANES] for pair in pairs]

    def store(out, lanes_from, blocks):
        for pair, block in zip(pairs, blocks):
            out[:, lanes_from + pair * LANES : lanes_from + (pair + 1) * LANES] = block.astype(out.dtype)

    k, v = blocks_of(projected, width), blocks_of(projected, 2 * width)
    q2 = [split_heads(block) for block in blocks_of(projected, 0)]
    dm2 = [split_heads(block) for block in blocks_of(d_mixed, 0)]
    scores = [jnp.where(allowed, dot(k[p], q2[p], NT) * factor, -1e30) for p in pairs]
    d_probs = [dot(v[p], dm2[p], NT) for p in pairs]
    exponents = [jnp.exp(s - jnp.max(s, 0, keepdims=True)) for s in scores]
    probs = [e * (1.0 / jnp.sum(e, 0, keepdims=True)) for e in exponents]
    probs_b = [p.astype(BF) for p in probs]
    store(right, 3 * width, [join_heads(dot(probs_b[p], v[p], TN)) for p in pairs])
    store(right, 2 * width, [dot(probs_b[p], dm2[p], NN) for p in pairs])
    d_scores = [
        (probs[p] * (d_probs[p] - jnp.sum(d_probs[p] * probs[p], 0, keepdims=True)) * factor).astype(BF)
        for p in pairs
    ]
    store(right, 0, [join_heads(dot(d_scores[p], k[p], TN)) for p in pairs])
    store(right, width, [dot(d_scores[p], q2[p], NN) for p in pairs])

    normed_t[...] = transpose_bf16(normed)
    grads_t[...] = transpose_bf16(grads)
    for index, source in enumerate((normed_t, grads_t)):
        shares(source, left_send.at[index], lon, 1 - core, lon_size)
        shares(source, left_keep.at[index], lon, core, lon_size)


def keep_kernel(*refs):
    *windows, keep_a, keep_b = refs
    windows = [windows[:2], windows[2:]]
    lat, core, size = place()
    for slot in range(1, size, 2):
        put_chunks((keep_a, keep_b), slot // 2, slot_product(slot, size, lat, core, windows))


def rest_kernel(_, __, *refs):
    *windows, send_rest, keep_rest = refs
    windows = windows[:3], windows[3:]
    lat, core, size = place()
    for slot in range(0, size, 2):
        send_rest[slot // 2] = slot_product(slot, size, lat, 1 - core, [(w[2], w[1]) for w in windows]).astype(BF)
    for slot in range(0, size, 2):
        keep_rest[slot // 2] = slot_product(slot, size, lat, core, [(w[0], w[1]) for w in windows]).astype(BF)


def output_kernel(_, *refs):
    (*windows, qkv_weight, proj_weight, inner_results, outer_results) = refs
    per_window = windows[:3], windows[3:]
    width = proj_weight.shape[0]
    x, grads, right = (jnp.concatenate([w[i][...] for w in per_window], axis=0) for i in range(3))
    d_projected, mixed = right[:, : 3 * width], right[:, 3 * width :]
    x = x.astype(F32)
    normed, inv_std = normalise(x)
    output = (x + dot(mixed, proj_weight[...], NN)).astype(BF)
    d_normed = dot(d_projected, qkv_weight[...], NT)
    d_inputs = grads.astype(F32) + inv_std * (
        d_normed
        - jnp.mean(d_normed, -1, keepdims=True)
        - normed * jnp.mean(d_normed * normed, -1, keepdims=True)
    )
    d_inputs = d_inputs.astype(BF)
    for at, out in ((0, inner_results), (WIN, outer_results)):
        out[:, :width] = output[at : at + WIN]
        out[:, width:] = d_inputs[at : at + WIN]


def pack_lon_kernel(outer_results, lon_out):
    outer_x = outer_results[...].astype(F32)[:HALF].astype(BF)
    lon_out[...] = dot(puts(last_rows, QUARTER, HALF), outer_x, NN).astype(BF)


def pack_diag_kernel(_, outer_results, diag_out):
    outer_y = outer_results[...].astype(F32)[HALF:].astype(BF)
    diag_out[...] = dot(puts(last_rows, QUARTER, HALF), outer_y, NN).astype(BF)


def pack_lat_kernel(_, inner_results, outer_results, lat_out):
    inner_y = inner_results[...].astype(F32)[HALF:]
    outer_y = outer_results[...].astype(F32)[HALF:].astype(BF)
    lat_out[...] = jnp.concatenate([inner_y, dot(puts(first_rows, QUARTER, HALF), outer_y, NN)], axis=0).astype(BF)


def place_kernel(inner_results, outer_results, lon_in, diag_in, placed):
    _, _, lon, diag, inner_own, outer_own = (source for source, _ in sources())

    def only_first(source):
        return lambda v: jnp.where(v < HALF, source(v), -1)

    placed[...] = (
        dot(puts(only_first(inner_own), TOKENS, WIN), inner_results[...], NN)
        + dot(puts(only_first(outer_own), TOKENS, WIN), outer_results[...], NN)
        + dot(puts(lon, TOKENS, QUARTER), lon_in[...], NN)
        + dot(puts(diag, TOKENS, QUARTER), diag_in[...], NN)
    )


def place_rest_kernel(placed, lat_in, field_out, d_fields, done):
    done[...] = jnp.zeros_like(done)
    width = field_out.shape[1]
    inner_lat, outer_lat, *_ = (source for source, _ in sources())

    def lat(v):
        return jnp.where(v < HALF, inner_lat(v), outer_lat(v - HALF))

    total = (placed[...] + dot(puts(lat, TOKENS, HALF + QUARTER), lat_in[...], NN)).astype(BF)
    field_out[...] = total[:, :width]
    d_fields[...] = total[:, width:]


def halve_kernel(chunk, _, *refs):
    *parts, _, send, keep = refs
    width = send.shape[2]

    def lanes(part):
        return slice(None) if part.shape[2] == width else slice(chunk * width, (chunk + 1) * width)

    for slot in range(send.shape[0]):
        for out, source in ((send, 2 * slot + 1), (keep, 2 * slot)):
            out[slot] = sum(part[source, :, lanes(part)].astype(F32) for part in parts).astype(BF)


def line_parts_kernel(*refs):
    chunks, (keep, *sends) = (refs[:1], refs[1:3]), refs[3:]
    rows = keep.shape[0]
    for step, out in enumerate((keep, *sends)):
        at = slice(step * rows, (step + 1) * rows)
        totals = [sum(part[0, at].astype(F32) for part in parts) for parts in chunks]
        out[...] = jnp.concatenate(totals, axis=1).astype(out.dtype)


def next_sum_kernel(_, *refs):
    sum_kernel(*refs)


def sum_kernel(*refs):
    *parts, out = refs
    total = parts[0][...].astype(F32)
    for part in parts[1:]:
        total = total + part[...].astype(F32)
    out[...] = total.astype(out.dtype)


def finish_kernel(_, *refs):
    *parts, qkv_out, proj_out = refs
    lat, _, size = place()
    width = parts[0].shape[1]
    for step, part in enumerate(parts):
        share = lat ^ step
        total = part[...].astype(F32)
        of_qkv = 3 * size // 4

        @pl.when(share < of_qkv)
        def _():
            qkv_out[:, pl.ds(pl.multiple_of(share * width, width), width)] = total

        @pl.when(share >= of_qkv)
        def _():
            proj_out[:, pl.ds(pl.multiple_of((share - of_qkv) * width, width), width)] = total


def call(kernel, outs, *args, name, flops=0, limit=32, scratch=(), unread=(), beside=False):
    vmem = pl.BlockSpec(memory_space=pltpu.VMEM)
    anywhere = pl.BlockSpec(memory_space=pl.ANY)
    shapes = [jax.ShapeDtypeStruct(shape, dtype) for shape, dtype in outs]
    nbytes = 0 if beside else sum(a.size * a.dtype.itemsize for a in (*args, *shapes))
    return pl.pallas_call(
        kernel,
        out_shape=shapes,
        in_specs=[anywhere if i in unread else vmem for i in range(len(args))],
        out_specs=[vmem] * len(shapes),
        scratch_shapes=scratch,
        compiler_params=pltpu.CompilerParams(vmem_limit_bytes=limit * 2**20),
        cost_estimate=pl.CostEstimate(flops=flops, bytes_accessed=nbytes, transcendentals=0),
        name=name,
    )(*args)


def routes(lat_size, lon_size):
    lat, lon, diag = [], [], []
    for i in range(lat_size):
        for j in range(lon_size):
            step = -1 if j % 2 == 0 else 1
            before = (j - 1) % lon_size
            me = i * lon_size + j
            lat.append((me, ((i + step) % lat_size) * lon_size + j))
            lon.append((me, i * lon_size + before))
            diag.append((me, ((i - step) % lat_size) * lon_size + before))
    return lat, lon, diag


def per_device(fields, cotangent, qkv_weight, proj_weight):
    levels, row_count, col_count, width = fields.shape
    lat_size, lon_size = lax.axis_size("lat"), lax.axis_size("lon")
    both = ("lat", "lon")
    lat_route, lon_route, diag_route = routes(lat_size, lon_size)

    def back(route):
        return [(target, source) for source, target in route]

    own_fields = fields.reshape(TOKENS, width)
    own_grads = cotangent.reshape(TOKENS, width)
    lengths = (HALF, QUARTER, QUARTER, QUARTER, HALF, HALF)
    picked = call(order_kernel, [((rows, TOKENS), BF) for rows in lengths], name="order", flops=LOAD)
    pick_inner, pick_outer, pick_lon, pick_diag, pick_own, pick_outer_own = picked
    whole, half = ((HALF, 2 * width), F32), ((HALF, 2 * width), BF)
    quarter = ((QUARTER, 2 * width), BF)
    inner_lat, lon_piece = call(
        pack_kernel, [half, quarter], own_fields, own_grads, pick_inner, pick_lon, name="pack", flops=LOAD
    )
    outer_lat, diag_piece, outer_own, inner_own = call(
        pack_rest_kernel, [quarter, quarter, whole, whole],
        lon_piece, own_fields, own_grads, pick_outer, pick_diag, pick_outer_own, pick_own,
        name="pack_rest", flops=5 * 10**8, unread=(0,),
    )
    own_parts = call(
        own_kernel, [((HALF, lanes), F32) for lanes in (width, 3 * width, width)],
        inner_own, qkv_weight, proj_weight,
        name="own", flops=5 * 10**8,
    )
    inner_in = lax.ppermute(inner_lat, both, lat_route)
    lon_in = lax.ppermute(lon_piece, both, lon_route)
    outer_in = lax.ppermute(outer_lat, both, lat_route)
    diag_in = lax.ppermute(diag_piece, both, diag_route)

    split = (lat_size, width // 2, 4 * width // lat_size)
    halves = ((lat_size // 2, *split[1:]), BF)
    chunk = ((lat_size // 2, split[1], split[2] // 2), BF)
    per_window = [
        ((WIN, width), BF),
        ((WIN, width), BF),
        ((2, width // 2, WIN), BF),
        ((WIN, 4 * width), BF),
        ((2, width // 2, WIN), BF),
    ]
    scratch = [pltpu.VMEM((width, WIN), BF)] * 2
    grad_so_far, *inner = call(
        inner_kernel, [(halves[0], F32), *per_window], inner_own, *own_parts, inner_in, qkv_weight, proj_weight,
        name="inner", flops=10**9, scratch=scratch,
    )
    send_a, send_b, *outer = call(
        outer_kernel, [chunk, chunk, *per_window],
        outer_own, lon_in, outer_in, diag_in, qkv_weight, proj_weight, grad_so_far,
        name="outer", flops=10**9, scratch=scratch,
    )
    sibling = [(j, j ^ 1) for j in range(lon_size)]
    arrived = [lax.ppermute(send, "lon", sibling) for send in (send_a, send_b)]
    keep = call(keep_kernel, [chunk, chunk], *inner[2:4], *outer[2:4], name="keep", flops=10**9)

    def halving(phase, send):
        route = [
            (i * lon_size + j, (i ^ (1 << (phase if j % 2 == 0 else bits - 1 - phase))) * lon_size + j)
            for i in range(lat_size)
            for j in range(lon_size)
        ]
        return lax.ppermute(send, both, route)

    bits = lat_size.bit_length() - 1
    sends = [keep[0]]
    for mine, theirs in zip(keep, arrived):
        sends += call(next_sum_kernel, [chunk], sends[-1], mine, theirs, name="chip_sum", unread=(0,))
    sends = sends[1:]
    received = [halving(0, send) for send in sends]
    send_rest, keep_rest = call(
        rest_kernel, [halves, halves], *sends, *inner[2:], *outer[2:], name="rest", unread=(0, 1), beside=True
    )
    received_rest = lax.ppermute(send_rest, "lon", sibling)
    results = call(
        output_kernel, [((WIN, 2 * width), BF)] * 2,
        keep_rest, *inner[:2], inner[3], *outer[:2], outer[3], qkv_weight, proj_weight,
        name="outputs", unread=(0,), flops=10**10,
    )
    (lon_back,) = call(pack_lon_kernel, [quarter], results[1], name="pack_lon", beside=True)
    lon_home = lax.ppermute(lon_back, both, back(lon_route))
    kept = [[keep_rest, received_rest, part] for part in received]
    slots = lat_size // 2
    for phase in range(1, bits):
        slots //= 2
        stay = ((slots, *chunk[0][1:]), BF)
        after = results[0]
        for index in range(2):
            send, keep = call(
                functools.partial(halve_kernel, index), [stay, stay], after, *kept[index],
                after, name=f"halve{slots}", unread=(0, 1 + len(kept[index])),
            )
            kept[index] = [keep, halving(phase, send)]
            after = send

    (diag_back,) = call(pack_diag_kernel, [quarter], send, results[1], name="pack_diag", unread=(0,))
    diag_home = lax.ppermute(diag_back, both, back(diag_route))

    rows = width // lon_size
    share = ((rows, split[2]), BF)
    (first_chunk,) = call(
        next_sum_kernel, [((1, split[1], split[2] // 2), F32)], lon_home, *kept[0],
        name="first_chunk", flops=LATER, unread=(0,),
    )
    parts = call(
        line_parts_kernel, [share] * (lon_size // 2), first_chunk, *kept[1], name="line_parts", flops=PARTS
    )
    arrived = [
        lax.ppermute(parts[step], "lon", [(j, j ^ (2 * step)) for j in range(lon_size)])
        for step in range(lon_size // 2 - 1, 0, -1)
    ]
    (lat_back,) = call(
        pack_lat_kernel, [((HALF + QUARTER, 2 * width), BF)], parts[1], *results, name="pack_lat", unread=(0,)
    )
    lat_home = lax.ppermute(lat_back, both, back(lat_route))
    (placed,) = call(
        place_kernel, [((TOKENS, 2 * width), F32)], *results, lon_home, diag_home, name="place"
    )
    (line_sum,) = call(
        next_sum_kernel, [share], placed, parts[0], *arrived, name="line_sum", flops=LONG, unread=(0,)
    )
    shared = [
        lax.ppermute(line_sum, "lat", [(i, i ^ step) for i in range(lat_size)]) for step in range(1, lat_size)
    ]
    field_out, d_fields, done = call(
        place_rest_kernel,
        [((TOKENS, width), BF), ((TOKENS, width), BF), ((8, LANES), F32)],
        placed, lat_home,
        name="place_rest",
    )
    qkv_grad, proj_grad = call(
        finish_kernel,
        [((rows, 3 * width), F32), ((rows, width), F32)],
        done, line_sum, *shared,
        name="finish", unread=(0,),
    )
    return (field_out.reshape(fields.shape), d_fields.reshape(fields.shape), qkv_grad, jnp.transpose(proj_grad))


def solution(mesh):
    placed = (P(None, "lat", "lon", None), P(None, "lat", "lon", None), P(), P())
    return jax.shard_map(
        per_device,
        mesh=mesh,
        in_specs=placed,
        out_specs=(
            P(None, "lat", "lon", None),
            P(None, "lat", "lon", None),
            P("lon", None),
            P(None, "lon"),
        ),
        check_vma=False,
    )
```

```python
import functools

import jax
import jax.numpy as jnp
from jax import lax
from jax.experimental import pallas as pl
from jax.experimental.pallas import tpu as pltpu
from jax.sharding import PartitionSpec as P

HEADS = 8
WIN_LAT = 6
WIN_LON = 12
LEVELS = 2
COLS = 24
HALF_LAT = WIN_LAT // 2
HALF_LON = WIN_LON // 2
HALF = LEVELS * HALF_LAT * WIN_LON
WIN = 2 * HALF
TOKENS = 2 * WIN
QUARTER = HALF // 2
LANES = 128

epsilon = 1e-05
LONG = 13 * 10**8
LOAD = 5 * 10**9
LATER = 10**9
PARTS = 5 * 10**9
BF = jnp.bfloat16
F32 = jnp.float32


def dot(a, b, dims):
    return lax.dot_general(a, b, (dims, ((), ())), preferred_element_type=F32)


NN = ((1,), (0,))
NT = ((1,), (1,))
TN = ((0,), (0,))


def div(x, by):
    return (x * ((65536 + by - 1) // by)) >> 16


def own_token(level, row, col):
    return level * (WIN_LAT * COLS) + row * COLS + col


def inner_token(v, first):
    level = div(v, HALF_LAT * WIN_LON)
    rest = v - level * (HALF_LAT * WIN_LON)
    row = div(rest, WIN_LON)
    return own_token(level, first + row, HALF_LON + rest - row * WIN_LON)


def half_token(v, first, col):
    level = div(v, HALF_LAT * HALF_LON)
    rest = v - level * (HALF_LAT * HALF_LON)
    row = div(rest, HALF_LON)
    return jnp.where(v < QUARTER, own_token(level, first + row, col + rest - row * HALF_LON), -1)


def sources():
    even = lax.rem(lax.axis_index("lon"), 2) == 0
    sent = jnp.where(even, 0, HALF_LAT)
    kept = HALF_LAT - sent
    outer = HALF_LON + WIN_LON
    return (
        (lambda v: inner_token(v, sent), HALF),
        (lambda v: half_token(v, sent, outer), QUARTER),
        (lambda v: half_token(v, sent, 0), QUARTER),
        (lambda v: half_token(v, kept, 0), QUARTER),
        (lambda v: inner_token(v, kept), HALF),
        (lambda v: half_token(v, kept, outer), HALF),
    )


def picks(source, rows, columns):
    index = source(lax.broadcasted_iota(jnp.int32, (rows, 1), 0))
    return (index == lax.broadcasted_iota(jnp.int32, (rows, columns), 1)).astype(BF)


def puts(source, rows, columns):
    index = source(lax.broadcasted_iota(jnp.int32, (1, columns), 1))
    return (lax.broadcasted_iota(jnp.int32, (rows, columns), 0) == index).astype(BF)


def first_rows(v):
    return v


def last_rows(v):
    return v - QUARTER


def order_kernel(*outs):
    for out, (source, rows) in zip(outs, sources()):
        out[...] = picks(source, rows, TOKENS)


def pack_kernel(fields, cotangent, *refs):
    count = len(refs) // 2
    width = fields.shape[1]
    for pick, out in zip(refs[:count], refs[count:]):
        out[:, :width] = dot(pick[...], fields[...], NN).astype(out.dtype)
        out[:, width:] = dot(pick[...], cotangent[...], NN).astype(out.dtype)


def swap_bits(index, size, core):
    bits = size.bit_length() - 1
    turned = sum(((index >> b) & 1) << (bits - 1 - b) for b in range(bits))
    return jnp.where(core == 0, turned, index)


def shares(transposed, out, lon, core_of, lon_size):
    rows = transposed.shape[0] // lon_size
    chip = lon >> 1
    for step in range(lon_size // 2):
        start = pl.multiple_of(((chip ^ step) * 2 + core_of) * rows, rows)
        out[step * rows : (step + 1) * rows, :] = transposed[pl.ds(start, rows), :]


def transpose_bf16(block):
    return jnp.transpose(block.astype(F32)).astype(BF)


def slot_product(slot, size, lat, core, windows):
    share = lat ^ swap_bits(slot, size, core)
    total = None
    for left, right in windows:
        lanes = right.shape[1] // size
        of_proj = (share >= 3 * size // 4).astype(jnp.int32)
        part = dot(left[of_proj], right[:, pl.ds(pl.multiple_of(share * lanes, lanes), lanes)], NN)
        total = part if total is None else total + part
    return total


def normalise(x):
    mean = jnp.mean(x, -1, keepdims=True)
    centred = x - mean
    variance = jnp.mean(centred * centred, -1, keepdims=True)
    inv_std = lax.rsqrt(variance + epsilon)
    return centred * inv_std, inv_std


def project(both, qkv_weight, proj_weight):
    width = both.shape[1] // 2
    normed, _ = normalise(both[:, :width])
    projected = dot(normed.astype(BF), qkv_weight[...], NN)
    return normed, projected, dot(both[:, width:].astype(BF), proj_weight[...], NT)


def pack_rest_kernel(_, *refs):
    pack_kernel(*refs)


def own_kernel(inner_own, qkv_weight, proj_weight, normed, projected, d_mixed):
    normed[...], projected[...], d_mixed[...] = project(inner_own[...], qkv_weight, proj_weight)


def inner_kernel(own, own_normed, own_projected, own_d_mixed, lat_in, qkv_weight, proj_weight, send_grad, *refs):
    arrived = lat_in[...].astype(F32)
    parts = project(arrived, qkv_weight, proj_weight)
    both = jnp.concatenate([own[...], arrived], axis=0)
    mine = own_normed, own_projected, own_d_mixed
    parts = [jnp.concatenate([first[...], second], axis=0) for first, second in zip(mine, parts)]
    one_window(both, *parts, *refs)
    *_, right, left, _, _ = refs
    lat, core, size = place()
    for slot in range(1, size, 2):
        send_grad[slot // 2] = slot_product(slot, size, lat, 1 - core, [(left, right)])


def outer_kernel(own, lon_in, lat_in, diag_in, qkv_weight, proj_weight, grad_so_far, send_a, send_b, *refs):
    last = picks(last_rows, HALF, QUARTER)
    both = jnp.concatenate(
        [
            own[...] + dot(last, lon_in[...], NN),
            dot(picks(first_rows, HALF, QUARTER), lat_in[...], NN) + dot(last, diag_in[...], NN),
        ],
        axis=0,
    )
    one_window(both, *project(both, qkv_weight, proj_weight), *refs)
    *_, right, left, _, _ = refs
    lat, core, size = place()
    for slot in range(1, size, 2):
        total = grad_so_far[slot // 2] + slot_product(slot, size, lat, 1 - core, [(left, right)])
        put_chunks((send_a, send_b), slot // 2, total)


def put_chunks(outs, slot, total):
    width = outs[0].shape[2]
    for chunk, out in enumerate(outs):
        out[slot] = total[:, chunk * width : (chunk + 1) * width].astype(BF)


def place():
    return lax.axis_index("lat"), lax.rem(lax.axis_index("lon"), 2), lax.axis_size("lat")


def one_window(
    both, normed, projected, d_mixed,
    windows_out, grads_out, left_keep, right, left_send, normed_t, grads_t,
):
    width = both.shape[1] // 2
    lat, core, lat_size = place()
    lon, lon_size = lax.axis_index("lon"), lax.axis_size("lon")
    even = core == 0
    blocks = both[:, :width], both[:, width:]
    x = blocks[0]
    windows_out[...] = x.astype(BF)
    grads = blocks[1].astype(BF)
    grads_out[...] = grads
    projected, d_mixed = projected.astype(BF), d_mixed.astype(BF)

    head_size = width // HEADS
    factor = head_size ** (-0.5)
    apart = jnp.where(even, lat == lat_size - 1, lat == 0).astype(jnp.int32)
    half_b = (lax.broadcasted_iota(jnp.int32, (WIN, 2 * WIN), 0) >= HALF).astype(jnp.int32)
    at_a = lax.broadcasted_iota(jnp.int32, (WIN, 2 * WIN), 1)
    at_a = jnp.where(at_a >= WIN, at_a - WIN, at_a)
    half_a = (at_a >= HALF).astype(jnp.int32)
    allowed = ((half_a != half_b).astype(jnp.int32) * apart) == 0
    first_head = lax.broadcasted_iota(jnp.int32, (WIN, LANES), 1) < head_size
    zero = jnp.zeros((WIN, LANES), BF)

    def split_heads(block):
        return jnp.concatenate([jnp.where(first_head, block, zero), jnp.where(first_head, zero, block)], axis=0)

    def join_heads(block):
        return jnp.where(first_head, block[:WIN], block[WIN:]).astype(BF)

    pairs = range(width // LANES)

    def blocks_of(array, lanes_from):
        return [array[:, lanes_from + pair * LANES : lanes_from + (pair + 1) * LANES] for pair in pairs]

    def store(out, lanes_from, blocks):
        for pair, block in zip(pairs, blocks):
            out[:, lanes_from + pair * LANES : lanes_from + (pair + 1) * LANES] = block.astype(out.dtype)

    k, v = blocks_of(projected, width), blocks_of(projected, 2 * width)
    q2 = [split_heads(block) for block in blocks_of(projected, 0)]
    dm2 = [split_heads(block) for block in blocks_of(d_mixed, 0)]
    scores = [jnp.where(allowed, dot(k[p], q2[p], NT) * factor, -1e30) for p in pairs]
    d_probs = [dot(v[p], dm2[p], NT) for p in pairs]
    exponents = [jnp.exp(s - jnp.max(s, 0, keepdims=True)) for s in scores]
    probs = [e * (1.0 / jnp.sum(e, 0, keepdims=True)) for e in exponents]
    probs_b = [p.astype(BF) for p in probs]
    store(right, 3 * width, [join_heads(dot(probs_b[p], v[p], TN)) for p in pairs])
    store(right, 2 * width, [dot(probs_b[p], dm2[p], NN) for p in pairs])
    d_scores = [
        (probs[p] * (d_probs[p] - jnp.sum(d_probs[p] * probs[p], 0, keepdims=True)) * factor).astype(BF)
        for p in pairs
    ]
    store(right, 0, [join_heads(dot(d_scores[p], k[p], TN)) for p in pairs])
    store(right, width, [dot(d_scores[p], q2[p], NN) for p in pairs])

    normed_t[...] = transpose_bf16(normed)
    grads_t[...] = transpose_bf16(grads)
    for index, source in enumerate((normed_t, grads_t)):
        shares(source, left_send.at[index], lon, 1 - core, lon_size)
        shares(source, left_keep.at[index], lon, core, lon_size)


def keep_kernel(*refs):
    *windows, keep_a, keep_b = refs
    windows = [windows[:2], windows[2:]]
    lat, core, size = place()
    for slot in range(1, size, 2):
        put_chunks((keep_a, keep_b), slot // 2, slot_product(slot, size, lat, core, windows))


def rest_kernel(_, __, *refs):
    *windows, send_rest, keep_rest = refs
    windows = windows[:3], windows[3:]
    lat, core, size = place()
    for slot in range(0, size, 2):
        send_rest[slot // 2] = slot_product(slot, size, lat, 1 - core, [(w[2], w[1]) for w in windows]).astype(BF)
    for slot in range(0, size, 2):
        keep_rest[slot // 2] = slot_product(slot, size, lat, core, [(w[0], w[1]) for w in windows]).astype(BF)


def output_kernel(_, *refs):
    (*windows, qkv_weight, proj_weight, inner_results, outer_results) = refs
    per_window = windows[:3], windows[3:]
    width = proj_weight.shape[0]
    x, grads, right = (jnp.concatenate([w[i][...] for w in per_window], axis=0) for i in range(3))
    d_projected, mixed = right[:, : 3 * width], right[:, 3 * width :]
    x = x.astype(F32)
    normed, inv_std = normalise(x)
    output = (x + dot(mixed, proj_weight[...], NN)).astype(BF)
    d_normed = dot(d_projected, qkv_weight[...], NT)
    d_inputs = grads.astype(F32) + inv_std * (
        d_normed
        - jnp.mean(d_normed, -1, keepdims=True)
        - normed * jnp.mean(d_normed * normed, -1, keepdims=True)
    )
    d_inputs = d_inputs.astype(BF)
    for at, out in ((0, inner_results), (WIN, outer_results)):
        out[:, :width] = output[at : at + WIN]
        out[:, width:] = d_inputs[at : at + WIN]


def pack_lon_kernel(outer_results, lon_out):
    outer_x = outer_results[...].astype(F32)[:HALF].astype(BF)
    lon_out[...] = dot(puts(last_rows, QUARTER, HALF), outer_x, NN).astype(BF)


def pack_diag_kernel(_, outer_results, diag_out):
    outer_y = outer_results[...].astype(F32)[HALF:].astype(BF)
    diag_out[...] = dot(puts(last_rows, QUARTER, HALF), outer_y, NN).astype(BF)


def pack_lat_kernel(_, inner_results, outer_results, lat_out):
    inner_y = inner_results[...].astype(F32)[HALF:]
    outer_y = outer_results[...].astype(F32)[HALF:].astype(BF)
    lat_out[...] = jnp.concatenate([inner_y, dot(puts(first_rows, QUARTER, HALF), outer_y, NN)], axis=0).astype(BF)


def place_kernel(inner_results, outer_results, lon_in, diag_in, placed):
    _, _, lon, diag, inner_own, outer_own = (source for source, _ in sources())

    def only_first(source):
        return lambda v: jnp.where(v < HALF, source(v), -1)

    placed[...] = (
        dot(puts(only_first(inner_own), TOKENS, WIN), inner_results[...], NN)
        + dot(puts(only_first(outer_own), TOKENS, WIN), outer_results[...], NN)
        + dot(puts(lon, TOKENS, QUARTER), lon_in[...], NN)
        + dot(puts(diag, TOKENS, QUARTER), diag_in[...], NN)
    )


def place_rest_kernel(placed, lat_in, field_out, d_fields, done):
    done[...] = jnp.zeros_like(done)
    width = field_out.shape[1]
    inner_lat, outer_lat, *_ = (source for source, _ in sources())

    def lat(v):
        return jnp.where(v < HALF, inner_lat(v), outer_lat(v - HALF))

    total = (placed[...] + dot(puts(lat, TOKENS, HALF + QUARTER), lat_in[...], NN)).astype(BF)
    field_out[...] = total[:, :width]
    d_fields[...] = total[:, width:]


def halve_kernel(chunk, _, *refs):
    *parts, _, send, keep = refs
    width = send.shape[2]

    def lanes(part):
        return slice(None) if part.shape[2] == width else slice(chunk * width, (chunk + 1) * width)

    for slot in range(send.shape[0]):
        for out, source in ((send, 2 * slot + 1), (keep, 2 * slot)):
            out[slot] = sum(part[source, :, lanes(part)].astype(F32) for part in parts).astype(BF)


def line_parts_kernel(*refs):
    chunks, (keep, *sends) = (refs[:1], refs[1:3]), refs[3:]
    rows = keep.shape[0]
    for step, out in enumerate((keep, *sends)):
        at = slice(step * rows, (step + 1) * rows)
        totals = [sum(part[0, at].astype(F32) for part in parts) for parts in chunks]
        out[...] = jnp.concatenate(totals, axis=1).astype(out.dtype)


def next_sum_kernel(_, *refs):
    sum_kernel(*refs)


def sum_kernel(*refs):
    *parts, out = refs
    total = parts[0][...].astype(F32)
    for part in parts[1:]:
        total = total + part[...].astype(F32)
    out[...] = total.astype(out.dtype)


def finish_kernel(_, *refs):
    *parts, qkv_out, proj_out = refs
    lat, _, size = place()
    width = parts[0].shape[1]
    for step, part in enumerate(parts):
        share = lat ^ step
        total = part[...].astype(F32)
        of_qkv = 3 * size // 4

        @pl.when(share < of_qkv)
        def _():
            qkv_out[:, pl.ds(pl.multiple_of(share * width, width), width)] = total

        @pl.when(share >= of_qkv)
        def _():
            proj_out[:, pl.ds(pl.multiple_of((share - of_qkv) * width, width), width)] = total


def call(kernel, outs, *args, name, flops=0, limit=32, scratch=(), unread=(), beside=False):
    vmem = pl.BlockSpec(memory_space=pltpu.VMEM)
    anywhere = pl.BlockSpec(memory_space=pl.ANY)
    shapes = [jax.ShapeDtypeStruct(shape, dtype) for shape, dtype in outs]
    nbytes = 0 if beside else sum(a.size * a.dtype.itemsize for a in (*args, *shapes))
    return pl.pallas_call(
        kernel,
        out_shape=shapes,
        in_specs=[anywhere if i in unread else vmem for i in range(len(args))],
        out_specs=[vmem] * len(shapes),
        scratch_shapes=scratch,
        compiler_params=pltpu.CompilerParams(vmem_limit_bytes=limit * 2**20),
        cost_estimate=pl.CostEstimate(flops=flops, bytes_accessed=nbytes, transcendentals=0),
        name=name,
    )(*args)


def routes(lat_size, lon_size):
    lat, lon, diag = [], [], []
    for i in range(lat_size):
        for j in range(lon_size):
            step = -1 if j % 2 == 0 else 1
            before = (j - 1) % lon_size
            me = i * lon_size + j
            lat.append((me, ((i + step) % lat_size) * lon_size + j))
            lon.append((me, i * lon_size + before))
            diag.append((me, ((i - step) % lat_size) * lon_size + before))
    return lat, lon, diag


def per_device(fields, cotangent, qkv_weight, proj_weight):
    levels, row_count, col_count, width = fields.shape
    lat_size, lon_size = lax.axis_size("lat"), lax.axis_size("lon")
    both = ("lat", "lon")
    lat_route, lon_route, diag_route = routes(lat_size, lon_size)

    def back(route):
        return [(target, source) for source, target in route]

    own_fields = fields.reshape(TOKENS, width)
    own_grads = cotangent.reshape(TOKENS, width)
    lengths = (HALF, QUARTER, QUARTER, QUARTER, HALF, HALF)
    picked = call(order_kernel, [((rows, TOKENS), BF) for rows in lengths], name="order", flops=LOAD)
    pick_inner, pick_outer, pick_lon, pick_diag, pick_own, pick_outer_own = picked
    whole, half = ((HALF, 2 * width), F32), ((HALF, 2 * width), BF)
    quarter = ((QUARTER, 2 * width), BF)
    inner_lat, lon_piece = call(
        pack_kernel, [half, quarter], own_fields, own_grads, pick_inner, pick_lon, name="pack", flops=LOAD
    )
    outer_lat, diag_piece, outer_own, inner_own = call(
        pack_rest_kernel, [quarter, quarter, whole, whole],
        lon_piece, own_fields, own_grads, pick_outer, pick_diag, pick_outer_own, pick_own,
        name="pack_rest", flops=5 * 10**8, unread=(0,),
    )
    own_parts = call(
        own_kernel, [((HALF, lanes), F32) for lanes in (width, 3 * width, width)],
        inner_own, qkv_weight, proj_weight,
        name="own", flops=5 * 10**8,
    )
    inner_in = lax.ppermute(inner_lat, both, lat_route)
    lon_in = lax.ppermute(lon_piece, both, lon_route)
    outer_in = lax.ppermute(outer_lat, both, lat_route)
    diag_in = lax.ppermute(diag_piece, both, diag_route)

    split = (lat_size, width // 2, 4 * width // lat_size)
    halves = ((lat_size // 2, *split[1:]), BF)
    chunk = ((lat_size // 2, split[1], split[2] // 2), BF)
    per_window = [
        ((WIN, width), BF),
        ((WIN, width), BF),
        ((2, width // 2, WIN), BF),
        ((WIN, 4 * width), BF),
        ((2, width // 2, WIN), BF),
    ]
    scratch = [pltpu.VMEM((width, WIN), BF)] * 2
    grad_so_far, *inner = call(
        inner_kernel, [(halves[0], F32), *per_window], inner_own, *own_parts, inner_in, qkv_weight, proj_weight,
        name="inner", flops=10**9, scratch=scratch,
    )
    send_a, send_b, *outer = call(
        outer_kernel, [chunk, chunk, *per_window],
        outer_own, lon_in, outer_in, diag_in, qkv_weight, proj_weight, grad_so_far,
        name="outer", flops=10**9, scratch=scratch,
    )
    sibling = [(j, j ^ 1) for j in range(lon_size)]
    arrived = [lax.ppermute(send, "lon", sibling) for send in (send_a, send_b)]
    keep = call(keep_kernel, [chunk, chunk], *inner[2:4], *outer[2:4], name="keep", flops=10**9)

    def halving(phase, send):
        route = [
            (i * lon_size + j, (i ^ (1 << (phase if j % 2 else bits - 1 - phase))) * lon_size + j)
            for i in range(lat_size)
            for j in range(lon_size)
        ]
        return lax.ppermute(send, both, route)

    bits = lat_size.bit_length() - 1
    sends = [keep[0]]
    for mine, theirs in zip(keep, arrived):
        sends += call(next_sum_kernel, [chunk], sends[-1], mine, theirs, name="chip_sum", unread=(0,))
    sends = sends[1:]
    received = [halving(0, send) for send in sends]
    send_rest, keep_rest = call(
        rest_kernel, [halves, halves], *sends, *inner[2:], *outer[2:], name="rest", unread=(0, 1), beside=True
    )
    received_rest = lax.ppermute(send_rest, "lon", sibling)
    results = call(
        output_kernel, [((WIN, 2 * width), BF)] * 2,
        keep_rest, *inner[:2], inner[3], *outer[:2], outer[3], qkv_weight, proj_weight,
        name="outputs", unread=(0,), flops=10**10,
    )
    (lon_back,) = call(pack_lon_kernel, [quarter], results[1], name="pack_lon", beside=True)
    lon_home = lax.ppermute(lon_back, both, back(lon_route))
    kept = [[keep_rest, received_rest, part] for part in received]
    slots = lat_size // 2
    for phase in range(1, bits):
        slots //= 2
        stay = ((slots, *chunk[0][1:]), BF)
        after = results[0]
        for index in range(2):
            send, keep = call(
                functools.partial(halve_kernel, index), [stay, stay], after, *kept[index],
                after, name=f"halve{slots}", unread=(0, 1 + len(kept[index])),
            )
            kept[index] = [keep, halving(phase, send)]
            after = send

    (diag_back,) = call(pack_diag_kernel, [quarter], send, results[1], name="pack_diag", unread=(0,))
    diag_home = lax.ppermute(diag_back, both, back(diag_route))

    rows = width // lon_size
    share = ((rows, split[2]), BF)
    (first_chunk,) = call(
        next_sum_kernel, [((1, split[1], split[2] // 2), F32)], lon_home, *kept[0],
        name="first_chunk", flops=LATER, unread=(0,),
    )
    parts = call(
        line_parts_kernel, [share] * (lon_size // 2), first_chunk, *kept[1], name="line_parts", flops=PARTS
    )
    arrived = [
        lax.ppermute(parts[step], "lon", [(j, j ^ (2 * step)) for j in range(lon_size)])
        for step in range(lon_size // 2 - 1, 0, -1)
    ]
    (lat_back,) = call(
        pack_lat_kernel, [((HALF + QUARTER, 2 * width), BF)], parts[1], *results, name="pack_lat", unread=(0,)
    )
    lat_home = lax.ppermute(lat_back, both, back(lat_route))
    (placed,) = call(
        place_kernel, [((TOKENS, 2 * width), F32)], *results, lon_home, diag_home, name="place"
    )
    (line_sum,) = call(
        next_sum_kernel, [share], placed, parts[0], *arrived, name="line_sum", flops=LONG, unread=(0,)
    )
    shared = [
        lax.ppermute(line_sum, "lat", [(i, i ^ step) for i in range(lat_size)]) for step in range(1, lat_size)
    ]
    field_out, d_fields, done = call(
        place_rest_kernel,
        [((TOKENS, width), BF), ((TOKENS, width), BF), ((8, LANES), F32)],
        placed, lat_home,
        name="place_rest",
    )
    qkv_grad, proj_grad = call(
        finish_kernel,
        [((rows, 3 * width), F32), ((rows, width), F32)],
        done, line_sum, *shared,
        name="finish", unread=(0,),
    )
    return (field_out.reshape(fields.shape), d_fields.reshape(fields.shape), qkv_grad, jnp.transpose(proj_grad))


def solution(mesh):
    placed = (P(None, "lat", "lon", None), P(None, "lat", "lon", None), P(), P())
    return jax.shard_map(
        per_device,
        mesh=mesh,
        in_specs=placed,
        out_specs=(
            P(None, "lat", "lon", None),
            P(None, "lat", "lon", None),
            P("lon", None),
            P(None, "lon"),
        ),
        check_vma=False,
    )
```

```python
import functools

import jax
import jax.numpy as jnp
from jax import lax
from jax.experimental import pallas as pl
from jax.experimental.pallas import tpu as pltpu
from jax.sharding import PartitionSpec as P

HEADS = 8
WIN_LAT = 6
WIN_LON = 12
LEVELS = 2
COLS = 24
HALF_LAT = WIN_LAT // 2
HALF_LON = WIN_LON // 2
HALF = LEVELS * HALF_LAT * WIN_LON
WIN = 2 * HALF
TOKENS = 2 * WIN
QUARTER = HALF // 2
LANES = 128

epsilon = 1e-05
LONG = 13 * 10**8
LOAD = 5 * 10**9
LATER = 10**9
PARTS = 5 * 10**9
BF = jnp.bfloat16
F32 = jnp.float32


def dot(a, b, dims):
    return lax.dot_general(a, b, (dims, ((), ())), preferred_element_type=F32)


NN = ((1,), (0,))
NT = ((1,), (1,))
TN = ((0,), (0,))


def div(x, by):
    return (x * ((65536 + by - 1) // by)) >> 16


def own_token(level, row, col):
    return level * (WIN_LAT * COLS) + row * COLS + col


def inner_token(v, first):
    level = div(v, HALF_LAT * WIN_LON)
    rest = v - level * (HALF_LAT * WIN_LON)
    row = div(rest, WIN_LON)
    return own_token(level, first + row, HALF_LON + rest - row * WIN_LON)


def half_token(v, first, col):
    level = div(v, HALF_LAT * HALF_LON)
    rest = v - level * (HALF_LAT * HALF_LON)
    row = div(rest, HALF_LON)
    return jnp.where(v < QUARTER, own_token(level, first + row, col + rest - row * HALF_LON), -1)


def sources():
    even = lax.rem(lax.axis_index("lon"), 2) == 0
    sent = jnp.where(even, 0, HALF_LAT)
    kept = HALF_LAT - sent
    outer = HALF_LON + WIN_LON
    return (
        (lambda v: inner_token(v, sent), HALF),
        (lambda v: half_token(v, sent, outer), QUARTER),
        (lambda v: half_token(v, sent, 0), QUARTER),
        (lambda v: half_token(v, kept, 0), QUARTER),
        (lambda v: inner_token(v, kept), HALF),
        (lambda v: half_token(v, kept, outer), HALF),
    )


def picks(source, rows, columns):
    index = source(lax.broadcasted_iota(jnp.int32, (rows, 1), 0))
    return (index == lax.broadcasted_iota(jnp.int32, (rows, columns), 1)).astype(BF)


def puts(source, rows, columns):
    index = source(lax.broadcasted_iota(jnp.int32, (1, columns), 1))
    return (lax.broadcasted_iota(jnp.int32, (rows, columns), 0) == index).astype(BF)


def first_rows(v):
    return v


def last_rows(v):
    return v - QUARTER


def order_kernel(*outs):
    for out, (source, rows) in zip(outs, sources()):
        out[...] = picks(source, rows, TOKENS)


def pack_kernel(fields, cotangent, *refs):
    count = len(refs) // 2
    width = fields.shape[1]
    for pick, out in zip(refs[:count], refs[count:]):
        out[:, :width] = dot(pick[...], fields[...], NN).astype(out.dtype)
        out[:, width:] = dot(pick[...], cotangent[...], NN).astype(out.dtype)


def swap_bits(index, size, core):
    bits = size.bit_length() - 1
    turned = sum(((index >> b) & 1) << (bits - 1 - b) for b in range(bits))
    return jnp.where(core == 0, index, turned)


def shares(transposed, out, lon, core_of, lon_size):
    rows = transposed.shape[0] // lon_size
    chip = lon >> 1
    for step in range(lon_size // 2):
        start = pl.multiple_of(((chip ^ step) * 2 + core_of) * rows, rows)
        out[step * rows : (step + 1) * rows, :] = transposed[pl.ds(start, rows), :]


def transpose_bf16(block):
    return jnp.transpose(block.astype(F32)).astype(BF)


def slot_product(slot, size, lat, core, windows):
    share = lat ^ swap_bits(slot, size, core)
    total = None
    for left, right in windows:
        lanes = right.shape[1] // size
        of_proj = (share >= 3 * size // 4).astype(jnp.int32)
        part = dot(left[of_proj], right[:, pl.ds(pl.multiple_of(share * lanes, lanes), lanes)], NN)
        total = part if total is None else total + part
    return total


def normalise(x):
    mean = jnp.mean(x, -1, keepdims=True)
    centred = x - mean
    variance = jnp.mean(centred * centred, -1, keepdims=True)
    inv_std = lax.rsqrt(variance + epsilon)
    return centred * inv_std, inv_std


def project(both, qkv_weight, proj_weight):
    width = both.shape[1] // 2
    normed, _ = normalise(both[:, :width])
    projected = dot(normed.astype(BF), qkv_weight[...], NN)
    return normed, projected, dot(both[:, width:].astype(BF), proj_weight[...], NT)


def pack_rest_kernel(_, *refs):
    pack_kernel(*refs)


def own_kernel(inner_own, qkv_weight, proj_weight, normed, projected, d_mixed):
    normed[...], projected[...], d_mixed[...] = project(inner_own[...], qkv_weight, proj_weight)


def inner_kernel(own, own_normed, own_projected, own_d_mixed, lat_in, qkv_weight, proj_weight, send_grad, *refs):
    arrived = lat_in[...].astype(F32)
    parts = project(arrived, qkv_weight, proj_weight)
    both = jnp.concatenate([own[...], arrived], axis=0)
    mine = own_normed, own_projected, own_d_mixed
    parts = [jnp.concatenate([first[...], second], axis=0) for first, second in zip(mine, parts)]
    one_window(both, *parts, *refs)
    *_, right, left, _, _ = refs
    lat, core, size = place()
    for slot in range(1, size, 2):
        send_grad[slot // 2] = slot_product(slot, size, lat, 1 - core, [(left, right)])


def outer_kernel(own, lon_in, lat_in, diag_in, qkv_weight, proj_weight, grad_so_far, send_a, send_b, *refs):
    last = picks(last_rows, HALF, QUARTER)
    both = jnp.concatenate(
        [
            own[...] + dot(last, lon_in[...], NN),
            dot(picks(first_rows, HALF, QUARTER), lat_in[...], NN) + dot(last, diag_in[...], NN),
        ],
        axis=0,
    )
    one_window(both, *project(both, qkv_weight, proj_weight), *refs)
    *_, right, left, _, _ = refs
    lat, core, size = place()
    for slot in range(1, size, 2):
        total = grad_so_far[slot // 2] + slot_product(slot, size, lat, 1 - core, [(left, right)])
        put_chunks((send_a, send_b), slot // 2, total)


def put_chunks(outs, slot, total):
    width = outs[0].shape[2]
    for chunk, out in enumerate(outs):
        out[slot] = total[:, chunk * width : (chunk + 1) * width].astype(BF)


def place():
    return lax.axis_index("lat"), lax.rem(lax.axis_index("lon"), 2), lax.axis_size("lat")


def one_window(
    both, normed, projected, d_mixed,
    windows_out, grads_out, left_keep, right, left_send, normed_t, grads_t,
):
    width = both.shape[1] // 2
    lat, core, lat_size = place()
    lon, lon_size = lax.axis_index("lon"), lax.axis_size("lon")
    even = core == 0
    blocks = both[:, :width], both[:, width:]
    x = blocks[0]
    windows_out[...] = x.astype(BF)
    grads = blocks[1].astype(BF)
    grads_out[...] = grads
    projected, d_mixed = projected.astype(BF), d_mixed.astype(BF)

    head_size = width // HEADS
    factor = head_size ** (-0.5)
    apart = jnp.where(even, lat == lat_size - 1, lat == 0).astype(jnp.int32)
    half_b = (lax.broadcasted_iota(jnp.int32, (WIN, 2 * WIN), 0) >= HALF).astype(jnp.int32)
    at_a = lax.broadcasted_iota(jnp.int32, (WIN, 2 * WIN), 1)
    at_a = jnp.where(at_a >= WIN, at_a - WIN, at_a)
    half_a = (at_a >= HALF).astype(jnp.int32)
    allowed = ((half_a != half_b).astype(jnp.int32) * apart) == 0
    first_head = lax.broadcasted_iota(jnp.int32, (WIN, LANES), 1) < head_size
    zero = jnp.zeros((WIN, LANES), BF)

    def split_heads(block):
        return jnp.concatenate([jnp.where(first_head, block, zero), jnp.where(first_head, zero, block)], axis=0)

    def join_heads(block):
        return jnp.where(first_head, block[:WIN], block[WIN:]).astype(BF)

    pairs = range(width // LANES)

    def blocks_of(array, lanes_from):
        return [array[:, lanes_from + pair * LANES : lanes_from + (pair + 1) * LANES] for pair in pairs]

    def store(out, lanes_from, blocks):
        for pair, block in zip(pairs, blocks):
            out[:, lanes_from + pair * LANES : lanes_from + (pair + 1) * LANES] = block.astype(out.dtype)

    k, v = blocks_of(projected, width), blocks_of(projected, 2 * width)
    q2 = [split_heads(block) for block in blocks_of(projected, 0)]
    dm2 = [split_heads(block) for block in blocks_of(d_mixed, 0)]
    scores = [jnp.where(allowed, dot(k[p], q2[p], NT) * factor, -1e30) for p in pairs]
    d_probs = [dot(v[p], dm2[p], NT) for p in pairs]
    exponents = [jnp.exp(s - jnp.max(s, 0, keepdims=True)) for s in scores]
    probs = [e * (1.0 / jnp.sum(e, 0, keepdims=True)) for e in exponents]
    probs_b = [p.astype(BF) for p in probs]
    store(right, 3 * width, [join_heads(dot(probs_b[p], v[p], TN)) for p in pairs])
    store(right, 2 * width, [dot(probs_b[p], dm2[p], NN) for p in pairs])
    d_scores = [
        (probs[p] * (d_probs[p] - jnp.sum(d_probs[p] * probs[p], 0, keepdims=True)) * factor).astype(BF)
        for p in pairs
    ]
    store(right, 0, [join_heads(dot(d_scores[p], k[p], TN)) for p in pairs])
    store(right, width, [dot(d_scores[p], q2[p], NN) for p in pairs])

    normed_t[...] = transpose_bf16(normed)
    grads_t[...] = transpose_bf16(grads)
    for index, source in enumerate((normed_t, grads_t)):
        shares(source, left_send.at[index], lon, 1 - core, lon_size)
        shares(source, left_keep.at[index], lon, core, lon_size)


def keep_kernel(*refs):
    *windows, keep_a, keep_b = refs
    windows = [windows[:2], windows[2:]]
    lat, core, size = place()
    for slot in range(1, size, 2):
        put_chunks((keep_a, keep_b), slot // 2, slot_product(slot, size, lat, core, windows))


def rest_kernel(_, __, *refs):
    *windows, send_rest, keep_rest = refs
    windows = windows[:3], windows[3:]
    lat, core, size = place()
    for slot in range(0, size, 2):
        send_rest[slot // 2] = slot_product(slot, size, lat, 1 - core, [(w[2], w[1]) for w in windows]).astype(BF)
    for slot in range(0, size, 2):
        keep_rest[slot // 2] = slot_product(slot, size, lat, core, [(w[0], w[1]) for w in windows]).astype(BF)


def output_kernel(_, *refs):
    (*windows, qkv_weight, proj_weight, inner_results, outer_results) = refs
    per_window = windows[:3], windows[3:]
    width = proj_weight.shape[0]
    x, grads, right = (jnp.concatenate([w[i][...] for w in per_window], axis=0) for i in range(3))
    d_projected, mixed = right[:, : 3 * width], right[:, 3 * width :]
    x = x.astype(F32)
    normed, inv_std = normalise(x)
    output = (x + dot(mixed, proj_weight[...], NN)).astype(BF)
    d_normed = dot(d_projected, qkv_weight[...], NT)
    d_inputs = grads.astype(F32) + inv_std * (
        d_normed
        - jnp.mean(d_normed, -1, keepdims=True)
        - normed * jnp.mean(d_normed * normed, -1, keepdims=True)
    )
    d_inputs = d_inputs.astype(BF)
    for at, out in ((0, inner_results), (WIN, outer_results)):
        out[:, :width] = output[at : at + WIN]
        out[:, width:] = d_inputs[at : at + WIN]


def pack_lon_kernel(outer_results, lon_out):
    outer_x = outer_results[...].astype(F32)[:HALF].astype(BF)
    lon_out[...] = dot(puts(last_rows, QUARTER, HALF), outer_x, NN).astype(BF)


def pack_diag_kernel(_, outer_results, diag_out):
    outer_y = outer_results[...].astype(F32)[HALF:].astype(BF)
    diag_out[...] = dot(puts(last_rows, QUARTER, HALF), outer_y, NN).astype(BF)


def pack_lat_kernel(_, inner_results, outer_results, lat_out):
    inner_y = inner_results[...].astype(F32)[HALF:]
    outer_y = outer_results[...].astype(F32)[HALF:].astype(BF)
    lat_out[...] = jnp.concatenate([inner_y, dot(puts(first_rows, QUARTER, HALF), outer_y, NN)], axis=0).astype(BF)


def place_kernel(inner_results, outer_results, lon_in, diag_in, placed):
    _, _, lon, diag, inner_own, outer_own = (source for source, _ in sources())

    def only_first(source):
        return lambda v: jnp.where(v < HALF, source(v), -1)

    placed[...] = (
        dot(puts(only_first(inner_own), TOKENS, WIN), inner_results[...], NN)
        + dot(puts(only_first(outer_own), TOKENS, WIN), outer_results[...], NN)
        + dot(puts(lon, TOKENS, QUARTER), lon_in[...], NN)
        + dot(puts(diag, TOKENS, QUARTER), diag_in[...], NN)
    )


def place_rest_kernel(placed, lat_in, field_out, d_fields, done):
    done[...] = jnp.zeros_like(done)
    width = field_out.shape[1]
    inner_lat, outer_lat, *_ = (source for source, _ in sources())

    def lat(v):
        return jnp.where(v < HALF, inner_lat(v), outer_lat(v - HALF))

    total = (placed[...] + dot(puts(lat, TOKENS, HALF + QUARTER), lat_in[...], NN)).astype(BF)
    field_out[...] = total[:, :width]
    d_fields[...] = total[:, width:]


def halve_kernel(chunk, _, *refs):
    *parts, _, send, keep = refs
    width = send.shape[2]

    def lanes(part):
        return slice(None) if part.shape[2] == width else slice(chunk * width, (chunk + 1) * width)

    for slot in range(send.shape[0]):
        for out, source in ((send, 2 * slot + 1), (keep, 2 * slot)):
            out[slot] = sum(part[source, :, lanes(part)].astype(F32) for part in parts).astype(BF)


def line_parts_kernel(*refs):
    chunks, (keep, *sends) = (refs[:1], refs[1:3]), refs[3:]
    rows = keep.shape[0]
    for step, out in enumerate((keep, *sends)):
        at = slice(step * rows, (step + 1) * rows)
        totals = [sum(part[0, at].astype(F32) for part in parts) for parts in chunks]
        out[...] = jnp.concatenate(totals, axis=1).astype(out.dtype)


def next_sum_kernel(_, *refs):
    sum_kernel(*refs)


def sum_kernel(*refs):
    *parts, out = refs
    total = parts[0][...].astype(F32)
    for part in parts[1:]:
        total = total + part[...].astype(F32)
    out[...] = total.astype(out.dtype)


def finish_kernel(_, *refs):
    *parts, qkv_out, proj_out = refs
    lat, _, size = place()
    width = parts[0].shape[1]
    for step, part in enumerate(parts):
        share = lat ^ step
        total = part[...].astype(F32)
        of_qkv = 3 * size // 4

        @pl.when(share < of_qkv)
        def _():
            qkv_out[:, pl.ds(pl.multiple_of(share * width, width), width)] = total

        @pl.when(share >= of_qkv)
        def _():
            proj_out[:, pl.ds(pl.multiple_of((share - of_qkv) * width, width), width)] = total


def call(kernel, outs, *args, name, flops=0, limit=32, scratch=(), unread=(), beside=False):
    vmem = pl.BlockSpec(memory_space=pltpu.VMEM)
    anywhere = pl.BlockSpec(memory_space=pl.ANY)
    shapes = [jax.ShapeDtypeStruct(shape, dtype) for shape, dtype in outs]
    nbytes = 0 if beside else sum(a.size * a.dtype.itemsize for a in (*args, *shapes))
    return pl.pallas_call(
        kernel,
        out_shape=shapes,
        in_specs=[anywhere if i in unread else vmem for i in range(len(args))],
        out_specs=[vmem] * len(shapes),
        scratch_shapes=scratch,
        compiler_params=pltpu.CompilerParams(vmem_limit_bytes=limit * 2**20),
        cost_estimate=pl.CostEstimate(flops=flops, bytes_accessed=nbytes, transcendentals=0),
        name=name,
    )(*args)


def routes(lat_size, lon_size):
    lat, lon, diag = [], [], []
    for i in range(lat_size):
        for j in range(lon_size):
            step = -1 if j % 2 == 0 else 1
            before = (j - 1) % lon_size
            me = i * lon_size + j
            lat.append((me, ((i + step) % lat_size) * lon_size + j))
            lon.append((me, i * lon_size + before))
            diag.append((me, ((i - step) % lat_size) * lon_size + before))
    return lat, lon, diag


def per_device(fields, cotangent, qkv_weight, proj_weight):
    levels, row_count, col_count, width = fields.shape
    lat_size, lon_size = lax.axis_size("lat"), lax.axis_size("lon")
    both = ("lat", "lon")
    lat_route, lon_route, diag_route = routes(lat_size, lon_size)

    def back(route):
        return [(target, source) for source, target in route]

    own_fields = fields.reshape(TOKENS, width)
    own_grads = cotangent.reshape(TOKENS, width)
    lengths = (HALF, QUARTER, QUARTER, QUARTER, HALF, HALF)
    picked = call(order_kernel, [((rows, TOKENS), BF) for rows in lengths], name="order", flops=LOAD)
    pick_inner, pick_outer, pick_lon, pick_diag, pick_own, pick_outer_own = picked
    whole, half = ((HALF, 2 * width), F32), ((HALF, 2 * width), BF)
    quarter = ((QUARTER, 2 * width), BF)
    inner_lat, lon_piece = call(
        pack_kernel, [half, quarter], own_fields, own_grads, pick_inner, pick_lon, name="pack", flops=LOAD
    )
    outer_lat, diag_piece, outer_own, inner_own = call(
        pack_rest_kernel, [quarter, quarter, whole, whole],
        lon_piece, own_fields, own_grads, pick_outer, pick_diag, pick_outer_own, pick_own,
        name="pack_rest", flops=5 * 10**8, unread=(0,),
    )
    own_parts = call(
        own_kernel, [((HALF, lanes), F32) for lanes in (width, 3 * width, width)],
        inner_own, qkv_weight, proj_weight,
        name="own", flops=5 * 10**8,
    )
    inner_in = lax.ppermute(inner_lat, both, lat_route)
    lon_in = lax.ppermute(lon_piece, both, lon_route)
    outer_in = lax.ppermute(outer_lat, both, lat_route)
    diag_in = lax.ppermute(diag_piece, both, diag_route)

    split = (lat_size, width // 2, 4 * width // lat_size)
    halves = ((lat_size // 2, *split[1:]), BF)
    chunk = ((lat_size // 2, split[1], split[2] // 2), BF)
    per_window = [
        ((WIN, width), BF),
        ((WIN, width), BF),
        ((2, width // 2, WIN), BF),
        ((WIN, 4 * width), BF),
        ((2, width // 2, WIN), BF),
    ]
    scratch = [pltpu.VMEM((width, WIN), BF)] * 2
    grad_so_far, *inner = call(
        inner_kernel, [(halves[0], F32), *per_window], inner_own, *own_parts, inner_in, qkv_weight, proj_weight,
        name="inner", flops=10**9, scratch=scratch,
    )
    send_a, send_b, *outer = call(
        outer_kernel, [chunk, chunk, *per_window],
        outer_own, lon_in, outer_in, diag_in, qkv_weight, proj_weight, grad_so_far,
        name="outer", flops=10**9, scratch=scratch,
    )
    sibling = [(j, j ^ 1) for j in range(lon_size)]
    arrived = [lax.ppermute(send, "lon", sibling) for send in (send_a, send_b)]
    keep = call(keep_kernel, [chunk, chunk], *inner[2:4], *outer[2:4], name="keep", flops=10**9)

    def halving(phase, send):
        route = [
            (i * lon_size + j, (i ^ (1 << (phase if j % 2 == 0 else bits - 1 - phase))) * lon_size + j)
            for i in range(lat_size)
            for j in range(lon_size)
        ]
        return lax.ppermute(send, both, route)

    bits = lat_size.bit_length() - 1
    sends = [keep[0]]
    for mine, theirs in zip(keep, arrived):
        sends += call(next_sum_kernel, [chunk], sends[-1], mine, theirs, name="chip_sum", unread=(0,))
    sends = sends[1:]
    received = [halving(0, send) for send in sends]
    send_rest, keep_rest = call(
        rest_kernel, [halves, halves], *sends, *inner[2:], *outer[2:], name="rest", unread=(0, 1), beside=True
    )
    received_rest = lax.ppermute(send_rest, "lon", sibling)
    results = call(
        output_kernel, [((WIN, 2 * width), BF)] * 2,
        keep_rest, *inner[:2], inner[3], *outer[:2], outer[3], qkv_weight, proj_weight,
        name="outputs", unread=(0,), flops=10**10,
    )
    (lon_back,) = call(pack_lon_kernel, [quarter], results[1], name="pack_lon", beside=True)
    lon_home = lax.ppermute(lon_back, both, back(lon_route))
    kept = [[keep_rest, received_rest, part] for part in received]
    slots = lat_size // 2
    for phase in range(1, bits):
        slots //= 2
        stay = ((slots, *chunk[0][1:]), BF)
        after = results[0]
        for index in range(2):
            send, keep = call(
                functools.partial(halve_kernel, index), [stay, stay], after, *kept[index],
                after, name=f"halve{slots}", unread=(0, 1 + len(kept[index])),
            )
            kept[index] = [keep, halving(phase, send)]
            after = send

    rows = width // lon_size
    share = ((rows, split[2]), BF)
    (first_chunk,) = call(
        next_sum_kernel, [((1, split[1], split[2] // 2), F32)], lon_home, *kept[0],
        name="first_chunk", flops=LATER, unread=(0,),
    )
    (diag_back,) = call(pack_diag_kernel, [quarter], first_chunk, results[1], name="pack_diag", unread=(0,))
    diag_home = lax.ppermute(diag_back, both, back(diag_route))
    parts = call(
        line_parts_kernel, [share] * (lon_size // 2), first_chunk, *kept[1], name="line_parts", flops=PARTS
    )
    arrived = [
        lax.ppermute(parts[step], "lon", [(j, j ^ (2 * step)) for j in range(lon_size)])
        for step in range(lon_size // 2 - 1, 0, -1)
    ]
    (lat_back,) = call(
        pack_lat_kernel, [((HALF + QUARTER, 2 * width), BF)], parts[1], *results, name="pack_lat", unread=(0,)
    )
    lat_home = lax.ppermute(lat_back, both, back(lat_route))
    (placed,) = call(
        place_kernel, [((TOKENS, 2 * width), F32)], *results, lon_home, diag_home, name="place"
    )
    (line_sum,) = call(
        next_sum_kernel, [share], placed, parts[0], *arrived, name="line_sum", flops=LONG, unread=(0,)
    )
    shared = [
        lax.ppermute(line_sum, "lat", [(i, i ^ step) for i in range(lat_size)]) for step in range(1, lat_size)
    ]
    field_out, d_fields, done = call(
        place_rest_kernel,
        [((TOKENS, width), BF), ((TOKENS, width), BF), ((8, LANES), F32)],
        placed, lat_home,
        name="place_rest",
    )
    qkv_grad, proj_grad = call(
        finish_kernel,
        [((rows, 3 * width), F32), ((rows, width), F32)],
        done, line_sum, *shared,
        name="finish", unread=(0,),
    )
    return (field_out.reshape(fields.shape), d_fields.reshape(fields.shape), qkv_grad, jnp.transpose(proj_grad))


def solution(mesh):
    placed = (P(None, "lat", "lon", None), P(None, "lat", "lon", None), P(), P())
    return jax.shard_map(
        per_device,
        mesh=mesh,
        in_specs=placed,
        out_specs=(
            P(None, "lat", "lon", None),
            P(None, "lat", "lon", None),
            P("lon", None),
            P(None, "lon"),
        ),
        check_vma=False,
    )
```

```python
import functools

import jax
import jax.numpy as jnp
from jax import lax
from jax.experimental import pallas as pl
from jax.experimental.pallas import tpu as pltpu
from jax.sharding import PartitionSpec as P

HEADS = 8
WIN_LAT = 6
WIN_LON = 12
LEVELS = 2
COLS = 24
HALF_LAT = WIN_LAT // 2
HALF_LON = WIN_LON // 2
HALF = LEVELS * HALF_LAT * WIN_LON
WIN = 2 * HALF
TOKENS = 2 * WIN
QUARTER = HALF // 2
LANES = 128

epsilon = 1e-05
LONG = 13 * 10**8
LOAD = 5 * 10**9
LATER = 10**9
PARTS = 5 * 10**9
BF = jnp.bfloat16
F32 = jnp.float32


def dot(a, b, dims):
    return lax.dot_general(a, b, (dims, ((), ())), preferred_element_type=F32)


NN = ((1,), (0,))
NT = ((1,), (1,))
TN = ((0,), (0,))


def div(x, by):
    return (x * ((65536 + by - 1) // by)) >> 16


def own_token(level, row, col):
    return level * (WIN_LAT * COLS) + row * COLS + col


def inner_token(v, first):
    level = div(v, HALF_LAT * WIN_LON)
    rest = v - level * (HALF_LAT * WIN_LON)
    row = div(rest, WIN_LON)
    return own_token(level, first + row, HALF_LON + rest - row * WIN_LON)


def half_token(v, first, col):
    level = div(v, HALF_LAT * HALF_LON)
    rest = v - level * (HALF_LAT * HALF_LON)
    row = div(rest, HALF_LON)
    return jnp.where(v < QUARTER, own_token(level, first + row, col + rest - row * HALF_LON), -1)


def sources():
    even = lax.rem(lax.axis_index("lon"), 2) == 0
    sent = jnp.where(even, 0, HALF_LAT)
    kept = HALF_LAT - sent
    outer = HALF_LON + WIN_LON
    return (
        (lambda v: inner_token(v, sent), HALF),
        (lambda v: half_token(v, sent, outer), QUARTER),
        (lambda v: half_token(v, sent, 0), QUARTER),
        (lambda v: half_token(v, kept, 0), QUARTER),
        (lambda v: inner_token(v, kept), HALF),
        (lambda v: half_token(v, kept, outer), HALF),
    )


def picks(source, rows, columns):
    index = source(lax.broadcasted_iota(jnp.int32, (rows, 1), 0))
    return (index == lax.broadcasted_iota(jnp.int32, (rows, columns), 1)).astype(BF)


def puts(source, rows, columns):
    index = source(lax.broadcasted_iota(jnp.int32, (1, columns), 1))
    return (lax.broadcasted_iota(jnp.int32, (rows, columns), 0) == index).astype(BF)


def first_rows(v):
    return v


def last_rows(v):
    return v - QUARTER


def order_kernel(*outs):
    for out, (source, rows) in zip(outs, sources()):
        out[...] = picks(source, rows, TOKENS)


def pack_kernel(fields, cotangent, *refs):
    count = len(refs) // 2
    width = fields.shape[1]
    for pick, out in zip(refs[:count], refs[count:]):
        out[:, :width] = dot(pick[...], fields[...], NN).astype(out.dtype)
        out[:, width:] = dot(pick[...], cotangent[...], NN).astype(out.dtype)


def swap_bits(index, size, core):
    bits = size.bit_length() - 1
    turned = sum(((index >> b) & 1) << (bits - 1 - b) for b in range(bits))
    return jnp.where(core == 0, index, turned)


def shares(transposed, out, lon, core_of, lon_size):
    rows = transposed.shape[0] // lon_size
    chip = lon >> 1
    for step in range(lon_size // 2):
        start = pl.multiple_of(((chip ^ step) * 2 + core_of) * rows, rows)
        out[step * rows : (step + 1) * rows, :] = transposed[pl.ds(start, rows), :]


def transpose_bf16(block):
    return jnp.transpose(block.astype(F32)).astype(BF)


def slot_product(slot, size, lat, core, windows):
    share = lat ^ swap_bits(slot, size, core)
    total = None
    for left, right in windows:
        lanes = right.shape[1] // size
        of_proj = (share >= 3 * size // 4).astype(jnp.int32)
        part = dot(left[of_proj], right[:, pl.ds(pl.multiple_of(share * lanes, lanes), lanes)], NN)
        total = part if total is None else total + part
    return total


def normalise(x):
    mean = jnp.mean(x, -1, keepdims=True)
    centred = x - mean
    variance = jnp.mean(centred * centred, -1, keepdims=True)
    inv_std = lax.rsqrt(variance + epsilon)
    return centred * inv_std, inv_std


def project(both, qkv_weight, proj_weight):
    width = both.shape[1] // 2
    normed, _ = normalise(both[:, :width])
    projected = dot(normed.astype(BF), qkv_weight[...], NN)
    return normed, projected, dot(both[:, width:].astype(BF), proj_weight[...], NT)


def pack_rest_kernel(_, *refs):
    pack_kernel(*refs)


def own_kernel(inner_own, qkv_weight, proj_weight, normed, projected, d_mixed):
    normed[...], projected[...], d_mixed[...] = project(inner_own[...], qkv_weight, proj_weight)


def inner_kernel(own, own_normed, own_projected, own_d_mixed, lat_in, qkv_weight, proj_weight, send_grad, *refs):
    arrived = lat_in[...].astype(F32)
    parts = project(arrived, qkv_weight, proj_weight)
    both = jnp.concatenate([own[...], arrived], axis=0)
    mine = own_normed, own_projected, own_d_mixed
    parts = [jnp.concatenate([first[...], second], axis=0) for first, second in zip(mine, parts)]
    one_window(both, *parts, *refs)
    *_, right, left, _, _ = refs
    lat, core, size = place()
    for slot in range(1, size, 2):
        send_grad[slot // 2] = slot_product(slot, size, lat, 1 - core, [(left, right)])


def outer_kernel(own, lon_in, diag_in, lat_in, qkv_weight, proj_weight, grad_so_far, send_a, send_b, *refs):
    last = picks(last_rows, HALF, QUARTER)
    both = jnp.concatenate(
        [
            own[...] + dot(last, lon_in[...], NN),
            dot(picks(first_rows, HALF, QUARTER), lat_in[...], NN) + dot(last, diag_in[...], NN),
        ],
        axis=0,
    )
    one_window(both, *project(both, qkv_weight, proj_weight), *refs)
    *_, right, left, _, _ = refs
    lat, core, size = place()
    for slot in range(1, size, 2):
        total = grad_so_far[slot // 2] + slot_product(slot, size, lat, 1 - core, [(left, right)])
        put_chunks((send_a, send_b), slot // 2, total)


def put_chunks(outs, slot, total):
    width = outs[0].shape[2]
    for chunk, out in enumerate(outs):
        out[slot] = total[:, chunk * width : (chunk + 1) * width].astype(BF)


def place():
    return lax.axis_index("lat"), lax.rem(lax.axis_index("lon"), 2), lax.axis_size("lat")


def one_window(
    both, normed, projected, d_mixed,
    windows_out, grads_out, left_keep, right, left_send, normed_t, grads_t,
):
    width = both.shape[1] // 2
    lat, core, lat_size = place()
    lon, lon_size = lax.axis_index("lon"), lax.axis_size("lon")
    even = core == 0
    blocks = both[:, :width], both[:, width:]
    x = blocks[0]
    windows_out[...] = x.astype(BF)
    grads = blocks[1].astype(BF)
    grads_out[...] = grads
    projected, d_mixed = projected.astype(BF), d_mixed.astype(BF)

    head_size = width // HEADS
    factor = head_size ** (-0.5)
    apart = jnp.where(even, lat == lat_size - 1, lat == 0).astype(jnp.int32)
    half_b = (lax.broadcasted_iota(jnp.int32, (WIN, 2 * WIN), 0) >= HALF).astype(jnp.int32)
    at_a = lax.broadcasted_iota(jnp.int32, (WIN, 2 * WIN), 1)
    at_a = jnp.where(at_a >= WIN, at_a - WIN, at_a)
    half_a = (at_a >= HALF).astype(jnp.int32)
    allowed = ((half_a != half_b).astype(jnp.int32) * apart) == 0
    first_head = lax.broadcasted_iota(jnp.int32, (WIN, LANES), 1) < head_size
    zero = jnp.zeros((WIN, LANES), BF)

    def split_heads(block):
        return jnp.concatenate([jnp.where(first_head, block, zero), jnp.where(first_head, zero, block)], axis=0)

    def join_heads(block):
        return jnp.where(first_head, block[:WIN], block[WIN:]).astype(BF)

    pairs = range(width // LANES)

    def blocks_of(array, lanes_from):
        return [array[:, lanes_from + pair * LANES : lanes_from + (pair + 1) * LANES] for pair in pairs]

    def store(out, lanes_from, blocks):
        for pair, block in zip(pairs, blocks):
            out[:, lanes_from + pair * LANES : lanes_from + (pair + 1) * LANES] = block.astype(out.dtype)

    k, v = blocks_of(projected, width), blocks_of(projected, 2 * width)
    q2 = [split_heads(block) for block in blocks_of(projected, 0)]
    dm2 = [split_heads(block) for block in blocks_of(d_mixed, 0)]
    scores = [jnp.where(allowed, dot(k[p], q2[p], NT) * factor, -1e30) for p in pairs]
    d_probs = [dot(v[p], dm2[p], NT) for p in pairs]
    exponents = [jnp.exp(s - jnp.max(s, 0, keepdims=True)) for s in scores]
    probs = [e * (1.0 / jnp.sum(e, 0, keepdims=True)) for e in exponents]
    probs_b = [p.astype(BF) for p in probs]
    store(right, 3 * width, [join_heads(dot(probs_b[p], v[p], TN)) for p in pairs])
    store(right, 2 * width, [dot(probs_b[p], dm2[p], NN) for p in pairs])
    d_scores = [
        (probs[p] * (d_probs[p] - jnp.sum(d_probs[p] * probs[p], 0, keepdims=True)) * factor).astype(BF)
        for p in pairs
    ]
    store(right, 0, [join_heads(dot(d_scores[p], k[p], TN)) for p in pairs])
    store(right, width, [dot(d_scores[p], q2[p], NN) for p in pairs])

    normed_t[...] = transpose_bf16(normed)
    grads_t[...] = transpose_bf16(grads)
    for index, source in enumerate((normed_t, grads_t)):
        shares(source, left_send.at[index], lon, 1 - core, lon_size)
        shares(source, left_keep.at[index], lon, core, lon_size)


def keep_kernel(*refs):
    *windows, keep_a, keep_b = refs
    windows = [windows[:2], windows[2:]]
    lat, core, size = place()
    for slot in range(1, size, 2):
        put_chunks((keep_a, keep_b), slot // 2, slot_product(slot, size, lat, core, windows))


def rest_kernel(_, __, *refs):
    *windows, send_rest, keep_rest = refs
    windows = windows[:3], windows[3:]
    lat, core, size = place()
    for slot in range(0, size, 2):
        send_rest[slot // 2] = slot_product(slot, size, lat, 1 - core, [(w[2], w[1]) for w in windows]).astype(BF)
    for slot in range(0, size, 2):
        keep_rest[slot // 2] = slot_product(slot, size, lat, core, [(w[0], w[1]) for w in windows]).astype(BF)


def output_kernel(_, *refs):
    (*windows, qkv_weight, proj_weight, inner_results, outer_results) = refs
    per_window = windows[:3], windows[3:]
    width = proj_weight.shape[0]
    x, grads, right = (jnp.concatenate([w[i][...] for w in per_window], axis=0) for i in range(3))
    d_projected, mixed = right[:, : 3 * width], right[:, 3 * width :]
    x = x.astype(F32)
    normed, inv_std = normalise(x)
    output = (x + dot(mixed, proj_weight[...], NN)).astype(BF)
    d_normed = dot(d_projected, qkv_weight[...], NT)
    d_inputs = grads.astype(F32) + inv_std * (
        d_normed
        - jnp.mean(d_normed, -1, keepdims=True)
        - normed * jnp.mean(d_normed * normed, -1, keepdims=True)
    )
    d_inputs = d_inputs.astype(BF)
    for at, out in ((0, inner_results), (WIN, outer_results)):
        out[:, :width] = output[at : at + WIN]
        out[:, width:] = d_inputs[at : at + WIN]


def pack_lon_kernel(outer_results, lon_out):
    outer_x = outer_results[...].astype(F32)[:HALF].astype(BF)
    lon_out[...] = dot(puts(last_rows, QUARTER, HALF), outer_x, NN).astype(BF)


def pack_diag_kernel(_, outer_results, diag_out):
    outer_y = outer_results[...].astype(F32)[HALF:].astype(BF)
    diag_out[...] = dot(puts(last_rows, QUARTER, HALF), outer_y, NN).astype(BF)


def pack_lat_kernel(_, inner_results, outer_results, lat_out):
    inner_y = inner_results[...].astype(F32)[HALF:]
    outer_y = outer_results[...].astype(F32)[HALF:].astype(BF)
    lat_out[...] = jnp.concatenate([inner_y, dot(puts(first_rows, QUARTER, HALF), outer_y, NN)], axis=0).astype(BF)


def place_kernel(inner_results, outer_results, lon_in, diag_in, placed):
    _, _, lon, diag, inner_own, outer_own = (source for source, _ in sources())

    def only_first(source):
        return lambda v: jnp.where(v < HALF, source(v), -1)

    placed[...] = (
        dot(puts(only_first(inner_own), TOKENS, WIN), inner_results[...], NN)
        + dot(puts(only_first(outer_own), TOKENS, WIN), outer_results[...], NN)
        + dot(puts(lon, TOKENS, QUARTER), lon_in[...], NN)
        + dot(puts(diag, TOKENS, QUARTER), diag_in[...], NN)
    )


def place_rest_kernel(placed, lat_in, field_out, d_fields, done):
    done[...] = jnp.zeros_like(done)
    width = field_out.shape[1]
    inner_lat, outer_lat, *_ = (source for source, _ in sources())

    def lat(v):
        return jnp.where(v < HALF, inner_lat(v), outer_lat(v - HALF))

    total = (placed[...] + dot(puts(lat, TOKENS, HALF + QUARTER), lat_in[...], NN)).astype(BF)
    field_out[...] = total[:, :width]
    d_fields[...] = total[:, width:]


def halve_kernel(chunk, _, *refs):
    *parts, _, send, keep = refs
    width = send.shape[2]

    def lanes(part):
        return slice(None) if part.shape[2] == width else slice(chunk * width, (chunk + 1) * width)

    for slot in range(send.shape[0]):
        for out, source in ((send, 2 * slot + 1), (keep, 2 * slot)):
            out[slot] = sum(part[source, :, lanes(part)].astype(F32) for part in parts).astype(BF)


def line_parts_kernel(*refs):
    chunks, (keep, *sends) = (refs[:1], refs[1:3]), refs[3:]
    rows = keep.shape[0]
    for step, out in enumerate((keep, *sends)):
        at = slice(step * rows, (step + 1) * rows)
        totals = [sum(part[0, at].astype(F32) for part in parts) for parts in chunks]
        out[...] = jnp.concatenate(totals, axis=1).astype(out.dtype)


def next_sum_kernel(_, *refs):
    sum_kernel(*refs)


def sum_kernel(*refs):
    *parts, out = refs
    total = parts[0][...].astype(F32)
    for part in parts[1:]:
        total = total + part[...].astype(F32)
    out[...] = total.astype(out.dtype)


def finish_kernel(_, *refs):
    *parts, qkv_out, proj_out = refs
    lat, _, size = place()
    width = parts[0].shape[1]
    for step, part in enumerate(parts):
        share = lat ^ step
        total = part[...].astype(F32)
        of_qkv = 3 * size // 4

        @pl.when(share < of_qkv)
        def _():
            qkv_out[:, pl.ds(pl.multiple_of(share * width, width), width)] = total

        @pl.when(share >= of_qkv)
        def _():
            proj_out[:, pl.ds(pl.multiple_of((share - of_qkv) * width, width), width)] = total


def call(kernel, outs, *args, name, flops=0, limit=32, scratch=(), unread=(), beside=False):
    vmem = pl.BlockSpec(memory_space=pltpu.VMEM)
    anywhere = pl.BlockSpec(memory_space=pl.ANY)
    shapes = [jax.ShapeDtypeStruct(shape, dtype) for shape, dtype in outs]
    nbytes = 0 if beside else sum(a.size * a.dtype.itemsize for a in (*args, *shapes))
    return pl.pallas_call(
        kernel,
        out_shape=shapes,
        in_specs=[anywhere if i in unread else vmem for i in range(len(args))],
        out_specs=[vmem] * len(shapes),
        scratch_shapes=scratch,
        compiler_params=pltpu.CompilerParams(vmem_limit_bytes=limit * 2**20),
        cost_estimate=pl.CostEstimate(flops=flops, bytes_accessed=nbytes, transcendentals=0),
        name=name,
    )(*args)


def routes(lat_size, lon_size):
    lat, lon, diag = [], [], []
    for i in range(lat_size):
        for j in range(lon_size):
            step = -1 if j % 2 == 0 else 1
            before = (j - 1) % lon_size
            me = i * lon_size + j
            lat.append((me, ((i + step) % lat_size) * lon_size + j))
            lon.append((me, i * lon_size + before))
            diag.append((me, ((i - step) % lat_size) * lon_size + before))
    return lat, lon, diag


def per_device(fields, cotangent, qkv_weight, proj_weight):
    levels, row_count, col_count, width = fields.shape
    lat_size, lon_size = lax.axis_size("lat"), lax.axis_size("lon")
    both = ("lat", "lon")
    lat_route, lon_route, diag_route = routes(lat_size, lon_size)

    def back(route):
        return [(target, source) for source, target in route]

    own_fields = fields.reshape(TOKENS, width)
    own_grads = cotangent.reshape(TOKENS, width)
    lengths = (HALF, QUARTER, QUARTER, QUARTER, HALF, HALF)
    picked = call(order_kernel, [((rows, TOKENS), BF) for rows in lengths], name="order", flops=LOAD)
    pick_inner, pick_outer, pick_lon, pick_diag, pick_own, pick_outer_own = picked
    whole, half = ((HALF, 2 * width), F32), ((HALF, 2 * width), BF)
    quarter = ((QUARTER, 2 * width), BF)
    inner_lat, lon_piece = call(
        pack_kernel, [half, quarter], own_fields, own_grads, pick_inner, pick_lon, name="pack", flops=LOAD
    )
    outer_lat, diag_piece, outer_own, inner_own = call(
        pack_rest_kernel, [quarter, quarter, whole, whole],
        lon_piece, own_fields, own_grads, pick_outer, pick_diag, pick_outer_own, pick_own,
        name="pack_rest", flops=5 * 10**8, unread=(0,),
    )
    own_parts = call(
        own_kernel, [((HALF, lanes), F32) for lanes in (width, 3 * width, width)],
        inner_own, qkv_weight, proj_weight,
        name="own", flops=5 * 10**8,
    )
    inner_in = lax.ppermute(inner_lat, both, lat_route)
    lon_in = lax.ppermute(lon_piece, both, lon_route)
    outer_in = lax.ppermute(outer_lat, both, lat_route)
    diag_in = lax.ppermute(diag_piece, both, diag_route)

    split = (lat_size, width // 2, 4 * width // lat_size)
    halves = ((lat_size // 2, *split[1:]), BF)
    chunk = ((lat_size // 2, split[1], split[2] // 2), BF)
    per_window = [
        ((WIN, width), BF),
        ((WIN, width), BF),
        ((2, width // 2, WIN), BF),
        ((WIN, 4 * width), BF),
        ((2, width // 2, WIN), BF),
    ]
    scratch = [pltpu.VMEM((width, WIN), BF)] * 2
    grad_so_far, *inner = call(
        inner_kernel, [(halves[0], F32), *per_window], inner_own, *own_parts, inner_in, qkv_weight, proj_weight,
        name="inner", flops=10**9, scratch=scratch,
    )
    send_a, send_b, *outer = call(
        outer_kernel, [chunk, chunk, *per_window],
        outer_own, lon_in, diag_in, outer_in, qkv_weight, proj_weight, grad_so_far,
        name="outer", flops=10**9, scratch=scratch,
    )
    sibling = [(j, j ^ 1) for j in range(lon_size)]
    arrived = [lax.ppermute(send, "lon", sibling) for send in (send_a, send_b)]
    keep = call(keep_kernel, [chunk, chunk], *inner[2:4], *outer[2:4], name="keep", flops=10**9)

    def halving(phase, send):
        route = [
            (i * lon_size + j, (i ^ (1 << (phase if j % 2 == 0 else bits - 1 - phase))) * lon_size + j)
            for i in range(lat_size)
            for j in range(lon_size)
        ]
        return lax.ppermute(send, both, route)

    bits = lat_size.bit_length() - 1
    sends = [keep[0]]
    for mine, theirs in zip(keep, arrived):
        sends += call(next_sum_kernel, [chunk], sends[-1], mine, theirs, name="chip_sum", unread=(0,))
    sends = sends[1:]
    received = [halving(0, send) for send in sends]
    send_rest, keep_rest = call(
        rest_kernel, [halves, halves], *sends, *inner[2:], *outer[2:], name="rest", unread=(0, 1), beside=True
    )
    received_rest = lax.ppermute(send_rest, "lon", sibling)
    results = call(
        output_kernel, [((WIN, 2 * width), BF)] * 2,
        keep_rest, *inner[:2], inner[3], *outer[:2], outer[3], qkv_weight, proj_weight,
        name="outputs", unread=(0,), flops=10**10,
    )
    (lon_back,) = call(pack_lon_kernel, [quarter], results[1], name="pack_lon", beside=True)
    lon_home = lax.ppermute(lon_back, both, back(lon_route))
    kept = [[keep_rest, received_rest, part] for part in received]
    slots = lat_size // 2
    for phase in range(1, bits):
        slots //= 2
        stay = ((slots, *chunk[0][1:]), BF)
        after = results[0]
        for index in range(2):
            send, keep = call(
                functools.partial(halve_kernel, index), [stay, stay], after, *kept[index],
                after, name=f"halve{slots}", unread=(0, 1 + len(kept[index])),
            )
            kept[index] = [keep, halving(phase, send)]
            after = send

    (diag_back,) = call(pack_diag_kernel, [quarter], send, results[1], name="pack_diag", unread=(0,))
    diag_home = lax.ppermute(diag_back, both, back(diag_route))

    rows = width // lon_size
    share = ((rows, split[2]), BF)
    (first_chunk,) = call(
        next_sum_kernel, [((1, split[1], split[2] // 2), F32)], lon_home, *kept[0],
        name="first_chunk", flops=LATER, unread=(0,),
    )
    parts = call(
        line_parts_kernel, [share] * (lon_size // 2), first_chunk, *kept[1], name="line_parts", flops=PARTS
    )
    arrived = [
        lax.ppermute(parts[step], "lon", [(j, j ^ (2 * step)) for j in range(lon_size)])
        for step in range(lon_size // 2 - 1, 0, -1)
    ]
    (lat_back,) = call(
        pack_lat_kernel, [((HALF + QUARTER, 2 * width), BF)], parts[1], *results, name="pack_lat", unread=(0,)
    )
    lat_home = lax.ppermute(lat_back, both, back(lat_route))
    (placed,) = call(
        place_kernel, [((TOKENS, 2 * width), F32)], *results, lon_home, diag_home, name="place"
    )
    (line_sum,) = call(
        next_sum_kernel, [share], placed, parts[0], *arrived, name="line_sum", flops=LONG, unread=(0,)
    )
    shared = [
        lax.ppermute(line_sum, "lat", [(i, i ^ step) for i in range(lat_size)]) for step in range(1, lat_size)
    ]
    field_out, d_fields, done = call(
        place_rest_kernel,
        [((TOKENS, width), BF), ((TOKENS, width), BF), ((8, LANES), F32)],
        placed, lat_home,
        name="place_rest",
    )
    qkv_grad, proj_grad = call(
        finish_kernel,
        [((rows, 3 * width), F32), ((rows, width), F32)],
        done, line_sum, *shared,
        name="finish", unread=(0,),
    )
    return (field_out.reshape(fields.shape), d_fields.reshape(fields.shape), qkv_grad, jnp.transpose(proj_grad))


def solution(mesh):
    placed = (P(None, "lat", "lon", None), P(None, "lat", "lon", None), P(), P())
    return jax.shard_map(
        per_device,
        mesh=mesh,
        in_specs=placed,
        out_specs=(
            P(None, "lat", "lon", None),
            P(None, "lat", "lon", None),
            P("lon", None),
            P(None, "lon"),
        ),
        check_vma=False,
    )
```

```python
import functools

import jax
import jax.numpy as jnp
from jax import lax
from jax.experimental import pallas as pl
from jax.experimental.pallas import tpu as pltpu
from jax.sharding import PartitionSpec as P

HEADS = 8
WIN_LAT = 6
WIN_LON = 12
LEVELS = 2
COLS = 24
HALF_LAT = WIN_LAT // 2
HALF_LON = WIN_LON // 2
HALF = LEVELS * HALF_LAT * WIN_LON
WIN = 2 * HALF
TOKENS = 2 * WIN
QUARTER = HALF // 2
LANES = 128
FINISH_ROWS = 16

epsilon = 1e-05
LONG = 13 * 10**8
LOAD = 5 * 10**9
LATER = 10**9
PARTS = 5 * 10**9
BF = jnp.bfloat16
F32 = jnp.float32


def dot(a, b, dims):
    return lax.dot_general(a, b, (dims, ((), ())), preferred_element_type=F32)


NN = ((1,), (0,))
NT = ((1,), (1,))
TN = ((0,), (0,))


def div(x, by):
    return (x * ((65536 + by - 1) // by)) >> 16


def own_token(level, row, col):
    return level * (WIN_LAT * COLS) + row * COLS + col


def inner_token(v, first):
    level = div(v, HALF_LAT * WIN_LON)
    rest = v - level * (HALF_LAT * WIN_LON)
    row = div(rest, WIN_LON)
    return own_token(level, first + row, HALF_LON + rest - row * WIN_LON)


def half_token(v, first, col):
    level = div(v, HALF_LAT * HALF_LON)
    rest = v - level * (HALF_LAT * HALF_LON)
    row = div(rest, HALF_LON)
    return jnp.where(v < QUARTER, own_token(level, first + row, col + rest - row * HALF_LON), -1)


def sources():
    even = lax.rem(lax.axis_index("lon"), 2) == 0
    sent = jnp.where(even, 0, HALF_LAT)
    kept = HALF_LAT - sent
    outer = HALF_LON + WIN_LON
    return (
        (lambda v: inner_token(v, sent), HALF),
        (lambda v: half_token(v, sent, outer), QUARTER),
        (lambda v: half_token(v, sent, 0), QUARTER),
        (lambda v: half_token(v, kept, 0), QUARTER),
        (lambda v: inner_token(v, kept), HALF),
        (lambda v: half_token(v, kept, outer), HALF),
    )


def picks(source, rows, columns):
    index = source(lax.broadcasted_iota(jnp.int32, (rows, 1), 0))
    return (index == lax.broadcasted_iota(jnp.int32, (rows, columns), 1)).astype(BF)


def puts(source, rows, columns):
    index = source(lax.broadcasted_iota(jnp.int32, (1, columns), 1))
    return (lax.broadcasted_iota(jnp.int32, (rows, columns), 0) == index).astype(BF)


def first_rows(v):
    return v


def last_rows(v):
    return v - QUARTER


def order_kernel(*outs):
    for out, (source, rows) in zip(outs, sources()):
        out[...] = picks(source, rows, TOKENS)


def pack_kernel(fields, cotangent, *refs):
    count = len(refs) // 2
    width = fields.shape[1]
    for pick, out in zip(refs[:count], refs[count:]):
        out[:, :width] = dot(pick[...], fields[...], NN).astype(out.dtype)
        out[:, width:] = dot(pick[...], cotangent[...], NN).astype(out.dtype)


def swap_bits(index, size, core):
    bits = size.bit_length() - 1
    turned = sum(((index >> b) & 1) << (bits - 1 - b) for b in range(bits))
    return jnp.where(core == 0, index, turned)


def shares(transposed, out, lon, core_of, lon_size):
    rows = transposed.shape[0] // lon_size
    chip = lon >> 1
    for step in range(lon_size // 2):
        start = pl.multiple_of(((chip ^ step) * 2 + core_of) * rows, rows)
        out[step * rows : (step + 1) * rows, :] = transposed[pl.ds(start, rows), :]


def transpose_bf16(block):
    return jnp.transpose(block.astype(F32)).astype(BF)


def slot_product(slot, size, lat, core, windows):
    share = lat ^ swap_bits(slot, size, core)
    total = None
    for left, right in windows:
        lanes = right.shape[1] // size
        of_proj = (share >= 3 * size // 4).astype(jnp.int32)
        part = dot(left[of_proj], right[:, pl.ds(pl.multiple_of(share * lanes, lanes), lanes)], NN)
        total = part if total is None else total + part
    return total


def normalise(x):
    mean = jnp.mean(x, -1, keepdims=True)
    centred = x - mean
    variance = jnp.mean(centred * centred, -1, keepdims=True)
    inv_std = lax.rsqrt(variance + epsilon)
    return centred * inv_std, inv_std


def project(both, qkv_weight, proj_weight):
    width = both.shape[1] // 2
    normed, _ = normalise(both[:, :width])
    projected = dot(normed.astype(BF), qkv_weight[...], NN)
    return normed, projected, dot(both[:, width:].astype(BF), proj_weight[...], NT)


def pack_rest_kernel(_, *refs):
    pack_kernel(*refs)


def own_kernel(inner_own, qkv_weight, proj_weight, normed, projected, d_mixed):
    normed[...], projected[...], d_mixed[...] = project(inner_own[...], qkv_weight, proj_weight)


def inner_kernel(own, own_normed, own_projected, own_d_mixed, lat_in, qkv_weight, proj_weight, send_grad, *refs):
    arrived = lat_in[...].astype(F32)
    parts = project(arrived, qkv_weight, proj_weight)
    both = jnp.concatenate([own[...], arrived], axis=0)
    mine = own_normed, own_projected, own_d_mixed
    parts = [jnp.concatenate([first[...], second], axis=0) for first, second in zip(mine, parts)]
    one_window(both, *parts, *refs)
    *_, right, left, _, _ = refs
    lat, core, size = place()
    for slot in range(1, size, 2):
        send_grad[slot // 2] = slot_product(slot, size, lat, 1 - core, [(left, right)])


def outer_kernel(own, lon_in, lat_in, diag_in, qkv_weight, proj_weight, grad_so_far, send_a, send_b, *refs):
    last = picks(last_rows, HALF, QUARTER)
    both = jnp.concatenate(
        [
            own[...] + dot(last, lon_in[...], NN),
            dot(picks(first_rows, HALF, QUARTER), lat_in[...], NN) + dot(last, diag_in[...], NN),
        ],
        axis=0,
    )
    one_window(both, *project(both, qkv_weight, proj_weight), *refs)
    *_, right, left, _, _ = refs
    lat, core, size = place()
    for slot in range(1, size, 2):
        total = grad_so_far[slot // 2] + slot_product(slot, size, lat, 1 - core, [(left, right)])
        put_chunks((send_a, send_b), slot // 2, total)


def put_chunks(outs, slot, total):
    width = outs[0].shape[2]
    for chunk, out in enumerate(outs):
        out[slot] = total[:, chunk * width : (chunk + 1) * width].astype(BF)


def place():
    return lax.axis_index("lat"), lax.rem(lax.axis_index("lon"), 2), lax.axis_size("lat")


def one_window(
    both, normed, projected, d_mixed,
    windows_out, grads_out, left_keep, right, left_send, normed_t, grads_t,
):
    width = both.shape[1] // 2
    lat, core, lat_size = place()
    lon, lon_size = lax.axis_index("lon"), lax.axis_size("lon")
    even = core == 0
    blocks = both[:, :width], both[:, width:]
    x = blocks[0]
    windows_out[...] = x.astype(BF)
    grads = blocks[1].astype(BF)
    grads_out[...] = grads
    projected, d_mixed = projected.astype(BF), d_mixed.astype(BF)

    head_size = width // HEADS
    factor = head_size ** (-0.5)
    apart = jnp.where(even, lat == lat_size - 1, lat == 0).astype(jnp.int32)
    half_b = (lax.broadcasted_iota(jnp.int32, (WIN, 2 * WIN), 0) >= HALF).astype(jnp.int32)
    at_a = lax.broadcasted_iota(jnp.int32, (WIN, 2 * WIN), 1)
    at_a = jnp.where(at_a >= WIN, at_a - WIN, at_a)
    half_a = (at_a >= HALF).astype(jnp.int32)
    allowed = ((half_a != half_b).astype(jnp.int32) * apart) == 0
    first_head = lax.broadcasted_iota(jnp.int32, (WIN, LANES), 1) < head_size
    zero = jnp.zeros((WIN, LANES), BF)

    def split_heads(block):
        return jnp.concatenate([jnp.where(first_head, block, zero), jnp.where(first_head, zero, block)], axis=0)

    def join_heads(block):
        return jnp.where(first_head, block[:WIN], block[WIN:]).astype(BF)

    pairs = range(width // LANES)

    def blocks_of(array, lanes_from):
        return [array[:, lanes_from + pair * LANES : lanes_from + (pair + 1) * LANES] for pair in pairs]

    def store(out, lanes_from, blocks):
        for pair, block in zip(pairs, blocks):
            out[:, lanes_from + pair * LANES : lanes_from + (pair + 1) * LANES] = block.astype(out.dtype)

    k, v = blocks_of(projected, width), blocks_of(projected, 2 * width)
    q2 = [split_heads(block) for block in blocks_of(projected, 0)]
    dm2 = [split_heads(block) for block in blocks_of(d_mixed, 0)]
    scores = [jnp.where(allowed, dot(k[p], q2[p], NT) * factor, -1e30) for p in pairs]
    d_probs = [dot(v[p], dm2[p], NT) for p in pairs]
    exponents = [jnp.exp(s - jnp.max(s, 0, keepdims=True)) for s in scores]
    probs = [e * (1.0 / jnp.sum(e, 0, keepdims=True)) for e in exponents]
    probs_b = [p.astype(BF) for p in probs]
    store(right, 3 * width, [join_heads(dot(probs_b[p], v[p], TN)) for p in pairs])
    store(right, 2 * width, [dot(probs_b[p], dm2[p], NN) for p in pairs])
    d_scores = [
        (probs[p] * (d_probs[p] - jnp.sum(d_probs[p] * probs[p], 0, keepdims=True)) * factor).astype(BF)
        for p in pairs
    ]
    store(right, 0, [join_heads(dot(d_scores[p], k[p], TN)) for p in pairs])
    store(right, width, [dot(d_scores[p], q2[p], NN) for p in pairs])

    normed_t[...] = transpose_bf16(normed)
    grads_t[...] = transpose_bf16(grads)
    for index, source in enumerate((normed_t, grads_t)):
        shares(source, left_send.at[index], lon, 1 - core, lon_size)
        shares(source, left_keep.at[index], lon, core, lon_size)


def keep_kernel(*refs):
    *windows, keep_a, keep_b = refs
    windows = [windows[:2], windows[2:]]
    lat, core, size = place()
    for slot in range(1, size, 2):
        put_chunks((keep_a, keep_b), slot // 2, slot_product(slot, size, lat, core, windows))


def rest_kernel(_, __, *refs):
    *windows, send_rest, keep_rest = refs
    windows = windows[:3], windows[3:]
    lat, core, size = place()
    for slot in range(0, size, 2):
        send_rest[slot // 2] = slot_product(slot, size, lat, 1 - core, [(w[2], w[1]) for w in windows]).astype(BF)
    for slot in range(0, size, 2):
        keep_rest[slot // 2] = slot_product(slot, size, lat, core, [(w[0], w[1]) for w in windows]).astype(BF)


def output_kernel(_, *refs):
    (*windows, qkv_weight, proj_weight, inner_results, outer_results) = refs
    per_window = windows[:3], windows[3:]
    width = proj_weight.shape[0]
    x, grads, right = (jnp.concatenate([w[i][...] for w in per_window], axis=0) for i in range(3))
    d_projected, mixed = right[:, : 3 * width], right[:, 3 * width :]
    x = x.astype(F32)
    normed, inv_std = normalise(x)
    output = (x + dot(mixed, proj_weight[...], NN)).astype(BF)
    d_normed = dot(d_projected, qkv_weight[...], NT)
    d_inputs = grads.astype(F32) + inv_std * (
        d_normed
        - jnp.mean(d_normed, -1, keepdims=True)
        - normed * jnp.mean(d_normed * normed, -1, keepdims=True)
    )
    d_inputs = d_inputs.astype(BF)
    for at, out in ((0, inner_results), (WIN, outer_results)):
        out[:, :width] = output[at : at + WIN]
        out[:, width:] = d_inputs[at : at + WIN]


def pack_lon_kernel(outer_results, lon_out):
    outer_x = outer_results[...].astype(F32)[:HALF].astype(BF)
    lon_out[...] = dot(puts(last_rows, QUARTER, HALF), outer_x, NN).astype(BF)


def pack_diag_kernel(_, outer_results, diag_out):
    outer_y = outer_results[...].astype(F32)[HALF:].astype(BF)
    diag_out[...] = dot(puts(last_rows, QUARTER, HALF), outer_y, NN).astype(BF)


def pack_lat_kernel(_, inner_results, outer_results, lat_out):
    inner_y = inner_results[...].astype(F32)[HALF:]
    outer_y = outer_results[...].astype(F32)[HALF:].astype(BF)
    lat_out[...] = jnp.concatenate([inner_y, dot(puts(first_rows, QUARTER, HALF), outer_y, NN)], axis=0).astype(BF)


def place_kernel(inner_results, outer_results, lon_in, diag_in, placed):
    _, _, lon, diag, inner_own, outer_own = (source for source, _ in sources())

    def only_first(source):
        return lambda v: jnp.where(v < HALF, source(v), -1)

    placed[...] = (
        dot(puts(only_first(inner_own), TOKENS, WIN), inner_results[...], NN)
        + dot(puts(only_first(outer_own), TOKENS, WIN), outer_results[...], NN)
        + dot(puts(lon, TOKENS, QUARTER), lon_in[...], NN)
        + dot(puts(diag, TOKENS, QUARTER), diag_in[...], NN)
    )


def place_rest_kernel(placed, lat_in, field_out, d_fields, done):
    done[...] = jnp.zeros_like(done)
    width = field_out.shape[1]
    inner_lat, outer_lat, *_ = (source for source, _ in sources())

    def lat(v):
        return jnp.where(v < HALF, inner_lat(v), outer_lat(v - HALF))

    total = (placed[...] + dot(puts(lat, TOKENS, HALF + QUARTER), lat_in[...], NN)).astype(BF)
    field_out[...] = total[:, :width]
    d_fields[...] = total[:, width:]


def halve_kernel(chunk, _, *refs):
    *parts, _, send, keep = refs
    width = send.shape[2]

    def lanes(part):
        return slice(None) if part.shape[2] == width else slice(chunk * width, (chunk + 1) * width)

    for slot in range(send.shape[0]):
        for out, source in ((send, 2 * slot + 1), (keep, 2 * slot)):
            out[slot] = sum(part[source, :, lanes(part)].astype(F32) for part in parts).astype(BF)


def line_parts_kernel(*refs):
    chunks, (keep, *sends) = (refs[:1], refs[1:3]), refs[3:]
    rows = keep.shape[0]
    for step, out in enumerate((keep, *sends)):
        at = slice(step * rows, (step + 1) * rows)
        totals = [sum(part[0, at].astype(F32) for part in parts) for parts in chunks]
        out[...] = jnp.concatenate(totals, axis=1).astype(out.dtype)


def next_sum_kernel(_, *refs):
    sum_kernel(*refs)


def sum_kernel(*refs):
    *parts, out = refs
    total = parts[0][...].astype(F32)
    for part in parts[1:]:
        total = total + part[...].astype(F32)
    out[...] = total.astype(out.dtype)


def finish_kernel(_, *refs):
    *parts, qkv_out, proj_out, total, done = refs
    lat = lax.axis_index("lat")
    width, split = parts[0].shape[1], qkv_out.shape[1]
    copies = []
    for block in range(total.shape[0] // FINISH_ROWS):
        rows = slice(block * FINISH_ROWS, (block + 1) * FINISH_ROWS)
        for step, part in enumerate(parts):
            total[rows, pl.ds(pl.multiple_of((lat ^ step) * width, width), width)] = part[rows, :].astype(F32)
        for index, (out, lanes) in enumerate(((qkv_out, slice(0, split)), (proj_out, slice(split, total.shape[1])))):
            copies.append(pltpu.make_async_copy(total.at[rows, lanes], out.at[rows, :], done.at[block, index]))
            copies[-1].start()
    for copy in copies:
        copy.wait()


def call(kernel, outs, *args, name, flops=0, limit=32, scratch=(), unread=(), beside=False):
    vmem = pl.BlockSpec(memory_space=pltpu.VMEM)
    anywhere = pl.BlockSpec(memory_space=pl.ANY)
    shapes = [jax.ShapeDtypeStruct(shape, dtype) for shape, dtype in outs]
    nbytes = 0 if beside else sum(a.size * a.dtype.itemsize for a in (*args, *shapes))
    return pl.pallas_call(
        kernel,
        out_shape=shapes,
        in_specs=[anywhere if i in unread else vmem for i in range(len(args))],
        out_specs=[vmem] * len(shapes),
        scratch_shapes=scratch,
        compiler_params=pltpu.CompilerParams(vmem_limit_bytes=limit * 2**20),
        cost_estimate=pl.CostEstimate(flops=flops, bytes_accessed=nbytes, transcendentals=0),
        name=name,
    )(*args)


def routes(lat_size, lon_size):
    lat, lon, diag = [], [], []
    for i in range(lat_size):
        for j in range(lon_size):
            step = -1 if j % 2 == 0 else 1
            before = (j - 1) % lon_size
            me = i * lon_size + j
            lat.append((me, ((i + step) % lat_size) * lon_size + j))
            lon.append((me, i * lon_size + before))
            diag.append((me, ((i - step) % lat_size) * lon_size + before))
    return lat, lon, diag


def per_device(fields, cotangent, qkv_weight, proj_weight):
    levels, row_count, col_count, width = fields.shape
    lat_size, lon_size = lax.axis_size("lat"), lax.axis_size("lon")
    both = ("lat", "lon")
    lat_route, lon_route, diag_route = routes(lat_size, lon_size)

    def back(route):
        return [(target, source) for source, target in route]

    own_fields = fields.reshape(TOKENS, width)
    own_grads = cotangent.reshape(TOKENS, width)
    lengths = (HALF, QUARTER, QUARTER, QUARTER, HALF, HALF)
    picked = call(order_kernel, [((rows, TOKENS), BF) for rows in lengths], name="order", flops=LOAD)
    pick_inner, pick_outer, pick_lon, pick_diag, pick_own, pick_outer_own = picked
    whole, half = ((HALF, 2 * width), F32), ((HALF, 2 * width), BF)
    quarter = ((QUARTER, 2 * width), BF)
    inner_lat, lon_piece = call(
        pack_kernel, [half, quarter], own_fields, own_grads, pick_inner, pick_lon, name="pack", flops=LOAD
    )
    outer_lat, diag_piece, outer_own, inner_own = call(
        pack_rest_kernel, [quarter, quarter, whole, whole],
        lon_piece, own_fields, own_grads, pick_outer, pick_diag, pick_outer_own, pick_own,
        name="pack_rest", flops=5 * 10**8, unread=(0,),
    )
    own_parts = call(
        own_kernel, [((HALF, lanes), F32) for lanes in (width, 3 * width, width)],
        inner_own, qkv_weight, proj_weight,
        name="own", flops=5 * 10**8,
    )
    inner_in = lax.ppermute(inner_lat, both, lat_route)
    lon_in = lax.ppermute(lon_piece, both, lon_route)
    outer_in = lax.ppermute(outer_lat, both, lat_route)
    diag_in = lax.ppermute(diag_piece, both, diag_route)

    split = (lat_size, width // 2, 4 * width // lat_size)
    halves = ((lat_size // 2, *split[1:]), BF)
    chunk = ((lat_size // 2, split[1], split[2] // 2), BF)
    per_window = [
        ((WIN, width), BF),
        ((WIN, width), BF),
        ((2, width // 2, WIN), BF),
        ((WIN, 4 * width), BF),
        ((2, width // 2, WIN), BF),
    ]
    scratch = [pltpu.VMEM((width, WIN), BF)] * 2
    grad_so_far, *inner = call(
        inner_kernel, [(halves[0], F32), *per_window], inner_own, *own_parts, inner_in, qkv_weight, proj_weight,
        name="inner", flops=10**9, scratch=scratch,
    )
    send_a, send_b, *outer = call(
        outer_kernel, [chunk, chunk, *per_window],
        outer_own, lon_in, outer_in, diag_in, qkv_weight, proj_weight, grad_so_far,
        name="outer", flops=10**9, scratch=scratch,
    )
    sibling = [(j, j ^ 1) for j in range(lon_size)]
    arrived = [lax.ppermute(send, "lon", sibling) for send in (send_a, send_b)]
    keep = call(keep_kernel, [chunk, chunk], *inner[2:4], *outer[2:4], name="keep", flops=10**9)

    def halving(phase, send):
        route = [
            (i * lon_size + j, (i ^ (1 << (phase if j % 2 == 0 else bits - 1 - phase))) * lon_size + j)
            for i in range(lat_size)
            for j in range(lon_size)
        ]
        return lax.ppermute(send, both, route)

    bits = lat_size.bit_length() - 1
    sends = [keep[0]]
    for mine, theirs in zip(keep, arrived):
        sends += call(next_sum_kernel, [chunk], sends[-1], mine, theirs, name="chip_sum", unread=(0,))
    sends = sends[1:]
    received = [halving(0, send) for send in sends]
    send_rest, keep_rest = call(
        rest_kernel, [halves, halves], *sends, *inner[2:], *outer[2:], name="rest", unread=(0, 1), beside=True
    )
    received_rest = lax.ppermute(send_rest, "lon", sibling)
    results = call(
        output_kernel, [((WIN, 2 * width), BF)] * 2,
        keep_rest, *inner[:2], inner[3], *outer[:2], outer[3], qkv_weight, proj_weight,
        name="outputs", unread=(0,), flops=10**10,
    )
    (lon_back,) = call(pack_lon_kernel, [quarter], results[1], name="pack_lon", beside=True)
    lon_home = lax.ppermute(lon_back, both, back(lon_route))
    kept = [[keep_rest, received_rest, part] for part in received]
    slots = lat_size // 2
    for phase in range(1, bits):
        slots //= 2
        stay = ((slots, *chunk[0][1:]), BF)
        after = results[0]
        for index in range(2):
            send, keep = call(
                functools.partial(halve_kernel, index), [stay, stay], after, *kept[index],
                after, name=f"halve{slots}", unread=(0, 1 + len(kept[index])),
            )
            kept[index] = [keep, halving(phase, send)]
            after = send

    (diag_back,) = call(pack_diag_kernel, [quarter], send, results[1], name="pack_diag", unread=(0,))
    diag_home = lax.ppermute(diag_back, both, back(diag_route))

    rows = width // lon_size
    share = ((rows, split[2]), BF)
    (first_chunk,) = call(
        next_sum_kernel, [((1, split[1], split[2] // 2), F32)], lon_home, *kept[0],
        name="first_chunk", flops=LATER, unread=(0,),
    )
    parts = call(
        line_parts_kernel, [share] * (lon_size // 2), first_chunk, *kept[1], name="line_parts", flops=PARTS
    )
    arrived = [
        lax.ppermute(parts[step], "lon", [(j, j ^ (2 * step)) for j in range(lon_size)])
        for step in range(lon_size // 2 - 1, 0, -1)
    ]
    (lat_back,) = call(
        pack_lat_kernel, [((HALF + QUARTER, 2 * width), BF)], parts[1], *results, name="pack_lat", unread=(0,)
    )
    lat_home = lax.ppermute(lat_back, both, back(lat_route))
    (placed,) = call(
        place_kernel, [((TOKENS, 2 * width), F32)], *results, lon_home, diag_home, name="place"
    )
    (line_sum,) = call(
        next_sum_kernel, [share], placed, parts[0], *arrived, name="line_sum", flops=LONG, unread=(0,)
    )
    shared = [
        lax.ppermute(line_sum, "lat", [(i, i ^ step) for i in range(lat_size)]) for step in range(1, lat_size)
    ]
    field_out, d_fields, done = call(
        place_rest_kernel,
        [((TOKENS, width), BF), ((TOKENS, width), BF), ((8, LANES), F32)],
        placed, lat_home,
        name="place_rest",
    )
    vmem, anywhere = pl.BlockSpec(memory_space=pltpu.VMEM), pl.BlockSpec(memory_space=pl.ANY)
    qkv_grad, proj_grad = pl.pallas_call(
        finish_kernel,
        out_shape=[jax.ShapeDtypeStruct((rows, lanes * width), F32) for lanes in (3, 1)],
        in_specs=[anywhere, *[vmem] * lat_size],
        out_specs=[anywhere, anywhere],
        scratch_shapes=[
            pltpu.VMEM((rows, 4 * width), F32),
            pltpu.SemaphoreType.DMA((rows // FINISH_ROWS, 2)),
        ],
        compiler_params=pltpu.CompilerParams(vmem_limit_bytes=32 * 2**20),
        cost_estimate=pl.CostEstimate(flops=0, bytes_accessed=10**6, transcendentals=0),
        name="finish",
    )(done, line_sum, *shared)
    return (field_out.reshape(fields.shape), d_fields.reshape(fields.shape), qkv_grad, jnp.transpose(proj_grad))


def solution(mesh):
    placed = (P(None, "lat", "lon", None), P(None, "lat", "lon", None), P(), P())
    return jax.shard_map(
        per_device,
        mesh=mesh,
        in_specs=placed,
        out_specs=(
            P(None, "lat", "lon", None),
            P(None, "lat", "lon", None),
            P("lon", None),
            P(None, "lon"),
        ),
        check_vma=False,
    )
```

```python
import functools

import jax
import jax.numpy as jnp
from jax import lax
from jax.experimental import pallas as pl
from jax.experimental.pallas import tpu as pltpu
from jax.sharding import PartitionSpec as P

HEADS = 8
WIN_LAT = 6
WIN_LON = 12
LEVELS = 2
COLS = 24
HALF_LAT = WIN_LAT // 2
HALF_LON = WIN_LON // 2
HALF = LEVELS * HALF_LAT * WIN_LON
WIN = 2 * HALF
TOKENS = 2 * WIN
QUARTER = HALF // 2
LANES = 128

epsilon = 1e-05
LONG = 13 * 10**8
LOAD = 5 * 10**9
LATER = 10**9
PARTS = 5 * 10**9
BF = jnp.bfloat16
F32 = jnp.float32


def dot(a, b, dims):
    return lax.dot_general(a, b, (dims, ((), ())), preferred_element_type=F32)


NN = ((1,), (0,))
NT = ((1,), (1,))
TN = ((0,), (0,))


def div(x, by):
    return (x * ((65536 + by - 1) // by)) >> 16


def own_token(level, row, col):
    return level * (WIN_LAT * COLS) + row * COLS + col


def inner_token(v, first):
    level = div(v, HALF_LAT * WIN_LON)
    rest = v - level * (HALF_LAT * WIN_LON)
    row = div(rest, WIN_LON)
    return own_token(level, first + row, HALF_LON + rest - row * WIN_LON)


def half_token(v, first, col):
    level = div(v, HALF_LAT * HALF_LON)
    rest = v - level * (HALF_LAT * HALF_LON)
    row = div(rest, HALF_LON)
    return jnp.where(v < QUARTER, own_token(level, first + row, col + rest - row * HALF_LON), -1)


def sources():
    even = lax.rem(lax.axis_index("lon"), 2) == 0
    sent = jnp.where(even, 0, HALF_LAT)
    kept = HALF_LAT - sent
    outer = HALF_LON + WIN_LON
    return (
        (lambda v: inner_token(v, sent), HALF),
        (lambda v: half_token(v, sent, outer), QUARTER),
        (lambda v: half_token(v, sent, 0), QUARTER),
        (lambda v: half_token(v, kept, 0), QUARTER),
        (lambda v: inner_token(v, kept), HALF),
        (lambda v: half_token(v, kept, outer), HALF),
    )


def picks(source, rows, columns):
    index = source(lax.broadcasted_iota(jnp.int32, (rows, 1), 0))
    return (index == lax.broadcasted_iota(jnp.int32, (rows, columns), 1)).astype(BF)


def puts(source, rows, columns):
    index = source(lax.broadcasted_iota(jnp.int32, (1, columns), 1))
    return (lax.broadcasted_iota(jnp.int32, (rows, columns), 0) == index).astype(BF)


def first_rows(v):
    return v


def last_rows(v):
    return v - QUARTER


def order_kernel(*outs):
    for out, (source, rows) in zip(outs, sources()):
        out[...] = picks(source, rows, TOKENS)


def pack_kernel(fields, cotangent, *refs):
    count = len(refs) // 2
    width = fields.shape[1]
    for pick, out in zip(refs[:count], refs[count:]):
        out[:, :width] = dot(pick[...], fields[...], NN).astype(out.dtype)
        out[:, width:] = dot(pick[...], cotangent[...], NN).astype(out.dtype)


def swap_bits(index, size, core):
    bits = size.bit_length() - 1
    turned = sum(((index >> b) & 1) << (bits - 1 - b) for b in range(bits))
    return jnp.where(core == 0, index, turned)


def shares(transposed, out, lon, core_of, lon_size):
    rows = transposed.shape[0] // lon_size
    chip = lon >> 1
    for step in range(lon_size // 2):
        start = pl.multiple_of(((chip ^ step) * 2 + core_of) * rows, rows)
        out[step * rows : (step + 1) * rows, :] = transposed[pl.ds(start, rows), :]


def transpose_bf16(block):
    return jnp.transpose(block.astype(F32)).astype(BF)


def slot_product(slot, size, lat, core, windows, chunk=None):
    share = lat ^ swap_bits(slot, size, core)
    total = None
    for left, right in windows:
        lanes = right.shape[1] // size
        of_proj = (share >= 3 * size // 4).astype(jnp.int32)
        half = lanes // 2
        start, width = (share * lanes, lanes) if chunk is None else (share * lanes + chunk * half, half)
        part = dot(left[of_proj], right[:, pl.ds(pl.multiple_of(start, half), width)], NN)
        total = part if total is None else total + part
    return total


def normalise(x):
    mean = jnp.mean(x, -1, keepdims=True)
    centred = x - mean
    variance = jnp.mean(centred * centred, -1, keepdims=True)
    inv_std = lax.rsqrt(variance + epsilon)
    return centred * inv_std, inv_std


def project(both, qkv_weight, proj_weight):
    width = both.shape[1] // 2
    normed, _ = normalise(both[:, :width])
    projected = dot(normed.astype(BF), qkv_weight[...], NN)
    return normed, projected, dot(both[:, width:].astype(BF), proj_weight[...], NT)


def pack_rest_kernel(_, *refs):
    pack_kernel(*refs)


def own_kernel(inner_own, qkv_weight, proj_weight, normed, projected, d_mixed):
    normed[...], projected[...], d_mixed[...] = project(inner_own[...], qkv_weight, proj_weight)


def inner_kernel(own, own_normed, own_projected, own_d_mixed, lat_in, qkv_weight, proj_weight, send_grad, *refs):
    arrived = lat_in[...].astype(F32)
    parts = project(arrived, qkv_weight, proj_weight)
    both = jnp.concatenate([own[...], arrived], axis=0)
    mine = own_normed, own_projected, own_d_mixed
    parts = [jnp.concatenate([first[...], second], axis=0) for first, second in zip(mine, parts)]
    one_window(both, *parts, *refs)
    *_, right, left, _, _ = refs
    lat, core, size = place()
    for slot in range(1, size, 2):
        send_grad[slot // 2] = slot_product(slot, size, lat, 1 - core, [(left, right)], 0)


def outer_kernel(own, lon_in, lat_in, diag_in, qkv_weight, proj_weight, grad_so_far, send_a, *refs):
    last = picks(last_rows, HALF, QUARTER)
    both = jnp.concatenate(
        [
            own[...] + dot(last, lon_in[...], NN),
            dot(picks(first_rows, HALF, QUARTER), lat_in[...], NN) + dot(last, diag_in[...], NN),
        ],
        axis=0,
    )
    one_window(both, *project(both, qkv_weight, proj_weight), *refs)
    *_, right, left, _, _ = refs
    lat, core, size = place()
    for slot in range(1, size, 2):
        total = grad_so_far[slot // 2] + slot_product(slot, size, lat, 1 - core, [(left, right)], 0)
        send_a[slot // 2] = total.astype(BF)


def put_chunks(outs, slot, total):
    width = outs[0].shape[2]
    for chunk, out in enumerate(outs):
        out[slot] = total[:, chunk * width : (chunk + 1) * width].astype(BF)


def place():
    return lax.axis_index("lat"), lax.rem(lax.axis_index("lon"), 2), lax.axis_size("lat")


def one_window(
    both, normed, projected, d_mixed,
    windows_out, grads_out, left_keep, right, left_send, normed_t, grads_t,
):
    width = both.shape[1] // 2
    lat, core, lat_size = place()
    lon, lon_size = lax.axis_index("lon"), lax.axis_size("lon")
    even = core == 0
    blocks = both[:, :width], both[:, width:]
    x = blocks[0]
    windows_out[...] = x.astype(BF)
    grads = blocks[1].astype(BF)
    grads_out[...] = grads
    projected, d_mixed = projected.astype(BF), d_mixed.astype(BF)

    head_size = width // HEADS
    factor = head_size ** (-0.5)
    apart = jnp.where(even, lat == lat_size - 1, lat == 0).astype(jnp.int32)
    half_b = (lax.broadcasted_iota(jnp.int32, (WIN, 2 * WIN), 0) >= HALF).astype(jnp.int32)
    at_a = lax.broadcasted_iota(jnp.int32, (WIN, 2 * WIN), 1)
    at_a = jnp.where(at_a >= WIN, at_a - WIN, at_a)
    half_a = (at_a >= HALF).astype(jnp.int32)
    allowed = ((half_a != half_b).astype(jnp.int32) * apart) == 0
    first_head = lax.broadcasted_iota(jnp.int32, (WIN, LANES), 1) < head_size
    zero = jnp.zeros((WIN, LANES), BF)

    def split_heads(block):
        return jnp.concatenate([jnp.where(first_head, block, zero), jnp.where(first_head, zero, block)], axis=0)

    def join_heads(block):
        return jnp.where(first_head, block[:WIN], block[WIN:]).astype(BF)

    pairs = range(width // LANES)

    def blocks_of(array, lanes_from):
        return [array[:, lanes_from + pair * LANES : lanes_from + (pair + 1) * LANES] for pair in pairs]

    def store(out, lanes_from, blocks):
        for pair, block in zip(pairs, blocks):
            out[:, lanes_from + pair * LANES : lanes_from + (pair + 1) * LANES] = block.astype(out.dtype)

    k, v = blocks_of(projected, width), blocks_of(projected, 2 * width)
    q2 = [split_heads(block) for block in blocks_of(projected, 0)]
    dm2 = [split_heads(block) for block in blocks_of(d_mixed, 0)]
    scores = [jnp.where(allowed, dot(k[p], q2[p], NT) * factor, -1e30) for p in pairs]
    d_probs = [dot(v[p], dm2[p], NT) for p in pairs]
    exponents = [jnp.exp(s - jnp.max(s, 0, keepdims=True)) for s in scores]
    probs = [e * (1.0 / jnp.sum(e, 0, keepdims=True)) for e in exponents]
    probs_b = [p.astype(BF) for p in probs]
    store(right, 3 * width, [join_heads(dot(probs_b[p], v[p], TN)) for p in pairs])
    store(right, 2 * width, [dot(probs_b[p], dm2[p], NN) for p in pairs])
    d_scores = [
        (probs[p] * (d_probs[p] - jnp.sum(d_probs[p] * probs[p], 0, keepdims=True)) * factor).astype(BF)
        for p in pairs
    ]
    store(right, 0, [join_heads(dot(d_scores[p], k[p], TN)) for p in pairs])
    store(right, width, [dot(d_scores[p], q2[p], NN) for p in pairs])

    normed_t[...] = transpose_bf16(normed)
    grads_t[...] = transpose_bf16(grads)
    for index, source in enumerate((normed_t, grads_t)):
        shares(source, left_send.at[index], lon, 1 - core, lon_size)
        shares(source, left_keep.at[index], lon, core, lon_size)


def keep_kernel(*refs):
    *windows, send_b, keep_a, keep_b = refs
    windows = windows[:3], windows[3:]
    lat, core, size = place()
    for slot in range(1, size, 2):
        total = slot_product(slot, size, lat, 1 - core, [(w[2], w[1]) for w in windows], 1)
        send_b[slot // 2] = total.astype(BF)
    for slot in range(1, size, 2):
        put_chunks((keep_a, keep_b), slot // 2, slot_product(slot, size, lat, core, [w[:2] for w in windows]))


def rest_kernel(_, __, *refs):
    *windows, send_rest, keep_rest = refs
    windows = windows[:3], windows[3:]
    lat, core, size = place()
    for slot in range(0, size, 2):
        send_rest[slot // 2] = slot_product(slot, size, lat, 1 - core, [(w[2], w[1]) for w in windows]).astype(BF)
    for slot in range(0, size, 2):
        keep_rest[slot // 2] = slot_product(slot, size, lat, core, [(w[0], w[1]) for w in windows]).astype(BF)


def output_kernel(_, *refs):
    (*windows, qkv_weight, proj_weight, inner_results, outer_results) = refs
    per_window = windows[:3], windows[3:]
    width = proj_weight.shape[0]
    x, grads, right = (jnp.concatenate([w[i][...] for w in per_window], axis=0) for i in range(3))
    d_projected, mixed = right[:, : 3 * width], right[:, 3 * width :]
    x = x.astype(F32)
    normed, inv_std = normalise(x)
    output = (x + dot(mixed, proj_weight[...], NN)).astype(BF)
    d_normed = dot(d_projected, qkv_weight[...], NT)
    d_inputs = grads.astype(F32) + inv_std * (
        d_normed
        - jnp.mean(d_normed, -1, keepdims=True)
        - normed * jnp.mean(d_normed * normed, -1, keepdims=True)
    )
    d_inputs = d_inputs.astype(BF)
    for at, out in ((0, inner_results), (WIN, outer_results)):
        out[:, :width] = output[at : at + WIN]
        out[:, width:] = d_inputs[at : at + WIN]


def pack_lon_kernel(outer_results, lon_out):
    outer_x = outer_results[...].astype(F32)[:HALF].astype(BF)
    lon_out[...] = dot(puts(last_rows, QUARTER, HALF), outer_x, NN).astype(BF)


def pack_diag_kernel(_, outer_results, diag_out):
    outer_y = outer_results[...].astype(F32)[HALF:].astype(BF)
    diag_out[...] = dot(puts(last_rows, QUARTER, HALF), outer_y, NN).astype(BF)


def pack_lat_kernel(_, inner_results, outer_results, lat_out):
    inner_y = inner_results[...].astype(F32)[HALF:]
    outer_y = outer_results[...].astype(F32)[HALF:].astype(BF)
    lat_out[...] = jnp.concatenate([inner_y, dot(puts(first_rows, QUARTER, HALF), outer_y, NN)], axis=0).astype(BF)


def place_kernel(inner_results, outer_results, lon_in, diag_in, placed):
    _, _, lon, diag, inner_own, outer_own = (source for source, _ in sources())

    def only_first(source):
        return lambda v: jnp.where(v < HALF, source(v), -1)

    placed[...] = (
        dot(puts(only_first(inner_own), TOKENS, WIN), inner_results[...], NN)
        + dot(puts(only_first(outer_own), TOKENS, WIN), outer_results[...], NN)
        + dot(puts(lon, TOKENS, QUARTER), lon_in[...], NN)
        + dot(puts(diag, TOKENS, QUARTER), diag_in[...], NN)
    )


def place_rest_kernel(placed, lat_in, field_out, d_fields, done):
    done[...] = jnp.zeros_like(done)
    width = field_out.shape[1]
    inner_lat, outer_lat, *_ = (source for source, _ in sources())

    def lat(v):
        return jnp.where(v < HALF, inner_lat(v), outer_lat(v - HALF))

    total = (placed[...] + dot(puts(lat, TOKENS, HALF + QUARTER), lat_in[...], NN)).astype(BF)
    field_out[...] = total[:, :width]
    d_fields[...] = total[:, width:]


def halve_kernel(chunk, _, *refs):
    *parts, _, send, keep = refs
    width = send.shape[2]

    def lanes(part):
        return slice(None) if part.shape[2] == width else slice(chunk * width, (chunk + 1) * width)

    for slot in range(send.shape[0]):
        for out, source in ((send, 2 * slot + 1), (keep, 2 * slot)):
            out[slot] = sum(part[source, :, lanes(part)].astype(F32) for part in parts).astype(BF)


def line_parts_kernel(*refs):
    chunks, (keep, *sends) = (refs[:1], refs[1:3]), refs[3:]
    rows = keep.shape[0]
    for step, out in enumerate((keep, *sends)):
        at = slice(step * rows, (step + 1) * rows)
        totals = [sum(part[0, at].astype(F32) for part in parts) for parts in chunks]
        out[...] = jnp.concatenate(totals, axis=1).astype(out.dtype)


def next_sum_kernel(_, *refs):
    sum_kernel(*refs)


def sum_kernel(*refs):
    *parts, out = refs
    total = parts[0][...].astype(F32)
    for part in parts[1:]:
        total = total + part[...].astype(F32)
    out[...] = total.astype(out.dtype)


def finish_kernel(_, *refs):
    *parts, qkv_out, proj_out = refs
    lat, _, size = place()
    width = parts[0].shape[1]
    for step, part in enumerate(parts):
        share = lat ^ step
        total = part[...].astype(F32)
        of_qkv = 3 * size // 4

        @pl.when(share < of_qkv)
        def _():
            qkv_out[:, pl.ds(pl.multiple_of(share * width, width), width)] = total

        @pl.when(share >= of_qkv)
        def _():
            proj_out[:, pl.ds(pl.multiple_of((share - of_qkv) * width, width), width)] = total


def call(kernel, outs, *args, name, flops=0, limit=32, scratch=(), unread=(), beside=False):
    vmem = pl.BlockSpec(memory_space=pltpu.VMEM)
    anywhere = pl.BlockSpec(memory_space=pl.ANY)
    shapes = [jax.ShapeDtypeStruct(shape, dtype) for shape, dtype in outs]
    nbytes = 0 if beside else sum(a.size * a.dtype.itemsize for a in (*args, *shapes))
    return pl.pallas_call(
        kernel,
        out_shape=shapes,
        in_specs=[anywhere if i in unread else vmem for i in range(len(args))],
        out_specs=[vmem] * len(shapes),
        scratch_shapes=scratch,
        compiler_params=pltpu.CompilerParams(vmem_limit_bytes=limit * 2**20),
        cost_estimate=pl.CostEstimate(flops=flops, bytes_accessed=nbytes, transcendentals=0),
        name=name,
    )(*args)


def routes(lat_size, lon_size):
    lat, lon, diag = [], [], []
    for i in range(lat_size):
        for j in range(lon_size):
            step = -1 if j % 2 == 0 else 1
            before = (j - 1) % lon_size
            me = i * lon_size + j
            lat.append((me, ((i + step) % lat_size) * lon_size + j))
            lon.append((me, i * lon_size + before))
            diag.append((me, ((i - step) % lat_size) * lon_size + before))
    return lat, lon, diag


def per_device(fields, cotangent, qkv_weight, proj_weight):
    levels, row_count, col_count, width = fields.shape
    lat_size, lon_size = lax.axis_size("lat"), lax.axis_size("lon")
    both = ("lat", "lon")
    lat_route, lon_route, diag_route = routes(lat_size, lon_size)

    def back(route):
        return [(target, source) for source, target in route]

    own_fields = fields.reshape(TOKENS, width)
    own_grads = cotangent.reshape(TOKENS, width)
    lengths = (HALF, QUARTER, QUARTER, QUARTER, HALF, HALF)
    picked = call(order_kernel, [((rows, TOKENS), BF) for rows in lengths], name="order", flops=LOAD)
    pick_inner, pick_outer, pick_lon, pick_diag, pick_own, pick_outer_own = picked
    whole, half = ((HALF, 2 * width), F32), ((HALF, 2 * width), BF)
    quarter = ((QUARTER, 2 * width), BF)
    inner_lat, lon_piece = call(
        pack_kernel, [half, quarter], own_fields, own_grads, pick_inner, pick_lon, name="pack", flops=LOAD
    )
    outer_lat, diag_piece, outer_own, inner_own = call(
        pack_rest_kernel, [quarter, quarter, whole, whole],
        lon_piece, own_fields, own_grads, pick_outer, pick_diag, pick_outer_own, pick_own,
        name="pack_rest", flops=5 * 10**8, unread=(0,),
    )
    own_parts = call(
        own_kernel, [((HALF, lanes), F32) for lanes in (width, 3 * width, width)],
        inner_own, qkv_weight, proj_weight,
        name="own", flops=5 * 10**8,
    )
    inner_in = lax.ppermute(inner_lat, both, lat_route)
    lon_in = lax.ppermute(lon_piece, both, lon_route)
    outer_in = lax.ppermute(outer_lat, both, lat_route)
    diag_in = lax.ppermute(diag_piece, both, diag_route)

    split = (lat_size, width // 2, 4 * width // lat_size)
    halves = ((lat_size // 2, *split[1:]), BF)
    chunk = ((lat_size // 2, split[1], split[2] // 2), BF)
    per_window = [
        ((WIN, width), BF),
        ((WIN, width), BF),
        ((2, width // 2, WIN), BF),
        ((WIN, 4 * width), BF),
        ((2, width // 2, WIN), BF),
    ]
    scratch = [pltpu.VMEM((width, WIN), BF)] * 2
    grad_so_far, *inner = call(
        inner_kernel, [(chunk[0], F32), *per_window], inner_own, *own_parts, inner_in, qkv_weight, proj_weight,
        name="inner", flops=10**9, scratch=scratch,
    )
    send_a, *outer = call(
        outer_kernel, [chunk, *per_window],
        outer_own, lon_in, outer_in, diag_in, qkv_weight, proj_weight, grad_so_far,
        name="outer", flops=10**9, scratch=scratch,
    )
    sibling = [(j, j ^ 1) for j in range(lon_size)]
    send_b, *keep = call(keep_kernel, [chunk] * 3, *inner[2:], *outer[2:], name="keep", flops=10**9)
    arrived = [lax.ppermute(send, "lon", sibling) for send in (send_a, send_b)]

    def halving(phase, send):
        route = [
            (i * lon_size + j, (i ^ (1 << (phase if j % 2 == 0 else bits - 1 - phase))) * lon_size + j)
            for i in range(lat_size)
            for j in range(lon_size)
        ]
        return lax.ppermute(send, both, route)

    bits = lat_size.bit_length() - 1
    sends = [keep[0]]
    for mine, theirs in zip(keep, arrived):
        sends += call(next_sum_kernel, [chunk], sends[-1], mine, theirs, name="chip_sum", unread=(0,))
    sends = sends[1:]
    received = [halving(0, send) for send in sends]
    send_rest, keep_rest = call(
        rest_kernel, [halves, halves], *sends, *inner[2:], *outer[2:], name="rest", unread=(0, 1), beside=True
    )
    received_rest = lax.ppermute(send_rest, "lon", sibling)
    results = call(
        output_kernel, [((WIN, 2 * width), BF)] * 2,
        keep_rest, *inner[:2], inner[3], *outer[:2], outer[3], qkv_weight, proj_weight,
        name="outputs", unread=(0,), flops=10**10,
    )
    (lon_back,) = call(pack_lon_kernel, [quarter], results[1], name="pack_lon", beside=True)
    lon_home = lax.ppermute(lon_back, both, back(lon_route))
    kept = [[keep_rest, received_rest, part] for part in received]
    slots = lat_size // 2
    for phase in range(1, bits):
        slots //= 2
        stay = ((slots, *chunk[0][1:]), BF)
        after = results[0]
        for index in range(2):
            send, keep = call(
                functools.partial(halve_kernel, index), [stay, stay], after, *kept[index],
                after, name=f"halve{slots}", unread=(0, 1 + len(kept[index])),
            )
            kept[index] = [keep, halving(phase, send)]
            after = send

    (diag_back,) = call(pack_diag_kernel, [quarter], send, results[1], name="pack_diag", unread=(0,))
    diag_home = lax.ppermute(diag_back, both, back(diag_route))

    rows = width // lon_size
    share = ((rows, split[2]), BF)
    (first_chunk,) = call(
        next_sum_kernel, [((1, split[1], split[2] // 2), F32)], lon_home, *kept[0],
        name="first_chunk", flops=LATER, unread=(0,),
    )
    parts = call(
        line_parts_kernel, [share] * (lon_size // 2), first_chunk, *kept[1], name="line_parts", flops=PARTS
    )
    arrived = [
        lax.ppermute(parts[step], "lon", [(j, j ^ (2 * step)) for j in range(lon_size)])
        for step in range(lon_size // 2 - 1, 0, -1)
    ]
    (lat_back,) = call(
        pack_lat_kernel, [((HALF + QUARTER, 2 * width), BF)], parts[1], *results, name="pack_lat", unread=(0,)
    )
    lat_home = lax.ppermute(lat_back, both, back(lat_route))
    (placed,) = call(
        place_kernel, [((TOKENS, 2 * width), F32)], *results, lon_home, diag_home, name="place"
    )
    (line_sum,) = call(
        next_sum_kernel, [share], placed, parts[0], *arrived, name="line_sum", flops=LONG, unread=(0,)
    )
    shared = [
        lax.ppermute(line_sum, "lat", [(i, i ^ step) for i in range(lat_size)]) for step in range(1, lat_size)
    ]
    field_out, d_fields, done = call(
        place_rest_kernel,
        [((TOKENS, width), BF), ((TOKENS, width), BF), ((8, LANES), F32)],
        placed, lat_home,
        name="place_rest",
    )
    qkv_grad, proj_grad = call(
        finish_kernel,
        [((rows, 3 * width), F32), ((rows, width), F32)],
        done, line_sum, *shared,
        name="finish", unread=(0,),
    )
    return (field_out.reshape(fields.shape), d_fields.reshape(fields.shape), qkv_grad, jnp.transpose(proj_grad))


def solution(mesh):
    placed = (P(None, "lat", "lon", None), P(None, "lat", "lon", None), P(), P())
    return jax.shard_map(
        per_device,
        mesh=mesh,
        in_specs=placed,
        out_specs=(
            P(None, "lat", "lon", None),
            P(None, "lat", "lon", None),
            P("lon", None),
            P(None, "lon"),
        ),
        check_vma=False,
    )
```

```python
import functools

import jax
import jax.numpy as jnp
from jax import lax
from jax.experimental import pallas as pl
from jax.experimental.pallas import tpu as pltpu
from jax.sharding import PartitionSpec as P

HEADS = 8
WIN_LAT = 6
WIN_LON = 12
LEVELS = 2
COLS = 24
HALF_LAT = WIN_LAT // 2
HALF_LON = WIN_LON // 2
HALF = LEVELS * HALF_LAT * WIN_LON
WIN = 2 * HALF
TOKENS = 2 * WIN
QUARTER = HALF // 2
LANES = 128

epsilon = 1e-05
LONG = 13 * 10**8
LOAD = 5 * 10**9
LATER = 10**9
PARTS = 5 * 10**9
BF = jnp.bfloat16
F32 = jnp.float32


def dot(a, b, dims):
    return lax.dot_general(a, b, (dims, ((), ())), preferred_element_type=F32)


NN = ((1,), (0,))
NT = ((1,), (1,))
TN = ((0,), (0,))


def div(x, by):
    return (x * ((65536 + by - 1) // by)) >> 16


def own_token(level, row, col):
    return level * (WIN_LAT * COLS) + row * COLS + col


def inner_token(v, first):
    level = div(v, HALF_LAT * WIN_LON)
    rest = v - level * (HALF_LAT * WIN_LON)
    row = div(rest, WIN_LON)
    return own_token(level, first + row, HALF_LON + rest - row * WIN_LON)


def half_token(v, first, col):
    level = div(v, HALF_LAT * HALF_LON)
    rest = v - level * (HALF_LAT * HALF_LON)
    row = div(rest, HALF_LON)
    return jnp.where(v < QUARTER, own_token(level, first + row, col + rest - row * HALF_LON), -1)


def sources():
    even = lax.rem(lax.axis_index("lon"), 2) == 0
    sent = jnp.where(even, 0, HALF_LAT)
    kept = HALF_LAT - sent
    outer = HALF_LON + WIN_LON
    return (
        (lambda v: inner_token(v, sent), HALF),
        (lambda v: half_token(v, sent, outer), QUARTER),
        (lambda v: half_token(v, sent, 0), QUARTER),
        (lambda v: half_token(v, kept, 0), QUARTER),
        (lambda v: inner_token(v, kept), HALF),
        (lambda v: half_token(v, kept, outer), HALF),
    )


def picks(source, rows, columns):
    index = source(lax.broadcasted_iota(jnp.int32, (rows, 1), 0))
    return (index == lax.broadcasted_iota(jnp.int32, (rows, columns), 1)).astype(BF)


def puts(source, rows, columns):
    index = source(lax.broadcasted_iota(jnp.int32, (1, columns), 1))
    return (lax.broadcasted_iota(jnp.int32, (rows, columns), 0) == index).astype(BF)


def first_rows(v):
    return v


def last_rows(v):
    return v - QUARTER


def order_kernel(*outs):
    for out, (source, rows) in zip(outs, sources()):
        out[...] = picks(source, rows, TOKENS)


def pack_kernel(fields, cotangent, *refs):
    count = len(refs) // 2
    width = fields.shape[1]
    for pick, out in zip(refs[:count], refs[count:]):
        out[:, :width] = dot(pick[...], fields[...], NN).astype(out.dtype)
        out[:, width:] = dot(pick[...], cotangent[...], NN).astype(out.dtype)


def swap_bits(index, size, core):
    bits = size.bit_length() - 1
    turned = sum(((index >> b) & 1) << (bits - 1 - b) for b in range(bits))
    return jnp.where(core == 0, index, turned)


def shares(transposed, out, lon, core_of, lon_size):
    rows = transposed.shape[0] // lon_size
    chip = lon >> 1
    for step in range(lon_size // 2):
        start = pl.multiple_of(((chip ^ step) * 2 + core_of) * rows, rows)
        out[step * rows : (step + 1) * rows, :] = transposed[pl.ds(start, rows), :]


def transpose_bf16(block):
    return jnp.transpose(block.astype(F32)).astype(BF)


def slot_product(slot, size, lat, core, windows):
    share = lat ^ swap_bits(slot, size, core)
    total = None
    for left, right in windows:
        lanes = right.shape[1] // size
        of_proj = (share >= 3 * size // 4).astype(jnp.int32)
        part = dot(left[of_proj], right[:, pl.ds(pl.multiple_of(share * lanes, lanes), lanes)], NN)
        total = part if total is None else total + part
    return total


def normalise(x):
    mean = jnp.mean(x, -1, keepdims=True)
    centred = x - mean
    variance = jnp.mean(centred * centred, -1, keepdims=True)
    inv_std = lax.rsqrt(variance + epsilon)
    return centred * inv_std, inv_std


def project(both, qkv_weight, proj_weight):
    width = both.shape[1] // 2
    normed, _ = normalise(both[:, :width])
    projected = dot(normed.astype(BF), qkv_weight[...], NN)
    return normed, projected, dot(both[:, width:].astype(BF), proj_weight[...], NT)


def pack_rest_kernel(_, *refs):
    pack_kernel(*refs)


def own_kernel(
    fields, cotangent, pick_outer, pick_inner, qkv_weight, proj_weight,
    outer_own, inner_own, normed, projected, d_mixed,
):
    pack_kernel(fields, cotangent, pick_outer, pick_inner, outer_own, inner_own)
    normed[...], projected[...], d_mixed[...] = project(inner_own[...], qkv_weight, proj_weight)


def inner_kernel(own, own_normed, own_projected, own_d_mixed, lat_in, qkv_weight, proj_weight, send_grad, *refs):
    arrived = lat_in[...].astype(F32)
    parts = project(arrived, qkv_weight, proj_weight)
    both = jnp.concatenate([own[...], arrived], axis=0)
    mine = own_normed, own_projected, own_d_mixed
    parts = [jnp.concatenate([first[...], second], axis=0) for first, second in zip(mine, parts)]
    one_window(both, *parts, *refs)
    *_, right, left, _, _ = refs
    lat, core, size = place()
    for slot in range(1, size, 2):
        send_grad[slot // 2] = slot_product(slot, size, lat, 1 - core, [(left, right)])


def outer_kernel(own, lon_in, lat_in, diag_in, qkv_weight, proj_weight, grad_so_far, send_a, send_b, *refs):
    last = picks(last_rows, HALF, QUARTER)
    both = jnp.concatenate(
        [
            own[...] + dot(last, lon_in[...], NN),
            dot(picks(first_rows, HALF, QUARTER), lat_in[...], NN) + dot(last, diag_in[...], NN),
        ],
        axis=0,
    )
    one_window(both, *project(both, qkv_weight, proj_weight), *refs)
    *_, right, left, _, _ = refs
    lat, core, size = place()
    for slot in range(1, size, 2):
        total = grad_so_far[slot // 2] + slot_product(slot, size, lat, 1 - core, [(left, right)])
        put_chunks((send_a, send_b), slot // 2, total)


def put_chunks(outs, slot, total):
    width = outs[0].shape[2]
    for chunk, out in enumerate(outs):
        out[slot] = total[:, chunk * width : (chunk + 1) * width].astype(BF)


def place():
    return lax.axis_index("lat"), lax.rem(lax.axis_index("lon"), 2), lax.axis_size("lat")


def one_window(
    both, normed, projected, d_mixed,
    windows_out, grads_out, left_keep, right, left_send, normed_t, grads_t,
):
    width = both.shape[1] // 2
    lat, core, lat_size = place()
    lon, lon_size = lax.axis_index("lon"), lax.axis_size("lon")
    even = core == 0
    blocks = both[:, :width], both[:, width:]
    x = blocks[0]
    windows_out[...] = x.astype(BF)
    grads = blocks[1].astype(BF)
    grads_out[...] = grads
    projected, d_mixed = projected.astype(BF), d_mixed.astype(BF)

    head_size = width // HEADS
    factor = head_size ** (-0.5)
    apart = jnp.where(even, lat == lat_size - 1, lat == 0).astype(jnp.int32)
    half_b = (lax.broadcasted_iota(jnp.int32, (WIN, 2 * WIN), 0) >= HALF).astype(jnp.int32)
    at_a = lax.broadcasted_iota(jnp.int32, (WIN, 2 * WIN), 1)
    at_a = jnp.where(at_a >= WIN, at_a - WIN, at_a)
    half_a = (at_a >= HALF).astype(jnp.int32)
    allowed = ((half_a != half_b).astype(jnp.int32) * apart) == 0
    first_head = lax.broadcasted_iota(jnp.int32, (WIN, LANES), 1) < head_size
    zero = jnp.zeros((WIN, LANES), BF)

    def split_heads(block):
        return jnp.concatenate([jnp.where(first_head, block, zero), jnp.where(first_head, zero, block)], axis=0)

    def join_heads(block):
        return jnp.where(first_head, block[:WIN], block[WIN:]).astype(BF)

    pairs = range(width // LANES)

    def blocks_of(array, lanes_from):
        return [array[:, lanes_from + pair * LANES : lanes_from + (pair + 1) * LANES] for pair in pairs]

    def store(out, lanes_from, blocks):
        for pair, block in zip(pairs, blocks):
            out[:, lanes_from + pair * LANES : lanes_from + (pair + 1) * LANES] = block.astype(out.dtype)

    k, v = blocks_of(projected, width), blocks_of(projected, 2 * width)
    q2 = [split_heads(block) for block in blocks_of(projected, 0)]
    dm2 = [split_heads(block) for block in blocks_of(d_mixed, 0)]
    scores = [jnp.where(allowed, dot(k[p], q2[p], NT) * factor, -1e30) for p in pairs]
    d_probs = [dot(v[p], dm2[p], NT) for p in pairs]
    exponents = [jnp.exp(s - jnp.max(s, 0, keepdims=True)) for s in scores]
    probs = [e * (1.0 / jnp.sum(e, 0, keepdims=True)) for e in exponents]
    probs_b = [p.astype(BF) for p in probs]
    store(right, 3 * width, [join_heads(dot(probs_b[p], v[p], TN)) for p in pairs])
    store(right, 2 * width, [dot(probs_b[p], dm2[p], NN) for p in pairs])
    d_scores = [
        (probs[p] * (d_probs[p] - jnp.sum(d_probs[p] * probs[p], 0, keepdims=True)) * factor).astype(BF)
        for p in pairs
    ]
    store(right, 0, [join_heads(dot(d_scores[p], k[p], TN)) for p in pairs])
    store(right, width, [dot(d_scores[p], q2[p], NN) for p in pairs])

    normed_t[...] = transpose_bf16(normed)
    grads_t[...] = transpose_bf16(grads)
    for index, source in enumerate((normed_t, grads_t)):
        shares(source, left_send.at[index], lon, 1 - core, lon_size)
        shares(source, left_keep.at[index], lon, core, lon_size)


def keep_kernel(*refs):
    *windows, keep_a, keep_b = refs
    windows = [windows[:2], windows[2:]]
    lat, core, size = place()
    for slot in range(1, size, 2):
        put_chunks((keep_a, keep_b), slot // 2, slot_product(slot, size, lat, core, windows))


def rest_kernel(_, __, *refs):
    *windows, send_rest, keep_rest = refs
    windows = windows[:3], windows[3:]
    lat, core, size = place()
    for slot in range(0, size, 2):
        send_rest[slot // 2] = slot_product(slot, size, lat, 1 - core, [(w[2], w[1]) for w in windows]).astype(BF)
    for slot in range(0, size, 2):
        keep_rest[slot // 2] = slot_product(slot, size, lat, core, [(w[0], w[1]) for w in windows]).astype(BF)


def output_kernel(_, *refs):
    (*windows, qkv_weight, proj_weight, inner_results, outer_results) = refs
    per_window = windows[:3], windows[3:]
    width = proj_weight.shape[0]
    x, grads, right = (jnp.concatenate([w[i][...] for w in per_window], axis=0) for i in range(3))
    d_projected, mixed = right[:, : 3 * width], right[:, 3 * width :]
    x = x.astype(F32)
    normed, inv_std = normalise(x)
    output = (x + dot(mixed, proj_weight[...], NN)).astype(BF)
    d_normed = dot(d_projected, qkv_weight[...], NT)
    d_inputs = grads.astype(F32) + inv_std * (
        d_normed
        - jnp.mean(d_normed, -1, keepdims=True)
        - normed * jnp.mean(d_normed * normed, -1, keepdims=True)
    )
    d_inputs = d_inputs.astype(BF)
    for at, out in ((0, inner_results), (WIN, outer_results)):
        out[:, :width] = output[at : at + WIN]
        out[:, width:] = d_inputs[at : at + WIN]


def pack_lon_kernel(outer_results, lon_out):
    outer_x = outer_results[...].astype(F32)[:HALF].astype(BF)
    lon_out[...] = dot(puts(last_rows, QUARTER, HALF), outer_x, NN).astype(BF)


def pack_diag_kernel(_, outer_results, diag_out):
    outer_y = outer_results[...].astype(F32)[HALF:].astype(BF)
    diag_out[...] = dot(puts(last_rows, QUARTER, HALF), outer_y, NN).astype(BF)


def pack_lat_kernel(_, inner_results, outer_results, lat_out):
    inner_y = inner_results[...].astype(F32)[HALF:]
    outer_y = outer_results[...].astype(F32)[HALF:].astype(BF)
    lat_out[...] = jnp.concatenate([inner_y, dot(puts(first_rows, QUARTER, HALF), outer_y, NN)], axis=0).astype(BF)


def place_kernel(inner_results, outer_results, lon_in, diag_in, placed):
    _, _, lon, diag, inner_own, outer_own = (source for source, _ in sources())

    def only_first(source):
        return lambda v: jnp.where(v < HALF, source(v), -1)

    placed[...] = (
        dot(puts(only_first(inner_own), TOKENS, WIN), inner_results[...], NN)
        + dot(puts(only_first(outer_own), TOKENS, WIN), outer_results[...], NN)
        + dot(puts(lon, TOKENS, QUARTER), lon_in[...], NN)
        + dot(puts(diag, TOKENS, QUARTER), diag_in[...], NN)
    )


def place_rest_kernel(placed, lat_in, field_out, d_fields, done):
    done[...] = jnp.zeros_like(done)
    width = field_out.shape[1]
    inner_lat, outer_lat, *_ = (source for source, _ in sources())

    def lat(v):
        return jnp.where(v < HALF, inner_lat(v), outer_lat(v - HALF))

    total = (placed[...] + dot(puts(lat, TOKENS, HALF + QUARTER), lat_in[...], NN)).astype(BF)
    field_out[...] = total[:, :width]
    d_fields[...] = total[:, width:]


def halve_kernel(chunk, _, *refs):
    *parts, _, send, keep = refs
    width = send.shape[2]

    def lanes(part):
        return slice(None) if part.shape[2] == width else slice(chunk * width, (chunk + 1) * width)

    for slot in range(send.shape[0]):
        for out, source in ((send, 2 * slot + 1), (keep, 2 * slot)):
            out[slot] = sum(part[source, :, lanes(part)].astype(F32) for part in parts).astype(BF)


def line_parts_kernel(*refs):
    chunks, (keep, *sends) = (refs[:1], refs[1:3]), refs[3:]
    rows = keep.shape[0]
    for step, out in enumerate((keep, *sends)):
        at = slice(step * rows, (step + 1) * rows)
        totals = [sum(part[0, at].astype(F32) for part in parts) for parts in chunks]
        out[...] = jnp.concatenate(totals, axis=1).astype(out.dtype)


def next_sum_kernel(_, *refs):
    sum_kernel(*refs)


def sum_kernel(*refs):
    *parts, out = refs
    total = parts[0][...].astype(F32)
    for part in parts[1:]:
        total = total + part[...].astype(F32)
    out[...] = total.astype(out.dtype)


def finish_kernel(_, *refs):
    *parts, qkv_out, proj_out = refs
    lat, _, size = place()
    width = parts[0].shape[1]
    for step, part in enumerate(parts):
        share = lat ^ step
        total = part[...].astype(F32)
        of_qkv = 3 * size // 4

        @pl.when(share < of_qkv)
        def _():
            qkv_out[:, pl.ds(pl.multiple_of(share * width, width), width)] = total

        @pl.when(share >= of_qkv)
        def _():
            proj_out[:, pl.ds(pl.multiple_of((share - of_qkv) * width, width), width)] = total


def call(kernel, outs, *args, name, flops=0, limit=32, scratch=(), unread=(), beside=False):
    vmem = pl.BlockSpec(memory_space=pltpu.VMEM)
    anywhere = pl.BlockSpec(memory_space=pl.ANY)
    shapes = [jax.ShapeDtypeStruct(shape, dtype) for shape, dtype in outs]
    nbytes = 0 if beside else sum(a.size * a.dtype.itemsize for a in (*args, *shapes))
    return pl.pallas_call(
        kernel,
        out_shape=shapes,
        in_specs=[anywhere if i in unread else vmem for i in range(len(args))],
        out_specs=[vmem] * len(shapes),
        scratch_shapes=scratch,
        compiler_params=pltpu.CompilerParams(vmem_limit_bytes=limit * 2**20),
        cost_estimate=pl.CostEstimate(flops=flops, bytes_accessed=nbytes, transcendentals=0),
        name=name,
    )(*args)


def routes(lat_size, lon_size):
    lat, lon, diag = [], [], []
    for i in range(lat_size):
        for j in range(lon_size):
            step = -1 if j % 2 == 0 else 1
            before = (j - 1) % lon_size
            me = i * lon_size + j
            lat.append((me, ((i + step) % lat_size) * lon_size + j))
            lon.append((me, i * lon_size + before))
            diag.append((me, ((i - step) % lat_size) * lon_size + before))
    return lat, lon, diag


def per_device(fields, cotangent, qkv_weight, proj_weight):
    levels, row_count, col_count, width = fields.shape
    lat_size, lon_size = lax.axis_size("lat"), lax.axis_size("lon")
    both = ("lat", "lon")
    lat_route, lon_route, diag_route = routes(lat_size, lon_size)

    def back(route):
        return [(target, source) for source, target in route]

    own_fields = fields.reshape(TOKENS, width)
    own_grads = cotangent.reshape(TOKENS, width)
    lengths = (HALF, QUARTER, QUARTER, QUARTER, HALF, HALF)
    picked = call(order_kernel, [((rows, TOKENS), BF) for rows in lengths], name="order", flops=LOAD)
    pick_inner, pick_outer, pick_lon, pick_diag, pick_own, pick_outer_own = picked
    whole, half = ((HALF, 2 * width), F32), ((HALF, 2 * width), BF)
    quarter = ((QUARTER, 2 * width), BF)
    inner_lat, lon_piece = call(
        pack_kernel, [half, quarter], own_fields, own_grads, pick_inner, pick_lon, name="pack", flops=LOAD
    )
    outer_lat, diag_piece = call(
        pack_rest_kernel, [quarter, quarter], lon_piece, own_fields, own_grads, pick_outer, pick_diag,
        name="pack_rest", flops=5 * 10**8, unread=(0,),
    )
    outer_own, inner_own, *own_parts = call(
        own_kernel, [whole, whole, *(((HALF, lanes), F32) for lanes in (width, 3 * width, width))],
        own_fields, own_grads, pick_outer_own, pick_own, qkv_weight, proj_weight,
        name="own", flops=5 * 10**8,
    )
    inner_in = lax.ppermute(inner_lat, both, lat_route)
    lon_in = lax.ppermute(lon_piece, both, lon_route)
    outer_in = lax.ppermute(outer_lat, both, lat_route)
    diag_in = lax.ppermute(diag_piece, both, diag_route)

    split = (lat_size, width // 2, 4 * width // lat_size)
    halves = ((lat_size // 2, *split[1:]), BF)
    chunk = ((lat_size // 2, split[1], split[2] // 2), BF)
    per_window = [
        ((WIN, width), BF),
        ((WIN, width), BF),
        ((2, width // 2, WIN), BF),
        ((WIN, 4 * width), BF),
        ((2, width // 2, WIN), BF),
    ]
    scratch = [pltpu.VMEM((width, WIN), BF)] * 2
    grad_so_far, *inner = call(
        inner_kernel, [(halves[0], F32), *per_window], inner_own, *own_parts, inner_in, qkv_weight, proj_weight,
        name="inner", flops=10**9, scratch=scratch,
    )
    send_a, send_b, *outer = call(
        outer_kernel, [chunk, chunk, *per_window],
        outer_own, lon_in, outer_in, diag_in, qkv_weight, proj_weight, grad_so_far,
        name="outer", flops=10**9, scratch=scratch,
    )
    sibling = [(j, j ^ 1) for j in range(lon_size)]
    arrived = [lax.ppermute(send, "lon", sibling) for send in (send_a, send_b)]
    keep = call(keep_kernel, [chunk, chunk], *inner[2:4], *outer[2:4], name="keep", flops=10**9)

    def halving(phase, send):
        route = [
            (i * lon_size + j, (i ^ (1 << (phase if j % 2 == 0 else bits - 1 - phase))) * lon_size + j)
            for i in range(lat_size)
            for j in range(lon_size)
        ]
        return lax.ppermute(send, both, route)

    bits = lat_size.bit_length() - 1
    sends = [keep[0]]
    for mine, theirs in zip(keep, arrived):
        sends += call(next_sum_kernel, [chunk], sends[-1], mine, theirs, name="chip_sum", unread=(0,))
    sends = sends[1:]
    received = [halving(0, send) for send in sends]
    send_rest, keep_rest = call(
        rest_kernel, [halves, halves], *sends, *inner[2:], *outer[2:], name="rest", unread=(0, 1), beside=True
    )
    received_rest = lax.ppermute(send_rest, "lon", sibling)
    results = call(
        output_kernel, [((WIN, 2 * width), BF)] * 2,
        keep_rest, *inner[:2], inner[3], *outer[:2], outer[3], qkv_weight, proj_weight,
        name="outputs", unread=(0,), flops=10**10,
    )
    (lon_back,) = call(pack_lon_kernel, [quarter], results[1], name="pack_lon", beside=True)
    lon_home = lax.ppermute(lon_back, both, back(lon_route))
    kept = [[keep_rest, received_rest, part] for part in received]
    slots = lat_size // 2
    for phase in range(1, bits):
        slots //= 2
        stay = ((slots, *chunk[0][1:]), BF)
        after = results[0]
        for index in range(2):
            send, keep = call(
                functools.partial(halve_kernel, index), [stay, stay], after, *kept[index],
                after, name=f"halve{slots}", unread=(0, 1 + len(kept[index])),
            )
            kept[index] = [keep, halving(phase, send)]
            after = send

    (diag_back,) = call(pack_diag_kernel, [quarter], send, results[1], name="pack_diag", unread=(0,))
    diag_home = lax.ppermute(diag_back, both, back(diag_route))

    rows = width // lon_size
    share = ((rows, split[2]), BF)
    (first_chunk,) = call(
        next_sum_kernel, [((1, split[1], split[2] // 2), F32)], lon_home, *kept[0],
        name="first_chunk", flops=LATER, unread=(0,),
    )
    parts = call(
        line_parts_kernel, [share] * (lon_size // 2), first_chunk, *kept[1], name="line_parts", flops=PARTS
    )
    arrived = [
        lax.ppermute(parts[step], "lon", [(j, j ^ (2 * step)) for j in range(lon_size)])
        for step in range(lon_size // 2 - 1, 0, -1)
    ]
    (lat_back,) = call(
        pack_lat_kernel, [((HALF + QUARTER, 2 * width), BF)], parts[1], *results, name="pack_lat", unread=(0,)
    )
    lat_home = lax.ppermute(lat_back, both, back(lat_route))
    (placed,) = call(
        place_kernel, [((TOKENS, 2 * width), F32)], *results, lon_home, diag_home, name="place"
    )
    (line_sum,) = call(
        next_sum_kernel, [share], placed, parts[0], *arrived, name="line_sum", flops=LONG, unread=(0,)
    )
    shared = [
        lax.ppermute(line_sum, "lat", [(i, i ^ step) for i in range(lat_size)]) for step in range(1, lat_size)
    ]
    field_out, d_fields, done = call(
        place_rest_kernel,
        [((TOKENS, width), BF), ((TOKENS, width), BF), ((8, LANES), F32)],
        placed, lat_home,
        name="place_rest",
    )
    qkv_grad, proj_grad = call(
        finish_kernel,
        [((rows, 3 * width), F32), ((rows, width), F32)],
        done, line_sum, *shared,
        name="finish", unread=(0,),
    )
    return (field_out.reshape(fields.shape), d_fields.reshape(fields.shape), qkv_grad, jnp.transpose(proj_grad))


def solution(mesh):
    placed = (P(None, "lat", "lon", None), P(None, "lat", "lon", None), P(), P())
    return jax.shard_map(
        per_device,
        mesh=mesh,
        in_specs=placed,
        out_specs=(
            P(None, "lat", "lon", None),
            P(None, "lat", "lon", None),
            P("lon", None),
            P(None, "lon"),
        ),
        check_vma=False,
    )
```

```python
import functools

import jax
import jax.numpy as jnp
from jax import lax
from jax.experimental import pallas as pl
from jax.experimental.pallas import tpu as pltpu
from jax.sharding import PartitionSpec as P

HEADS = 8
WIN_LAT = 6
WIN_LON = 12
LEVELS = 2
COLS = 24
HALF_LAT = WIN_LAT // 2
HALF_LON = WIN_LON // 2
HALF = LEVELS * HALF_LAT * WIN_LON
WIN = 2 * HALF
TOKENS = 2 * WIN
QUARTER = HALF // 2
LANES = 128

epsilon = 1e-05
LONG = 13 * 10**8
LOAD = 5 * 10**9
LATER = 10**9
PARTS = 5 * 10**9
BF = jnp.bfloat16
F32 = jnp.float32


def dot(a, b, dims):
    return lax.dot_general(a, b, (dims, ((), ())), preferred_element_type=F32)


NN = ((1,), (0,))
NT = ((1,), (1,))
TN = ((0,), (0,))


def div(x, by):
    return (x * ((65536 + by - 1) // by)) >> 16


def own_token(level, row, col):
    return level * (WIN_LAT * COLS) + row * COLS + col


def inner_token(v, first):
    level = div(v, HALF_LAT * WIN_LON)
    rest = v - level * (HALF_LAT * WIN_LON)
    row = div(rest, WIN_LON)
    return own_token(level, first + row, HALF_LON + rest - row * WIN_LON)


def half_token(v, first, col):
    level = div(v, HALF_LAT * HALF_LON)
    rest = v - level * (HALF_LAT * HALF_LON)
    row = div(rest, HALF_LON)
    return jnp.where(v < QUARTER, own_token(level, first + row, col + rest - row * HALF_LON), -1)


def sources():
    even = lax.rem(lax.axis_index("lon"), 2) == 0
    sent = jnp.where(even, 0, HALF_LAT)
    kept = HALF_LAT - sent
    outer = HALF_LON + WIN_LON
    return (
        (lambda v: inner_token(v, sent), HALF),
        (lambda v: half_token(v, sent, outer), QUARTER),
        (lambda v: half_token(v, sent, 0), QUARTER),
        (lambda v: half_token(v, kept, 0), QUARTER),
        (lambda v: inner_token(v, kept), HALF),
        (lambda v: half_token(v, kept, outer), HALF),
    )


def picks(source, rows, columns):
    index = source(lax.broadcasted_iota(jnp.int32, (rows, 1), 0))
    return (index == lax.broadcasted_iota(jnp.int32, (rows, columns), 1)).astype(BF)


def puts(source, rows, columns):
    index = source(lax.broadcasted_iota(jnp.int32, (1, columns), 1))
    return (lax.broadcasted_iota(jnp.int32, (rows, columns), 0) == index).astype(BF)


def first_rows(v):
    return v


def last_rows(v):
    return v - QUARTER


def order_kernel(*outs):
    for out, (source, rows) in zip(outs, sources()):
        out[...] = picks(source, rows, TOKENS)


def pack_kernel(fields, cotangent, *refs):
    count = len(refs) // 2
    width = fields.shape[1]
    for pick, out in zip(refs[:count], refs[count:]):
        out[:, :width] = dot(pick[...], fields[...], NN).astype(out.dtype)
        out[:, width:] = dot(pick[...], cotangent[...], NN).astype(out.dtype)


def swap_bits(index, size, core):
    bits = size.bit_length() - 1
    turned = sum(((index >> b) & 1) << (bits - 1 - b) for b in range(bits))
    return jnp.where(core == 0, index, turned)


def shares(transposed, out, lon, core_of, lon_size):
    rows = transposed.shape[0] // lon_size
    chip = lon >> 1
    for step in range(lon_size // 2):
        start = pl.multiple_of(((chip ^ step) * 2 + core_of) * rows, rows)
        out[step * rows : (step + 1) * rows, :] = transposed[pl.ds(start, rows), :]


def transpose_bf16(block):
    return jnp.transpose(block.astype(F32)).astype(BF)


def slot_product(slot, size, lat, core, windows):
    share = lat ^ swap_bits(slot, size, core)
    total = None
    for left, right in windows:
        lanes = right.shape[1] // size
        of_proj = (share >= 3 * size // 4).astype(jnp.int32)
        part = dot(left[of_proj], right[:, pl.ds(pl.multiple_of(share * lanes, lanes), lanes)], NN)
        total = part if total is None else total + part
    return total


def normalise(x):
    mean = jnp.mean(x, -1, keepdims=True)
    centred = x - mean
    variance = jnp.mean(centred * centred, -1, keepdims=True)
    inv_std = lax.rsqrt(variance + epsilon)
    return centred * inv_std, inv_std


def project(both, qkv_weight, proj_weight):
    width = both.shape[1] // 2
    normed, _ = normalise(both[:, :width])
    projected = dot(normed.astype(BF), qkv_weight[...], NN)
    return normed, projected, dot(both[:, width:].astype(BF), proj_weight[...], NT)


def pack_rest_kernel(_, *refs):
    pack_kernel(*refs)


def own_kernel(
    fields, cotangent, pick_outer, pick_inner, qkv_weight, proj_weight,
    outer_own, inner_own, normed, projected, d_mixed,
):
    pack_kernel(fields, cotangent, pick_outer, pick_inner, outer_own, inner_own)
    normed[...], projected[...], d_mixed[...] = project(inner_own[...], qkv_weight, proj_weight)


def inner_kernel(own, own_normed, own_projected, own_d_mixed, lat_in, qkv_weight, proj_weight, send_grad, *refs):
    arrived = lat_in[...].astype(F32)
    parts = project(arrived, qkv_weight, proj_weight)
    both = jnp.concatenate([own[...], arrived], axis=0)
    mine = own_normed, own_projected, own_d_mixed
    parts = [jnp.concatenate([first[...], second], axis=0) for first, second in zip(mine, parts)]
    one_window(both, *parts, *refs)
    *_, right, left, _, _ = refs
    lat, core, size = place()
    for slot in range(1, size, 2):
        send_grad[slot // 2] = slot_product(slot, size, lat, 1 - core, [(left, right)])


def outer_kernel(own, lon_in, lat_in, diag_in, qkv_weight, proj_weight, grad_so_far, send_a, send_b, *refs):
    last = picks(last_rows, HALF, QUARTER)
    both = jnp.concatenate(
        [
            own[...] + dot(last, lon_in[...], NN),
            dot(picks(first_rows, HALF, QUARTER), lat_in[...], NN) + dot(last, diag_in[...], NN),
        ],
        axis=0,
    )
    one_window(both, *project(both, qkv_weight, proj_weight), *refs)
    *_, right, left, _, _ = refs
    lat, core, size = place()
    for slot in range(1, size, 2):
        total = grad_so_far[slot // 2] + slot_product(slot, size, lat, 1 - core, [(left, right)])
        put_chunks((send_a, send_b), slot // 2, total)


def put_chunks(outs, slot, total):
    width = outs[0].shape[2]
    for chunk, out in enumerate(outs):
        out[slot] = total[:, chunk * width : (chunk + 1) * width].astype(BF)


def place():
    return lax.axis_index("lat"), lax.rem(lax.axis_index("lon"), 2), lax.axis_size("lat")


def one_window(
    both, normed, projected, d_mixed,
    windows_out, grads_out, left_keep, right, left_send, normed_t, grads_t,
):
    width = both.shape[1] // 2
    lat, core, lat_size = place()
    lon, lon_size = lax.axis_index("lon"), lax.axis_size("lon")
    even = core == 0
    blocks = both[:, :width], both[:, width:]
    x = blocks[0]
    windows_out[...] = x.astype(BF)
    grads = blocks[1].astype(BF)
    grads_out[...] = grads
    projected, d_mixed = projected.astype(BF), d_mixed.astype(BF)

    head_size = width // HEADS
    factor = head_size ** (-0.5)
    apart = jnp.where(even, lat == lat_size - 1, lat == 0).astype(jnp.int32)
    half_b = (lax.broadcasted_iota(jnp.int32, (WIN, 2 * WIN), 0) >= HALF).astype(jnp.int32)
    at_a = lax.broadcasted_iota(jnp.int32, (WIN, 2 * WIN), 1)
    at_a = jnp.where(at_a >= WIN, at_a - WIN, at_a)
    half_a = (at_a >= HALF).astype(jnp.int32)
    allowed = ((half_a != half_b).astype(jnp.int32) * apart) == 0
    first_head = lax.broadcasted_iota(jnp.int32, (WIN, LANES), 1) < head_size
    zero = jnp.zeros((WIN, LANES), BF)

    def split_heads(block):
        return jnp.concatenate([jnp.where(first_head, block, zero), jnp.where(first_head, zero, block)], axis=0)

    def join_heads(block):
        return jnp.where(first_head, block[:WIN], block[WIN:]).astype(BF)

    pairs = range(width // LANES)

    def blocks_of(array, lanes_from):
        return [array[:, lanes_from + pair * LANES : lanes_from + (pair + 1) * LANES] for pair in pairs]

    def store(out, lanes_from, blocks):
        for pair, block in zip(pairs, blocks):
            out[:, lanes_from + pair * LANES : lanes_from + (pair + 1) * LANES] = block.astype(out.dtype)

    k, v = blocks_of(projected, width), blocks_of(projected, 2 * width)
    q2 = [split_heads(block) for block in blocks_of(projected, 0)]
    dm2 = [split_heads(block) for block in blocks_of(d_mixed, 0)]
    scores = [jnp.where(allowed, dot(k[p], q2[p], NT) * factor, -1e30) for p in pairs]
    d_probs = [dot(v[p], dm2[p], NT) for p in pairs]
    exponents = [jnp.exp(s - jnp.max(s, 0, keepdims=True)) for s in scores]
    probs = [e * (1.0 / jnp.sum(e, 0, keepdims=True)) for e in exponents]
    probs_b = [p.astype(BF) for p in probs]
    store(right, 3 * width, [join_heads(dot(probs_b[p], v[p], TN)) for p in pairs])
    store(right, 2 * width, [dot(probs_b[p], dm2[p], NN) for p in pairs])
    d_scores = [
        (probs[p] * (d_probs[p] - jnp.sum(d_probs[p] * probs[p], 0, keepdims=True)) * factor).astype(BF)
        for p in pairs
    ]
    store(right, 0, [join_heads(dot(d_scores[p], k[p], TN)) for p in pairs])
    store(right, width, [dot(d_scores[p], q2[p], NN) for p in pairs])

    normed_t[...] = transpose_bf16(normed)
    grads_t[...] = transpose_bf16(grads)
    for index, source in enumerate((normed_t, grads_t)):
        shares(source, left_send.at[index], lon, 1 - core, lon_size)
        shares(source, left_keep.at[index], lon, core, lon_size)


def keep_kernel(*refs):
    *windows, keep_a, keep_b = refs
    windows = [windows[:2], windows[2:]]
    lat, core, size = place()
    for slot in range(1, size, 2):
        put_chunks((keep_a, keep_b), slot // 2, slot_product(slot, size, lat, core, windows))


def rest_kernel(_, __, *refs):
    *windows, send_rest, keep_rest = refs
    windows = windows[:3], windows[3:]
    lat, core, size = place()
    for slot in range(0, size, 2):
        send_rest[slot // 2] = slot_product(slot, size, lat, 1 - core, [(w[2], w[1]) for w in windows]).astype(BF)
    for slot in range(0, size, 2):
        keep_rest[slot // 2] = slot_product(slot, size, lat, core, [(w[0], w[1]) for w in windows]).astype(BF)


def output_kernel(_, *refs):
    (*windows, qkv_weight, proj_weight, inner_results, outer_results) = refs
    per_window = windows[:3], windows[3:]
    width = proj_weight.shape[0]
    x, grads, right = (jnp.concatenate([w[i][...] for w in per_window], axis=0) for i in range(3))
    d_projected, mixed = right[:, : 3 * width], right[:, 3 * width :]
    x = x.astype(F32)
    normed, inv_std = normalise(x)
    output = (x + dot(mixed, proj_weight[...], NN)).astype(BF)
    d_normed = dot(d_projected, qkv_weight[...], NT)
    d_inputs = grads.astype(F32) + inv_std * (
        d_normed
        - jnp.mean(d_normed, -1, keepdims=True)
        - normed * jnp.mean(d_normed * normed, -1, keepdims=True)
    )
    d_inputs = d_inputs.astype(BF)
    for at, out in ((0, inner_results), (WIN, outer_results)):
        out[:, :width] = output[at : at + WIN]
        out[:, width:] = d_inputs[at : at + WIN]


def pack_lon_kernel(outer_results, lon_out):
    outer_x = outer_results[...].astype(F32)[:HALF].astype(BF)
    lon_out[...] = dot(puts(last_rows, QUARTER, HALF), outer_x, NN).astype(BF)


def pack_diag_kernel(_, outer_results, diag_out):
    outer_y = outer_results[...].astype(F32)[HALF:].astype(BF)
    diag_out[...] = dot(puts(last_rows, QUARTER, HALF), outer_y, NN).astype(BF)


def pack_lat_kernel(_, inner_results, outer_results, lat_out):
    inner_y = inner_results[...].astype(F32)[HALF:]
    outer_y = outer_results[...].astype(F32)[HALF:].astype(BF)
    lat_out[...] = jnp.concatenate([inner_y, dot(puts(first_rows, QUARTER, HALF), outer_y, NN)], axis=0).astype(BF)


def place_kernel(inner_results, outer_results, lon_in, diag_in, placed):
    _, _, lon, diag, inner_own, outer_own = (source for source, _ in sources())

    def only_first(source):
        return lambda v: jnp.where(v < HALF, source(v), -1)

    placed[...] = (
        dot(puts(only_first(inner_own), TOKENS, WIN), inner_results[...], NN)
        + dot(puts(only_first(outer_own), TOKENS, WIN), outer_results[...], NN)
        + dot(puts(lon, TOKENS, QUARTER), lon_in[...], NN)
        + dot(puts(diag, TOKENS, QUARTER), diag_in[...], NN)
    )


def place_rest_kernel(placed, lat_in, field_out, d_fields, done):
    done[...] = jnp.zeros_like(done)
    width = field_out.shape[1]
    inner_lat, outer_lat, *_ = (source for source, _ in sources())

    def lat(v):
        return jnp.where(v < HALF, inner_lat(v), outer_lat(v - HALF))

    total = (placed[...] + dot(puts(lat, TOKENS, HALF + QUARTER), lat_in[...], NN)).astype(BF)
    field_out[...] = total[:, :width]
    d_fields[...] = total[:, width:]


def halve_kernel(chunk, _, *refs):
    *parts, _, send, keep = refs
    width = send.shape[2]

    def lanes(part):
        return slice(None) if part.shape[2] == width else slice(chunk * width, (chunk + 1) * width)

    for slot in range(send.shape[0]):
        for out, source in ((send, 2 * slot + 1), (keep, 2 * slot)):
            out[slot] = sum(part[source, :, lanes(part)].astype(F32) for part in parts).astype(BF)


def line_parts_kernel(*refs):
    chunks, (keep, *sends) = (refs[:1], refs[1:3]), refs[3:]
    rows = keep.shape[0]
    for step, out in enumerate((keep, *sends)):
        at = slice(step * rows, (step + 1) * rows)
        totals = [sum(part[0, at].astype(F32) for part in parts) for parts in chunks]
        out[...] = jnp.concatenate(totals, axis=1).astype(out.dtype)


def next_sum_kernel(_, *refs):
    sum_kernel(*refs)


def sum_kernel(*refs):
    *parts, out = refs
    total = parts[0][...].astype(F32)
    for part in parts[1:]:
        total = total + part[...].astype(F32)
    out[...] = total.astype(out.dtype)


def finish_kernel(_, *refs):
    *parts, qkv_out, proj_out = refs
    lat, _, size = place()
    width = parts[0].shape[1]
    for step, part in enumerate(parts):
        share = lat ^ step
        total = part[...].astype(F32)
        of_qkv = 3 * size // 4

        @pl.when(share < of_qkv)
        def _():
            qkv_out[:, pl.ds(pl.multiple_of(share * width, width), width)] = total

        @pl.when(share >= of_qkv)
        def _():
            proj_out[:, pl.ds(pl.multiple_of((share - of_qkv) * width, width), width)] = total


def call(kernel, outs, *args, name, flops=0, limit=32, scratch=(), unread=(), beside=False):
    vmem = pl.BlockSpec(memory_space=pltpu.VMEM)
    anywhere = pl.BlockSpec(memory_space=pl.ANY)
    shapes = [jax.ShapeDtypeStruct(shape, dtype) for shape, dtype in outs]
    nbytes = 0 if beside else sum(a.size * a.dtype.itemsize for a in (*args, *shapes))
    return pl.pallas_call(
        kernel,
        out_shape=shapes,
        in_specs=[anywhere if i in unread else vmem for i in range(len(args))],
        out_specs=[vmem] * len(shapes),
        scratch_shapes=scratch,
        compiler_params=pltpu.CompilerParams(vmem_limit_bytes=limit * 2**20),
        cost_estimate=pl.CostEstimate(flops=flops, bytes_accessed=nbytes, transcendentals=0),
        name=name,
    )(*args)


def routes(lat_size, lon_size):
    lat, lon, diag = [], [], []
    for i in range(lat_size):
        for j in range(lon_size):
            step = -1 if j % 2 == 0 else 1
            before = (j - 1) % lon_size
            me = i * lon_size + j
            lat.append((me, ((i + step) % lat_size) * lon_size + j))
            lon.append((me, i * lon_size + before))
            diag.append((me, ((i - step) % lat_size) * lon_size + before))
    return lat, lon, diag


def per_device(fields, cotangent, qkv_weight, proj_weight):
    levels, row_count, col_count, width = fields.shape
    lat_size, lon_size = lax.axis_size("lat"), lax.axis_size("lon")
    both = ("lat", "lon")
    lat_route, lon_route, diag_route = routes(lat_size, lon_size)

    def back(route):
        return [(target, source) for source, target in route]

    own_fields = fields.reshape(TOKENS, width)
    own_grads = cotangent.reshape(TOKENS, width)
    lengths = (HALF, QUARTER, QUARTER, QUARTER, HALF, HALF)
    picked = call(order_kernel, [((rows, TOKENS), BF) for rows in lengths], name="order", flops=LOAD)
    pick_inner, pick_outer, pick_lon, pick_diag, pick_own, pick_outer_own = picked
    whole, half = ((HALF, 2 * width), F32), ((HALF, 2 * width), BF)
    quarter = ((QUARTER, 2 * width), BF)
    (inner_lat,) = call(pack_kernel, [half], own_fields, own_grads, pick_inner, name="pack", flops=LOAD)
    (lon_piece,) = call(
        pack_rest_kernel, [quarter], inner_lat, own_fields, own_grads, pick_lon, name="pack_piece", unread=(0,)
    )
    outer_lat, diag_piece = call(
        pack_rest_kernel, [quarter, quarter], lon_piece, own_fields, own_grads, pick_outer, pick_diag,
        name="pack_rest", flops=5 * 10**8, unread=(0,),
    )
    outer_own, inner_own, *own_parts = call(
        own_kernel, [whole, whole, *(((HALF, lanes), F32) for lanes in (width, 3 * width, width))],
        own_fields, own_grads, pick_outer_own, pick_own, qkv_weight, proj_weight,
        name="own", flops=5 * 10**8,
    )
    inner_in = lax.ppermute(inner_lat, both, lat_route)
    lon_in = lax.ppermute(lon_piece, both, lon_route)
    outer_in = lax.ppermute(outer_lat, both, lat_route)
    diag_in = lax.ppermute(diag_piece, both, diag_route)

    split = (lat_size, width // 2, 4 * width // lat_size)
    halves = ((lat_size // 2, *split[1:]), BF)
    chunk = ((lat_size // 2, split[1], split[2] // 2), BF)
    per_window = [
        ((WIN, width), BF),
        ((WIN, width), BF),
        ((2, width // 2, WIN), BF),
        ((WIN, 4 * width), BF),
        ((2, width // 2, WIN), BF),
    ]
    scratch = [pltpu.VMEM((width, WIN), BF)] * 2
    grad_so_far, *inner = call(
        inner_kernel, [(halves[0], F32), *per_window], inner_own, *own_parts, inner_in, qkv_weight, proj_weight,
        name="inner", flops=10**9, scratch=scratch,
    )
    send_a, send_b, *outer = call(
        outer_kernel, [chunk, chunk, *per_window],
        outer_own, lon_in, outer_in, diag_in, qkv_weight, proj_weight, grad_so_far,
        name="outer", flops=10**9, scratch=scratch,
    )
    sibling = [(j, j ^ 1) for j in range(lon_size)]
    arrived = [lax.ppermute(send, "lon", sibling) for send in (send_a, send_b)]
    keep = call(keep_kernel, [chunk, chunk], *inner[2:4], *outer[2:4], name="keep", flops=10**9)

    def halving(phase, send):
        route = [
            (i * lon_size + j, (i ^ (1 << (phase if j % 2 == 0 else bits - 1 - phase))) * lon_size + j)
            for i in range(lat_size)
            for j in range(lon_size)
        ]
        return lax.ppermute(send, both, route)

    bits = lat_size.bit_length() - 1
    sends = [keep[0]]
    for mine, theirs in zip(keep, arrived):
        sends += call(next_sum_kernel, [chunk], sends[-1], mine, theirs, name="chip_sum", unread=(0,))
    sends = sends[1:]
    received = [halving(0, send) for send in sends]
    send_rest, keep_rest = call(
        rest_kernel, [halves, halves], *sends, *inner[2:], *outer[2:], name="rest", unread=(0, 1), beside=True
    )
    received_rest = lax.ppermute(send_rest, "lon", sibling)
    results = call(
        output_kernel, [((WIN, 2 * width), BF)] * 2,
        keep_rest, *inner[:2], inner[3], *outer[:2], outer[3], qkv_weight, proj_weight,
        name="outputs", unread=(0,), flops=10**10,
    )
    (lon_back,) = call(pack_lon_kernel, [quarter], results[1], name="pack_lon", beside=True)
    lon_home = lax.ppermute(lon_back, both, back(lon_route))
    kept = [[keep_rest, received_rest, part] for part in received]
    slots = lat_size // 2
    for phase in range(1, bits):
        slots //= 2
        stay = ((slots, *chunk[0][1:]), BF)
        after = results[0]
        for index in range(2):
            send, keep = call(
                functools.partial(halve_kernel, index), [stay, stay], after, *kept[index],
                after, name=f"halve{slots}", unread=(0, 1 + len(kept[index])),
            )
            kept[index] = [keep, halving(phase, send)]
            after = send

    (diag_back,) = call(pack_diag_kernel, [quarter], send, results[1], name="pack_diag", unread=(0,))
    diag_home = lax.ppermute(diag_back, both, back(diag_route))

    rows = width // lon_size
    share = ((rows, split[2]), BF)
    (first_chunk,) = call(
        next_sum_kernel, [((1, split[1], split[2] // 2), F32)], lon_home, *kept[0],
        name="first_chunk", flops=LATER, unread=(0,),
    )
    parts = call(
        line_parts_kernel, [share] * (lon_size // 2), first_chunk, *kept[1], name="line_parts", flops=PARTS
    )
    arrived = [
        lax.ppermute(parts[step], "lon", [(j, j ^ (2 * step)) for j in range(lon_size)])
        for step in range(lon_size // 2 - 1, 0, -1)
    ]
    (lat_back,) = call(
        pack_lat_kernel, [((HALF + QUARTER, 2 * width), BF)], parts[1], *results, name="pack_lat", unread=(0,)
    )
    lat_home = lax.ppermute(lat_back, both, back(lat_route))
    (placed,) = call(
        place_kernel, [((TOKENS, 2 * width), F32)], *results, lon_home, diag_home, name="place"
    )
    (line_sum,) = call(
        next_sum_kernel, [share], placed, parts[0], *arrived, name="line_sum", flops=LONG, unread=(0,)
    )
    shared = [
        lax.ppermute(line_sum, "lat", [(i, i ^ step) for i in range(lat_size)]) for step in range(1, lat_size)
    ]
    field_out, d_fields, done = call(
        place_rest_kernel,
        [((TOKENS, width), BF), ((TOKENS, width), BF), ((8, LANES), F32)],
        placed, lat_home,
        name="place_rest",
    )
    qkv_grad, proj_grad = call(
        finish_kernel,
        [((rows, 3 * width), F32), ((rows, width), F32)],
        done, line_sum, *shared,
        name="finish", unread=(0,),
    )
    return (field_out.reshape(fields.shape), d_fields.reshape(fields.shape), qkv_grad, jnp.transpose(proj_grad))


def solution(mesh):
    placed = (P(None, "lat", "lon", None), P(None, "lat", "lon", None), P(), P())
    return jax.shard_map(
        per_device,
        mesh=mesh,
        in_specs=placed,
        out_specs=(
            P(None, "lat", "lon", None),
            P(None, "lat", "lon", None),
            P("lon", None),
            P(None, "lon"),
        ),
        check_vma=False,
    )
```
